32 devices in a mesh: rows: 8 (over z, x), width: 4 (over y, core).
Axes of the slice: x: 2, y: 2, z: 4, core: 2. Of those that a mesh axis runs over, the one named last changes fastest.
Arguments:
- x_in: bfloat16 [768, 4096], P('width', 'rows'), may hold values from -6 to 6
- history: bfloat16 [30, 768, 4096], P(None, 'width', 'rows'), may hold values from -6 to 6
- cotangent: bfloat16 [768, 4096], P('width', 'rows'), may hold values from -6 to 6
- counts: int32 [8], P('rows'), may hold values from 128 to 512, as said below
- positions: int32 [4096], P('rows'), may hold values from 0 to 1022, as said below
- mix_weights: float32 [30], replicated, may hold values from -0.3 to 0.3
- self_weight: float32 [1], replicated, may hold values from 0.7 to 1.3
- first_norm_gain: float32 [768], P('width'), may hold values from 0.5 to 1.5
- first_norm_bias: float32 [768], P('width'), may hold values from -3 to 3
- w_qkv: bfloat16 [3, 768, 768], P(None, 'width'), may hold values from -0.21875 to 0.21875
- w_out: bfloat16 [768, 768], P('width'), may hold values from -0.875 to 0.875
- second_norm_gain: float32 [768], P('width'), may hold values from 0.5 to 1.5
- second_norm_bias: float32 [768], P('width'), may hold values from -3 to 3
- w_up: bfloat16 [768, 3072], P(None, 'width'), may hold values from -0.21875 to 0.21875
- w_down: bfloat16 [3072, 768], P('width'), may hold values from -0.109375 to 0.109375
Outputs:
- mixed: bfloat16 [768, 4096], P('width', 'rows')
- d_input: float32 [768, 4096], P('width', 'rows')
- d_history: bfloat16 [30, 768, 4096], P(None, 'width', 'rows')
- d_mix: float32 [30], replicated
- d_self: float32 [1], replicated
- d_gain1: float32 [768], P('width')
- d_bias1: float32 [768], P('width')
- d_w_qkv: float32 [3, 768, 768], P(None, 'width')
- d_w_out: float32 [768, 768], P('width')
- d_gain2: float32 [768], P('width')
- d_bias2: float32 [768], P('width')
- d_w_up: float32 [768, 3072], P(None, 'width')
- d_w_down: float32 [3072, 768], P('width')
The draws below stay inside these ranges and needn't reach their ends.
Inputs may be any that keep to these rules, and one draw needn't show every extreme that they name: `counts`: one sequence has 512 real tokens and another 512 // 4; real tokens come first in a sequence. `positions`: 0 at the first token of each sequence, strictly increasing within it by 1 to 3.
All inputs are finite; a program needn't handle non-finite values.
Results may differ from the reference program's by a relative error of at most 0.011.
Values may be sent and summed in bfloat16 or wider, within the bound.
No kernel may reach another device: no remote copies, remote signals or barrier semaphores. Data moves between devices by JAX's collectives and lax.ppermute only.
A program may use at most 128 MiB of HBM per device.

```python
import jax
import jax.numpy as jnp
from jax import lax

D = 768
HEADS = 12
HEAD_DIM = 64
FF = 3072
HIST = 30
TOK_DEV = 512
SEQS = 8
TOKENS = 4096


def draw_counts(key, part):
    key = jax.random.fold_in(key, 11)
    base_key, pick_key = jax.random.split(key)
    values = jax.random.randint(base_key, (SEQS,), TOK_DEV // 4, TOK_DEV + 1)
    shuffled = jax.random.permutation(pick_key, SEQS)
    values = values.at[shuffled[0]].set(TOK_DEV)
    values = values.at[shuffled[1]].set(TOK_DEV // 4)
    return values.astype(jnp.int32)


def draw_positions(key, part):
    key = jax.random.fold_in(key, 23)
    random_bits = jax.random.randint(key, (SEQS, TOK_DEV), 0, 2)
    offsets = jnp.arange(TOK_DEV, dtype=jnp.int32)
    inner_rows = (offsets > 0) & (offsets < TOK_DEV - 1)
    random_bits = jnp.where(inner_rows[None, :], random_bits, 0)
    return (2 * offsets[None, :] - random_bits).reshape(TOKENS).astype(jnp.int32)


def level_of(own_key, shape, cuts, least, largest):
    loudness = 1.0
    for dim, blocks in cuts:
        draws = jax.random.uniform(jax.random.fold_in(jax.random.fold_in(own_key, 6), dim), (blocks,), jnp.float32, least / len(cuts), largest / len(cuts))
        loudness = loudness * jnp.repeat(jnp.exp(draws), shape[dim] // blocks).reshape((-1,) + (1,) * (len(shape) - 1 - dim))
    return loudness


def noise(rng, extent, width, limit, shards=(), kind=jnp.bfloat16):
    drawn = width * jax.random.normal(rng, extent, jnp.float32)
    if shards:
        drawn = drawn * level_of(rng, extent, shards, -0.22, 0.18)
    return jnp.clip(drawn, -limit, limit).astype(kind)


def setup_inputs(seed: int = 0) -> dict:
    arg_keys = jax.random.split(jax.random.key(seed), 16)
    x_in = noise(arg_keys[0], (D, TOKENS), 1.0, 6.0, ((0, 4), (1, 8)))
    history = noise(arg_keys[1], (HIST, D, TOKENS), 1.0, 6.0, ((1, 4), (2, 8)))
    cotangent = noise(arg_keys[2], (D, TOKENS), 1.0, 6.0, ((0, 4), (1, 8)))
    counts = draw_counts(jax.random.fold_in(arg_keys[15], 71), 0)
    positions = draw_positions(jax.random.fold_in(arg_keys[15], 71), 0)
    mix_weights = jnp.clip(jax.random.uniform(arg_keys[5], (HIST,), jnp.float32, -0.3, 0.3), -0.3, 0.3)
    self_weight = jnp.clip(1.0 + 0.06 * jax.random.normal(arg_keys[6], (1,), jnp.float32), 0.7, 1.3)
    first_norm_gain = jnp.clip(1.0 + 0.1 * jax.random.normal(arg_keys[7], (D,), jnp.float32), 0.5, 1.5)
    first_norm_bias = noise(arg_keys[8], (D,), 0.3, 3.0, ((0, 4),), jnp.float32)
    w_qkv = noise(arg_keys[9], (3, D, D), D ** -0.5, 0.21875, ((1, 4),))
    w_out = noise(arg_keys[10], (D, D), (D // 16) ** -0.5, 0.875, ((0, 4),))
    second_norm_gain = jnp.clip(1.0 + 0.1 * jax.random.normal(arg_keys[11], (D,), jnp.float32), 0.5, 1.5)
    second_norm_bias = noise(arg_keys[12], (D,), 0.3, 3.0, ((0, 4),), jnp.float32)
    w_up = noise(arg_keys[13], (D, FF), D ** -0.5, 0.21875, ((1, 4),))
    w_down = noise(arg_keys[14], (FF, D), FF ** -0.5, 0.109375, ((0, 4),))
    return {"x_in": x_in, "history": history, "cotangent": cotangent, "counts": counts, "positions": positions, "mix_weights": mix_weights, "self_weight": self_weight, "first_norm_gain": first_norm_gain, "first_norm_bias": first_norm_bias, "w_qkv": w_qkv, "w_out": w_out, "second_norm_gain": second_norm_gain, "second_norm_bias": second_norm_bias, "w_up": w_up, "w_down": w_down}


@jax.custom_vjp
def low(v):
    return lax.optimization_barrier(v.astype(jnp.bfloat16)).astype(jnp.float32)

@jax.custom_vjp
def low_back(v):
    return v

def low_keep(v):
    return (low(v), None)

def low_pass(kept, grad):
    return (grad,)

def back_keep(v):
    return (v, None)

def back_low(kept, grad):
    return (low(grad),)
low.defvjp(low_keep, low_pass)
low_back.defvjp(back_keep, back_low)
EPSILON = 1e-05
HIGHEST_PRECISION = lax.Precision.HIGHEST

def layer_norm(values, layernorm_gain, norm_bias):
    centre = values - lax.optimization_barrier(jnp.mean(values, axis=-1, keepdims=True))
    spread = lax.optimization_barrier(jnp.mean(centre * centre, axis=-1, keepdims=True))
    return centre * lax.rsqrt(spread + EPSILON) * layernorm_gain + norm_bias

def angle_table(positions, head_width):
    freq_index = jnp.arange(head_width // 2, dtype=jnp.float32)
    inverse = 1.0 / 10000.0 ** (freq_index * 2.0 / head_width)
    return positions.astype(jnp.float32)[:, None] * inverse[None, :]

def rotary(values, angles):
    half_width = values.shape[-1] // 2
    cosine = jnp.cos(angles)[:, None, :]
    sine_table = jnp.sin(angles)[:, None, :]
    front_part = values[..., :half_width]
    back_part = values[..., half_width:]
    return jnp.concatenate([front_part * cosine - back_part * sine_table, back_part * cosine + front_part * sine_table], axis=-1)

def block(input_rows, positions, gain_one, bias_one, qkv_weight, out_weight, gain_two, bias_two, up_weight, down_weight):
    length = input_rows.shape[0]
    normed = low(layer_norm(input_rows, gain_one, bias_one))
    project = low_back(jnp.dot(normed, qkv_weight, precision=HIGHEST_PRECISION)).reshape(length, 3, HEADS, HEAD_DIM)
    angles = angle_table(positions, HEAD_DIM)
    queries = low(rotary(project[:, 0], angles))
    keys_rot = low(rotary(project[:, 1], angles))
    values_in = low(project[:, 2])
    scores = low_back(jnp.einsum('qhd,khd->hqk', queries, keys_rot, precision=HIGHEST_PRECISION) * HEAD_DIM ** (-0.5))
    causal = jnp.arange(length)[:, None] >= jnp.arange(length)[None, :]
    scores = jnp.where(causal[None], scores, -1e+30)
    soft_weights = jax.nn.softmax(scores, axis=-1)
    mixed_heads = jnp.einsum('hqk,khd->qhd', low(soft_weights), values_in, precision=HIGHEST_PRECISION).reshape(length, HEADS * HEAD_DIM)
    mixed_heads = low(low_back(mixed_heads))
    attended = low_back(jnp.dot(mixed_heads, out_weight, precision=HIGHEST_PRECISION))
    between_layers = input_rows + attended
    second_normalized = low(layer_norm(between_layers, gain_two, bias_two))
    hidden = low_back(jnp.dot(second_normalized, up_weight, precision=HIGHEST_PRECISION))
    active = low(jax.nn.gelu(hidden))
    return between_layers + low_back(jnp.dot(active, down_weight, precision=HIGHEST_PRECISION))

def reference(x_in, history, cotangent, counts, positions, mix_weights, self_weight, first_norm_gain, first_norm_bias, w_qkv, w_out, second_norm_gain, second_norm_bias, w_up, w_down):
    device_rows = TOKENS // TOK_DEV
    seq_positions = positions.reshape(device_rows, TOK_DEV)

    def forward(input_rows, mixing, self_mix, gain_one, bias_one, qkv_blocks, out_weight, gain_two, bias_two, up_weight, down_weight, past_layers):
        qkv_weight = jnp.transpose(qkv_blocks, (2, 0, 1)).reshape(D, 3 * D)

        def one_sequence(seq_pair):
            return block(seq_pair[0], seq_pair[1], gain_one, bias_one, qkv_weight, out_weight, gain_two, bias_two, up_weight, down_weight)
        token_major = input_rows.T.reshape(device_rows, TOK_DEV, D)
        outputs = lax.map(jax.checkpoint(one_sequence), (token_major, seq_positions))
        outputs = outputs.reshape(TOKENS, D).T

        def add_layer(running, layer_pair):
            return (running + layer_pair[0] * layer_pair[1].astype(jnp.float32), None)
        mixed_out, unused = lax.scan(add_layer, self_mix[0] * outputs, (mixing, past_layers))
        return mixed_out
    live_total = jnp.sum(counts).astype(jnp.float32)
    loss_scale = jnp.float32(TOKENS) / live_total
    live_rows = jnp.arange(TOKENS) % TOK_DEV < jnp.repeat(counts, TOK_DEV)
    grad_out = cotangent.astype(jnp.float32) * jnp.where(live_rows, loss_scale, 0.0)[None, :]
    primals = (x_in.astype(jnp.float32), mix_weights, self_weight, first_norm_gain, first_norm_bias, w_qkv.astype(jnp.float32), w_out.astype(jnp.float32), second_norm_gain, second_norm_bias, w_up.astype(jnp.float32), w_down.astype(jnp.float32), history)
    mixed_out, pullback = jax.vjp(forward, *primals)
    gradients = pullback(grad_out)
    return (mixed_out.astype(jnp.bfloat16), gradients[0], gradients[11], gradients[1], gradients[2], gradients[3], gradients[4], gradients[5], gradients[6], gradients[7], gradients[8], gradients[9], gradients[10])
```

```python
import functools

import jax
import jax.numpy as jnp
from jax import lax
from jax.experimental import pallas as pl
from jax.experimental.pallas import tpu as pltpu
from jax.sharding import PartitionSpec as P

HEAD_DIM = 64
EPSILON = 1e-05
BF16 = jnp.bfloat16
F32 = jnp.float32
VMEM_LIMIT = 56 * 1024 * 1024


def radices(count):
    found = []
    for radix in (2, 4, 8, 8, 8):
        if count % radix == 0 and count > 1:
            found.append(radix)
            count //= radix
    if count > 1:
        found.append(count)
    return found


def chunks_of(count, rows):
    while rows % (16 * count):
        count //= 2
    return count


def xor_send(value, axis, size, offset):
    return lax.ppermute(value, axis, [(i, i ^ offset) for i in range(size)])


def tree_sum(parts):
    while len(parts) > 1:
        parts = [parts[i] + parts[i + 1] for i in range(0, len(parts), 2)]
    return parts[0]


def sum_small(value, axis, size):
    stride = 1
    for radix in radices(size):
        value = tree_sum([value] + [xor_send(value, axis, size, e * stride) for e in range(1, radix)])
        stride *= radix
    return value


def by_width(pieces, width_index):
    low, high = width_index % 2 == 1, width_index // 2 == 1
    first = jnp.where(low, jnp.concatenate([pieces[1], pieces[0]]), jnp.concatenate([pieces[0], pieces[1]]))
    second = jnp.where(low, jnp.concatenate([pieces[3], pieces[2]]), jnp.concatenate([pieces[2], pieces[3]]))
    return jnp.where(high, jnp.concatenate([second, first]), jnp.concatenate([first, second]))


def gather_width(shard, width_index, width):
    near = xor_send(shard, "width", width, 1)
    far = xor_send(shard, "width", width, 2)
    both = xor_send(far, "width", width, 1)
    return by_width([shard, near, far, both], width_index)


def swap_halves(value):
    half = value.shape[-1] // 2
    return jnp.concatenate([value[..., half:], value[..., :half]], axis=-1)


def weight_gradient_kernel(pairs, me_ref, *refs):
    operands, (send_ref, keep_ref), (scratch,) = refs[: 2 * pairs], refs[2 * pairs : -1], refs[-1:]
    half, rows = keep_ref.shape[0], keep_ref.shape[1]
    start = 0
    for i in range(pairs):
        left, right = operands[2 * i], operands[2 * i + 1]
        count = left.shape[0]
        scratch[start : start + count] = lax.dot_general(
            left[...], right[...], (((1,), (1,)), ((), ())), preferred_element_type=F32
        )
        start += count
    for place in range(half):
        for low, target in ((1, send_ref), (0, keep_ref)):
            chunk = (me_ref[0] % (2 * half)) ^ (2 * place + low)
            target[place] = scratch[pl.ds(pl.multiple_of(chunk * rows, rows), rows), :].astype(BF16)


def weight_gradient(me, row_devices, *operands):
    pairs = len(operands) // 2
    total = sum(operands[2 * i].shape[0] for i in range(pairs))
    columns = operands[1].shape[0]
    count = chunks_of(row_devices, total)
    out = jax.ShapeDtypeStruct((count // 2, total // count, columns), BF16)
    vmem = pl.BlockSpec(memory_space=pltpu.VMEM)
    return pl.pallas_call(
        functools.partial(weight_gradient_kernel, pairs),
        out_shape=(out, out),
        in_specs=[pl.BlockSpec(memory_space=pltpu.SMEM)] + [vmem] * (2 * pairs),
        out_specs=(vmem, vmem),
        scratch_shapes=[pltpu.VMEM((total, columns), F32)],
        compiler_params=pltpu.CompilerParams(vmem_limit_bytes=VMEM_LIMIT),
        cost_estimate=pl.CostEstimate(
            flops=2 * total * columns * operands[0].shape[1], bytes_accessed=4 * total * columns, transcendentals=0
        ),
    )(me, *operands)


def place_kernel(bounds, me_ref, *refs):
    pieces, outs = refs[: -len(bounds)], refs[-len(bounds) :]
    rows = pieces[0].shape[0]
    for e, piece in enumerate(pieces):
        chunk = (me_ref[0] % len(pieces)) ^ e
        for (start, stop), out in zip(bounds, outs):

            @pl.when((chunk * rows >= start) & (chunk * rows < stop))
            def _():
                at = pl.multiple_of(chunk * rows - start, rows)
                out[pl.ds(at, rows), :] = piece[...].astype(F32)


def place(me, pieces, sizes):
    columns = pieces[0].shape[1]
    bounds, start = [], 0
    for size in sizes:
        bounds.append((start, start + size))
        start += size
    vmem = pl.BlockSpec(memory_space=pltpu.VMEM)
    return pl.pallas_call(
        functools.partial(place_kernel, tuple(bounds)),
        out_shape=tuple(jax.ShapeDtypeStruct((size, columns), F32) for size in sizes),
        in_specs=[pl.BlockSpec(memory_space=pltpu.SMEM)] + [vmem] * len(pieces),
        out_specs=tuple(vmem for _ in sizes),
        compiler_params=pltpu.CompilerParams(vmem_limit_bytes=VMEM_LIMIT),
        cost_estimate=pl.CostEstimate(flops=0, bytes_accessed=6 * start * columns, transcendentals=0),
    )(me, *pieces)


def reduce_gradient(me, row_devices, sizes, send, keep):
    count = 2 * send.shape[0]
    stages = radices(count)
    recv = xor_send(send, "rows", row_devices, 1)
    value = (keep.astype(F32) + recv.astype(F32)).astype(BF16)
    stride = 2
    for radix in stages[1:]:
        value = value.reshape((-1, radix) + value.shape[1:])
        parts = [value[:, 0]] + [xor_send(value[:, e], "rows", row_devices, e * stride) for e in range(1, radix)]
        value = tree_sum([part.astype(F32) for part in parts]).astype(BF16)
        stride *= radix
    chunk = value.reshape(value.shape[-2:])
    for radix in radices(row_devices // count):
        parts = [chunk] + [xor_send(chunk, "rows", row_devices, e * stride) for e in range(1, radix)]
        chunk = tree_sum([part.astype(F32) for part in parts]).astype(BF16)
        stride *= radix
    pieces = [chunk]
    strides = [1]
    for radix in stages[:-1]:
        strides.append(strides[-1] * radix)
    for radix, stride in reversed(list(zip(stages, strides))):
        grown = [None] * (len(pieces) * radix)
        for i, piece in enumerate(pieces):
            grown[i * radix] = piece
            for e in range(1, radix):
                grown[i * radix + e] = xor_send(piece, "rows", row_devices, e * stride)
        pieces = grown
    return place(me, pieces, sizes)


def history_kernel(mix_ref, history_ref, grad_ref, running_ref, d_history_ref, d_mix_ref):
    grad = grad_ref[...]
    layers = history_ref.shape[0]
    running = jnp.zeros_like(grad)
    sums = []
    for j in range(layers):
        layer = history_ref[j].astype(F32)
        weight = mix_ref[j]
        running = running + weight * layer
        d_history_ref[j] = (weight * grad).astype(BF16)
        sums.append(jnp.sum(grad * layer, axis=0, keepdims=True))
    running_ref[...] = running
    d_mix_ref[0] = jnp.concatenate(sums, axis=0)


def mix_history(mix_weights, history, grad):
    layers, features, tokens = history.shape
    block = 32
    steps = features // block
    return pl.pallas_call(
        history_kernel,
        grid=(steps,),
        out_shape=(
            jax.ShapeDtypeStruct((features, tokens), F32),
            jax.ShapeDtypeStruct(history.shape, BF16),
            jax.ShapeDtypeStruct((steps, layers, tokens), F32),
        ),
        in_specs=[
            pl.BlockSpec(memory_space=pltpu.SMEM),
            pl.BlockSpec((layers, block, tokens), lambda i: (0, i, 0)),
            pl.BlockSpec((block, tokens), lambda i: (i, 0)),
        ],
        out_specs=(
            pl.BlockSpec((block, tokens), lambda i: (i, 0)),
            pl.BlockSpec((layers, block, tokens), lambda i: (0, i, 0)),
            pl.BlockSpec((1, layers, tokens), lambda i: (i, 0, 0)),
        ),
        compiler_params=pltpu.CompilerParams(vmem_limit_bytes=VMEM_LIMIT),
        cost_estimate=pl.CostEstimate(
            flops=6 * history.size, bytes_accessed=4 * history.size, transcendentals=0
        ),
    )(mix_weights, history, grad)


def dot(left, right, left_dim, right_dim):
    return lax.dot_general(left, right, (((left_dim,), (right_dim,)), ((), ())), preferred_element_type=F32)


def normalise(values):
    centred = values - jnp.mean(values, axis=0, keepdims=True)
    scale = lax.rsqrt(jnp.mean(centred * centred, axis=0, keepdims=True) + EPSILON)
    return centred * scale, scale


def rotate(values, cosine, sine):
    front, back = jnp.split(values, 2, axis=1)
    return jnp.concatenate([front * cosine - back * sine, back * cosine + front * sine], axis=1)


def gelu_and_slope(hidden):
    inner = 0.7978845608028654 * (hidden + 0.044715 * hidden * hidden * hidden)
    curve = jnp.tanh(inner)
    slope = 0.5 * (1.0 + curve) + 0.5 * hidden * (1.0 - curve * curve) * 0.7978845608028654 * (
        1.0 + 3 * 0.044715 * hidden * hidden
    )
    return 0.5 * hidden * (1.0 + curve), slope


def local(
    width,
    row_devices,
    x_in,
    history,
    cotangent,
    counts,
    positions,
    mix_weights,
    self_weight,
    first_norm_gain,
    first_norm_bias,
    w_qkv,
    w_out,
    second_norm_gain,
    second_norm_bias,
    w_up,
    w_down,
):
    part, tokens = x_in.shape
    model = w_out.shape[1]
    heads = part // HEAD_DIM
    half = tokens // 2
    at_width = lax.axis_index("width")
    odd = at_width % 2
    me = lax.axis_index("rows").astype(jnp.int32)[None]
    score_scale = HEAD_DIM ** (-0.5)

    def own_first(value):
        return jnp.where(odd == 1, swap_halves(value), value)

    def own_rows(value, index):
        return lax.dynamic_slice_in_dim(value, index * part, part, 0)

    def to_rows_of_width(partial):
        blocks = partial.reshape(width // 2, 2, part, tokens)
        send = swap_halves(lax.dynamic_index_in_dim(blocks, 1 - odd, 1, False).astype(BF16))
        keep = lax.dynamic_index_in_dim(blocks, odd, 1, False)
        chip = keep + xor_send(send, "width", width, 1).astype(F32)
        side = at_width // 2
        send = lax.dynamic_index_in_dim(chip, 1 - side, 0, False).astype(BF16)
        return lax.dynamic_index_in_dim(chip, side, 0, False) + xor_send(send, "width", width, 2).astype(F32)

    def sum_own_tokens(weight, weight_dim, right):
        send = dot(weight, right[:, half:], weight_dim, 0).astype(BF16)
        recv = xor_send(send, "width", width, 1)
        chip = dot(weight, right[:, :half], weight_dim, 0) + recv.astype(F32)
        return chip + xor_send(chip.astype(BF16), "width", width, 2).astype(F32)

    def all_tokens(own):
        return jnp.concatenate([own, xor_send(own, "width", width, 1)], axis=1)

    def own_features(own):
        other = xor_send(own_rows(own, at_width ^ 1), "width", width, 1)
        return jnp.concatenate([own_rows(own, at_width), other], axis=1)

    x_full = own_first(gather_width(x_in, at_width, width))
    cot_full = own_first(gather_width(cotangent, at_width, width))
    norms = jnp.stack([first_norm_gain, first_norm_bias, second_norm_gain, second_norm_bias])
    norms = by_width(
        [norms.T] + [xor_send(norms, "width", width, e).T for e in range(1, width)], at_width
    )
    gain_one, bias_one, gain_two, bias_two = (norms[:, i : i + 1] for i in range(4))

    live_total = sum_small(counts, "rows", row_devices)
    loss_scale = jnp.float32(tokens * row_devices) / live_total[0].astype(F32)
    live = jnp.where(jnp.arange(tokens) < counts[0], loss_scale, 0.0)[None, :]

    order = jnp.arange(tokens)
    order = jnp.where(odd == 1, (order + half) % tokens, order)
    inverse = 1.0 / 10000.0 ** (jnp.arange(HEAD_DIM // 2, dtype=F32) * 2.0 / HEAD_DIM)
    angles = own_first(positions[None, :]).astype(F32) * inverse[:, None]
    cosine, sine = jnp.cos(angles)[None], jnp.sin(angles)[None]

    xhat_one, scale_one = normalise(x_full.astype(F32))
    normed_one = (xhat_one * gain_one + bias_one).astype(BF16)
    project = lax.dot_general(w_qkv, normed_one, (((2,), (0,)), ((), ())), preferred_element_type=F32)
    project = project.reshape(3, heads, HEAD_DIM, tokens)
    queries = rotate(project[0], cosine, sine).astype(BF16)
    keys = rotate(project[1], cosine, sine).astype(BF16)
    values = project[2].astype(BF16)
    scores = jnp.einsum("hds,hdt->hst", keys, queries, preferred_element_type=F32) * score_scale
    scores = jnp.where((order[:, None] <= order[None, :])[None], scores, -1e30)
    exponents = jnp.exp(scores - jnp.max(scores, axis=1, keepdims=True))
    probs = exponents / jnp.sum(exponents, axis=1, keepdims=True)
    probs_low = probs.astype(BF16)
    heads_out = jnp.einsum("hds,hst->hdt", values, probs_low, preferred_element_type=F32)
    heads_out = heads_out.reshape(part, tokens).astype(BF16)
    middle = x_full[:, :half].astype(F32) + sum_own_tokens(w_out, 0, heads_out)

    xhat_two, scale_two = normalise(middle)
    normed_two = all_tokens((xhat_two * gain_two + bias_two).astype(BF16))
    grad_full = own_first(live) * cot_full.astype(F32)
    g_out = (self_weight[0] * grad_full).astype(BF16)
    d_active = dot(w_down, g_out, 1, 0)
    hidden = dot(w_up, normed_two, 0, 0)
    active, slope = gelu_and_slope(hidden)
    active = active.astype(BF16)
    d_w_down = reduce_gradient(
        me, row_devices, (w_down.shape[0],), *weight_gradient(me, row_devices, active, g_out)
    )[0]
    d_hidden = (slope * d_active).astype(BF16)
    d_normed_two = sum_own_tokens(w_up, 1, d_hidden)
    d_w_up = reduce_gradient(
        me, row_devices, (w_up.shape[0],), *weight_gradient(me, row_devices, normed_two, d_hidden)
    )[0]

    d_gain_two = jnp.sum(d_normed_two * xhat_two, axis=1)
    d_bias_two = jnp.sum(d_normed_two, axis=1)
    lifted = d_normed_two * gain_two
    d_middle = self_weight[0] * grad_full[:, :half] + scale_two * (
        lifted
        - jnp.mean(lifted, axis=0, keepdims=True)
        - xhat_two * jnp.mean(lifted * xhat_two, axis=0, keepdims=True)
    )
    g_mid = all_tokens(d_middle.astype(BF16))
    d_heads = dot(w_out, g_mid, 1, 0).astype(BF16).reshape(heads, HEAD_DIM, tokens)
    d_probs = jnp.einsum("hds,hdt->hst", values, d_heads, preferred_element_type=F32)
    inner = jnp.sum(d_probs * probs, axis=1, keepdims=True)
    d_scores = (probs * (d_probs - inner)).astype(BF16)
    d_queries = jnp.einsum("hds,hst->hdt", keys, d_scores, preferred_element_type=F32) * score_scale
    d_keys = jnp.einsum("hdt,hst->hds", queries, d_scores, preferred_element_type=F32) * score_scale
    d_values = jnp.einsum("hdt,hst->hds", d_heads, probs_low, preferred_element_type=F32)
    d_project = jnp.stack([rotate(d_queries, cosine, -sine), rotate(d_keys, cosine, -sine), d_values])
    d_project = d_project.reshape(3 * part, tokens).astype(BF16)
    d_w_qkv, d_w_out = reduce_gradient(
        me,
        row_devices,
        (3 * part, part),
        *weight_gradient(me, row_devices, d_project, normed_one, heads_out, g_mid),
    )

    d_normed_one = dot(w_qkv.reshape(3 * part, model), d_project, 0, 0)
    lifted = d_normed_one * gain_one
    sums = jnp.stack([jnp.sum(lifted, axis=0), jnp.sum(lifted * xhat_one, axis=0)])
    sums = sums + swap_halves(xor_send(sums, "width", width, 1))
    sums = (sums + xor_send(sums, "width", width, 2)) / model
    own_one = to_rows_of_width(d_normed_one)
    own_xhat = own_rows(xhat_one, at_width)
    d_gain_one = jnp.sum(own_one * own_xhat, axis=1)
    d_bias_one = jnp.sum(own_one, axis=1)
    d_input = own_features(d_middle) + scale_one * (
        own_one * first_norm_gain[:, None] - sums[0:1] - own_xhat * sums[1:2]
    )

    output = own_first(own_features(middle) + to_rows_of_width(dot(w_down, active, 0, 0)))
    grad = cotangent.astype(F32) * live
    running, d_history, d_mix = mix_history(mix_weights, history, grad)
    mixed = (self_weight[0] * output + running).astype(BF16)
    d_mix = jnp.concatenate([jnp.sum(d_mix, axis=(0, 2)), jnp.sum(grad * output)[None]])
    d_mix = tree_sum([d_mix] + [xor_send(d_mix, "width", width, e) for e in range(1, width)])

    both = jnp.stack([d_gain_two, d_bias_two])
    mine = lax.dynamic_slice_in_dim(both, at_width * part, part, 1)
    theirs = lax.dynamic_slice_in_dim(both, (at_width ^ 1) * part, part, 1)
    both = mine + xor_send(theirs, "width", width, 1)
    small = jnp.concatenate([d_mix, d_gain_one, d_bias_one, both[0], both[1]])
    small = sum_small(small, "rows", row_devices)
    layers = mix_weights.shape[0]
    ends = [small[layers + 1 + i * part : layers + 1 + (i + 1) * part] for i in range(4)]
    return (
        mixed,
        own_first(d_input),
        d_history,
        small[:layers],
        small[layers : layers + 1],
        ends[0],
        ends[1],
        d_w_qkv.reshape(w_qkv.shape),
        d_w_out,
        ends[2],
        ends[3],
        d_w_up,
        d_w_down,
    )


def solution(mesh):
    return jax.shard_map(
        functools.partial(local, mesh.shape["width"], mesh.shape["rows"]),
        mesh=mesh,
        in_specs=(
            P("width", "rows"),
            P(None, "width", "rows"),
            P("width", "rows"),
            P("rows"),
            P("rows"),
            P(),
            P(),
            P("width"),
            P("width"),
            P(None, "width", None),
            P("width", None),
            P("width"),
            P("width"),
            P(None, "width"),
            P("width", None),
        ),
        out_specs=(
            P("width", "rows"),
            P("width", "rows"),
            P(None, "width", "rows"),
            P(),
            P(),
            P("width"),
            P("width"),
            P(None, "width", None),
            P("width", None),
            P("width"),
            P("width"),
            P(None, "width"),
            P("width", None),
        ),
        check_vma=False,
    )
```

```python
import functools

import jax
import jax.numpy as jnp
from jax import lax
from jax.experimental import pallas as pl
from jax.experimental.pallas import tpu as pltpu
from jax.sharding import PartitionSpec as P

HEAD_DIM = 64
EPSILON = 1e-05
BF16 = jnp.bfloat16
F32 = jnp.float32
STEP = 16


def shape(*dims, kind=F32):
    return jax.ShapeDtypeStruct(dims, kind)


def kernel(body, outs, scalars, arrays, scratch=(), flops=0, limit=12):
    return pl.pallas_call(
        body,
        out_shape=outs,
        in_specs=[pl.BlockSpec(memory_space=pltpu.SMEM)] * len(scalars)
        + [pl.BlockSpec(memory_space=pltpu.VMEM)] * len(arrays),
        out_specs=jax.tree.map(lambda _: pl.BlockSpec(memory_space=pltpu.VMEM), outs),
        scratch_shapes=list(scratch),
        compiler_params=pltpu.CompilerParams(vmem_limit_bytes=limit * 1024 * 1024),
        cost_estimate=pl.CostEstimate(flops=1024, bytes_accessed=1024, transcendentals=0),
    )(*scalars, *arrays)


def after(value, *others):
    return lax.optimization_barrier((value, others))[0]


def dot(left, right, left_dim, right_dim):
    return lax.dot_general(left, right, (((left_dim,), (right_dim,)), ((), ())), preferred_element_type=F32)


def rows_at(i):
    return pl.ds(pl.multiple_of(i * STEP, STEP), STEP)


def each_rows(count, body, start=None, first=0):
    return lax.fori_loop(first // STEP, count // STEP, body, start, unroll=4)


def column_sum(value):
    return jnp.sum(value, axis=0, keepdims=True)


def xor_send(value, axis, size, offset):
    return lax.ppermute(value, axis, [(i, i ^ offset) for i in range(size)])


def tree_sum(parts):
    while len(parts) > 1:
        parts = [parts[i] + parts[i + 1] for i in range(0, len(parts), 2)]
    return parts[0]


def sum_small(value, axis, size):
    stride = 1
    while stride < size:
        value = value + xor_send(value, axis, size, stride)
        stride *= 2
    return value


def gather_width(shard, width, order):
    far = xor_send(shard, "width", width, 2)
    near = xor_send(shard, "width", width, 1)
    both = xor_send(after(far, *order) if order else far, "width", width, 1)
    return [shard, near, far, both]


def chunks_of(count, rows):
    while rows % (16 * count):
        count //= 2
    return count


def digits_of(count, kind):
    if kind == "halving":
        strides = []
        stride = 1
        while stride < count:
            strides.append((stride, 2))
            stride *= 2
        return strides
    if kind == "crossed":
        strides = digits_of(count, "halving")
        return [strides[1], strides[0]] + strides[2:]
    if kind == "near":
        return [(1, 2), (2, count // 2)]
    return [(2, count // 2), (1, 2)]


def offsets_of(digits):
    found = [0]
    for stride, radix in digits:
        found = [low + e * stride for low in found for e in range(radix)]
    return found


class Stream:
    def __init__(self, row_devices, first, rows, kind):
        self.first, self.rows = first, rows
        self.count = chunks_of(row_devices, rows)
        self.row_devices = row_devices
        self.digits = digits_of(self.count, kind)
        self.chunk = rows // self.count

    def parts(self):
        stride, radix = self.digits[0]
        rest = offsets_of(self.digits[1:])
        return [[e * stride + low for low in rest] for e in range(radix)]

    def send(self, value, offset):
        return xor_send(value, "rows", self.row_devices, offset)


def weight_gradient_kernel(streams, pairs, me_ref, *refs):
    operands, outs, scratch = refs[: 2 * pairs], list(refs[2 * pairs : -1]), refs[-1]
    start = 0
    for i in range(pairs):
        left, right = operands[2 * i], operands[2 * i + 1]
        count = left.shape[0]
        scratch[start : start + count] = dot(left[...], right[...], 1, 1).astype(BF16)
        start += count
    for stream in streams:
        for offsets in stream.parts():
            out = outs.pop(0)
            for place, offset in enumerate(offsets):
                chunk = (me_ref[0] % stream.count) ^ offset
                at = pl.multiple_of(stream.first + chunk * stream.chunk, 16)
                out[place * stream.chunk : (place + 1) * stream.chunk] = scratch[pl.ds(at, stream.chunk), :]


def weight_gradient(me, streams, *operands):
    pairs = len(operands) // 2
    total = sum(operands[2 * i].shape[0] for i in range(pairs))
    columns, tokens = operands[1].shape
    outs = tuple(
        shape(len(offsets) * stream.chunk, columns, kind=BF16) for stream in streams for offsets in stream.parts()
    )
    found = list(
        kernel(
            functools.partial(weight_gradient_kernel, streams, pairs),
            outs,
            [me],
            operands,
            [pltpu.VMEM((total, columns), BF16)],
            2 * total * columns * tokens,
        )
    )
    return [[found.pop(0) for _ in stream.parts()] for stream in streams]


def start_stage(stream, parts, stage):
    stride, radix = stream.digits[stage]
    return [stream.send(parts[e], e * stride) for e in range(1, radix)]


def add_stage(stream, parts, received, stage):
    value = tree_sum([part.astype(F32) for part in [parts[0]] + received]).astype(BF16)
    if stage + 1 == len(stream.digits):
        return [value]
    radix = stream.digits[stage + 1][1]
    size = value.shape[0] // radix
    return [value[e * size : (e + 1) * size] for e in range(radix)]


def sum_rest(stream, value):
    stride = stream.count
    while stride < stream.row_devices:
        value = (value.astype(F32) + stream.send(value, stride).astype(F32)).astype(BF16)
        stride *= 2
    return value


def gather_stage(stream, value, stage):
    stride, radix = stream.digits[stage]
    return [value] + [stream.send(value, e * stride) for e in range(1, radix)]


def place_kernel(streams, bounds, me_ref, *refs):
    pieces, outs = list(refs[: -len(bounds)]), refs[-len(bounds) :]
    for stream in streams:
        for offsets in stream.parts():
            piece = pieces.pop(0)
            for place, offset in enumerate(offsets):
                chunk = (me_ref[0] % stream.count) ^ offset
                row = stream.first + chunk * stream.chunk
                for (first, last), out in zip(bounds, outs):

                    def store(out=out, first=first, piece=piece, place=place, row=row, size=stream.chunk):
                        at = pl.multiple_of(row - first, 16)
                        out[pl.ds(at, size), :] = piece[place * size : (place + 1) * size].astype(F32)

                    if len(bounds) == 1:
                        store()
                    else:
                        pl.when((row >= first) & (row < last))(store)


def place(me, streams, pieces, sizes):
    columns = pieces[0].shape[1]
    bounds, start = [], 0
    for size in sizes:
        bounds.append((start, start + size))
        start += size
    outs = tuple(shape(size, columns) for size in sizes)
    return kernel(functools.partial(place_kernel, streams, bounds), outs, [me], pieces, flops=start * columns)


def history_kernel(mix_ref, history_ref, cot_ref, live_ref, running_ref, d_history_ref, d_mix_ref):
    layers = history_ref.shape[0]
    features, tokens = cot_ref.shape

    @pl.when(pl.program_id(0) == 0)
    def _():
        d_mix_ref[...] = jnp.zeros_like(d_mix_ref)

    for i in range(features // STEP):
        rows = slice(i * STEP, (i + 1) * STEP)
        grad = cot_ref[rows].astype(F32) * live_ref[...]
        running = jnp.zeros_like(grad)
        for j in range(layers):
            layer = history_ref[j, rows].astype(F32)
            weight = mix_ref[j]
            running = running + weight * layer
            d_history_ref[j, rows] = (weight * grad).astype(BF16)
            terms = grad * layer
            terms = terms[: STEP // 2] + terms[STEP // 2 :]
            d_mix_ref[j] += sum(terms[:, k : k + 128] for k in range(0, tokens, 128))
        running_ref[rows] = running


def mix_history(mix_weights, history, cotangent, live):
    layers, features, tokens = history.shape
    block = 32
    return pl.pallas_call(
        history_kernel,
        grid=(features // block,),
        out_shape=(
            shape(features, tokens),
            shape(*history.shape, kind=BF16),
            shape(layers, STEP // 2, 128),
        ),
        in_specs=[
            pl.BlockSpec(memory_space=pltpu.SMEM),
            pl.BlockSpec((layers, block, tokens), lambda i: (0, i, 0)),
            pl.BlockSpec((block, tokens), lambda i: (i, 0)),
            pl.BlockSpec((1, tokens), lambda i: (0, 0)),
        ],
        out_specs=(
            pl.BlockSpec((block, tokens), lambda i: (i, 0)),
            pl.BlockSpec((layers, block, tokens), lambda i: (0, i, 0)),
            pl.BlockSpec((layers, STEP // 2, 128), lambda i: (0, 0, 0)),
        ),
        compiler_params=pltpu.CompilerParams(vmem_limit_bytes=12 * 1024 * 1024),
        cost_estimate=pl.CostEstimate(flops=1024, bytes_accessed=1024, transcendentals=0),
    )(mix_weights, history, cotangent, live)


def spread_of(load, count, width):
    zero = jnp.zeros((STEP, width), F32)
    mean = column_sum(each_rows(count, lambda i, acc: acc + load(i), zero)) / count

    def squares(i, acc):
        centred = load(i) - mean
        return acc + centred * centred

    return mean, lax.rsqrt(column_sum(each_rows(count, squares, zero)) / count + EPSILON)


def attention_kernel(
    at_ref, x0, x1, x2, x3, norms, cosine, sine, w_qkv, w_out,
    send, keep, x_half, x_all, normed, stats, qkv, heads_out, probs, project, scores,
):
    at = at_ref[0]
    part, tokens = x0.shape
    model = w_out.shape[1]
    half = tokens // 2
    for e, piece in enumerate((x0, x1, x2, x3)):
        x_all[pl.ds(pl.multiple_of((at ^ e) * part, 64), part), :] = piece[...]
    mean, scale = spread_of(lambda i: x_all[rows_at(i), :].astype(F32), model, tokens)
    stats[0:1] = mean
    stats[1:2] = scale

    def normalise(i, _):
        rows = rows_at(i)
        xhat = (x_all[rows, :].astype(F32) - mean) * scale
        normed[rows, :] = (xhat * norms[rows, 0:1] + norms[rows, 1:2]).astype(BF16)

    each_rows(model, normalise)
    project[...] = dot(w_qkv[...], normed[...], 1, 0)
    width = HEAD_DIM // 2
    for block, factor in ((0, HEAD_DIM ** (-0.5)), (1, 1.0)):
        for start in range(block * part, (block + 1) * part, HEAD_DIM):
            front, back = project[start : start + width], project[start + width : start + HEAD_DIM]
            cos, sin = cosine[...] * factor, sine[...] * factor
            qkv[start : start + width] = (front * cos - back * sin).astype(BF16)
            qkv[start + width : start + HEAD_DIM] = (back * cos + front * sin).astype(BF16)
    qkv[2 * part :] = project[2 * part :].astype(BF16)
    for h in range(part // HEAD_DIM):
        head = slice(h * HEAD_DIM, (h + 1) * HEAD_DIM)
        for t in range(2):
            now = slice(t * half, (t + 1) * half)
            count = (t + 1) * half
            query = qkv[head, now]
            key = qkv[part + h * HEAD_DIM : part + (h + 1) * HEAD_DIM, :count]
            value = qkv[2 * part + h * HEAD_DIM : 2 * part + (h + 1) * HEAD_DIM, :count]
            scores[:count] = dot(key, query, 0, 0)

            def masked_top(i, acc):
                rows = rows_at(i)
                behind = lax.broadcasted_iota(jnp.int32, (STEP, half), 0) + (i * STEP - t * half)
                found = jnp.where(behind <= lax.broadcasted_iota(jnp.int32, (STEP, half), 1), scores[rows, :], -1e30)
                scores[rows, :] = found
                return jnp.maximum(acc, found)

            top = each_rows(
                t * half, lambda i, acc: jnp.maximum(acc, scores[rows_at(i), :]), jnp.full((STEP, half), -1e30, F32)
            )
            top = jnp.max(each_rows(count, masked_top, top, first=t * half), axis=0, keepdims=True)

            def raise_rows(i, acc):
                rows = rows_at(i)
                found = jnp.exp(scores[rows, :] - top)
                scores[rows, :] = found
                return acc + found

            total = 1.0 / column_sum(each_rows(count, raise_rows, jnp.zeros((STEP, half), F32)))

            def settle(i, _):
                rows = rows_at(i)
                probs[h, rows, now] = (scores[rows, :] * total).astype(BF16)

            each_rows(count, settle)
            heads_out[head, now] = dot(value, probs[h, :count, now], 1, 0).astype(BF16)
    own = pl.multiple_of((at % 2) * half, half)
    other = pl.multiple_of((1 - at % 2) * half, half)
    send[...] = dot(w_out[...], heads_out[:, pl.ds(other, half)], 0, 0).astype(BF16)
    keep[...] = dot(w_out[...], heads_out[:, pl.ds(own, half)], 0, 0)
    x_half[...] = x_all[:, pl.ds(own, half)]


def output_gradient_kernel(at_ref, self_ref, c0, c1, c2, c3, live, w_down, g_out, d_active, cot_half, cot_all):
    at = at_ref[0]
    part, tokens = c0.shape
    half = tokens // 2
    for e, piece in enumerate((c0, c1, c2, c3)):
        cot_all[pl.ds(pl.multiple_of((at ^ e) * part, 64), part), :] = piece[...]
    for place, side in enumerate((at % 2, 1 - at % 2)):
        now = pl.ds(pl.multiple_of(side * half, half), half)
        factor = live[:, now]

        def scale(i, _, now=now, factor=factor, place=place):
            rows = rows_at(i)
            grad = cot_all[rows, now].astype(F32) * factor
            g_out[rows, place * half : (place + 1) * half] = (self_ref[0] * grad).astype(BF16)
            if place == 0:
                cot_half[rows, :] = cot_all[rows, now]

        each_rows(cot_all.shape[0], scale)
    d_active[...] = dot(w_down[...], g_out[...], 1, 0)


def middle_kernel(x_half, chip, received, norms, middle, stats, normed):
    model, half = chip.shape

    def add(i, _):
        rows = rows_at(i)
        middle[rows, :] = x_half[rows, :].astype(F32) + chip[rows, :] + received[rows, :].astype(F32)

    each_rows(model, add)
    mean, scale = spread_of(lambda i: middle[rows_at(i), :], model, half)
    stats[0:1] = mean
    stats[1:2] = scale

    def normalise(i, _):
        rows = rows_at(i)
        xhat = (middle[rows, :] - mean) * scale
        normed[rows, :] = (xhat * norms[rows, 2:3] + norms[rows, 3:4]).astype(BF16)

    each_rows(model, normalise)


def feed_forward_kernel(own, other, w_up, d_active, normed, active, d_hidden, send, keep, hidden):
    half = own.shape[1]
    normed[:, :half] = own[...]
    normed[:, half:] = other[...]
    hidden[...] = dot(w_up[...], normed[...], 0, 0)

    def bend(i, _):
        rows = rows_at(i)
        u = hidden[rows, :]
        squared = u * u
        curve = jnp.tanh(0.7978845608028654 * u * (1.0 + 0.044715 * squared))
        lifted = 0.5 * (1.0 + curve)
        active[rows, :] = (u * lifted).astype(BF16)
        slope = lifted + u * (0.5 * (1.0 - curve * curve)) * (
            0.7978845608028654 + (3 * 0.044715 * 0.7978845608028654) * squared
        )
        d_hidden[rows, :] = (slope * d_active[rows, :]).astype(BF16)

    each_rows(hidden.shape[0], bend)
    send[...] = dot(w_up[...], d_hidden[:, half:], 1, 0).astype(BF16)
    keep[...] = dot(w_up[...], d_hidden[:, :half], 1, 0)


def store_blocks(at, total, part, send, keep):
    for place in range(2):
        for low, out in ((1, send), (0, keep)):
            rows = pl.ds(pl.multiple_of((at ^ (2 * place + low)) * part, 64), part)
            out[place * part : (place + 1) * part] = total[rows, :].astype(out.dtype)


def output_kernel(at_ref, active, w_down, middle, send, keep, total):
    at = at_ref[0]
    model, half = middle.shape
    part = send.shape[0] // 2
    own = pl.ds(pl.multiple_of((at % 2) * half, half), half)
    other = pl.ds(pl.multiple_of((1 - at % 2) * half, half), half)
    total[:, own] = dot(w_down[...], active[:, :half], 0, 0) + 0.5 * middle[...]
    total[:, other] = dot(w_down[...], active[:, half:], 0, 0)
    store_blocks(at, total, part, send, keep)


def middle_gradient_kernel(
    at_ref, self_ref, chip, received, middle, stats, cot_half, live, norms, d_middle, g_mid, d_gain, d_bias, d_normed
):
    model, half = chip.shape
    mean, scale = stats[0:1], stats[1:2]
    zero = jnp.zeros((STEP, half), F32)

    def sums(i, acc):
        rows = rows_at(i)
        grad = chip[rows, :] + received[rows, :].astype(F32)
        d_normed[rows, :] = grad
        xhat = (middle[rows, :] - mean) * scale
        both = grad * xhat
        d_gain[rows, :] = jnp.sum(both, axis=1, keepdims=True)
        d_bias[rows, :] = jnp.sum(grad, axis=1, keepdims=True)
        gain = norms[rows, 2:3]
        return acc[0] + grad * gain, acc[1] + both * gain

    first, second = (column_sum(v) / model for v in each_rows(model, sums, (zero, zero)))
    own = pl.ds(pl.multiple_of((at_ref[0] % 2) * half, half), half)
    factor = self_ref[0] * live[:, own]

    def finish(i, _):
        rows = rows_at(i)
        xhat = (middle[rows, :] - mean) * scale
        found = cot_half[rows, :].astype(F32) * factor + scale * (
            d_normed[rows, :] * norms[rows, 2:3] - first - xhat * second
        )
        d_middle[rows, :] = found
        g_mid[rows, :] = found.astype(BF16)

    each_rows(model, finish)


def attention_gradient_kernel(
    at_ref, own, other, w_out, qkv, probs, cosine, sine,
    d_project, g_mid, d_heads, d_scores, products, d_queries, d_keys, d_values,
):
    at = at_ref[0]
    half = own.shape[1]
    part = w_out.shape[0]
    g_mid[:, pl.ds(pl.multiple_of((at % 2) * half, half), half)] = own[...]
    g_mid[:, pl.ds(pl.multiple_of((1 - at % 2) * half, half), half)] = other[...]
    d_heads[...] = dot(w_out[...], g_mid[...], 1, 0).astype(BF16)
    width = HEAD_DIM // 2
    for h in range(part // HEAD_DIM):
        head = slice(h * HEAD_DIM, (h + 1) * HEAD_DIM)
        query = qkv[head]
        key = qkv[part + h * HEAD_DIM : part + (h + 1) * HEAD_DIM]
        value = qkv[2 * part + h * HEAD_DIM : 2 * part + (h + 1) * HEAD_DIM]
        for t in range(2):
            now = slice(t * half, (t + 1) * half)
            count = (t + 1) * half
            products[:count] = dot(value[:, :count], d_heads[head, now], 0, 0)

            def weigh(i, acc):
                rows = rows_at(i)
                return acc + products[rows, :] * probs[h, rows, now].astype(F32)

            inner = column_sum(each_rows(count, weigh, jnp.zeros((STEP, half), F32)))

            def settle(i, _):
                rows = rows_at(i)
                d_scores[rows, :] = (probs[h, rows, now].astype(F32) * (products[rows, :] - inner)).astype(BF16)

            each_rows(count, settle)
            d_queries[:, now] = dot(key[:, :count], d_scores[:count], 1, 0) * HEAD_DIM ** (-0.5)
            d_key = dot(query[:, now], d_scores[:count], 1, 1)
            d_value = dot(d_heads[head, now], probs[h, :count, now], 1, 1)
            if t == 0:
                d_keys[:, :half] = d_key
                d_values[:, :half] = d_value
            else:
                d_keys[:, :half] += d_key[:, :half]
                d_values[:, :half] += d_value[:, :half]
                d_keys[:, half:] = d_key[:, half:]
                d_values[:, half:] = d_value[:, half:]
        for block, found in ((0, d_queries), (1, d_keys)):
            start = block * part + h * HEAD_DIM
            front, back = found[:width], found[width:]
            d_project[start : start + width] = (front * cosine[...] + back * sine[...]).astype(BF16)
            d_project[start + width : start + HEAD_DIM] = (back * cosine[...] - front * sine[...]).astype(BF16)
        d_project[2 * part + h * HEAD_DIM : 2 * part + (h + 1) * HEAD_DIM] = d_values[...].astype(BF16)


def input_gradient_kernel(
    at_ref, d_project, w_qkv, x_all, stats, d_middle, norms, send, keep, sums, d_gain, d_bias, total
):
    at = at_ref[0]
    model, half = d_middle.shape
    tokens = x_all.shape[1]
    part = send.shape[0] // 2
    total[...] = dot(w_qkv[...], d_project[...], 0, 0)
    mean, scale = stats[0:1], stats[1:2]
    zero = jnp.zeros((STEP, tokens), F32)
    own = pl.ds(pl.multiple_of((at % 2) * half, half), half)

    def body(i, acc):
        rows = rows_at(i)
        grad = total[rows, :]
        xhat = (x_all[rows, :].astype(F32) - mean) * scale
        both = grad * xhat
        d_gain[rows, :] = jnp.sum(both, axis=1, keepdims=True)
        d_bias[rows, :] = jnp.sum(grad, axis=1, keepdims=True)
        gain = norms[rows, 0:1]
        lifted = grad * gain
        total[rows, :] = lifted * scale
        total[rows, own] += 0.5 * d_middle[rows, :]
        return acc[0] + lifted, acc[1] + both * gain

    first, second = each_rows(model, body, (zero, zero))
    sums[0:1] = column_sum(first) / model
    sums[1:2] = column_sum(second) / model
    store_blocks(at, total, part, send, keep)


def local(
    width,
    row_devices,
    x_in,
    history,
    cotangent,
    counts,
    positions,
    mix_weights,
    self_weight,
    first_norm_gain,
    first_norm_bias,
    w_qkv,
    w_out,
    second_norm_gain,
    second_norm_bias,
    w_up,
    w_down,
):
    part, tokens = x_in.shape
    model = w_out.shape[1]
    hidden_units = w_up.shape[1]
    half = tokens // 2
    layers = mix_weights.shape[0]
    at_width = lax.axis_index("width")
    at = at_width.astype(jnp.int32)[None]
    me = lax.axis_index("rows").astype(jnp.int32)[None]
    to_width = lambda value, offset: xor_send(value, "width", width, offset)
    w_qkv = w_qkv.reshape(3 * part, model)

    x_pieces = gather_width(x_in, width, ())
    norms = jnp.stack([first_norm_gain, first_norm_bias, second_norm_gain, second_norm_bias])
    norms = after(norms, x_in)
    near = to_width(norms, 1)
    pair = jnp.where(at_width % 2 == 1, jnp.concatenate([near, norms], 1), jnp.concatenate([norms, near], 1))
    far = to_width(pair, 2)
    norms = jnp.where(at_width // 2 == 1, jnp.concatenate([far, pair], 1), jnp.concatenate([pair, far], 1)).T
    inverse = 1.0 / 10000.0 ** (jnp.arange(HEAD_DIM // 2, dtype=F32) * 2.0 / HEAD_DIM)
    angles = positions[None, :].astype(F32) * inverse[:, None]
    cosine, sine = jnp.cos(angles), jnp.sin(angles)
    live_total = counts
    for stride, radix in reversed(digits_of(row_devices, "near")):
        live_total = live_total + sum(
            xor_send(live_total, "rows", row_devices, e * stride) for e in range(1, radix)
        )
    loss_scale = jnp.float32(tokens * row_devices) / live_total[0].astype(F32)
    live = jnp.where(jnp.arange(tokens) < counts[0], loss_scale, 0.0)[None, :]

    send, keep, x_half, x_all, normed_one, stats_one, qkv, heads_out, probs = kernel(
        attention_kernel,
        (
            shape(model, half, kind=BF16),
            shape(model, half),
            shape(model, half, kind=BF16),
            shape(model, tokens, kind=BF16),
            shape(model, tokens, kind=BF16),
            shape(2, tokens),
            shape(3 * part, tokens, kind=BF16),
            shape(part, tokens, kind=BF16),
            shape(part // HEAD_DIM, tokens, tokens, kind=BF16),
        ),
        [at],
        [*x_pieces, after(norms, live), cosine, sine, w_qkv, w_out],
        [pltpu.VMEM((3 * part, tokens), F32), pltpu.VMEM((tokens, half), F32)],
        4 * 10**9,
    )
    chip = keep + to_width(send, 1).astype(F32)
    received = to_width(chip.astype(BF16), 2)
    cot_pieces = gather_width(after(cotangent, *x_pieces), width, (send,))

    g_out, d_active, cot_half = kernel(
        output_gradient_kernel,
        (shape(model, tokens, kind=BF16), shape(hidden_units, tokens), shape(model, half, kind=BF16)),
        [at, self_weight],
        [*cot_pieces, after(live, chip), w_down],
        [pltpu.VMEM((model, tokens), BF16)],
        10**9,
    )
    running, d_history, d_mix = mix_history(mix_weights, history, cotangent, after(live, d_active))

    middle, stats_two, normed_own = kernel(
        middle_kernel,
        (shape(model, half), shape(2, half), shape(model, half, kind=BF16)),
        [],
        [x_half, chip, after(received, running), norms],
        flops=10**8,
    )
    normed_two, active, d_hidden, send, keep = kernel(
        feed_forward_kernel,
        (
            shape(model, tokens, kind=BF16),
            shape(hidden_units, tokens, kind=BF16),
            shape(hidden_units, tokens, kind=BF16),
            shape(model, half, kind=BF16),
            shape(model, half),
        ),
        [],
        [normed_own, to_width(normed_own, 1), w_up, d_active],
        [pltpu.VMEM((hidden_units, tokens), F32)],
        2 * 10**9,
    )

    down = Stream(row_devices, 0, hidden_units, "halving")
    up = Stream(row_devices, 0, model, "crossed")
    down_parts = weight_gradient(me, [down], active, after(g_out, send))[0]
    down_got = start_stage(down, down_parts, 0)
    chip = keep + after(to_width(send, 1), *down_parts).astype(F32)
    received = to_width(chip.astype(BF16), 2)
    up_parts = weight_gradient(me, [up], normed_two, after(d_hidden, chip))[0]
    up_got = start_stage(up, up_parts, 0)

    blocks = (shape(2 * part, tokens, kind=BF16), shape(2 * part, tokens))
    out_send, out_keep = kernel(
        output_kernel,
        blocks,
        [at],
        [active, w_down, after(middle, *up_parts)],
        [pltpu.VMEM((model, tokens), F32)],
        10**9,
    )
    out_chip = out_keep + to_width(out_send, 1).astype(F32)
    output = out_chip[:part] + to_width(out_chip[part:].astype(BF16), 2).astype(F32)

    d_middle, g_own, d_gain_two, d_bias_two = kernel(
        middle_gradient_kernel,
        (shape(model, half), shape(model, half, kind=BF16), shape(model, 1), shape(model, 1)),
        [at, self_weight],
        [chip, after(received, out_chip), middle, stats_two, cot_half, live, norms],
        [pltpu.VMEM((model, half), F32)],
        10**8,
    )
    g_other = to_width(g_own, 1)
    down_parts = add_stage(down, down_parts, [after(v, g_own) for v in down_got], 0)
    down_got = start_stage(down, down_parts, 1)
    up_parts = add_stage(up, up_parts, [after(v, g_own) for v in up_got], 0)
    up_got = start_stage(up, up_parts, 1)
    d_project, g_mid = kernel(
        attention_gradient_kernel,
        (shape(3 * part, tokens, kind=BF16), shape(model, tokens, kind=BF16)),
        [at],
        [g_own, after(g_other, *down_parts, *up_parts), w_out, qkv, probs, cosine, sine],
        [
            pltpu.VMEM((part, tokens), BF16),
            pltpu.VMEM((tokens, half), BF16),
            pltpu.VMEM((tokens, half), F32),
            pltpu.VMEM((HEAD_DIM, tokens), F32),
            pltpu.VMEM((HEAD_DIM, tokens), F32),
            pltpu.VMEM((HEAD_DIM, tokens), F32),
        ],
        4 * 10**9,
    )
    tail_rows = 4 * part
    tail = [
        Stream(row_devices, 0, tail_rows * 2 // 3, "near"),
        Stream(row_devices, tail_rows * 2 // 3, tail_rows // 3, "far"),
    ]
    tail_parts = weight_gradient(me, tail, d_project, normed_one, heads_out, g_mid)
    tail_got = [start_stage(s, p, 0) for s, p in zip(tail, tail_parts)]

    in_send, in_keep, sums, d_gain_one, d_bias_one = kernel(
        input_gradient_kernel,
        blocks + (shape(2, tokens), shape(model, 1), shape(model, 1)),
        [at],
        [after(d_project, *tail_parts[0]), w_qkv, x_all, stats_one, d_middle, norms],
        [pltpu.VMEM((model, tokens), F32)],
        10**9,
    )
    in_near = to_width(in_send, 1)

    down_parts = add_stage(down, down_parts, [after(v, in_send) for v in down_got], 1)
    down_got = start_stage(down, down_parts, 2)
    up_parts = add_stage(up, up_parts, [after(v, in_send) for v in up_got], 1)
    up_got = start_stage(up, up_parts, 2)

    cot_wide = cotangent.astype(F32) * live
    mixed = (self_weight[0] * output + running).astype(BF16)
    d_mix = jnp.concatenate([jnp.sum(d_mix, axis=(1, 2)), jnp.sum(cot_wide * output)[None]])
    flat = jnp.concatenate(
        [d_gain_one[:, 0], d_bias_one[:, 0], 0.5 * d_gain_two[:, 0], 0.5 * d_bias_two[:, 0], sums[0], sums[1], d_mix]
    )
    flat = sum_small(flat, "width", width)
    in_chip = in_keep + in_near.astype(F32)
    in_total = in_chip[:part] + to_width(in_chip[part:].astype(BF16), 2).astype(F32)
    scale_one = stats_one[1:2]
    own_xhat = (x_in.astype(F32) - stats_one[0:1]) * scale_one
    d_input = in_total - scale_one * (
        flat[4 * model : 4 * model + tokens] + own_xhat * flat[4 * model + tokens : 4 * model + 2 * tokens]
    )
    ends = [lax.dynamic_slice_in_dim(flat, i * model + at_width * part, part) for i in range(4)]
    small = sum_small(jnp.concatenate([flat[4 * model + 2 * tokens :]] + ends), "rows", row_devices)
    ends = [small[layers + 1 + i * part : layers + 1 + (i + 1) * part] for i in range(4)]

    tail_parts = [add_stage(s, p, g, 0) for s, p, g in zip(tail, tail_parts, tail_got)]
    tail_got = [start_stage(s, p, 1) for s, p in zip(tail, tail_parts)]
    down_value = sum_rest(down, add_stage(down, down_parts, [after(v, *tail_parts[0]) for v in down_got], 2)[0])
    up_value = sum_rest(up, add_stage(up, up_parts, [after(v, *tail_parts[0]) for v in up_got], 2)[0])
    for stage in range(len(down.digits) - 1, 0, -1):
        down_value = jnp.concatenate(gather_stage(down, down_value, stage))
        up_value = jnp.concatenate(gather_stage(up, up_value, stage))
        if stage == len(down.digits) - 1:
            tail_values = [
                sum_rest(s, add_stage(s, p, [after(v, down_value) for v in g], 1)[0])
                for s, p, g in zip(tail, tail_parts, tail_got)
            ]
            tail_values = [jnp.concatenate(gather_stage(s, v, 1)) for s, v in zip(tail, tail_values)]
    down_pieces = gather_stage(down, down_value, 0)
    up_pieces = gather_stage(up, up_value, 0)
    tail_pieces = [piece for s, v in zip(tail, tail_values) for piece in gather_stage(s, v, 0)]
    d_w_down = place(me, [down], down_pieces, (hidden_units,))[0]
    d_w_up = place(me, [up], up_pieces, (model,))[0]
    d_w_qkv, d_w_out = place(me, tail, tail_pieces, (3 * part, part))
    return (
        mixed,
        d_input,
        d_history,
        small[:layers],
        small[layers : layers + 1],
        ends[0],
        ends[1],
        d_w_qkv.reshape(3, part, model),
        d_w_out,
        ends[2],
        ends[3],
        d_w_up,
        d_w_down,
    )


def solution(mesh):
    return jax.shard_map(
        functools.partial(local, mesh.shape["width"], mesh.shape["rows"]),
        mesh=mesh,
        in_specs=(
            P("width", "rows"),
            P(None, "width", "rows"),
            P("width", "rows"),
            P("rows"),
            P("rows"),
            P(),
            P(),
            P("width"),
            P("width"),
            P(None, "width", None),
            P("width", None),
            P("width"),
            P("width"),
            P(None, "width"),
            P("width", None),
        ),
        out_specs=(
            P("width", "rows"),
            P("width", "rows"),
            P(None, "width", "rows"),
            P(),
            P(),
            P("width"),
            P("width"),
            P(None, "width", None),
            P("width", None),
            P("width"),
            P("width"),
            P(None, "width"),
            P("width", None),
        ),
        check_vma=False,
    )
```

```python
import functools

import jax
import jax.numpy as jnp
from jax import lax
from jax.experimental import pallas as pl
from jax.experimental.pallas import tpu as pltpu
from jax.sharding import PartitionSpec as P

HEAD_DIM = 64
EPSILON = 1e-05
BF16 = jnp.bfloat16
F32 = jnp.float32
STEP = 16


def shape(*dims, kind=F32):
    return jax.ShapeDtypeStruct(dims, kind)


def kernel(body, outs, scalars, arrays, scratch=(), flops=0, limit=12):
    return pl.pallas_call(
        body,
        out_shape=outs,
        in_specs=[pl.BlockSpec(memory_space=pltpu.SMEM)] * len(scalars)
        + [pl.BlockSpec(memory_space=pltpu.VMEM)] * len(arrays),
        out_specs=jax.tree.map(lambda _: pl.BlockSpec(memory_space=pltpu.VMEM), outs),
        scratch_shapes=list(scratch),
        compiler_params=pltpu.CompilerParams(vmem_limit_bytes=limit * 1024 * 1024),
        cost_estimate=pl.CostEstimate(flops=1024, bytes_accessed=1024, transcendentals=0),
    )(*scalars, *arrays)


def after(value, *others):
    return lax.optimization_barrier((value, others))[0]


def dot(left, right, left_dim, right_dim):
    return lax.dot_general(left, right, (((left_dim,), (right_dim,)), ((), ())), preferred_element_type=F32)


def rows_at(i):
    return pl.ds(pl.multiple_of(i * STEP, STEP), STEP)


def each_rows(count, body, start=None, first=0):
    return lax.fori_loop(first // STEP, count // STEP, body, start, unroll=4)


def column_sum(value):
    return jnp.sum(value, axis=0, keepdims=True)


def xor_send(value, axis, size, offset):
    return lax.ppermute(value, axis, [(i, i ^ offset) for i in range(size)])


def add_kernel(count, cuts, *refs):
    parts, outs = refs[:count], refs[count:]

    def one(rows):
        found = parts[0][rows, :].astype(F32)
        for part in parts[1:]:
            found = found + part[rows, :].astype(F32)
        return found

    for (first, last), out in zip(cuts, outs):
        if (last - first) % STEP:
            out[...] = one(slice(first, last)).astype(out.dtype)
        else:

            def body(i, _, first=first, out=out):
                out[rows_at(i), :] = one(pl.ds(pl.multiple_of(first + i * STEP, STEP), STEP)).astype(out.dtype)

            each_rows(last - first, body)


def add(parts, *cuts):
    columns = parts[0].shape[1]
    outs = tuple(shape(last - first, columns, kind=kind) for first, last, kind in cuts)
    return list(kernel(functools.partial(add_kernel, len(parts), [cut[:2] for cut in cuts]), outs, [], parts))


def sum_small(value, axis, size):
    stride = 1
    while stride < size:
        value = add([value, xor_send(value, axis, size, stride)], (0, value.shape[0], F32))[0]
        stride *= 2
    return value


def join_kernel(*refs):
    out, start = refs[-1], 0
    for piece in refs[:-1]:
        out[start : start + piece.shape[0]] = piece[...]
        start += piece.shape[0]


def join(pieces):
    rows = sum(piece.shape[0] for piece in pieces)
    return kernel(join_kernel, shape(rows, pieces[0].shape[1], kind=pieces[0].dtype), [], pieces)


def count_kernel(*refs):
    refs[-1][0] = sum((ref[0] for ref in refs[1:-1]), refs[0][0])


def sum_counts(counts, row_devices):
    for stride, radix in reversed(digits_of(row_devices, "near")):
        parts = [counts] + [xor_send(counts, "rows", row_devices, e * stride) for e in range(1, radix)]
        counts = pl.pallas_call(
            count_kernel,
            out_shape=jax.ShapeDtypeStruct((1,), jnp.int32),
            in_specs=[pl.BlockSpec(memory_space=pltpu.SMEM)] * len(parts),
            out_specs=pl.BlockSpec(memory_space=pltpu.SMEM),
            compiler_params=pltpu.CompilerParams(vmem_limit_bytes=1024 * 1024),
        )(*parts)
    return counts


def chunks_of(count, rows):
    while rows % (16 * count):
        count //= 2
    return count


def digits_of(count, kind):
    if kind == "halving":
        strides = []
        stride = 1
        while stride < count:
            strides.append((stride, 2))
            stride *= 2
        return strides
    if kind == "crossed":
        strides = digits_of(count, "halving")
        return [strides[1], strides[0]] + strides[2:]
    if kind == "near":
        return [(1, 2), (2, count // 2)]
    return [(2, count // 2), (1, 2)]


def offsets_of(digits):
    found = [0]
    for stride, radix in digits:
        found = [low + e * stride for low in found for e in range(radix)]
    return found


class Stream:
    def __init__(self, row_devices, first, rows, kind):
        self.first, self.rows = first, rows
        self.count = chunks_of(row_devices, rows)
        self.row_devices = row_devices
        self.digits = digits_of(self.count, kind)
        self.chunk = rows // self.count

    def parts(self):
        stride, radix = self.digits[0]
        rest = offsets_of(self.digits[1:])
        return [[e * stride + low for low in rest] for e in range(radix)]

    def send(self, value, offset):
        return xor_send(value, "rows", self.row_devices, offset)


def weight_gradient_kernel(streams, pairs, me_ref, *refs):
    operands, outs, scratch = refs[: 2 * pairs], list(refs[2 * pairs : -1]), refs[-1]
    start = 0
    for i in range(pairs):
        left, right = operands[2 * i], operands[2 * i + 1]
        count = left.shape[0]
        scratch[start : start + count] = dot(left[...], right[...], 1, 1).astype(BF16)
        start += count
    for stream in streams:
        for offsets in stream.parts():
            out = outs.pop(0)
            for place, offset in enumerate(offsets):
                chunk = (me_ref[0] % stream.count) ^ offset
                at = pl.multiple_of(stream.first + chunk * stream.chunk, 16)
                out[place * stream.chunk : (place + 1) * stream.chunk] = scratch[pl.ds(at, stream.chunk), :]


def weight_gradient(me, streams, *operands):
    pairs = len(operands) // 2
    total = sum(operands[2 * i].shape[0] for i in range(pairs))
    columns, tokens = operands[1].shape
    outs = tuple(
        shape(len(offsets) * stream.chunk, columns, kind=BF16) for stream in streams for offsets in stream.parts()
    )
    found = list(
        kernel(
            functools.partial(weight_gradient_kernel, streams, pairs),
            outs,
            [me],
            operands,
            [pltpu.VMEM((total, columns), BF16)],
            2 * total * columns * tokens,
        )
    )
    return [[found.pop(0) for _ in stream.parts()] for stream in streams]


def start_stage(stream, parts, stage):
    stride, radix = stream.digits[stage]
    return [stream.send(parts[e], e * stride) for e in range(1, radix)]


def add_stage(stream, parts, received, stage):
    rows = parts[0].shape[0]
    radix = 1 if stage + 1 == len(stream.digits) else stream.digits[stage + 1][1]
    size = rows // radix
    return add([parts[0]] + received, *((e * size, (e + 1) * size, BF16) for e in range(radix)))


def sum_rest(stream, value):
    stride = stream.count
    while stride < stream.row_devices:
        value = add([value, stream.send(value, stride)], (0, value.shape[0], BF16))[0]
        stride *= 2
    return value


def gather_stage(stream, value, stage):
    stride, radix = stream.digits[stage]
    return [value] + [stream.send(value, e * stride) for e in range(1, radix)]


def place_kernel(streams, bounds, me_ref, *refs):
    pieces, outs = list(refs[: -len(bounds)]), refs[-len(bounds) :]
    for stream in streams:
        for offsets in stream.parts():
            piece = pieces.pop(0)
            for place, offset in enumerate(offsets):
                chunk = (me_ref[0] % stream.count) ^ offset
                row = stream.first + chunk * stream.chunk
                for (first, last), out in zip(bounds, outs):

                    def store(out=out, first=first, piece=piece, place=place, row=row, size=stream.chunk):
                        at = pl.multiple_of(row - first, 16)
                        out[pl.ds(at, size), :] = piece[place * size : (place + 1) * size].astype(F32)

                    if len(bounds) == 1:
                        store()
                    else:
                        pl.when((row >= first) & (row < last))(store)


def place(me, streams, pieces, sizes):
    columns = pieces[0].shape[1]
    bounds, start = [], 0
    for size in sizes:
        bounds.append((start, start + size))
        start += size
    outs = tuple(shape(size, columns) for size in sizes)
    return kernel(functools.partial(place_kernel, streams, bounds), outs, [me], pieces, flops=start * columns)


def live_row(all_tokens, counts_ref, total_ref, width, first):
    scale = jnp.full((1, width), all_tokens, F32) / (jnp.zeros((1, width), F32) + total_ref[0].astype(F32))
    place = lax.broadcasted_iota(jnp.int32, (1, width), 1) + first
    return jnp.where(place < counts_ref[0], scale, 0.0)


def history_kernel(
    all_tokens, mix_ref, counts_ref, total_ref, history_ref, cot_ref, running_ref, d_history_ref, d_mix_ref
):
    layers = history_ref.shape[0]
    features, tokens = cot_ref.shape
    live = live_row(all_tokens, counts_ref, total_ref, tokens, 0)

    @pl.when(pl.program_id(0) == 0)
    def _():
        d_mix_ref[...] = jnp.zeros_like(d_mix_ref)

    for i in range(features // STEP):
        rows = slice(i * STEP, (i + 1) * STEP)
        grad = cot_ref[rows].astype(F32) * live
        running = jnp.zeros_like(grad)
        for j in range(layers):
            layer = history_ref[j, rows].astype(F32)
            weight = mix_ref[j]
            running = running + weight * layer
            d_history_ref[j, rows] = (weight * grad).astype(BF16)
            terms = grad * layer
            terms = terms[: STEP // 2] + terms[STEP // 2 :]
            d_mix_ref[j] += sum(terms[:, k : k + 128] for k in range(0, tokens, 128))
        running_ref[rows] = running


def mix_history(all_tokens, mix_weights, counts, total, history, cotangent):
    layers, features, tokens = history.shape
    block = 32
    return pl.pallas_call(
        functools.partial(history_kernel, all_tokens),
        grid=(features // block,),
        out_shape=(
            shape(features, tokens),
            shape(*history.shape, kind=BF16),
            shape(layers, STEP // 2, 128),
        ),
        in_specs=[
            pl.BlockSpec(memory_space=pltpu.SMEM),
            pl.BlockSpec(memory_space=pltpu.SMEM),
            pl.BlockSpec(memory_space=pltpu.SMEM),
            pl.BlockSpec((layers, block, tokens), lambda i: (0, i, 0)),
            pl.BlockSpec((block, tokens), lambda i: (i, 0)),
        ],
        out_specs=(
            pl.BlockSpec((block, tokens), lambda i: (i, 0)),
            pl.BlockSpec((layers, block, tokens), lambda i: (0, i, 0)),
            pl.BlockSpec((layers, STEP // 2, 128), lambda i: (0, 0, 0)),
        ),
        compiler_params=pltpu.CompilerParams(vmem_limit_bytes=12 * 1024 * 1024),
        cost_estimate=pl.CostEstimate(flops=1024, bytes_accessed=1024, transcendentals=0),
    )(mix_weights, counts, total, history, cotangent)


def spread_of(load, count, width):
    zero = jnp.zeros((STEP, width), F32)
    mean = column_sum(each_rows(count, lambda i, acc: acc + load(i), zero)) / count

    def squares(i, acc):
        centred = load(i) - mean
        return acc + centred * centred

    return mean, lax.rsqrt(column_sum(each_rows(count, squares, zero)) / count + EPSILON)


def project_kernel(
    at_ref, x0, x1, x2, x3, n0, n1, n2, n3, cosine, sine, w_qkv, x_all, norms, normed, stats, qkv, project
):
    at = at_ref[0]
    part, tokens = x0.shape
    model = w_qkv.shape[1]
    for e, (piece, norm) in enumerate(((x0, n0), (x1, n1), (x2, n2), (x3, n3))):
        rows = pl.ds(pl.multiple_of((at ^ e) * part, 64), part)
        x_all[rows, :] = piece[...]
        norms[rows, :] = norm[...].T[:part]
    mean, scale = spread_of(lambda i: x_all[rows_at(i), :].astype(F32), model, tokens)
    stats[0:1] = mean
    stats[1:2] = scale

    def normalise(i, _):
        rows = rows_at(i)
        xhat = (x_all[rows, :].astype(F32) - mean) * scale
        normed[rows, :] = (xhat * norms[rows, 0:1] + norms[rows, 1:2]).astype(BF16)

    each_rows(model, normalise)
    project[...] = dot(w_qkv[...], normed[...], 1, 0)
    width = HEAD_DIM // 2
    for block, factor in ((0, HEAD_DIM ** (-0.5)), (1, 1.0)):
        for start in range(block * part, (block + 1) * part, HEAD_DIM):
            front, back = project[start : start + width], project[start + width : start + HEAD_DIM]
            cos, sin = cosine[...] * factor, sine[...] * factor
            qkv[start : start + width] = (front * cos - back * sin).astype(BF16)
            qkv[start + width : start + HEAD_DIM] = (back * cos + front * sin).astype(BF16)
    qkv[2 * part :] = project[2 * part :].astype(BF16)


def attention_kernel(at_ref, qkv, w_out, x_all, send, keep, x_half, heads_out, probs, scores):
    at = at_ref[0]
    part, tokens = heads_out.shape
    half = tokens // 2
    for h in range(part // HEAD_DIM):
        head = slice(h * HEAD_DIM, (h + 1) * HEAD_DIM)
        for t in range(2):
            now = slice(t * half, (t + 1) * half)
            count = (t + 1) * half
            query = qkv[head, now]
            key = qkv[part + h * HEAD_DIM : part + (h + 1) * HEAD_DIM, :count]
            value = qkv[2 * part + h * HEAD_DIM : 2 * part + (h + 1) * HEAD_DIM, :count]
            scores[:count] = dot(key, query, 0, 0)

            def masked_top(i, acc):
                rows = rows_at(i)
                behind = lax.broadcasted_iota(jnp.int32, (STEP, half), 0) + (i * STEP - t * half)
                found = jnp.where(behind <= lax.broadcasted_iota(jnp.int32, (STEP, half), 1), scores[rows, :], -1e30)
                scores[rows, :] = found
                return jnp.maximum(acc, found)

            top = each_rows(
                t * half, lambda i, acc: jnp.maximum(acc, scores[rows_at(i), :]), jnp.full((STEP, half), -1e30, F32)
            )
            top = jnp.max(each_rows(count, masked_top, top, first=t * half), axis=0, keepdims=True)

            def raise_rows(i, acc):
                rows = rows_at(i)
                found = jnp.exp(scores[rows, :] - top)
                scores[rows, :] = found
                return acc + found

            total = 1.0 / column_sum(each_rows(count, raise_rows, jnp.zeros((STEP, half), F32)))

            def settle(i, _):
                rows = rows_at(i)
                probs[h, rows, now] = (scores[rows, :] * total).astype(BF16)

            each_rows(count, settle)
            heads_out[head, now] = dot(value, probs[h, :count, now], 1, 0).astype(BF16)
    own = pl.multiple_of((at % 2) * half, half)
    other = pl.multiple_of((1 - at % 2) * half, half)
    send[...] = dot(w_out[...], heads_out[:, pl.ds(other, half)], 0, 0).astype(BF16)
    keep[...] = dot(w_out[...], heads_out[:, pl.ds(own, half)], 0, 0)
    x_half[...] = x_all[:, pl.ds(own, half)]


def output_gradient_kernel(
    all_tokens, at_ref, self_ref, counts_ref, total_ref, c0, c1, c2, c3, w_down, g_out, d_active, cot_half, cot_all
):
    at = at_ref[0]
    part, tokens = c0.shape
    half = tokens // 2
    for e, piece in enumerate((c0, c1, c2, c3)):
        cot_all[pl.ds(pl.multiple_of((at ^ e) * part, 64), part), :] = piece[...]
    for place, side in enumerate((at % 2, 1 - at % 2)):
        now = pl.ds(pl.multiple_of(side * half, half), half)
        factor = live_row(all_tokens, counts_ref, total_ref, half, side * half)

        def scale(i, _, now=now, factor=factor, place=place):
            rows = rows_at(i)
            grad = cot_all[rows, now].astype(F32) * factor
            g_out[rows, place * half : (place + 1) * half] = (self_ref[0] * grad).astype(BF16)
            if place == 0:
                cot_half[rows, :] = cot_all[rows, now]

        each_rows(cot_all.shape[0], scale)
    d_active[...] = dot(w_down[...], g_out[...], 1, 0)


def middle_kernel(x_half, chip, received, norms, middle, stats, normed):
    model, half = chip.shape

    def add(i, _):
        rows = rows_at(i)
        middle[rows, :] = x_half[rows, :].astype(F32) + chip[rows, :] + received[rows, :].astype(F32)

    each_rows(model, add)
    mean, scale = spread_of(lambda i: middle[rows_at(i), :], model, half)
    stats[0:1] = mean
    stats[1:2] = scale

    def normalise(i, _):
        rows = rows_at(i)
        xhat = (middle[rows, :] - mean) * scale
        normed[rows, :] = (xhat * norms[rows, 2:3] + norms[rows, 3:4]).astype(BF16)

    each_rows(model, normalise)


def feed_forward_kernel(own, other, w_up, d_active, normed, active, d_hidden, send, keep, hidden):
    half = own.shape[1]
    normed[:, :half] = own[...]
    normed[:, half:] = other[...]
    hidden[...] = dot(w_up[...], normed[...], 0, 0)

    def bend(i, _):
        rows = rows_at(i)
        u = hidden[rows, :]
        squared = u * u
        curve = jnp.tanh(0.7978845608028654 * u * (1.0 + 0.044715 * squared))
        lifted = 0.5 * (1.0 + curve)
        active[rows, :] = (u * lifted).astype(BF16)
        slope = lifted + u * (0.5 * (1.0 - curve * curve)) * (
            0.7978845608028654 + (3 * 0.044715 * 0.7978845608028654) * squared
        )
        d_hidden[rows, :] = (slope * d_active[rows, :]).astype(BF16)

    each_rows(hidden.shape[0], bend)
    send[...] = dot(w_up[...], d_hidden[:, half:], 1, 0).astype(BF16)
    keep[...] = dot(w_up[...], d_hidden[:, :half], 1, 0)


def store_blocks(at, total, part, send, keep):
    for place in range(2):
        for low, out in ((1, send), (0, keep)):
            rows = pl.ds(pl.multiple_of((at ^ (2 * place + low)) * part, 64), part)
            out[place * part : (place + 1) * part] = total[rows, :].astype(out.dtype)


def output_kernel(at_ref, active, w_down, middle, send, keep, total):
    at = at_ref[0]
    model, half = middle.shape
    part = send.shape[0] // 2
    own = pl.ds(pl.multiple_of((at % 2) * half, half), half)
    other = pl.ds(pl.multiple_of((1 - at % 2) * half, half), half)
    total[:, own] = dot(w_down[...], active[:, :half], 0, 0) + 0.5 * middle[...]
    total[:, other] = dot(w_down[...], active[:, half:], 0, 0)
    store_blocks(at, total, part, send, keep)


def fold_lanes(value):
    return sum(value[:, k : k + 128] for k in range(0, value.shape[1], 128))


def as_row(columns):
    return column_sum(columns[...].T)


def middle_gradient_kernel(
    all_tokens, at_ref, self_ref, counts_ref, total_ref, chip, received, middle, stats, cot_half, norms,
    d_middle, g_mid, gains, d_normed, gain_sums, bias_sums,
):
    model, half = chip.shape
    mean, scale = stats[0:1], stats[1:2]
    zero = jnp.zeros((STEP, half), F32)

    def sums(i, acc):
        rows = rows_at(i)
        grad = chip[rows, :] + received[rows, :].astype(F32)
        d_normed[rows, :] = grad
        xhat = (middle[rows, :] - mean) * scale
        both = grad * xhat
        gain_sums[rows, :] = fold_lanes(both)
        bias_sums[rows, :] = fold_lanes(grad)
        gain = norms[rows, 2:3]
        return acc[0] + grad * gain, acc[1] + both * gain

    first, second = (column_sum(v) / model for v in each_rows(model, sums, (zero, zero)))
    factor = self_ref[0] * live_row(all_tokens, counts_ref, total_ref, half, (at_ref[0] % 2) * half)

    def finish(i, _):
        rows = rows_at(i)
        xhat = (middle[rows, :] - mean) * scale
        found = cot_half[rows, :].astype(F32) * factor + scale * (
            d_normed[rows, :] * norms[rows, 2:3] - first - xhat * second
        )
        d_middle[rows, :] = found
        g_mid[rows, :] = found.astype(BF16)

    each_rows(model, finish)
    gains[0:1] = as_row(gain_sums)
    gains[1:2] = as_row(bias_sums)


def attention_gradient_kernel(
    at_ref, own, other, w_out, qkv, probs, cosine, sine,
    d_project, g_mid, d_heads, d_scores, products, d_queries, d_keys, d_values,
):
    at = at_ref[0]
    half = own.shape[1]
    part = w_out.shape[0]
    g_mid[:, pl.ds(pl.multiple_of((at % 2) * half, half), half)] = own[...]
    g_mid[:, pl.ds(pl.multiple_of((1 - at % 2) * half, half), half)] = other[...]
    d_heads[...] = dot(w_out[...], g_mid[...], 1, 0).astype(BF16)
    width = HEAD_DIM // 2
    for h in range(part // HEAD_DIM):
        head = slice(h * HEAD_DIM, (h + 1) * HEAD_DIM)
        query = qkv[head]
        key = qkv[part + h * HEAD_DIM : part + (h + 1) * HEAD_DIM]
        value = qkv[2 * part + h * HEAD_DIM : 2 * part + (h + 1) * HEAD_DIM]
        for t in range(2):
            now = slice(t * half, (t + 1) * half)
            count = (t + 1) * half
            products[:count] = dot(value[:, :count], d_heads[head, now], 0, 0)

            def weigh(i, acc):
                rows = rows_at(i)
                return acc + products[rows, :] * probs[h, rows, now].astype(F32)

            inner = column_sum(each_rows(count, weigh, jnp.zeros((STEP, half), F32)))

            def settle(i, _):
                rows = rows_at(i)
                d_scores[rows, :] = (probs[h, rows, now].astype(F32) * (products[rows, :] - inner)).astype(BF16)

            each_rows(count, settle)
            d_queries[:, now] = dot(key[:, :count], d_scores[:count], 1, 0) * HEAD_DIM ** (-0.5)
            d_key = dot(query[:, now], d_scores[:count], 1, 1)
            d_value = dot(d_heads[head, now], probs[h, :count, now], 1, 1)
            if t == 0:
                d_keys[:, :half] = d_key
                d_values[:, :half] = d_value
            else:
                d_keys[:, :half] += d_key[:, :half]
                d_values[:, :half] += d_value[:, :half]
                d_keys[:, half:] = d_key[:, half:]
                d_values[:, half:] = d_value[:, half:]
        for block, found in ((0, d_queries), (1, d_keys)):
            start = block * part + h * HEAD_DIM
            front, back = found[:width], found[width:]
            d_project[start : start + width] = (front * cosine[...] + back * sine[...]).astype(BF16)
            d_project[start + width : start + HEAD_DIM] = (back * cosine[...] - front * sine[...]).astype(BF16)
        d_project[2 * part + h * HEAD_DIM : 2 * part + (h + 1) * HEAD_DIM] = d_values[...].astype(BF16)


def input_gradient_kernel(
    at_ref, d_project, w_qkv, x_all, stats, d_middle, norms, gains, mix, send, keep, sums, total, gain_sums, bias_sums
):
    at = at_ref[0]
    model, half = d_middle.shape
    tokens = x_all.shape[1]
    part = send.shape[0] // 2
    total[...] = dot(w_qkv[...], d_project[...], 0, 0)
    mean, scale = stats[0:1], stats[1:2]
    zero = jnp.zeros((STEP, tokens), F32)
    own = pl.ds(pl.multiple_of((at % 2) * half, half), half)

    def body(i, acc):
        rows = rows_at(i)
        grad = total[rows, :]
        xhat = (x_all[rows, :].astype(F32) - mean) * scale
        both = grad * xhat
        gain_sums[rows, :] = fold_lanes(both)
        bias_sums[rows, :] = fold_lanes(grad)
        gain = norms[rows, 0:1]
        lifted = grad * gain
        total[rows, :] = lifted * scale
        total[rows, own] += 0.5 * d_middle[rows, :]
        return acc[0] + lifted, acc[1] + both * gain

    first, second = each_rows(model, body, (zero, zero))
    store_blocks(at, total, part, send, keep)
    sums[...] = jnp.zeros_like(sums)
    sums[0:1] = as_row(gain_sums)
    sums[1:2] = as_row(bias_sums)
    sums[2:4] = 0.5 * gains[...]
    sums[4:5, :tokens] = column_sum(first) / model
    sums[5:6, :tokens] = column_sum(second) / model
    sums[6:7, :128] = mix[...]


def mixed_kernel(
    all_tokens, self_ref, counts_ref, total_ref, chip, received, running, cotangent, d_mix, mixed, row, table
):
    layers = d_mix.shape[0]
    part, tokens = chip.shape
    live = live_row(all_tokens, counts_ref, total_ref, tokens, 0)

    def body(i, acc):
        rows = rows_at(i)
        output = chip[rows, :] + received[rows, :].astype(F32)
        mixed[rows, :] = (self_ref[0] * output + running[rows, :]).astype(BF16)
        return acc + fold_lanes(cotangent[rows, :].astype(F32) * live * output)

    found = each_rows(part, body, jnp.zeros((STEP, 128), F32))
    table[...] = jnp.zeros_like(table)
    table[:layers] = jnp.sum(d_mix[...], axis=1)
    table[layers : layers + 1] = column_sum(found)
    row[...] = as_row(table)


def d_input_kernel(chip, received, x_in, stats, sums, d_input):
    part, tokens = chip.shape
    mean, scale = stats[0:1], stats[1:2]
    first, second = sums[4:5, :tokens], sums[5:6, :tokens]

    def body(i, _):
        rows = rows_at(i)
        xhat = (x_in[rows, :].astype(F32) - mean) * scale
        d_input[rows, :] = chip[rows, :] + received[rows, :].astype(F32) - scale * (first + xhat * second)

    each_rows(part, body)


def local(
    width,
    row_devices,
    x_in,
    history,
    cotangent,
    counts,
    positions,
    mix_weights,
    self_weight,
    first_norm_gain,
    first_norm_bias,
    w_qkv,
    w_out,
    second_norm_gain,
    second_norm_bias,
    w_up,
    w_down,
):
    part, tokens = x_in.shape
    model = w_out.shape[1]
    hidden_units = w_up.shape[1]
    half = tokens // 2
    layers = mix_weights.shape[0]
    all_tokens = float(tokens * row_devices)
    at_width = lax.axis_index("width")
    at = at_width.astype(jnp.int32)[None]
    me = lax.axis_index("rows").astype(jnp.int32)[None]
    norms = jnp.pad(
        jnp.stack([first_norm_gain, first_norm_bias, second_norm_gain, second_norm_bias]), ((0, 124), (0, -part % 128))
    )
    inverse = 1.0 / 10000.0 ** (jnp.arange(HEAD_DIM // 2, dtype=F32) * 2.0 / HEAD_DIM)
    angles = positions[None, :].astype(F32) * inverse[:, None]
    cosine, sine = jnp.cos(angles), jnp.sin(angles)
    to_width = lambda value, offset: xor_send(value, "width", width, offset)
    w_qkv = w_qkv.reshape(3 * part, model)
    x_in, cotangent, counts = after((x_in, cotangent, counts), at, me)

    x_far, x_near = to_width(x_in, 2), to_width(x_in, 1)
    cot_far, cot_near = to_width(cotangent, 2), to_width(cotangent, 1)
    norms = [norms[:8]] + [to_width(norms[:8], e) for e in range(1, width)]
    total = sum_counts(counts, row_devices)
    x_both, cot_both = to_width(x_far, 1), to_width(cot_far, 1)

    x_all, norms, normed_one, stats_one, qkv = kernel(
        project_kernel,
        (
            shape(model, tokens, kind=BF16),
            shape(model, 8),
            shape(model, tokens, kind=BF16),
            shape(2, tokens),
            shape(3 * part, tokens, kind=BF16),
        ),
        [at],
        [x_in, x_near, x_far, x_both, *norms, cosine, sine, w_qkv],
        [pltpu.VMEM((3 * part, tokens), F32)],
    )
    send, keep, x_half, heads_out, probs = kernel(
        attention_kernel,
        (
            shape(model, half, kind=BF16),
            shape(model, half),
            shape(model, half, kind=BF16),
            shape(part, tokens, kind=BF16),
            shape(part // HEAD_DIM, tokens, tokens, kind=BF16),
        ),
        [at],
        [after(qkv, cot_far, total), w_out, x_all],
        [pltpu.VMEM((tokens, half), F32)],
    )
    chip, send = add([keep, to_width(send, 1)], (0, model, F32), (0, model, BF16))
    received = to_width(send, 2)

    running, d_history, d_mix = mix_history(
        all_tokens, mix_weights, counts, total, history, after(cotangent, chip)
    )
    g_out, d_active, cot_half = kernel(
        functools.partial(output_gradient_kernel, all_tokens),
        (shape(model, tokens, kind=BF16), shape(hidden_units, tokens), shape(model, half, kind=BF16)),
        [at, self_weight, counts, total],
        [cotangent, cot_near, cot_far, cot_both, after(w_down, running)],
        [pltpu.VMEM((model, tokens), BF16)],
    )

    middle, stats_two, normed_own = kernel(
        middle_kernel,
        (shape(model, half), shape(2, half), shape(model, half, kind=BF16)),
        [],
        [x_half, chip, after(received, g_out), norms],
    )
    normed_two, active, d_hidden, send, keep = kernel(
        feed_forward_kernel,
        (
            shape(model, tokens, kind=BF16),
            shape(hidden_units, tokens, kind=BF16),
            shape(hidden_units, tokens, kind=BF16),
            shape(model, half, kind=BF16),
            shape(model, half),
        ),
        [],
        [normed_own, to_width(normed_own, 1), w_up, d_active],
        [pltpu.VMEM((hidden_units, tokens), F32)],
    )

    down = Stream(row_devices, 0, hidden_units, "halving")
    up = Stream(row_devices, 0, model, "crossed")
    down_parts = weight_gradient(me, [down], active, after(g_out, send))[0]
    down_got = start_stage(down, down_parts, 0)
    chip, send = add([keep, after(to_width(send, 1), *down_parts)], (0, model, F32), (0, model, BF16))
    received = to_width(send, 2)
    up_parts = weight_gradient(me, [up], normed_two, after(d_hidden, chip))[0]
    up_got = start_stage(up, up_parts, 0)

    blocks = (shape(2 * part, tokens, kind=BF16), shape(2 * part, tokens))
    out_send, out_keep = kernel(
        output_kernel,
        blocks,
        [at],
        [active, w_down, after(middle, *up_parts)],
        [pltpu.VMEM((model, tokens), F32)],
    )
    out_near = to_width(out_send, 1)

    d_middle, g_own, gains_two = kernel(
        functools.partial(middle_gradient_kernel, all_tokens),
        (shape(model, half), shape(model, half, kind=BF16), shape(2, model)),
        [at, self_weight, counts, total],
        [chip, after(received, out_keep), middle, stats_two, cot_half, norms],
        [pltpu.VMEM((model, half), F32), pltpu.VMEM((model, 128), F32), pltpu.VMEM((model, 128), F32)],
    )
    g_other = to_width(g_own, 1)
    down_parts = add_stage(down, down_parts, [after(v, g_own) for v in down_got], 0)
    down_got = start_stage(down, down_parts, 1)
    up_parts = add_stage(up, up_parts, [after(v, down_parts[0]) for v in up_got], 0)
    up_got = start_stage(up, up_parts, 1)
    d_project, g_mid = kernel(
        attention_gradient_kernel,
        (shape(3 * part, tokens, kind=BF16), shape(model, tokens, kind=BF16)),
        [at],
        [g_own, after(g_other, *up_parts), w_out, qkv, probs, cosine, sine],
        [
            pltpu.VMEM((part, tokens), BF16),
            pltpu.VMEM((tokens, half), BF16),
            pltpu.VMEM((tokens, half), F32),
            pltpu.VMEM((HEAD_DIM, tokens), F32),
            pltpu.VMEM((HEAD_DIM, tokens), F32),
            pltpu.VMEM((HEAD_DIM, tokens), F32),
        ],
    )
    tail_rows = 4 * part
    tail = [
        Stream(row_devices, 0, tail_rows * 2 // 3, "near"),
        Stream(row_devices, tail_rows * 2 // 3, tail_rows // 3, "far"),
    ]
    tail_parts = weight_gradient(me, tail, d_project, normed_one, heads_out, g_mid)
    tail_got = [start_stage(s, p, 0) for s, p in zip(tail, tail_parts)]

    out_chip, out_send = add(
        [out_keep, after(out_near, *tail_parts[0])], (0, part, F32), (part, 2 * part, BF16)
    )
    out_far = to_width(out_send, 2)
    down_parts = add_stage(down, down_parts, [after(v, out_send) for v in down_got], 1)
    down_got = start_stage(down, down_parts, 2)
    up_parts = add_stage(up, up_parts, [after(v, down_parts[0]) for v in up_got], 1)
    up_got = start_stage(up, up_parts, 2)
    mixed, mix_row = kernel(
        functools.partial(mixed_kernel, all_tokens),
        (shape(part, tokens, kind=BF16), shape(1, 128)),
        [self_weight, counts, total],
        [out_chip, after(out_far, up_parts[0]), running, cotangent, d_mix],
        [pltpu.VMEM((128, 128), F32)],
    )
    in_send, in_keep, sums = kernel(
        input_gradient_kernel,
        blocks + (shape(8, model),),
        [at],
        [d_project, w_qkv, x_all, stats_one, d_middle, norms, gains_two, mix_row],
        [pltpu.VMEM((model, tokens), F32), pltpu.VMEM((model, 128), F32), pltpu.VMEM((model, 128), F32)],
    )
    in_near = to_width(in_send, 1)
    tail_parts = [
        add_stage(s, p, [after(v, in_send) for v in g], 0) for s, p, g in zip(tail, tail_parts, tail_got)
    ]
    tail_got = [start_stage(s, p, 1) for s, p in zip(tail, tail_parts)]
    in_chip, in_send = add(
        [in_keep, after(in_near, *tail_parts[0], *tail_parts[1])], (0, part, F32), (part, 2 * part, BF16)
    )
    in_far = to_width(in_send, 2)
    sums = sum_small(after(sums, in_send), "width", width)
    down_value = sum_rest(down, add_stage(down, down_parts, [after(v, in_send) for v in down_got], 2)[0])
    up_value = sum_rest(up, add_stage(up, up_parts, [after(v, down_value) for v in up_got], 2)[0])
    for stage in range(len(down.digits) - 1, 0, -1):
        down_value = join(gather_stage(down, down_value, stage))
        up_value = join(gather_stage(up, up_value, stage))
        if stage == len(down.digits) - 1:
            d_input = kernel(
                d_input_kernel,
                shape(part, tokens),
                [],
                [in_chip, after(in_far, down_value), x_in, stats_one, sums],
            )
            tail_values = [
                sum_rest(s, add_stage(s, p, [after(v, d_input) for v in g], 1)[0])
                for s, p, g in zip(tail, tail_parts, tail_got)
            ]
            tail_values = [join(gather_stage(s, v, 1)) for s, v in zip(tail, tail_values)]
            small = sum_small(after(sums, d_input), "rows", row_devices)
    down_pieces = gather_stage(down, down_value, 0)
    up_pieces = gather_stage(up, up_value, 0)
    tail_pieces = [piece for s, v in zip(tail, tail_values) for piece in gather_stage(s, v, 0)]
    d_w_down = place(me, [down], down_pieces, (hidden_units,))[0]
    d_w_up = place(me, [up], up_pieces, (model,))[0]
    d_w_qkv, d_w_out = place(me, tail, tail_pieces, (3 * part, part))
    small = after(small, d_w_qkv)
    ends = [lax.dynamic_slice(small, (i, at_width * part), (1, part))[0] for i in range(4)]
    return (
        mixed,
        d_input,
        d_history,
        small[6, :layers],
        small[6, layers : layers + 1],
        ends[0],
        ends[1],
        d_w_qkv.reshape(3, part, model),
        d_w_out,
        ends[2],
        ends[3],
        d_w_up,
        d_w_down,
    )


def solution(mesh):
    return jax.shard_map(
        functools.partial(local, mesh.shape["width"], mesh.shape["rows"]),
        mesh=mesh,
        in_specs=(
            P("width", "rows"),
            P(None, "width", "rows"),
            P("width", "rows"),
            P("rows"),
            P("rows"),
            P(),
            P(),
            P("width"),
            P("width"),
            P(None, "width", None),
            P("width", None),
            P("width"),
            P("width"),
            P(None, "width"),
            P("width", None),
        ),
        out_specs=(
            P("width", "rows"),
            P("width", "rows"),
            P(None, "width", "rows"),
            P(),
            P(),
            P("width"),
            P("width"),
            P(None, "width", None),
            P("width", None),
            P("width"),
            P("width"),
            P(None, "width"),
            P("width", None),
        ),
        check_vma=False,
    )
```

```python
import functools

import jax
import jax.numpy as jnp
import numpy as np
from jax import lax
from jax.experimental import pallas as pl
from jax.experimental.pallas import tpu as pltpu
from jax.sharding import PartitionSpec as P

HEAD_DIM = 64
EPSILON = 1e-05
BF16 = jnp.bfloat16
F32 = jnp.float32
STEP = 16


def shape(*dims, kind=F32):
    return jax.ShapeDtypeStruct(dims, kind)


class Order:
    last = None
    cost = 10**9


def kernel(body, outs, scalars, arrays, scratch=(), limit=12):
    arrays = list(arrays)
    if Order.last is not None:
        arrays[0] = after(arrays[0], Order.last)
    found = pl.pallas_call(
        body,
        out_shape=outs,
        in_specs=[pl.BlockSpec(memory_space=pltpu.SMEM)] * len(scalars)
        + [pl.BlockSpec(memory_space=pltpu.VMEM)] * len(arrays),
        out_specs=jax.tree.map(lambda _: pl.BlockSpec(memory_space=pltpu.VMEM), outs),
        scratch_shapes=list(scratch),
        compiler_params=pltpu.CompilerParams(vmem_limit_bytes=limit * 1024 * 1024),
        cost_estimate=pl.CostEstimate(flops=Order.cost, bytes_accessed=1024, transcendentals=0),
    )(*scalars, *arrays)
    Order.last = jax.tree.leaves(found)[0]
    return found


def after(value, *others):
    return lax.optimization_barrier((value, others))[0]


def dot(left, right, left_dim, right_dim):
    return lax.dot_general(left, right, (((left_dim,), (right_dim,)), ((), ())), preferred_element_type=F32)


def rows_at(i):
    return pl.ds(pl.multiple_of(i * STEP, STEP), STEP)


def each_rows(count, body, start=None, first=0):
    return lax.fori_loop(first // STEP, count // STEP, body, start, unroll=4)


def column_sum(value):
    return jnp.sum(value, axis=0, keepdims=True)


def xor_send(value, axis, size, offset):
    return lax.ppermute(value, axis, [(i, i ^ offset) for i in range(size)])


def add_kernel(count, cuts, *refs):
    parts, outs = refs[:count], refs[count:]

    def one(rows):
        found = parts[0][rows, :].astype(F32)
        for part in parts[1:]:
            found = found + part[rows, :].astype(F32)
        return found

    for (first, last), out in zip(cuts, outs):
        if (last - first) % STEP:
            out[...] = one(slice(first, last)).astype(out.dtype)
        else:

            def body(i, _, first=first, out=out):
                out[rows_at(i), :] = one(pl.ds(pl.multiple_of(first + i * STEP, STEP), STEP)).astype(out.dtype)

            each_rows(last - first, body)


def add(parts, *cuts):
    columns = parts[0].shape[1]
    outs = tuple(shape(last - first, columns, kind=kind) for first, last, kind in cuts)
    return list(kernel(functools.partial(add_kernel, len(parts), [cut[:2] for cut in cuts]), outs, [], parts))


def sum_small(value, axis, size):
    stride = 1
    while stride < size:
        value = add([value, xor_send(value, axis, size, stride)], (0, value.shape[0], F32))[0]
        stride *= 2
    return value


def join_kernel(*refs):
    out, start = refs[-1], 0
    for piece in refs[:-1]:
        out[start : start + piece.shape[0]] = piece[...]
        start += piece.shape[0]


def join(pieces):
    rows = sum(piece.shape[0] for piece in pieces)
    return kernel(join_kernel, shape(rows, pieces[0].shape[1], kind=pieces[0].dtype), [], pieces)


def chunks_of(count, rows):
    count = min(count, 8)
    while rows % (16 * count):
        count //= 2
    return count


def digits_of(count, kind):
    if kind == "halving":
        strides = []
        stride = 1
        while stride < count:
            strides.append((stride, 2))
            stride *= 2
        return strides
    strides = digits_of(count, "halving")
    return [strides[1], strides[0]] + strides[2:]


def offsets_of(digits):
    found = [0]
    for stride, radix in digits:
        found = [low + e * stride for low in found for e in range(radix)]
    return found


class Stream:
    def __init__(self, row_devices, first, rows, kind):
        self.first, self.rows = first, rows
        self.count = chunks_of(row_devices, rows)
        self.row_devices = row_devices
        self.digits = digits_of(self.count, kind)
        self.chunk = rows // self.count

    def parts(self):
        stride, radix = self.digits[0]
        rest = offsets_of(self.digits[1:])
        return [[e * stride + low for low in rest] for e in range(radix)]

    def send(self, value, offset):
        return xor_send(value, "rows", self.row_devices, offset)


def weight_gradient_kernel(streams, pairs, me_ref, *refs):
    operands, outs, scratch = refs[: 2 * pairs], list(refs[2 * pairs : -1]), refs[-1]
    start = 0
    for i in range(pairs):
        left, right = operands[2 * i], operands[2 * i + 1]
        count = left.shape[0]
        scratch[start : start + count] = dot(left[...], right[...], 1, 1).astype(BF16)
        start += count
    for stream in streams:
        for offsets in stream.parts():
            out = outs.pop(0)
            for place, offset in enumerate(offsets):
                chunk = (me_ref[0] % stream.count) ^ offset
                at = pl.multiple_of(stream.first + chunk * stream.chunk, 16)
                out[place * stream.chunk : (place + 1) * stream.chunk] = scratch[pl.ds(at, stream.chunk), :]


def weight_gradient(me, streams, *operands):
    pairs = len(operands) // 2
    total = sum(operands[2 * i].shape[0] for i in range(pairs))
    columns = operands[1].shape[0]
    outs = tuple(
        shape(len(offsets) * stream.chunk, columns, kind=BF16) for stream in streams for offsets in stream.parts()
    )
    found = list(
        kernel(
            functools.partial(weight_gradient_kernel, streams, pairs),
            outs,
            [me],
            operands,
            [pltpu.VMEM((total, columns), BF16)],
        )
    )
    return [[found.pop(0) for _ in stream.parts()] for stream in streams]


def start_stage(stream, parts, stage):
    stride, radix = stream.digits[stage]
    return [stream.send(parts[e], e * stride) for e in range(1, radix)]


def add_stage(stream, parts, received, stage):
    rows = parts[0].shape[0]
    radix = 1 if stage + 1 == len(stream.digits) else stream.digits[stage + 1][1]
    size = rows // radix
    return add([parts[0]] + received, *((e * size, (e + 1) * size, BF16) for e in range(radix)))


def sum_rest(stream, value):
    stride = stream.count
    while stride < stream.row_devices:
        value = add([value, stream.send(value, stride)], (0, value.shape[0], BF16))[0]
        stride *= 2
    return value


def gather_stage(stream, value, stage):
    stride, radix = stream.digits[stage]
    return [value] + [stream.send(value, e * stride) for e in range(1, radix)]


def place_kernel(streams, bounds, me_ref, *refs):
    pieces, outs = list(refs[: -len(bounds)]), refs[-len(bounds) :]
    for stream in streams:
        for offsets in stream.parts():
            piece = pieces.pop(0)
            for place, offset in enumerate(offsets):
                chunk = (me_ref[0] % stream.count) ^ offset
                row = stream.first + chunk * stream.chunk
                for (first, last), out in zip(bounds, outs):

                    def store(out=out, first=first, piece=piece, place=place, row=row, size=stream.chunk):
                        at = pl.multiple_of(row - first, 16)
                        out[pl.ds(at, size), :] = piece[place * size : (place + 1) * size].astype(F32)

                    if len(bounds) == 1:
                        store()
                    else:
                        pl.when((row >= first) & (row < last))(store)


def place(me, streams, pieces, sizes):
    columns = pieces[0].shape[1]
    bounds, start = [], 0
    for size in sizes:
        bounds.append((start, start + size))
        start += size
    outs = tuple(shape(size, columns) for size in sizes)
    return kernel(functools.partial(place_kernel, streams, bounds), outs, [me], pieces)


def live_row(all_tokens, counts_ref, total_ref, width, first):
    scale = jnp.full((1, width), all_tokens, F32) / jnp.broadcast_to(total_ref[0:1, 0:1], (1, width))
    place = lax.broadcasted_iota(jnp.int32, (1, width), 1) + first
    return jnp.where(place < counts_ref[0], scale, 0.0)


def history_block(live, mix_ref, d_mix_ref, history_ref, cot_ref, running_ref, d_history_ref):
    layers, block, tokens = history_ref.shape
    for i in range(block // STEP):
        rows = slice(i * STEP, (i + 1) * STEP)
        grad = cot_ref[rows].astype(F32) * live
        running = jnp.zeros_like(grad)
        for j in range(layers):
            layer = history_ref[j, rows].astype(F32)
            weight = mix_ref[j]
            running = running + weight * layer
            d_history_ref[j, rows] = (weight * grad).astype(BF16)
            terms = grad * layer
            terms = terms[: STEP // 2] + terms[STEP // 2 :]
            d_mix_ref[j] += sum(terms[:, k : k + 128] for k in range(0, tokens, 128))
        running_ref[rows] = running


def history_kernel(
    all_tokens, block, mix_ref, counts_ref, cot_ref, total_ref, history_ref, running_ref, d_history_ref, d_mix_ref
):
    layers, features, tokens = history_ref.shape
    live = live_row(all_tokens, counts_ref, total_ref, tokens, 0)
    d_mix_ref[...] = jnp.zeros_like(d_mix_ref)

    def body(history_part, d_history_part):
        at = pl.multiple_of(pl.program_id(0) * block, block)
        history_block(
            live, mix_ref, d_mix_ref, history_part, cot_ref.at[pl.ds(at, block)], running_ref.at[pl.ds(at, block)],
            d_history_part,
        )

    whole = pl.BlockSpec((layers, block, tokens), lambda i: (0, i, 0))
    pltpu.emit_pipeline(body, grid=(features // block,), in_specs=[whole], out_specs=[whole])(
        history_ref, d_history_ref
    )


def mix_history(all_tokens, mix_weights, counts, total, history, cotangent):
    layers, features, tokens = history.shape
    vmem, hbm = pl.BlockSpec(memory_space=pltpu.VMEM), pl.BlockSpec(memory_space=pltpu.HBM)
    smem = pl.BlockSpec(memory_space=pltpu.SMEM)
    found = pl.pallas_call(
        functools.partial(history_kernel, all_tokens, 32),
        out_shape=(
            shape(features, tokens),
            shape(*history.shape, kind=BF16),
            shape(layers, STEP // 2, 128),
        ),
        in_specs=[smem, smem, vmem, vmem, hbm],
        out_specs=(vmem, hbm, vmem),
        compiler_params=pltpu.CompilerParams(vmem_limit_bytes=12 * 1024 * 1024),
        cost_estimate=pl.CostEstimate(flops=Order.cost, bytes_accessed=1024, transcendentals=0),
    )(mix_weights, counts, after(cotangent, Order.last), total, history)
    Order.last = found[0]
    return found


def spread_of(load, count, width):
    zero = jnp.zeros((STEP, width), F32)
    mean = column_sum(each_rows(count, lambda i, acc: acc + load(i), zero)) / count

    def squares(i, acc):
        centred = load(i) - mean
        return acc + centred * centred

    return mean, lax.rsqrt(column_sum(each_rows(count, squares, zero)) / count + EPSILON)


def prepare_kernel(counts_ref, positions, rates, g1, b1, g2, b2, count, norms, cosine, sine):
    count[...] = jnp.zeros(count.shape, F32) + counts_ref[0].astype(F32)
    norms[...] = jnp.zeros_like(norms)
    for i, ref in enumerate((g1, b1, g2, b2)):
        norms[i : i + 1, : ref.shape[1]] = ref[...]
    angles = positions[...].astype(F32) * rates[...]
    cosine[...] = jnp.cos(angles)
    sine[...] = jnp.sin(angles)


def project_kernel(
    at_ref, x0, x1, x2, x3, n01, n23, cosine, sine, w_qkv, x_all, norms, normed, stats, qkv, project
):
    at = at_ref[0]
    part, tokens = x0.shape
    model = w_qkv.shape[1]
    near, far = n01[...].T, n23[...].T
    for e, (piece, norm) in enumerate(((x0, near), (x1, near), (x2, far), (x3, far))):
        rows = pl.ds(pl.multiple_of((at ^ e) * part, 64), part)
        x_all[rows, :] = piece[...]
        norms[rows, :] = norm[:part, 8 * (e % 2) : 8 * (e % 2) + 8]
    mean, scale = spread_of(lambda i: x_all[rows_at(i), :].astype(F32), model, tokens)
    stats[0:1] = mean
    stats[1:2] = scale

    def normalise(i, _):
        rows = rows_at(i)
        xhat = (x_all[rows, :].astype(F32) - mean) * scale
        normed[rows, :] = (xhat * norms[rows, 0:1] + norms[rows, 1:2]).astype(BF16)

    each_rows(model, normalise)
    project[...] = dot(w_qkv[...], normed[...], 1, 0)
    width = HEAD_DIM // 2
    for block, factor in ((0, HEAD_DIM ** (-0.5)), (1, 1.0)):
        for start in range(block * part, (block + 1) * part, HEAD_DIM):
            front, back = project[start : start + width], project[start + width : start + HEAD_DIM]
            cos, sin = cosine[...] * factor, sine[...] * factor
            qkv[start : start + width] = (front * cos - back * sin).astype(BF16)
            qkv[start + width : start + HEAD_DIM] = (back * cos + front * sin).astype(BF16)
    qkv[2 * part :] = project[2 * part :].astype(BF16)


def attention_kernel(at_ref, qkv, w_out, x_all, send, keep, x_half, heads_out, probs, scores):
    at = at_ref[0]
    part, tokens = heads_out.shape
    half = tokens // 2
    for h in range(part // HEAD_DIM):
        head = slice(h * HEAD_DIM, (h + 1) * HEAD_DIM)
        for t in range(2):
            now = slice(t * half, (t + 1) * half)
            count = (t + 1) * half
            query = qkv[head, now]
            key = qkv[part + h * HEAD_DIM : part + (h + 1) * HEAD_DIM, :count]
            value = qkv[2 * part + h * HEAD_DIM : 2 * part + (h + 1) * HEAD_DIM, :count]
            scores[:count] = dot(key, query, 0, 0)

            def masked_top(i, acc):
                rows = rows_at(i)
                behind = lax.broadcasted_iota(jnp.int32, (STEP, half), 0) + (i * STEP - t * half)
                found = jnp.where(behind <= lax.broadcasted_iota(jnp.int32, (STEP, half), 1), scores[rows, :], -1e30)
                scores[rows, :] = found
                return jnp.maximum(acc, found)

            top = each_rows(
                t * half, lambda i, acc: jnp.maximum(acc, scores[rows_at(i), :]), jnp.full((STEP, half), -1e30, F32)
            )
            top = jnp.max(each_rows(count, masked_top, top, first=t * half), axis=0, keepdims=True)

            def raise_rows(i, acc):
                rows = rows_at(i)
                found = jnp.exp(scores[rows, :] - top)
                scores[rows, :] = found
                return acc + found

            total = 1.0 / column_sum(each_rows(count, raise_rows, jnp.zeros((STEP, half), F32)))

            def settle(i, _):
                rows = rows_at(i)
                probs[h, rows, now] = (scores[rows, :] * total).astype(BF16)

            each_rows(count, settle)
            heads_out[head, now] = dot(value, probs[h, :count, now], 1, 0).astype(BF16)
    own = pl.multiple_of((at % 2) * half, half)
    other = pl.multiple_of((1 - at % 2) * half, half)
    send[...] = dot(w_out[...], heads_out[:, pl.ds(other, half)], 0, 0).astype(BF16)
    keep[...] = dot(w_out[...], heads_out[:, pl.ds(own, half)], 0, 0)
    x_half[...] = x_all[:, pl.ds(own, half)]


def output_gradient_kernel(
    all_tokens, at_ref, self_ref, counts_ref, c0, c1, c2, c3, total_ref, w_down, g_out, d_active, cot_half, cot_all
):
    at = at_ref[0]
    part, tokens = c0.shape
    half = tokens // 2
    for e, piece in enumerate((c0, c1, c2, c3)):
        cot_all[pl.ds(pl.multiple_of((at ^ e) * part, 64), part), :] = piece[...]
    for place, side in enumerate((at % 2, 1 - at % 2)):
        now = pl.ds(pl.multiple_of(side * half, half), half)
        factor = live_row(all_tokens, counts_ref, total_ref, half, side * half)

        def scale(i, _, now=now, factor=factor, place=place):
            rows = rows_at(i)
            grad = cot_all[rows, now].astype(F32) * factor
            g_out[rows, place * half : (place + 1) * half] = (self_ref[0] * grad).astype(BF16)
            if place == 0:
                cot_half[rows, :] = cot_all[rows, now]

        each_rows(cot_all.shape[0], scale)
    d_active[...] = dot(w_down[...], g_out[...], 1, 0)


def middle_kernel(x_half, chip, received, norms, middle, stats, normed):
    model, half = chip.shape

    def add(i, _):
        rows = rows_at(i)
        middle[rows, :] = x_half[rows, :].astype(F32) + chip[rows, :] + received[rows, :].astype(F32)

    each_rows(model, add)
    mean, scale = spread_of(lambda i: middle[rows_at(i), :], model, half)
    stats[0:1] = mean
    stats[1:2] = scale

    def normalise(i, _):
        rows = rows_at(i)
        xhat = (middle[rows, :] - mean) * scale
        normed[rows, :] = (xhat * norms[rows, 2:3] + norms[rows, 3:4]).astype(BF16)

    each_rows(model, normalise)


def feed_forward_kernel(own, other, w_up, d_active, normed, active, d_hidden, send, keep, hidden):
    half = own.shape[1]
    normed[:, :half] = own[...]
    normed[:, half:] = other[...]
    hidden[...] = dot(w_up[...], normed[...], 0, 0)

    def bend(i, _):
        rows = rows_at(i)
        u = hidden[rows, :]
        squared = u * u
        curve = jnp.tanh(0.7978845608028654 * u * (1.0 + 0.044715 * squared))
        lifted = 0.5 * (1.0 + curve)
        active[rows, :] = (u * lifted).astype(BF16)
        slope = lifted + u * (0.5 * (1.0 - curve * curve)) * (
            0.7978845608028654 + (3 * 0.044715 * 0.7978845608028654) * squared
        )
        d_hidden[rows, :] = (slope * d_active[rows, :]).astype(BF16)

    each_rows(hidden.shape[0], bend)
    send[...] = dot(w_up[...], d_hidden[:, half:], 1, 0).astype(BF16)
    keep[...] = dot(w_up[...], d_hidden[:, :half], 1, 0)


def store_blocks(at, total, part, send, keep):
    for place in range(2):
        for low, out in ((1, send), (0, keep)):
            rows = pl.ds(pl.multiple_of((at ^ (2 * place + low)) * part, 64), part)
            out[place * part : (place + 1) * part] = total[rows, :].astype(out.dtype)


def output_kernel(at_ref, active, w_down, middle, send, keep, total):
    at = at_ref[0]
    model, half = middle.shape
    part = send.shape[0] // 2
    own = pl.ds(pl.multiple_of((at % 2) * half, half), half)
    other = pl.ds(pl.multiple_of((1 - at % 2) * half, half), half)
    total[:, own] = dot(w_down[...], active[:, :half], 0, 0) + 0.5 * middle[...]
    total[:, other] = dot(w_down[...], active[:, half:], 0, 0)
    store_blocks(at, total, part, send, keep)


def fold_lanes(value):
    return sum(value[:, k : k + 128] for k in range(0, value.shape[1], 128))


def as_row(columns):
    return column_sum(columns[...].T)


def middle_gradient_kernel(
    all_tokens, at_ref, self_ref, counts_ref, chip, received, total_ref, middle, stats, cot_half, norms,
    d_middle, g_mid, gains, d_normed, gain_sums, bias_sums,
):
    model, half = chip.shape
    mean, scale = stats[0:1], stats[1:2]
    zero = jnp.zeros((STEP, half), F32)

    def sums(i, acc):
        rows = rows_at(i)
        grad = chip[rows, :] + received[rows, :].astype(F32)
        d_normed[rows, :] = grad
        xhat = (middle[rows, :] - mean) * scale
        both = grad * xhat
        gain_sums[rows, :] = fold_lanes(both)
        bias_sums[rows, :] = fold_lanes(grad)
        gain = norms[rows, 2:3]
        return acc[0] + grad * gain, acc[1] + both * gain

    first, second = (column_sum(v) / model for v in each_rows(model, sums, (zero, zero)))
    factor = self_ref[0] * live_row(all_tokens, counts_ref, total_ref, half, (at_ref[0] % 2) * half)

    def finish(i, _):
        rows = rows_at(i)
        xhat = (middle[rows, :] - mean) * scale
        found = cot_half[rows, :].astype(F32) * factor + scale * (
            d_normed[rows, :] * norms[rows, 2:3] - first - xhat * second
        )
        d_middle[rows, :] = found
        g_mid[rows, :] = found.astype(BF16)

    each_rows(model, finish)
    gains[0:1] = as_row(gain_sums)
    gains[1:2] = as_row(bias_sums)


def attention_gradient_kernel(
    at_ref, own, other, w_out, qkv, probs, cosine, sine,
    d_project, g_mid, d_heads, d_scores, products, d_queries, d_keys, d_values,
):
    at = at_ref[0]
    half = own.shape[1]
    part = w_out.shape[0]
    g_mid[:, pl.ds(pl.multiple_of((at % 2) * half, half), half)] = own[...]
    g_mid[:, pl.ds(pl.multiple_of((1 - at % 2) * half, half), half)] = other[...]
    d_heads[...] = dot(w_out[...], g_mid[...], 1, 0).astype(BF16)
    width = HEAD_DIM // 2
    for h in range(part // HEAD_DIM):
        head = slice(h * HEAD_DIM, (h + 1) * HEAD_DIM)
        query = qkv[head]
        key = qkv[part + h * HEAD_DIM : part + (h + 1) * HEAD_DIM]
        value = qkv[2 * part + h * HEAD_DIM : 2 * part + (h + 1) * HEAD_DIM]
        for t in range(2):
            now = slice(t * half, (t + 1) * half)
            count = (t + 1) * half
            products[:count] = dot(value[:, :count], d_heads[head, now], 0, 0)

            def weigh(i, acc):
                rows = rows_at(i)
                return acc + products[rows, :] * probs[h, rows, now].astype(F32)

            inner = column_sum(each_rows(count, weigh, jnp.zeros((STEP, half), F32)))

            def settle(i, _):
                rows = rows_at(i)
                d_scores[rows, :] = (probs[h, rows, now].astype(F32) * (products[rows, :] - inner)).astype(BF16)

            each_rows(count, settle)
            d_queries[:, now] = dot(key[:, :count], d_scores[:count], 1, 0) * HEAD_DIM ** (-0.5)
            d_key = dot(query[:, now], d_scores[:count], 1, 1)
            d_value = dot(d_heads[head, now], probs[h, :count, now], 1, 1)
            if t == 0:
                d_keys[:, :half] = d_key
                d_values[:, :half] = d_value
            else:
                d_keys[:, :half] += d_key[:, :half]
                d_values[:, :half] += d_value[:, :half]
                d_keys[:, half:] = d_key[:, half:]
                d_values[:, half:] = d_value[:, half:]
        for block, found in ((0, d_queries), (1, d_keys)):
            start = block * part + h * HEAD_DIM
            front, back = found[:width], found[width:]
            d_project[start : start + width] = (front * cosine[...] + back * sine[...]).astype(BF16)
            d_project[start + width : start + HEAD_DIM] = (back * cosine[...] - front * sine[...]).astype(BF16)
        d_project[2 * part + h * HEAD_DIM : 2 * part + (h + 1) * HEAD_DIM] = d_values[...].astype(BF16)


def input_gradient_kernel(
    at_ref, d_project, w_qkv, x_all, stats, d_middle, norms, gains, mix, send, keep, sums, total, gain_sums, bias_sums
):
    at = at_ref[0]
    model, half = d_middle.shape
    tokens = x_all.shape[1]
    part = send.shape[0] // 2
    total[...] = dot(w_qkv[...], d_project[...], 0, 0)
    mean, scale = stats[0:1], stats[1:2]
    zero = jnp.zeros((STEP, tokens), F32)
    own = pl.ds(pl.multiple_of((at % 2) * half, half), half)

    def body(i, acc):
        rows = rows_at(i)
        grad = total[rows, :]
        xhat = (x_all[rows, :].astype(F32) - mean) * scale
        both = grad * xhat
        gain_sums[rows, :] = fold_lanes(both)
        bias_sums[rows, :] = fold_lanes(grad)
        gain = norms[rows, 0:1]
        lifted = grad * gain
        total[rows, :] = lifted * scale
        total[rows, own] += 0.5 * d_middle[rows, :]
        return acc[0] + lifted, acc[1] + both * gain

    first, second = each_rows(model, body, (zero, zero))
    store_blocks(at, total, part, send, keep)
    sums[...] = jnp.zeros_like(sums)
    sums[0:1] = as_row(gain_sums)
    sums[1:2] = as_row(bias_sums)
    sums[2:4] = 0.5 * gains[...]
    sums[4:5, :tokens] = column_sum(first) / model
    sums[5:6, :tokens] = column_sum(second) / model
    sums[6:7, :128] = mix[...]


def mixed_kernel(
    all_tokens, self_ref, counts_ref, chip, received, total_ref, running, cotangent, d_mix, mixed, row, table
):
    layers = d_mix.shape[0]
    part, tokens = chip.shape
    live = live_row(all_tokens, counts_ref, total_ref, tokens, 0)

    def body(i, acc):
        rows = rows_at(i)
        output = chip[rows, :] + received[rows, :].astype(F32)
        mixed[rows, :] = (self_ref[0] * output + running[rows, :]).astype(BF16)
        return acc + fold_lanes(cotangent[rows, :].astype(F32) * live * output)

    found = each_rows(part, body, jnp.zeros((STEP, 128), F32))
    table[...] = jnp.zeros_like(table)
    table[:layers] = jnp.sum(d_mix[...], axis=1)
    table[layers : layers + 1] = column_sum(found)
    row[...] = as_row(table)


def ends_kernel(layers, width, at_ref, sums, d_mix, d_self, *ends):
    part = ends[0].shape[1]
    d_mix[...] = sums[6:7, :layers]
    d_self[...] = sums[6:7, layers : layers + 1]
    for i, end in enumerate(ends):
        found = sums[i : i + 1, :part]
        for w in range(1, width):
            found = jnp.where(at_ref[0] == w, sums[i : i + 1, w * part : (w + 1) * part], found)
        end[...] = found


def d_input_kernel(chip, received, x_in, stats, sums, d_input):
    part, tokens = chip.shape
    mean, scale = stats[0:1], stats[1:2]
    first, second = sums[4:5, :tokens], sums[5:6, :tokens]

    def body(i, _):
        rows = rows_at(i)
        xhat = (x_in[rows, :].astype(F32) - mean) * scale
        d_input[rows, :] = chip[rows, :] + received[rows, :].astype(F32) - scale * (first + xhat * second)

    each_rows(part, body)


def local(
    width,
    row_devices,
    x_in,
    history,
    cotangent,
    counts,
    positions,
    mix_weights,
    self_weight,
    first_norm_gain,
    first_norm_bias,
    w_qkv,
    w_out,
    second_norm_gain,
    second_norm_bias,
    w_up,
    w_down,
):
    part, tokens = x_in.shape
    model = w_out.shape[1]
    hidden_units = w_up.shape[1]
    half = tokens // 2
    layers = mix_weights.shape[0]
    all_tokens = float(tokens * row_devices)
    at = lax.axis_index("width").astype(jnp.int32)[None]
    me = lax.axis_index("rows").astype(jnp.int32)[None]
    Order.last, Order.cost = None, 10**9
    to_width = lambda value, offset: xor_send(value, "width", width, offset)
    to_row = lambda value, offset: xor_send(value, "rows", row_devices, offset)
    w_qkv = w_qkv.reshape(3 * part, model)
    rates = 1.0 / 10000.0 ** (np.arange(HEAD_DIM // 2) * 2.0 / HEAD_DIM)
    x_in, cotangent, counts = after((x_in, cotangent, counts), at, me)

    x_far, x_near = to_width(x_in, 2), to_width(x_in, 1)
    cot_now = after(cotangent, x_near)
    cot_far, cot_near = to_width(cot_now, 2), to_width(cot_now, 1)
    live_total, norms, cosine, sine = kernel(
        prepare_kernel,
        (
            shape(8, 128),
            shape(8, -(-part // 128) * 128),
            shape(HEAD_DIM // 2, tokens),
            shape(HEAD_DIM // 2, tokens),
        ),
        [counts],
        [
            after(positions[None, :], x_near),
            jnp.asarray(rates[:, None], F32),
            *(v[None, :] for v in (first_norm_gain, first_norm_bias, second_norm_gain, second_norm_bias)),
        ],
    )
    strides = [1 << i for i in range(row_devices.bit_length() - 1)]

    def grow_total(value, stride):
        return add([value, to_row(value, stride)], (0, 8, F32))[0]

    Order.cost = 10**9
    norms_near = join([norms, to_width(norms, 1)])
    norms_far = to_width(norms_near, 2)
    Order.cost = 10**10
    live_total = grow_total(live_total, strides[0])
    x_both = to_width(after(x_far, norms_near), 1)

    Order.cost = 10**8
    x_all, norms, normed_one, stats_one, qkv = kernel(
        project_kernel,
        (
            shape(model, tokens, kind=BF16),
            shape(model, 8),
            shape(model, tokens, kind=BF16),
            shape(2, tokens),
            shape(3 * part, tokens, kind=BF16),
        ),
        [at],
        [x_in, x_near, x_far, x_both, norms_near, norms_far, cosine, sine, w_qkv],
        [pltpu.VMEM((3 * part, tokens), F32)],
    )
    Order.cost = 10**9
    for stride in strides[1:-1]:
        live_total = grow_total(live_total, stride)
    cot_both = to_width(cot_far, 1)
    send, keep, x_half, heads_out, probs = kernel(
        attention_kernel,
        (
            shape(model, half, kind=BF16),
            shape(model, half),
            shape(model, half, kind=BF16),
            shape(part, tokens, kind=BF16),
            shape(part // HEAD_DIM, tokens, tokens, kind=BF16),
        ),
        [at],
        [after(qkv, cot_far), w_out, x_all],
        [pltpu.VMEM((tokens, half), F32)],
    )
    chip, send = add([keep, to_width(send, 1)], (0, model, F32), (0, model, BF16))
    received = to_width(send, 2)

    live_total = grow_total(live_total, strides[-1])
    running, d_history, d_mix = mix_history(all_tokens, mix_weights, counts, live_total, history, cotangent)
    g_out, d_active, cot_half = kernel(
        functools.partial(output_gradient_kernel, all_tokens),
        (shape(model, tokens, kind=BF16), shape(hidden_units, tokens), shape(model, half, kind=BF16)),
        [at, self_weight, counts],
        [cotangent, cot_near, cot_far, cot_both, live_total, w_down],
        [pltpu.VMEM((model, tokens), BF16)],
    )

    middle, stats_two, normed_own = kernel(
        middle_kernel,
        (shape(model, half), shape(2, half), shape(model, half, kind=BF16)),
        [],
        [x_half, chip, received, norms],
    )
    normed_two, active, d_hidden, send, keep = kernel(
        feed_forward_kernel,
        (
            shape(model, tokens, kind=BF16),
            shape(hidden_units, tokens, kind=BF16),
            shape(hidden_units, tokens, kind=BF16),
            shape(model, half, kind=BF16),
            shape(model, half),
        ),
        [],
        [normed_own, to_width(normed_own, 1), w_up, d_active],
        [pltpu.VMEM((hidden_units, tokens), F32)],
    )

    down = Stream(row_devices, 0, hidden_units, "halving")
    up = Stream(row_devices, 0, model, "crossed")
    down_parts = weight_gradient(me, [down], active, g_out)[0]
    down_got = start_stage(down, down_parts, 0)
    chip, send = add([keep, to_width(send, 1)], (0, model, F32), (0, model, BF16))
    received = to_width(send, 2)
    up_parts = weight_gradient(me, [up], normed_two, d_hidden)[0]
    up_got = start_stage(up, up_parts, 0)
    blocks = (shape(2 * part, tokens, kind=BF16), shape(2 * part, tokens))
    out_send, out_keep = kernel(
        output_kernel, blocks, [at], [active, w_down, middle], [pltpu.VMEM((model, tokens), F32)]
    )
    out_near = to_width(out_send, 1)

    d_middle, g_own, gains_two = kernel(
        functools.partial(middle_gradient_kernel, all_tokens),
        (shape(model, half), shape(model, half, kind=BF16), shape(2, model)),
        [at, self_weight, counts],
        [chip, received, live_total, middle, stats_two, cot_half, norms],
        [pltpu.VMEM((model, half), F32), pltpu.VMEM((model, 128), F32), pltpu.VMEM((model, 128), F32)],
    )
    g_other = to_width(g_own, 1)
    out_chip, out_send = add([out_keep, out_near], (0, part, F32), (part, 2 * part, BF16))
    out_far = to_width(out_send, 2)
    down_parts = add_stage(down, down_parts, down_got, 0)
    down_got = start_stage(down, down_parts, 1)
    up_parts = add_stage(up, up_parts, up_got, 0)
    up_got = start_stage(up, up_parts, 1)
    d_project, g_mid = kernel(
        attention_gradient_kernel,
        (shape(3 * part, tokens, kind=BF16), shape(model, tokens, kind=BF16)),
        [at],
        [g_own, g_other, w_out, qkv, probs, cosine, sine],
        [
            pltpu.VMEM((part, tokens), BF16),
            pltpu.VMEM((tokens, half), BF16),
            pltpu.VMEM((tokens, half), F32),
            pltpu.VMEM((HEAD_DIM, tokens), F32),
            pltpu.VMEM((HEAD_DIM, tokens), F32),
            pltpu.VMEM((HEAD_DIM, tokens), F32),
        ],
    )
    tail_rows = 4 * part
    tail = [
        Stream(row_devices, 0, tail_rows // 2, "halving"),
        Stream(row_devices, tail_rows // 2, tail_rows // 2, "crossed"),
    ]
    first, second = tail
    first_parts, second_parts = weight_gradient(me, tail, d_project, normed_one, heads_out, g_mid)
    first_got = start_stage(first, first_parts, 0)
    second_got = start_stage(second, second_parts, 0)

    Order.cost = 6 * 10**9
    mixed, mix_row = kernel(
        functools.partial(mixed_kernel, all_tokens),
        (shape(part, tokens, kind=BF16), shape(1, 128)),
        [self_weight, counts],
        [out_chip, out_far, live_total, running, cotangent, d_mix],
        [pltpu.VMEM((128, 128), F32)],
    )
    Order.cost = 10**8
    down_parts = add_stage(down, down_parts, down_got, 1)
    down_got = start_stage(down, down_parts, 2)
    in_send, in_keep, sums = kernel(
        input_gradient_kernel,
        blocks + (shape(8, model),),
        [at],
        [d_project, w_qkv, x_all, stats_one, d_middle, norms, gains_two, mix_row],
        [pltpu.VMEM((model, tokens), F32), pltpu.VMEM((model, 128), F32), pltpu.VMEM((model, 128), F32)],
    )
    in_near = to_width(in_send, 1)
    sums_got = to_width(sums, 1)
    up_parts = add_stage(up, up_parts, up_got, 1)
    up_got = start_stage(up, up_parts, 2)
    first_parts = add_stage(first, first_parts, first_got, 0)
    first_got = start_stage(first, first_parts, 1)
    Order.cost = 2 * 10**10
    second_parts = add_stage(second, second_parts, second_got, 0)
    second_got = start_stage(second, second_parts, 1)
    Order.cost = 10**9
    in_chip, in_send = add([in_keep, in_near], (0, part, F32), (part, 2 * part, BF16))
    in_far = to_width(in_send, 2)
    sums = add([sums, sums_got], (0, 8, F32))[0]
    sums_got = to_width(sums, 2)
    last = len(down.digits) - 1
    down_value = sum_rest(down, add_stage(down, down_parts, down_got, 2)[0])
    down_pieces = gather_stage(down, down_value, last)
    up_value = sum_rest(up, add_stage(up, up_parts, up_got, 2)[0])
    up_pieces = gather_stage(up, up_value, last)
    first_parts = add_stage(first, first_parts, first_got, 1)
    first_got = start_stage(first, first_parts, 2)
    second_parts = add_stage(second, second_parts, second_got, 1)
    second_got = start_stage(second, second_parts, 2)
    sums = add([sums, sums_got], (0, 8, F32))[0]
    sums_got = to_row(sums, strides[0])
    d_input = kernel(d_input_kernel, shape(part, tokens), [], [in_chip, in_far, x_in, stats_one, sums])
    down_pieces = gather_stage(down, join(down_pieces), last - 1)
    up_pieces = gather_stage(up, join(up_pieces), last - 1)
    first_value = sum_rest(first, add_stage(first, first_parts, first_got, 2)[0])
    first_pieces = gather_stage(first, first_value, last)
    second_value = sum_rest(second, add_stage(second, second_parts, second_got, 2)[0])
    second_pieces = gather_stage(second, second_value, last)
    for stride in strides[1:-1]:
        sums = add([sums, sums_got], (0, 8, F32))[0]
        sums_got = to_row(sums, stride)
    first_pieces = gather_stage(first, join(first_pieces), last - 1)
    second_pieces = gather_stage(second, join(second_pieces), last - 1)
    down_pieces = gather_stage(down, join(down_pieces), 0)
    up_pieces = gather_stage(up, join(up_pieces), 0)
    sums = add([sums, sums_got], (0, 8, F32))[0]
    sums_got = to_row(sums, strides[-1])
    first_pieces = gather_stage(first, join(first_pieces), 0)
    second_pieces = gather_stage(second, join(second_pieces), 0)
    sums = add([sums, sums_got], (0, 8, F32))[0]
    d_mix, d_self, *ends = kernel(
        functools.partial(ends_kernel, layers, width),
        (shape(1, layers), shape(1, 1)) + (shape(1, part),) * 4,
        [at],
        [sums],
    )
    d_w_down = place(me, [down], down_pieces, (hidden_units,))[0]
    d_w_up = place(me, [up], up_pieces, (model,))[0]
    d_w_qkv, d_w_out = place(me, tail, first_pieces + second_pieces, (3 * part, part))
    return (
        mixed,
        d_input,
        d_history,
        d_mix[0],
        d_self[0],
        ends[0][0],
        ends[1][0],
        d_w_qkv.reshape(3, part, model),
        d_w_out,
        ends[2][0],
        ends[3][0],
        d_w_up,
        d_w_down,
    )


def solution(mesh):
    return jax.shard_map(
        functools.partial(local, mesh.shape["width"], mesh.shape["rows"]),
        mesh=mesh,
        in_specs=(
            P("width", "rows"),
            P(None, "width", "rows"),
            P("width", "rows"),
            P("rows"),
            P("rows"),
            P(),
            P(),
            P("width"),
            P("width"),
            P(None, "width", None),
            P("width", None),
            P("width"),
            P("width"),
            P(None, "width"),
            P("width", None),
        ),
        out_specs=(
            P("width", "rows"),
            P("width", "rows"),
            P(None, "width", "rows"),
            P(),
            P(),
            P("width"),
            P("width"),
            P(None, "width", None),
            P("width", None),
            P("width"),
            P("width"),
            P(None, "width"),
            P("width", None),
        ),
        check_vma=False,
    )
```

```python
import functools

import jax
import jax.numpy as jnp
import numpy as np
from jax import lax
from jax.experimental import pallas as pl
from jax.experimental.pallas import tpu as pltpu
from jax.sharding import PartitionSpec as P

HEAD_DIM = 64
EPSILON = 1e-05
BF16 = jnp.bfloat16
F32 = jnp.float32
STEP = 16


def shape(*dims, kind=F32):
    return jax.ShapeDtypeStruct(dims, kind)


class Order:
    last = None
    cost = 10**9


def kernel(body, outs, scalars, arrays, scratch=(), limit=12):
    arrays = list(arrays)
    if Order.last is not None:
        arrays[0] = after(arrays[0], Order.last)
    found = pl.pallas_call(
        body,
        out_shape=outs,
        in_specs=[pl.BlockSpec(memory_space=pltpu.SMEM)] * len(scalars)
        + [pl.BlockSpec(memory_space=pltpu.VMEM)] * len(arrays),
        out_specs=jax.tree.map(lambda _: pl.BlockSpec(memory_space=pltpu.VMEM), outs),
        scratch_shapes=list(scratch),
        compiler_params=pltpu.CompilerParams(vmem_limit_bytes=limit * 1024 * 1024),
        cost_estimate=pl.CostEstimate(flops=Order.cost, bytes_accessed=1024, transcendentals=0),
    )(*scalars, *arrays)
    Order.last = jax.tree.leaves(found)[0]
    return found


def after(value, *others):
    return lax.optimization_barrier((value, others))[0]


def dot(left, right, left_dim, right_dim):
    return lax.dot_general(left, right, (((left_dim,), (right_dim,)), ((), ())), preferred_element_type=F32)


def rows_at(i):
    return pl.ds(pl.multiple_of(i * STEP, STEP), STEP)


def each_rows(count, body, start=None, first=0):
    return lax.fori_loop(first // STEP, count // STEP, body, start, unroll=4)


def column_sum(value):
    return jnp.sum(value, axis=0, keepdims=True)


def xor_send(value, axis, size, offset):
    return lax.ppermute(value, axis, [(i, i ^ offset) for i in range(size)])


def add_kernel(count, cuts, *refs):
    parts, outs = refs[:count], refs[count:]

    def one(rows):
        found = parts[0][rows, :].astype(F32)
        for part in parts[1:]:
            found = found + part[rows, :].astype(F32)
        return found

    for (first, last), out in zip(cuts, outs):
        if (last - first) % STEP:
            out[...] = one(slice(first, last)).astype(out.dtype)
        else:

            def body(i, _, first=first, out=out):
                out[rows_at(i), :] = one(pl.ds(pl.multiple_of(first + i * STEP, STEP), STEP)).astype(out.dtype)

            each_rows(last - first, body)


def add(parts, *cuts):
    columns = parts[0].shape[1]
    outs = tuple(shape(last - first, columns, kind=kind) for first, last, kind in cuts)
    return list(kernel(functools.partial(add_kernel, len(parts), [cut[:2] for cut in cuts]), outs, [], parts))


def sum_small(value, axis, size):
    stride = 1
    while stride < size:
        value = add([value, xor_send(value, axis, size, stride)], (0, value.shape[0], F32))[0]
        stride *= 2
    return value


def join_kernel(*refs):
    out, start = refs[-1], 0
    for piece in refs[:-1]:
        out[start : start + piece.shape[0]] = piece[...]
        start += piece.shape[0]


def join(pieces):
    rows = sum(piece.shape[0] for piece in pieces)
    return kernel(join_kernel, shape(rows, pieces[0].shape[1], kind=pieces[0].dtype), [], pieces)


def chunks_of(count, rows):
    count = min(count, 8)
    while rows % (16 * count):
        count //= 2
    return count


def digits_of(count, kind):
    if kind == "halving":
        strides = []
        stride = 1
        while stride < count:
            strides.append((stride, 2))
            stride *= 2
        return strides
    strides = digits_of(count, "halving")
    return [strides[1], strides[0]] + strides[2:]


def offsets_of(digits):
    found = [0]
    for stride, radix in digits:
        found = [low + e * stride for low in found for e in range(radix)]
    return found


class Stream:
    def __init__(self, row_devices, first, rows, kind):
        self.first, self.rows = first, rows
        self.count = chunks_of(row_devices, rows)
        self.row_devices = row_devices
        self.digits = digits_of(self.count, kind)
        self.chunk = rows // self.count

    def parts(self):
        stride, radix = self.digits[0]
        rest = offsets_of(self.digits[1:])
        return [[e * stride + low for low in rest] for e in range(radix)]

    def send(self, value, offset):
        return xor_send(value, "rows", self.row_devices, offset)


def weight_gradient_kernel(streams, pairs, me_ref, *refs):
    operands, outs, scratch = refs[: 2 * pairs], list(refs[2 * pairs : -1]), refs[-1]
    start = 0
    for i in range(pairs):
        left, right = operands[2 * i], operands[2 * i + 1]
        count = left.shape[0]
        scratch[start : start + count] = dot(left[...], right[...], 1, 1).astype(BF16)
        start += count
    for stream in streams:
        for offsets in stream.parts():
            out = outs.pop(0)
            for place, offset in enumerate(offsets):
                chunk = (me_ref[0] % stream.count) ^ offset
                at = pl.multiple_of(stream.first + chunk * stream.chunk, 16)
                out[place * stream.chunk : (place + 1) * stream.chunk] = scratch[pl.ds(at, stream.chunk), :]


def weight_gradient(me, streams, *operands):
    pairs = len(operands) // 2
    total = sum(operands[2 * i].shape[0] for i in range(pairs))
    columns = operands[1].shape[0]
    outs = tuple(
        shape(len(offsets) * stream.chunk, columns, kind=BF16) for stream in streams for offsets in stream.parts()
    )
    found = list(
        kernel(
            functools.partial(weight_gradient_kernel, streams, pairs),
            outs,
            [me],
            operands,
            [pltpu.VMEM((total, columns), BF16)],
        )
    )
    return [[found.pop(0) for _ in stream.parts()] for stream in streams]


def start_stage(stream, parts, stage):
    stride, radix = stream.digits[stage]
    return [stream.send(parts[e], e * stride) for e in range(1, radix)]


def add_stage(stream, parts, received, stage):
    rows = parts[0].shape[0]
    radix = 1 if stage + 1 == len(stream.digits) else stream.digits[stage + 1][1]
    size = rows // radix
    return add([parts[0]] + received, *((e * size, (e + 1) * size, BF16) for e in range(radix)))


def sum_rest(stream, value):
    stride = stream.count
    while stride < stream.row_devices:
        value = add([value, stream.send(value, stride)], (0, value.shape[0], BF16))[0]
        stride *= 2
    return value


def gather_stage(stream, value, stage):
    stride, radix = stream.digits[stage]
    return [value] + [stream.send(value, e * stride) for e in range(1, radix)]


def place_kernel(all_tokens, streams, bounds, me_ref, sums, *refs):
    pieces, outs = list(refs[: -len(bounds)]), refs[-len(bounds) :]
    scale = loss_scale(all_tokens, sums, outs[0].shape[1])
    for stream in streams:
        for offsets in stream.parts():
            piece = pieces.pop(0)
            for place, offset in enumerate(offsets):
                chunk = (me_ref[0] % stream.count) ^ offset
                row = stream.first + chunk * stream.chunk
                for (first, last), out in zip(bounds, outs):

                    def store(out=out, first=first, piece=piece, place=place, row=row, size=stream.chunk):
                        at = pl.multiple_of(row - first, 16)
                        out[pl.ds(at, size), :] = (
                            piece[place * size : (place + 1) * size].astype(F32) * scale
                        )

                    if len(bounds) == 1:
                        store()
                    else:
                        pl.when((row >= first) & (row < last))(store)


def place(all_tokens, me, sums, streams, pieces, sizes):
    columns = pieces[0].shape[1]
    bounds, start = [], 0
    for size in sizes:
        bounds.append((start, start + size))
        start += size
    outs = tuple(shape(size, columns) for size in sizes)
    return kernel(functools.partial(place_kernel, all_tokens, streams, bounds), outs, [me], [sums, *pieces])


def live_row(counts_ref, width, first):
    place = lax.broadcasted_iota(jnp.int32, (1, width), 1) + first
    return jnp.where(place < counts_ref[0], 1.0, 0.0)


def loss_scale(all_tokens, sums, width):
    return jnp.full((1, width), all_tokens, F32) / jnp.broadcast_to(sums[7:8, 0:1], (1, width))


def history_kernel(block, mix_ref, counts_ref, cot_ref, history_ref, running_ref, d_mix_ref):
    layers, features, tokens = history_ref.shape
    live = live_row(counts_ref, tokens, 0)
    d_mix_ref[...] = jnp.zeros_like(d_mix_ref)

    def body(history_part):
        for i in range(block // STEP):
            rows = slice(i * STEP, (i + 1) * STEP)
            own = pl.ds(pl.multiple_of(pl.program_id(0) * block + i * STEP, STEP), STEP)
            grad = cot_ref[own].astype(F32) * live
            running = jnp.zeros_like(grad)
            for j in range(layers):
                layer = history_part[j, rows].astype(F32)
                running = running + mix_ref[j] * layer
                terms = grad * layer
                terms = terms[: STEP // 2] + terms[STEP // 2 :]
                d_mix_ref[j] += sum(terms[:, k : k + 128] for k in range(0, tokens, 128))
            running_ref[own] = running

    whole = pl.BlockSpec((layers, block, tokens), lambda i: (0, i, 0))
    pltpu.emit_pipeline(body, grid=(features // block,), in_specs=[whole])(history_ref)


def d_history_kernel(all_tokens, block, mix_ref, counts_ref, cot_ref, sums, d_history_ref):
    layers, features, tokens = d_history_ref.shape
    factor = live_row(counts_ref, tokens, 0) * loss_scale(all_tokens, sums, tokens)

    def body(part):
        for i in range(block // STEP):
            rows = slice(i * STEP, (i + 1) * STEP)
            own = pl.ds(pl.multiple_of(pl.program_id(0) * block + i * STEP, STEP), STEP)
            grad = cot_ref[own].astype(F32) * factor
            for j in range(layers):
                part[j, rows] = (mix_ref[j] * grad).astype(BF16)

    whole = pl.BlockSpec((layers, block, tokens), lambda i: (0, i, 0))
    pltpu.emit_pipeline(body, grid=(features // block,), out_specs=[whole])(d_history_ref)


def history_call(body, outs, in_hbm, out_hbm, scalars, arrays):
    vmem, hbm = pl.BlockSpec(memory_space=pltpu.VMEM), pl.BlockSpec(memory_space=pltpu.HBM)
    arrays = [after(arrays[0], Order.last), *arrays[1:]]
    found = pl.pallas_call(
        body,
        out_shape=outs,
        in_specs=[pl.BlockSpec(memory_space=pltpu.SMEM)] * len(scalars) + [hbm if h else vmem for h in in_hbm],
        out_specs=tuple(hbm if h else vmem for h in out_hbm),
        compiler_params=pltpu.CompilerParams(vmem_limit_bytes=12 * 1024 * 1024),
        cost_estimate=pl.CostEstimate(flops=Order.cost, bytes_accessed=1024, transcendentals=0),
    )(*scalars, *arrays)
    Order.last = found[0]
    return found


def spread_of(load, count, width):
    zero = jnp.zeros((STEP, width), F32)
    mean = column_sum(each_rows(count, lambda i, acc: acc + load(i), zero)) / count

    def squares(i, acc):
        centred = load(i) - mean
        return acc + centred * centred

    return mean, lax.rsqrt(column_sum(each_rows(count, squares, zero)) / count + EPSILON)


def prepare_kernel(now, *refs):
    sources, (norms, cosine, sine), places, sem = refs[:6], refs[6:9], refs[9:15], refs[15]
    copies = [pltpu.make_async_copy(*pair, sem.at[i]) for i, pair in enumerate(zip(sources, places))]
    for copy in copies:
        copy.start()
    norms[...] = jnp.zeros_like(norms)
    for copy in copies:
        copy.wait()
    positions, rates, *vectors = places
    for i, ref in enumerate(vectors):
        norms[i : i + 1, : ref.shape[1]] = ref[...]
    angles = positions[...].astype(F32) * rates[...]
    cosine[...] = jnp.cos(angles)
    sine[...] = jnp.sin(angles)


def prepare(now, *sources):
    tokens, part = sources[0].shape[1], sources[2].shape[1]
    rates = sources[1].shape[0]
    vmem = pl.BlockSpec(memory_space=pltpu.VMEM)
    found = pl.pallas_call(
        prepare_kernel,
        out_shape=(shape(8, -(-part // 128) * 128), shape(rates, tokens), shape(rates, tokens)),
        in_specs=[vmem] + [pl.BlockSpec(memory_space=pltpu.HBM)] * len(sources),
        out_specs=(vmem,) * 3,
        scratch_shapes=[pltpu.VMEM(v.shape, v.dtype) for v in sources] + [pltpu.SemaphoreType.DMA((len(sources),))],
        compiler_params=pltpu.CompilerParams(vmem_limit_bytes=4 * 1024 * 1024),
        cost_estimate=pl.CostEstimate(flops=Order.cost, bytes_accessed=1024, transcendentals=0),
    )(now, *(pltpu.with_memory_space_constraint(v, pltpu.HBM) for v in sources))
    Order.last = found[0]
    return found


def norms_kernel(at_ref, n01, n23, norms):
    part = norms.shape[0] // 4
    near, far = n01[...].T, n23[...].T
    for e, norm in enumerate((near, near, far, far)):
        rows = pl.ds(pl.multiple_of((at_ref[0] ^ e) * part, 64), part)
        norms[rows, :] = norm[:part, 8 * (e % 2) : 8 * (e % 2) + 8]


def project_kernel(
    at_ref, x0, x1, x2, x3, norms, cosine, sine, w_qkv, w_out, x_all, normed, stats, qkv, project
):
    at = at_ref[0]
    part, tokens = x0.shape
    model = w_qkv.shape[1]
    for e, piece in enumerate((x0, x1, x2, x3)):
        x_all[pl.ds(pl.multiple_of((at ^ e) * part, 64), part), :] = piece[...]
    mean, scale = spread_of(lambda i: x_all[rows_at(i), :].astype(F32), model, tokens)
    stats[0:1] = mean
    stats[1:2] = scale

    def normalise(i, _):
        rows = rows_at(i)
        xhat = (x_all[rows, :].astype(F32) - mean) * scale
        normed[rows, :] = (xhat * norms[rows, 0:1] + norms[rows, 1:2]).astype(BF16)

    each_rows(model, normalise)
    project[...] = dot(w_qkv[...], normed[...], 1, 0)
    width = HEAD_DIM // 2
    for block, factor in ((0, HEAD_DIM ** (-0.5)), (1, 1.0)):
        for start in range(block * part, (block + 1) * part, HEAD_DIM):
            front, back = project[start : start + width], project[start + width : start + HEAD_DIM]
            cos, sin = cosine[...] * factor, sine[...] * factor
            qkv[start : start + width] = (front * cos - back * sin).astype(BF16)
            qkv[start + width : start + HEAD_DIM] = (back * cos + front * sin).astype(BF16)
    qkv[2 * part :] = project[2 * part :].astype(BF16)


def attention_kernel(at_ref, qkv, w_out, x_all, send, keep, x_half, heads_out, probs, scores):
    at = at_ref[0]
    part, tokens = heads_out.shape
    half = tokens // 2
    for h in range(part // HEAD_DIM):
        head = slice(h * HEAD_DIM, (h + 1) * HEAD_DIM)
        for t in range(2):
            now = slice(t * half, (t + 1) * half)
            count = (t + 1) * half
            query = qkv[head, now]
            key = qkv[part + h * HEAD_DIM : part + (h + 1) * HEAD_DIM, :count]
            value = qkv[2 * part + h * HEAD_DIM : 2 * part + (h + 1) * HEAD_DIM, :count]
            scores[:count] = dot(key, query, 0, 0)

            def masked_top(i, acc):
                rows = rows_at(i)
                behind = lax.broadcasted_iota(jnp.int32, (STEP, half), 0) + (i * STEP - t * half)
                found = jnp.where(behind <= lax.broadcasted_iota(jnp.int32, (STEP, half), 1), scores[rows, :], -1e30)
                scores[rows, :] = found
                return jnp.maximum(acc, found)

            top = each_rows(
                t * half, lambda i, acc: jnp.maximum(acc, scores[rows_at(i), :]), jnp.full((STEP, half), -1e30, F32)
            )
            top = jnp.max(each_rows(count, masked_top, top, first=t * half), axis=0, keepdims=True)

            def raise_rows(i, acc):
                rows = rows_at(i)
                found = jnp.exp(scores[rows, :] - top)
                scores[rows, :] = found
                return acc + found

            total = 1.0 / column_sum(each_rows(count, raise_rows, jnp.zeros((STEP, half), F32)))

            def settle(i, _):
                rows = rows_at(i)
                probs[h, rows, now] = (scores[rows, :] * total).astype(BF16)

            each_rows(count, settle)
            heads_out[head, now] = dot(value, probs[h, :count, now], 1, 0).astype(BF16)
    own = pl.multiple_of((at % 2) * half, half)
    other = pl.multiple_of((1 - at % 2) * half, half)
    send[...] = dot(w_out[...], heads_out[:, pl.ds(other, half)], 0, 0).astype(BF16)
    keep[...] = dot(w_out[...], heads_out[:, pl.ds(own, half)], 0, 0)
    x_half[...] = x_all[:, pl.ds(own, half)]


def output_gradient_kernel(
    at_ref, self_ref, counts_ref, c0, c1, c2, c3, w_down, g_out, d_active, cot_half, cot_all
):
    at = at_ref[0]
    part, tokens = c0.shape
    half = tokens // 2
    for e, piece in enumerate((c0, c1, c2, c3)):
        cot_all[pl.ds(pl.multiple_of((at ^ e) * part, 64), part), :] = piece[...]
    for place, side in enumerate((at % 2, 1 - at % 2)):
        now = pl.ds(pl.multiple_of(side * half, half), half)
        factor = live_row(counts_ref, half, side * half)

        def scale(i, _, now=now, factor=factor, place=place):
            rows = rows_at(i)
            grad = cot_all[rows, now].astype(F32) * factor
            g_out[rows, place * half : (place + 1) * half] = (self_ref[0] * grad).astype(BF16)
            if place == 0:
                cot_half[rows, :] = cot_all[rows, now]

        each_rows(cot_all.shape[0], scale)
    d_active[...] = dot(w_down[...], g_out[...], 1, 0)


def middle_kernel(x_half, chip, received, norms, middle, stats, normed):
    model, half = chip.shape

    def add(i, _):
        rows = rows_at(i)
        middle[rows, :] = x_half[rows, :].astype(F32) + chip[rows, :] + received[rows, :].astype(F32)

    each_rows(model, add)
    mean, scale = spread_of(lambda i: middle[rows_at(i), :], model, half)
    stats[0:1] = mean
    stats[1:2] = scale

    def normalise(i, _):
        rows = rows_at(i)
        xhat = (middle[rows, :] - mean) * scale
        normed[rows, :] = (xhat * norms[rows, 2:3] + norms[rows, 3:4]).astype(BF16)

    each_rows(model, normalise)


def feed_forward_kernel(own, other, w_up, d_active, normed, active, d_hidden, send, keep, hidden):
    half = own.shape[1]
    normed[:, :half] = own[...]
    normed[:, half:] = other[...]
    hidden[...] = dot(w_up[...], normed[...], 0, 0)

    def bend(i, _):
        rows = rows_at(i)
        u = hidden[rows, :]
        squared = u * u
        curve = jnp.tanh(0.7978845608028654 * u * (1.0 + 0.044715 * squared))
        lifted = 0.5 * (1.0 + curve)
        active[rows, :] = (u * lifted).astype(BF16)
        slope = lifted + u * (0.5 * (1.0 - curve * curve)) * (
            0.7978845608028654 + (3 * 0.044715 * 0.7978845608028654) * squared
        )
        d_hidden[rows, :] = (slope * d_active[rows, :]).astype(BF16)

    each_rows(hidden.shape[0], bend)
    send[...] = dot(w_up[...], d_hidden[:, half:], 1, 0).astype(BF16)
    keep[...] = dot(w_up[...], d_hidden[:, :half], 1, 0)


def store_blocks(at, total, part, send, keep):
    for place in range(2):
        for low, out in ((1, send), (0, keep)):
            rows = pl.ds(pl.multiple_of((at ^ (2 * place + low)) * part, 64), part)
            out[place * part : (place + 1) * part] = total[rows, :].astype(out.dtype)


def output_kernel(at_ref, active, w_down, middle, send, keep, total):
    at = at_ref[0]
    model, half = middle.shape
    part = send.shape[0] // 2
    own = pl.ds(pl.multiple_of((at % 2) * half, half), half)
    other = pl.ds(pl.multiple_of((1 - at % 2) * half, half), half)
    total[:, own] = dot(w_down[...], active[:, :half], 0, 0) + 0.5 * middle[...]
    total[:, other] = dot(w_down[...], active[:, half:], 0, 0)
    store_blocks(at, total, part, send, keep)


def fold_lanes(value):
    return sum(value[:, k : k + 128] for k in range(0, value.shape[1], 128))


def as_row(columns):
    return column_sum(columns[...].T)


def middle_gradient_kernel(
    at_ref, self_ref, counts_ref, chip, received, middle, stats, cot_half, norms,
    d_middle, g_mid, gains, d_normed, gain_sums, bias_sums,
):
    model, half = chip.shape
    mean, scale = stats[0:1], stats[1:2]
    zero = jnp.zeros((STEP, half), F32)

    def sums(i, acc):
        rows = rows_at(i)
        grad = chip[rows, :] + received[rows, :].astype(F32)
        d_normed[rows, :] = grad
        xhat = (middle[rows, :] - mean) * scale
        both = grad * xhat
        gain_sums[rows, :] = fold_lanes(both)
        bias_sums[rows, :] = fold_lanes(grad)
        gain = norms[rows, 2:3]
        return acc[0] + grad * gain, acc[1] + both * gain

    first, second = (column_sum(v) / model for v in each_rows(model, sums, (zero, zero)))
    factor = self_ref[0] * live_row(counts_ref, half, (at_ref[0] % 2) * half)

    def finish(i, _):
        rows = rows_at(i)
        xhat = (middle[rows, :] - mean) * scale
        found = cot_half[rows, :].astype(F32) * factor + scale * (
            d_normed[rows, :] * norms[rows, 2:3] - first - xhat * second
        )
        d_middle[rows, :] = found
        g_mid[rows, :] = found.astype(BF16)

    each_rows(model, finish)
    gains[0:1] = as_row(gain_sums)
    gains[1:2] = as_row(bias_sums)


def attention_gradient_kernel(
    at_ref, own, other, w_out, qkv, probs, cosine, sine,
    d_project, g_mid, d_heads, d_scores, products, d_queries, d_keys, d_values,
):
    at = at_ref[0]
    half = own.shape[1]
    part = w_out.shape[0]
    g_mid[:, pl.ds(pl.multiple_of((at % 2) * half, half), half)] = own[...]
    g_mid[:, pl.ds(pl.multiple_of((1 - at % 2) * half, half), half)] = other[...]
    d_heads[...] = dot(w_out[...], g_mid[...], 1, 0).astype(BF16)
    width = HEAD_DIM // 2
    for h in range(part // HEAD_DIM):
        head = slice(h * HEAD_DIM, (h + 1) * HEAD_DIM)
        query = qkv[head]
        key = qkv[part + h * HEAD_DIM : part + (h + 1) * HEAD_DIM]
        value = qkv[2 * part + h * HEAD_DIM : 2 * part + (h + 1) * HEAD_DIM]
        for t in range(2):
            now = slice(t * half, (t + 1) * half)
            count = (t + 1) * half
            products[:count] = dot(value[:, :count], d_heads[head, now], 0, 0)

            def weigh(i, acc):
                rows = rows_at(i)
                return acc + products[rows, :] * probs[h, rows, now].astype(F32)

            inner = column_sum(each_rows(count, weigh, jnp.zeros((STEP, half), F32)))

            def settle(i, _):
                rows = rows_at(i)
                d_scores[rows, :] = (probs[h, rows, now].astype(F32) * (products[rows, :] - inner)).astype(BF16)

            each_rows(count, settle)
            d_queries[:, now] = dot(key[:, :count], d_scores[:count], 1, 0) * HEAD_DIM ** (-0.5)
            d_key = dot(query[:, now], d_scores[:count], 1, 1)
            d_value = dot(d_heads[head, now], probs[h, :count, now], 1, 1)
            if t == 0:
                d_keys[:, :half] = d_key
                d_values[:, :half] = d_value
            else:
                d_keys[:, :half] += d_key[:, :half]
                d_values[:, :half] += d_value[:, :half]
                d_keys[:, half:] = d_key[:, half:]
                d_values[:, half:] = d_value[:, half:]
        for block, found in ((0, d_queries), (1, d_keys)):
            start = block * part + h * HEAD_DIM
            front, back = found[:width], found[width:]
            d_project[start : start + width] = (front * cosine[...] + back * sine[...]).astype(BF16)
            d_project[start + width : start + HEAD_DIM] = (back * cosine[...] - front * sine[...]).astype(BF16)
        d_project[2 * part + h * HEAD_DIM : 2 * part + (h + 1) * HEAD_DIM] = d_values[...].astype(BF16)


def input_gradient_kernel(
    width, at_ref, counts_ref, d_project, w_qkv, x_all, stats, d_middle, norms, gains, send, keep, sums, total, gain_sums, bias_sums
):
    at = at_ref[0]
    model, half = d_middle.shape
    tokens = x_all.shape[1]
    part = send.shape[0] // 2
    total[...] = dot(w_qkv[...], d_project[...], 0, 0)
    mean, scale = stats[0:1], stats[1:2]
    zero = jnp.zeros((STEP, tokens), F32)
    own = pl.ds(pl.multiple_of((at % 2) * half, half), half)

    def body(i, acc):
        rows = rows_at(i)
        grad = total[rows, :]
        xhat = (x_all[rows, :].astype(F32) - mean) * scale
        both = grad * xhat
        gain_sums[rows, :] = fold_lanes(both)
        bias_sums[rows, :] = fold_lanes(grad)
        gain = norms[rows, 0:1]
        lifted = grad * gain
        total[rows, :] = lifted * scale
        total[rows, own] += 0.5 * d_middle[rows, :]
        return acc[0] + lifted, acc[1] + both * gain

    first, second = each_rows(model, body, (zero, zero))
    store_blocks(at, total, part, send, keep)
    sums[...] = jnp.zeros_like(sums)
    sums[0:1] = as_row(gain_sums)
    sums[1:2] = as_row(bias_sums)
    sums[2:4] = 0.5 * gains[...]
    sums[4:5, :tokens] = column_sum(first) / model
    sums[5:6, :tokens] = column_sum(second) / model
    sums[7:8] = jnp.zeros((1, model), F32) + counts_ref[0].astype(F32) / width


def mixed_kernel(
    self_ref, counts_ref, chip, received, running, cotangent, d_mix, sums, mixed, all_sums, table
):
    layers = d_mix.shape[0]
    part, tokens = chip.shape
    live = live_row(counts_ref, tokens, 0)

    def body(i, acc):
        rows = rows_at(i)
        output = chip[rows, :] + received[rows, :].astype(F32)
        mixed[rows, :] = (self_ref[0] * output + running[rows, :]).astype(BF16)
        return acc + fold_lanes(cotangent[rows, :].astype(F32) * live * output)

    found = each_rows(part, body, jnp.zeros((STEP, 128), F32))
    table[...] = jnp.zeros_like(table)
    table[:layers] = jnp.sum(d_mix[...], axis=1)
    table[layers : layers + 1] = column_sum(found)
    all_sums[...] = sums[...]
    all_sums[6:7, :128] = as_row(table)


def ends_kernel(all_tokens, layers, width, at_ref, sums, d_mix, d_self, *ends):
    part = ends[0].shape[1]
    scale = loss_scale(all_tokens, sums, sums.shape[1])
    d_mix[...] = sums[6:7, :layers] * scale[:, :layers]
    d_self[...] = sums[6:7, layers : layers + 1] * scale[:, :1]
    for i, end in enumerate(ends):
        scaled = sums[i : i + 1] * scale
        found = scaled[:, :part]
        for w in range(1, width):
            found = jnp.where(at_ref[0] == w, scaled[:, w * part : (w + 1) * part], found)
        end[...] = found


def d_input_kernel(chip, received, x_in, stats, row_sums, found):
    part, tokens = chip.shape
    mean, scale = stats[0:1], stats[1:2]
    first, second = row_sums[4:5, :tokens], row_sums[5:6, :tokens]

    def body(i, _):
        rows = rows_at(i)
        xhat = (x_in[rows, :].astype(F32) - mean) * scale
        found[rows, :] = chip[rows, :] + received[rows, :].astype(F32) - scale * (first + xhat * second)

    each_rows(part, body)


def scale_kernel(all_tokens, found, sums, d_input):
    factor = loss_scale(all_tokens, sums, found.shape[1])

    def body(i, _):
        d_input[rows_at(i), :] = found[rows_at(i), :] * factor

    each_rows(found.shape[0], body)


def local(
    width,
    row_devices,
    x_in,
    history,
    cotangent,
    counts,
    positions,
    mix_weights,
    self_weight,
    first_norm_gain,
    first_norm_bias,
    w_qkv,
    w_out,
    second_norm_gain,
    second_norm_bias,
    w_up,
    w_down,
):
    part, tokens = x_in.shape
    model = w_out.shape[1]
    hidden_units = w_up.shape[1]
    half = tokens // 2
    layers = mix_weights.shape[0]
    all_tokens = float(tokens * row_devices)
    at = lax.axis_index("width").astype(jnp.int32)[None]
    me = lax.axis_index("rows").astype(jnp.int32)[None]
    Order.last, Order.cost = None, 10**8
    to_width = lambda value, offset: xor_send(value, "width", width, offset)
    to_row = lambda value, offset: xor_send(value, "rows", row_devices, offset)
    w_qkv = w_qkv.reshape(3 * part, model)
    rates = 1.0 / 10000.0 ** (np.arange(HEAD_DIM // 2) * 2.0 / HEAD_DIM)
    x_in, cotangent, counts = after((x_in, cotangent, counts), at, me)

    x_far, x_near = to_width(x_in, 2), to_width(x_in, 1)
    norms, cosine, sine = prepare(
        x_near,
        positions[None, :],
        jnp.asarray(rates[:, None], F32),
        *(v[None, :] for v in (first_norm_gain, first_norm_bias, second_norm_gain, second_norm_bias)),
    )
    strides = [1 << i for i in range(row_devices.bit_length() - 1)]
    norms_near = join([norms, to_width(norms, 1)])
    norms_far = to_width(norms_near, 2)
    norms = kernel(norms_kernel, shape(model, 8), [at], [norms_near, norms_far])
    x_both = to_width(after(x_far, norms), 1)
    cot_now = after(cotangent, x_far)
    cot_far, cot_near = to_width(cot_now, 2), to_width(cot_now, 1)

    x_all, normed_one, stats_one, qkv = kernel(
        project_kernel,
        (
            shape(model, tokens, kind=BF16),
            shape(model, tokens, kind=BF16),
            shape(2, tokens),
            shape(3 * part, tokens, kind=BF16),
        ),
        [at],
        [x_in, x_near, x_far, x_both, norms, cosine, sine, w_qkv, w_out],
        [pltpu.VMEM((3 * part, tokens), F32)],
    )
    Order.cost = 10**9
    send, keep, x_half, heads_out, probs = kernel(
        attention_kernel,
        (
            shape(model, half, kind=BF16),
            shape(model, half),
            shape(model, half, kind=BF16),
            shape(part, tokens, kind=BF16),
            shape(part // HEAD_DIM, tokens, tokens, kind=BF16),
        ),
        [at],
        [after(qkv, cot_far), w_out, x_all],
        [pltpu.VMEM((tokens, half), F32)],
    )
    chip, send = add([keep, to_width(send, 1)], (0, model, F32), (0, model, BF16))
    received = to_width(send, 2)
    cot_both = to_width(after(cot_far, chip), 1)

    running, d_mix = history_call(
        functools.partial(history_kernel, 32),
        (shape(part, tokens), shape(layers, STEP // 2, 128)),
        (False, True),
        (False, False),
        [mix_weights, counts],
        [cotangent, pltpu.with_memory_space_constraint(history, pltpu.HBM)],
    )
    g_out, d_active, cot_half = kernel(
        output_gradient_kernel,
        (shape(model, tokens, kind=BF16), shape(hidden_units, tokens), shape(model, half, kind=BF16)),
        [at, self_weight, counts],
        [cotangent, cot_near, cot_far, cot_both, w_down],
        [pltpu.VMEM((model, tokens), BF16)],
    )

    middle, stats_two, normed_own = kernel(
        middle_kernel,
        (shape(model, half), shape(2, half), shape(model, half, kind=BF16)),
        [],
        [x_half, chip, received, norms],
    )
    normed_two, active, d_hidden, send, keep = kernel(
        feed_forward_kernel,
        (
            shape(model, tokens, kind=BF16),
            shape(hidden_units, tokens, kind=BF16),
            shape(hidden_units, tokens, kind=BF16),
            shape(model, half, kind=BF16),
            shape(model, half),
        ),
        [],
        [normed_own, to_width(normed_own, 1), w_up, d_active],
        [pltpu.VMEM((hidden_units, tokens), F32)],
    )

    down = Stream(row_devices, 0, hidden_units, "halving")
    up = Stream(row_devices, 0, model, "crossed")
    down_parts = weight_gradient(me, [down], active, g_out)[0]
    down_got = start_stage(down, down_parts, 0)
    chip, send = add([keep, to_width(send, 1)], (0, model, F32), (0, model, BF16))
    received = to_width(send, 2)
    up_parts = weight_gradient(me, [up], normed_two, d_hidden)[0]
    up_got = start_stage(up, up_parts, 0)
    blocks = (shape(2 * part, tokens, kind=BF16), shape(2 * part, tokens))
    out_send, out_keep = kernel(
        output_kernel, blocks, [at], [active, w_down, middle], [pltpu.VMEM((model, tokens), F32)]
    )
    out_near = to_width(out_send, 1)

    d_middle, g_own, gains_two = kernel(
        middle_gradient_kernel,
        (shape(model, half), shape(model, half, kind=BF16), shape(2, model)),
        [at, self_weight, counts],
        [chip, received, middle, stats_two, cot_half, norms],
        [pltpu.VMEM((model, half), F32), pltpu.VMEM((model, 128), F32), pltpu.VMEM((model, 128), F32)],
    )
    g_other = to_width(g_own, 1)
    out_chip, out_send = add([out_keep, out_near], (0, part, F32), (part, 2 * part, BF16))
    out_far = to_width(out_send, 2)
    down_parts = add_stage(down, down_parts, down_got, 0)
    down_got = start_stage(down, down_parts, 1)
    up_parts = add_stage(up, up_parts, up_got, 0)
    up_got = start_stage(up, up_parts, 1)
    d_project, g_mid = kernel(
        attention_gradient_kernel,
        (shape(3 * part, tokens, kind=BF16), shape(model, tokens, kind=BF16)),
        [at],
        [g_own, g_other, w_out, qkv, probs, cosine, sine],
        [
            pltpu.VMEM((part, tokens), BF16),
            pltpu.VMEM((tokens, half), BF16),
            pltpu.VMEM((tokens, half), F32),
            pltpu.VMEM((HEAD_DIM, tokens), F32),
            pltpu.VMEM((HEAD_DIM, tokens), F32),
            pltpu.VMEM((HEAD_DIM, tokens), F32),
        ],
    )
    tail_rows = 4 * part
    tail = [
        Stream(row_devices, 0, tail_rows // 2, "halving"),
        Stream(row_devices, tail_rows // 2, tail_rows // 2, "crossed"),
    ]
    first, second = tail
    first_parts, second_parts = weight_gradient(me, tail, d_project, normed_one, heads_out, g_mid)
    first_got = start_stage(first, first_parts, 0)
    second_got = start_stage(second, second_parts, 0)

    Order.cost = 10**8
    down_parts = add_stage(down, down_parts, down_got, 1)
    down_got = start_stage(down, down_parts, 2)
    up_parts = add_stage(up, up_parts, up_got, 1)
    up_got = start_stage(up, up_parts, 2)
    in_send, in_keep, sums = kernel(
        functools.partial(input_gradient_kernel, width),
        blocks + (shape(8, model),),
        [at, counts],
        [d_project, w_qkv, x_all, stats_one, d_middle, norms, gains_two],
        [pltpu.VMEM((model, tokens), F32), pltpu.VMEM((model, 128), F32), pltpu.VMEM((model, 128), F32)],
    )
    in_near = to_width(in_send, 1)
    last = len(down.digits) - 1
    mixed, sums = kernel(
        mixed_kernel,
        (shape(part, tokens, kind=BF16), shape(8, model)),
        [self_weight, counts],
        [out_chip, out_far, running, cotangent, d_mix, sums],
        [pltpu.VMEM((128, 128), F32)],
    )
    sums_got = to_width(sums, 1)
    first_parts = add_stage(first, first_parts, first_got, 0)
    first_got = start_stage(first, first_parts, 1)
    second_parts = add_stage(second, second_parts, second_got, 0)
    second_got = start_stage(second, second_parts, 1)
    down_value = sum_rest(down, add_stage(down, down_parts, down_got, 2)[0])
    down_pieces = gather_stage(down, down_value, last)
    up_value = sum_rest(up, add_stage(up, up_parts, up_got, 2)[0])
    up_pieces = gather_stage(up, up_value, last)
    first_parts = add_stage(first, first_parts, first_got, 1)
    first_got = start_stage(first, first_parts, 2)
    second_parts = add_stage(second, second_parts, second_got, 1)
    second_got = start_stage(second, second_parts, 2)
    sums = add([sums, sums_got], (0, 8, F32))[0]
    sums_got = to_width(sums, 2)
    first_value = sum_rest(first, add_stage(first, first_parts, first_got, 2)[0])
    first_pieces = gather_stage(first, first_value, last)
    Order.cost = 2 * 10**10
    second_value = sum_rest(second, add_stage(second, second_parts, second_got, 2)[0])
    second_pieces = gather_stage(second, second_value, last)
    Order.cost = 10**8
    in_chip, in_send = add([in_keep, in_near], (0, part, F32), (part, 2 * part, BF16))
    in_far = to_width(in_send, 2)
    row_sums = add([sums, sums_got], (0, 8, F32))[0]
    sums_got = to_row(row_sums, strides[0])
    down_pieces = gather_stage(down, join(down_pieces), last - 1)
    up_pieces = gather_stage(up, join(up_pieces), last - 1)
    sums = row_sums
    for stride in strides[1:-1]:
        sums = add([sums, sums_got], (0, 8, F32))[0]
        sums_got = to_row(sums, stride)
    in_total = kernel(d_input_kernel, shape(part, tokens), [], [in_chip, in_far, x_in, stats_one, row_sums])
    first_pieces = gather_stage(first, join(first_pieces), last - 1)
    second_pieces = gather_stage(second, join(second_pieces), last - 1)
    sums = add([sums, sums_got], (0, 8, F32))[0]
    sums_got = to_row(sums, strides[-1])
    down_pieces = gather_stage(down, join(down_pieces), 0)
    up_pieces = gather_stage(up, join(up_pieces), 0)
    sums = add([sums, sums_got], (0, 8, F32))[0]
    d_input = kernel(
        functools.partial(scale_kernel, all_tokens), shape(part, tokens), [], [in_total, sums]
    )
    d_history = history_call(
        functools.partial(d_history_kernel, all_tokens, 32),
        (shape(*history.shape, kind=BF16),),
        (False, False),
        (True,),
        [mix_weights, counts],
        [cotangent, sums],
    )[0]
    d_mix, d_self, *ends = kernel(
        functools.partial(ends_kernel, all_tokens, layers, width),
        (shape(1, layers), shape(1, 1)) + (shape(1, part),) * 4,
        [at],
        [sums],
    )
    first_pieces = gather_stage(first, join(first_pieces), 0)
    Order.cost = 2 * 10**10
    second_pieces = gather_stage(second, join(second_pieces), 0)
    Order.cost = 10**8
    d_w_down = place(all_tokens, me, sums, [down], down_pieces, (hidden_units,))[0]
    d_w_up = place(all_tokens, me, sums, [up], up_pieces, (model,))[0]
    d_w_qkv, d_w_out = place(all_tokens, me, sums, tail, first_pieces + second_pieces, (3 * part, part))
    return (
        mixed,
        d_input,
        d_history,
        d_mix[0],
        d_self[0],
        ends[0][0],
        ends[1][0],
        d_w_qkv.reshape(3, part, model),
        d_w_out,
        ends[2][0],
        ends[3][0],
        d_w_up,
        d_w_down,
    )


def solution(mesh):
    return jax.shard_map(
        functools.partial(local, mesh.shape["width"], mesh.shape["rows"]),
        mesh=mesh,
        in_specs=(
            P("width", "rows"),
            P(None, "width", "rows"),
            P("width", "rows"),
            P("rows"),
            P("rows"),
            P(),
            P(),
            P("width"),
            P("width"),
            P(None, "width", None),
            P("width", None),
            P("width"),
            P("width"),
            P(None, "width"),
            P("width", None),
        ),
        out_specs=(
            P("width", "rows"),
            P("width", "rows"),
            P(None, "width", "rows"),
            P(),
            P(),
            P("width"),
            P("width"),
            P(None, "width", None),
            P("width", None),
            P("width"),
            P("width"),
            P(None, "width"),
            P("width", None),
        ),
        check_vma=False,
    )
```

```python
import functools

import jax
import jax.numpy as jnp
import numpy as np
from jax import lax
from jax.experimental import pallas as pl
from jax.experimental.pallas import tpu as pltpu
from jax.sharding import PartitionSpec as P

HEAD_DIM = 64
EPSILON = 1e-05
BF16 = jnp.bfloat16
F32 = jnp.float32
STEP = 16


def shape(*dims, kind=F32):
    return jax.ShapeDtypeStruct(dims, kind)


class Order:
    last = None
    cost = 10**9


def kernel(body, outs, scalars, arrays, scratch=(), limit=12, streamed=()):
    arrays = list(arrays)
    if Order.last is not None:
        arrays[0] = after(arrays[0], Order.last)
    spaces = [pltpu.VMEM] * len(arrays) + [pltpu.HBM] * len(streamed)
    arrays += [pltpu.with_memory_space_constraint(v, pltpu.HBM) for v in streamed]
    found = pl.pallas_call(
        body,
        out_shape=outs,
        in_specs=[pl.BlockSpec(memory_space=pltpu.SMEM)] * len(scalars)
        + [pl.BlockSpec(memory_space=space) for space in spaces],
        out_specs=jax.tree.map(lambda _: pl.BlockSpec(memory_space=pltpu.VMEM), outs),
        scratch_shapes=list(scratch),
        compiler_params=pltpu.CompilerParams(vmem_limit_bytes=limit * 1024 * 1024),
        cost_estimate=pl.CostEstimate(flops=Order.cost, bytes_accessed=1024, transcendentals=0),
    )(*scalars, *arrays)
    Order.last = jax.tree.leaves(found)[0]
    return found


def after(value, *others):
    return lax.optimization_barrier((value, others))[0]


def dot(left, right, left_dim, right_dim):
    return lax.dot_general(left, right, (((left_dim,), (right_dim,)), ((), ())), preferred_element_type=F32)


def rows_at(i):
    return pl.ds(pl.multiple_of(i * STEP, STEP), STEP)


def each_rows(count, body, start=None, first=0):
    return lax.fori_loop(first // STEP, count // STEP, body, start, unroll=4)


def column_sum(value):
    return jnp.sum(value, axis=0, keepdims=True)


def xor_send(value, axis, size, offset):
    return lax.ppermute(value, axis, [(i, i ^ offset) for i in range(size)])


def add_kernel(count, cuts, *refs):
    parts, outs = refs[:count], refs[count:]

    def one(rows):
        found = parts[0][rows, :].astype(F32)
        for part in parts[1:]:
            found = found + part[rows, :].astype(F32)
        return found

    for (first, last), out in zip(cuts, outs):
        if (last - first) % STEP:
            out[...] = one(slice(first, last)).astype(out.dtype)
        else:

            def body(i, _, first=first, out=out):
                out[rows_at(i), :] = one(pl.ds(pl.multiple_of(first + i * STEP, STEP), STEP)).astype(out.dtype)

            each_rows(last - first, body)


def add(parts, *cuts):
    columns = parts[0].shape[1]
    outs = tuple(shape(last - first, columns, kind=kind) for first, last, kind in cuts)
    return list(kernel(functools.partial(add_kernel, len(parts), [cut[:2] for cut in cuts]), outs, [], parts))


def sum_small(value, axis, size):
    stride = 1
    while stride < size:
        value = add([value, xor_send(value, axis, size, stride)], (0, value.shape[0], F32))[0]
        stride *= 2
    return value


def join_kernel(*refs):
    out, start = refs[-1], 0
    for piece in refs[:-1]:
        out[start : start + piece.shape[0]] = piece[...]
        start += piece.shape[0]


def join(pieces):
    rows = sum(piece.shape[0] for piece in pieces)
    return kernel(join_kernel, shape(rows, pieces[0].shape[1], kind=pieces[0].dtype), [], pieces)


def chunks_of(count, rows):
    count = min(count, 8)
    while rows % (16 * count):
        count //= 2
    return count


def digits_of(count, kind):
    if kind == "halving":
        strides = []
        stride = 1
        while stride < count:
            strides.append((stride, 2))
            stride *= 2
        return strides
    strides = digits_of(count, "halving")
    return [strides[1], strides[0]] + strides[2:]


def offsets_of(digits):
    found = [0]
    for stride, radix in digits:
        found = [low + e * stride for low in found for e in range(radix)]
    return found


class Stream:
    def __init__(self, row_devices, first, rows, kind):
        self.first, self.rows = first, rows
        self.count = chunks_of(row_devices, rows)
        self.row_devices = row_devices
        self.digits = digits_of(self.count, kind)
        self.chunk = rows // self.count

    def parts(self):
        stride, radix = self.digits[0]
        rest = offsets_of(self.digits[1:])
        return [[e * stride + low for low in rest] for e in range(radix)]

    def send(self, value, offset):
        return xor_send(value, "rows", self.row_devices, offset)


def weight_gradient_kernel(streams, pairs, me_ref, *refs):
    operands, outs, scratch = refs[: 2 * pairs], list(refs[2 * pairs : -1]), refs[-1]
    start = 0
    for i in range(pairs):
        left, right = operands[2 * i], operands[2 * i + 1]
        count = left.shape[0]
        scratch[start : start + count] = dot(left[...], right[...], 1, 1).astype(BF16)
        start += count
    for stream in streams:
        for offsets in stream.parts():
            out = outs.pop(0)
            for place, offset in enumerate(offsets):
                chunk = (me_ref[0] % stream.count) ^ offset
                at = pl.multiple_of(stream.first + chunk * stream.chunk, 16)
                out[place * stream.chunk : (place + 1) * stream.chunk] = scratch[pl.ds(at, stream.chunk), :]


def weight_gradient(me, streams, *operands):
    pairs = len(operands) // 2
    total = sum(operands[2 * i].shape[0] for i in range(pairs))
    columns = operands[1].shape[0]
    outs = tuple(
        shape(len(offsets) * stream.chunk, columns, kind=BF16) for stream in streams for offsets in stream.parts()
    )
    found = list(
        kernel(
            functools.partial(weight_gradient_kernel, streams, pairs),
            outs,
            [me],
            operands,
            [pltpu.VMEM((total, columns), BF16)],
        )
    )
    return [[found.pop(0) for _ in stream.parts()] for stream in streams]


def start_stage(stream, parts, stage):
    stride, radix = stream.digits[stage]
    return [stream.send(parts[e], e * stride) for e in range(1, radix)]


def add_stage(stream, parts, received, stage):
    rows = parts[0].shape[0]
    radix = 1 if stage + 1 == len(stream.digits) else stream.digits[stage + 1][1]
    size = rows // radix
    return add([parts[0]] + received, *((e * size, (e + 1) * size, BF16) for e in range(radix)))


def sum_rest(stream, value):
    stride = stream.count
    while stride < stream.row_devices:
        value = add([value, stream.send(value, stride)], (0, value.shape[0], BF16))[0]
        stride *= 2
    return value


def gather_stage(stream, value, stage):
    stride, radix = stream.digits[stage]
    return [value] + [stream.send(value, e * stride) for e in range(1, radix)]


def place_kernel(all_tokens, streams, bounds, me_ref, sums, *refs):
    pieces, outs = list(refs[: -len(bounds)]), refs[-len(bounds) :]
    scale = loss_scale(all_tokens, sums, outs[0].shape[1])
    for stream in streams:
        for offsets in stream.parts():
            piece = pieces.pop(0)
            for place, offset in enumerate(offsets):
                chunk = (me_ref[0] % stream.count) ^ offset
                row = stream.first + chunk * stream.chunk
                for (first, last), out in zip(bounds, outs):

                    def store(out=out, first=first, piece=piece, place=place, row=row, size=stream.chunk):
                        at = pl.multiple_of(row - first, 16)
                        out[pl.ds(at, size), :] = (
                            piece[place * size : (place + 1) * size].astype(F32) * scale
                        )

                    if len(bounds) == 1:
                        store()
                    else:
                        pl.when((row >= first) & (row < last))(store)


def place(all_tokens, me, sums, streams, pieces, sizes):
    columns = pieces[0].shape[1]
    bounds, start = [], 0
    for size in sizes:
        bounds.append((start, start + size))
        start += size
    outs = tuple(shape(size, columns) for size in sizes)
    return kernel(functools.partial(place_kernel, all_tokens, streams, bounds), outs, [me], [sums, *pieces])


def live_row(counts_ref, width, first):
    place = lax.broadcasted_iota(jnp.int32, (1, width), 1) + first
    return jnp.where(place < counts_ref[0], 1.0, 0.0)


def loss_scale(all_tokens, sums, width):
    return jnp.full((1, width), all_tokens, F32) / jnp.broadcast_to(sums[7:8, 0:1], (1, width))


def history_kernel(block, mix_ref, counts_ref, cot_ref, history_ref, running_ref, d_mix_ref):
    layers, features, tokens = history_ref.shape
    live = live_row(counts_ref, tokens, 0)
    d_mix_ref[...] = jnp.zeros_like(d_mix_ref)

    def body(history_part):
        for i in range(block // STEP):
            rows = slice(i * STEP, (i + 1) * STEP)
            own = pl.ds(pl.multiple_of(pl.program_id(0) * block + i * STEP, STEP), STEP)
            grad = cot_ref[own].astype(F32) * live
            running = jnp.zeros_like(grad)
            for j in range(layers):
                layer = history_part[j, rows].astype(F32)
                running = running + mix_ref[j] * layer
                terms = grad * layer
                terms = terms[: STEP // 2] + terms[STEP // 2 :]
                d_mix_ref[j] += sum(terms[:, k : k + 128] for k in range(0, tokens, 128))
            running_ref[own] = running

    whole = pl.BlockSpec((layers, block, tokens), lambda i: (0, i, 0))
    pltpu.emit_pipeline(body, grid=(features // block,), in_specs=[whole])(history_ref)


def d_history_kernel(all_tokens, block, mix_ref, counts_ref, cot_ref, sums, d_history_ref):
    layers, features, tokens = d_history_ref.shape
    factor = live_row(counts_ref, tokens, 0) * loss_scale(all_tokens, sums, tokens)

    def body(part):
        for i in range(block // STEP):
            rows = slice(i * STEP, (i + 1) * STEP)
            own = pl.ds(pl.multiple_of(pl.program_id(0) * block + i * STEP, STEP), STEP)
            grad = cot_ref[own].astype(F32) * factor
            for j in range(layers):
                part[j, rows] = (mix_ref[j] * grad).astype(BF16)

    whole = pl.BlockSpec((layers, block, tokens), lambda i: (0, i, 0))
    pltpu.emit_pipeline(body, grid=(features // block,), out_specs=[whole])(d_history_ref)


def history_call(body, outs, in_hbm, out_hbm, scalars, arrays):
    vmem, hbm = pl.BlockSpec(memory_space=pltpu.VMEM), pl.BlockSpec(memory_space=pltpu.HBM)
    arrays = [after(arrays[0], Order.last), *arrays[1:]]
    found = pl.pallas_call(
        body,
        out_shape=outs,
        in_specs=[pl.BlockSpec(memory_space=pltpu.SMEM)] * len(scalars) + [hbm if h else vmem for h in in_hbm],
        out_specs=tuple(hbm if h else vmem for h in out_hbm),
        compiler_params=pltpu.CompilerParams(vmem_limit_bytes=12 * 1024 * 1024),
        cost_estimate=pl.CostEstimate(flops=Order.cost, bytes_accessed=1024, transcendentals=0),
    )(*scalars, *arrays)
    Order.last = found[0]
    return found


def spread_of(load, count, width):
    zero = jnp.zeros((STEP, width), F32)
    mean = column_sum(each_rows(count, lambda i, acc: acc + load(i), zero)) / count

    def squares(i, acc):
        centred = load(i) - mean
        return acc + centred * centred

    return mean, lax.rsqrt(column_sum(each_rows(count, squares, zero)) / count + EPSILON)


def prepare_kernel(held, *refs):
    refs = refs[held:]
    sources, (norms, cosine, sine), places, sem = refs[:6], refs[6:9], refs[9:15], refs[15]
    copies = [pltpu.make_async_copy(*pair, sem.at[i]) for i, pair in enumerate(zip(sources, places))]
    for copy in copies:
        copy.start()
    norms[...] = jnp.zeros_like(norms)
    for copy in copies:
        copy.wait()
    positions, rates, *vectors = places
    for i, ref in enumerate(vectors):
        norms[i : i + 1, : ref.shape[1]] = ref[...]
    angles = positions[...].astype(F32) * rates[...]
    cosine[...] = jnp.cos(angles)
    sine[...] = jnp.sin(angles)


def prepare(held, *sources):
    tokens, part = sources[0].shape[1], sources[2].shape[1]
    rates = sources[1].shape[0]
    vmem = pl.BlockSpec(memory_space=pltpu.VMEM)
    found = pl.pallas_call(
        functools.partial(prepare_kernel, len(held)),
        out_shape=(shape(8, -(-part // 128) * 128), shape(rates, tokens), shape(rates, tokens)),
        in_specs=[vmem] * len(held) + [pl.BlockSpec(memory_space=pltpu.HBM)] * len(sources),
        out_specs=(vmem,) * 3,
        scratch_shapes=[pltpu.VMEM(v.shape, v.dtype) for v in sources] + [pltpu.SemaphoreType.DMA((len(sources),))],
        compiler_params=pltpu.CompilerParams(vmem_limit_bytes=4 * 1024 * 1024),
        cost_estimate=pl.CostEstimate(flops=Order.cost, bytes_accessed=1024, transcendentals=0),
    )(*held, *(pltpu.with_memory_space_constraint(v, pltpu.HBM) for v in sources))
    Order.last = found[0]
    return found


def norms_kernel(at_ref, n01, n23, norms):
    part = norms.shape[0] // 4
    near, far = n01[...].T, n23[...].T
    for e, norm in enumerate((near, near, far, far)):
        rows = pl.ds(pl.multiple_of((at_ref[0] ^ e) * part, 64), part)
        norms[rows, :] = norm[:part, 8 * (e % 2) : 8 * (e % 2) + 8]


def project_kernel(
    at_ref, x1, x2, x3, norms, cosine, sine, w_qkv, x0, x_all, normed, stats, qkv, project, own, sem
):
    at = at_ref[0]
    part, tokens = x1.shape
    model = w_qkv.shape[1]
    copy = pltpu.make_async_copy(x0, own, sem)
    copy.start()
    for e, piece in ((1, x1), (2, x2), (3, x3)):
        x_all[pl.ds(pl.multiple_of((at ^ e) * part, 64), part), :] = piece[...]
    copy.wait()
    x_all[pl.ds(pl.multiple_of(at * part, 64), part), :] = own[...]
    mean, scale = spread_of(lambda i: x_all[rows_at(i), :].astype(F32), model, tokens)
    stats[0:1] = mean
    stats[1:2] = scale

    def normalise(i, _):
        rows = rows_at(i)
        xhat = (x_all[rows, :].astype(F32) - mean) * scale
        normed[rows, :] = (xhat * norms[rows, 0:1] + norms[rows, 1:2]).astype(BF16)

    each_rows(model, normalise)
    project[...] = dot(w_qkv[...], normed[...], 1, 0)
    width = HEAD_DIM // 2
    for block, factor in ((0, HEAD_DIM ** (-0.5)), (1, 1.0)):
        for start in range(block * part, (block + 1) * part, HEAD_DIM):
            front, back = project[start : start + width], project[start + width : start + HEAD_DIM]
            cos, sin = cosine[...] * factor, sine[...] * factor
            qkv[start : start + width] = (front * cos - back * sin).astype(BF16)
            qkv[start + width : start + HEAD_DIM] = (back * cos + front * sin).astype(BF16)
    qkv[2 * part :] = project[2 * part :].astype(BF16)


def attention_kernel(at_ref, qkv, x_all, w_out_hbm, send, keep, x_half, heads_out, probs, scores, w_out, sem):
    at = at_ref[0]
    copy = pltpu.make_async_copy(w_out_hbm, w_out, sem)
    copy.start()
    part, tokens = heads_out.shape
    half = tokens // 2
    for h in range(part // HEAD_DIM):
        head = slice(h * HEAD_DIM, (h + 1) * HEAD_DIM)
        for t in range(2):
            now = slice(t * half, (t + 1) * half)
            count = (t + 1) * half
            query = qkv[head, now]
            key = qkv[part + h * HEAD_DIM : part + (h + 1) * HEAD_DIM, :count]
            value = qkv[2 * part + h * HEAD_DIM : 2 * part + (h + 1) * HEAD_DIM, :count]
            scores[:count] = dot(key, query, 0, 0)

            def masked_top(i, acc):
                rows = rows_at(i)
                behind = lax.broadcasted_iota(jnp.int32, (STEP, half), 0) + (i * STEP - t * half)
                found = jnp.where(behind <= lax.broadcasted_iota(jnp.int32, (STEP, half), 1), scores[rows, :], -1e30)
                scores[rows, :] = found
                return jnp.maximum(acc, found)

            top = each_rows(
                t * half, lambda i, acc: jnp.maximum(acc, scores[rows_at(i), :]), jnp.full((STEP, half), -1e30, F32)
            )
            top = jnp.max(each_rows(count, masked_top, top, first=t * half), axis=0, keepdims=True)

            def raise_rows(i, acc):
                rows = rows_at(i)
                found = jnp.exp(scores[rows, :] - top)
                scores[rows, :] = found
                return acc + found

            total = 1.0 / column_sum(each_rows(count, raise_rows, jnp.zeros((STEP, half), F32)))

            def settle(i, _):
                rows = rows_at(i)
                probs[h, rows, now] = (scores[rows, :] * total).astype(BF16)

            each_rows(count, settle)
            heads_out[head, now] = dot(value, probs[h, :count, now], 1, 0).astype(BF16)
    own = pl.multiple_of((at % 2) * half, half)
    other = pl.multiple_of((1 - at % 2) * half, half)
    copy.wait()
    send[...] = dot(w_out[...], heads_out[:, pl.ds(other, half)], 0, 0).astype(BF16)
    keep[...] = dot(w_out[...], heads_out[:, pl.ds(own, half)], 0, 0)
    x_half[...] = x_all[:, pl.ds(own, half)]


def output_gradient_kernel(
    at_ref, self_ref, counts_ref, c0, c1, c2, c3, w_down, g_out, d_active, cot_half, cot_all
):
    at = at_ref[0]
    part, tokens = c0.shape
    half = tokens // 2
    for e, piece in enumerate((c0, c1, c2, c3)):
        cot_all[pl.ds(pl.multiple_of((at ^ e) * part, 64), part), :] = piece[...]
    for place, side in enumerate((at % 2, 1 - at % 2)):
        now = pl.ds(pl.multiple_of(side * half, half), half)
        factor = live_row(counts_ref, half, side * half)

        def scale(i, _, now=now, factor=factor, place=place):
            rows = rows_at(i)
            grad = cot_all[rows, now].astype(F32) * factor
            g_out[rows, place * half : (place + 1) * half] = (self_ref[0] * grad).astype(BF16)
            if place == 0:
                cot_half[rows, :] = cot_all[rows, now]

        each_rows(cot_all.shape[0], scale)
    d_active[...] = dot(w_down[...], g_out[...], 1, 0)


def middle_kernel(x_half, chip, received, norms, middle, stats, normed):
    model, half = chip.shape

    def add(i, _):
        rows = rows_at(i)
        middle[rows, :] = x_half[rows, :].astype(F32) + chip[rows, :] + received[rows, :].astype(F32)

    each_rows(model, add)
    mean, scale = spread_of(lambda i: middle[rows_at(i), :], model, half)
    stats[0:1] = mean
    stats[1:2] = scale

    def normalise(i, _):
        rows = rows_at(i)
        xhat = (middle[rows, :] - mean) * scale
        normed[rows, :] = (xhat * norms[rows, 2:3] + norms[rows, 3:4]).astype(BF16)

    each_rows(model, normalise)


def feed_forward_kernel(own, other, w_up, d_active, normed, active, d_hidden, send, keep, hidden):
    half = own.shape[1]
    normed[:, :half] = own[...]
    normed[:, half:] = other[...]
    hidden[...] = dot(w_up[...], normed[...], 0, 0)

    def bend(i, _):
        rows = rows_at(i)
        u = hidden[rows, :]
        squared = u * u
        curve = jnp.tanh(0.7978845608028654 * u * (1.0 + 0.044715 * squared))
        lifted = 0.5 * (1.0 + curve)
        active[rows, :] = (u * lifted).astype(BF16)
        slope = lifted + u * (0.5 * (1.0 - curve * curve)) * (
            0.7978845608028654 + (3 * 0.044715 * 0.7978845608028654) * squared
        )
        d_hidden[rows, :] = (slope * d_active[rows, :]).astype(BF16)

    each_rows(hidden.shape[0], bend)
    send[...] = dot(w_up[...], d_hidden[:, half:], 1, 0).astype(BF16)
    keep[...] = dot(w_up[...], d_hidden[:, :half], 1, 0)


def store_blocks(at, total, part, near, *outs):
    for e, out in zip(near, outs):
        out[...] = total[pl.ds(pl.multiple_of((at ^ e) * part, 64), part), :].astype(out.dtype)


def output_kernel(at_ref, active, w_down, middle, send, send_far, keep, keep_far, total):
    at = at_ref[0]
    model, half = middle.shape
    part = send.shape[0]
    own = pl.ds(pl.multiple_of((at % 2) * half, half), half)
    other = pl.ds(pl.multiple_of((1 - at % 2) * half, half), half)
    total[:, own] = dot(w_down[...], active[:, :half], 0, 0) + 0.5 * middle[...]
    total[:, other] = dot(w_down[...], active[:, half:], 0, 0)
    store_blocks(at, total, part, (1, 3, 0, 2), send, send_far, keep, keep_far)


def fold_lanes(value):
    return sum(value[:, k : k + 128] for k in range(0, value.shape[1], 128))


def as_row(columns):
    return column_sum(columns[...].T)


def middle_gradient_kernel(
    at_ref, self_ref, counts_ref, chip, received, middle, stats, cot_half, norms,
    d_middle, g_mid, gains, d_normed, gain_sums, bias_sums,
):
    model, half = chip.shape
    mean, scale = stats[0:1], stats[1:2]
    zero = jnp.zeros((STEP, half), F32)

    def sums(i, acc):
        rows = rows_at(i)
        grad = chip[rows, :] + received[rows, :].astype(F32)
        d_normed[rows, :] = grad
        xhat = (middle[rows, :] - mean) * scale
        both = grad * xhat
        gain_sums[rows, :] = fold_lanes(both)
        bias_sums[rows, :] = fold_lanes(grad)
        gain = norms[rows, 2:3]
        return acc[0] + grad * gain, acc[1] + both * gain

    first, second = (column_sum(v) / model for v in each_rows(model, sums, (zero, zero)))
    factor = self_ref[0] * live_row(counts_ref, half, (at_ref[0] % 2) * half)

    def finish(i, _):
        rows = rows_at(i)
        xhat = (middle[rows, :] - mean) * scale
        found = cot_half[rows, :].astype(F32) * factor + scale * (
            d_normed[rows, :] * norms[rows, 2:3] - first - xhat * second
        )
        d_middle[rows, :] = found
        g_mid[rows, :] = found.astype(BF16)

    each_rows(model, finish)
    gains[0:1] = as_row(gain_sums)
    gains[1:2] = as_row(bias_sums)


def attention_gradient_kernel(
    at_ref, own, other, w_out, qkv, probs, cosine, sine,
    d_project, g_mid, d_heads, d_scores, products, d_queries, d_keys, d_values,
):
    at = at_ref[0]
    half = own.shape[1]
    part = w_out.shape[0]
    g_mid[:, pl.ds(pl.multiple_of((at % 2) * half, half), half)] = own[...]
    g_mid[:, pl.ds(pl.multiple_of((1 - at % 2) * half, half), half)] = other[...]
    d_heads[...] = dot(w_out[...], g_mid[...], 1, 0).astype(BF16)
    width = HEAD_DIM // 2
    for h in range(part // HEAD_DIM):
        head = slice(h * HEAD_DIM, (h + 1) * HEAD_DIM)
        query = qkv[head]
        key = qkv[part + h * HEAD_DIM : part + (h + 1) * HEAD_DIM]
        value = qkv[2 * part + h * HEAD_DIM : 2 * part + (h + 1) * HEAD_DIM]
        for t in range(2):
            now = slice(t * half, (t + 1) * half)
            count = (t + 1) * half
            products[:count] = dot(value[:, :count], d_heads[head, now], 0, 0)

            def weigh(i, acc):
                rows = rows_at(i)
                return acc + products[rows, :] * probs[h, rows, now].astype(F32)

            inner = column_sum(each_rows(count, weigh, jnp.zeros((STEP, half), F32)))

            def settle(i, _):
                rows = rows_at(i)
                d_scores[rows, :] = (probs[h, rows, now].astype(F32) * (products[rows, :] - inner)).astype(BF16)

            each_rows(count, settle)
            d_queries[:, now] = dot(key[:, :count], d_scores[:count], 1, 0) * HEAD_DIM ** (-0.5)
            d_key = dot(query[:, now], d_scores[:count], 1, 1)
            d_value = dot(d_heads[head, now], probs[h, :count, now], 1, 1)
            if t == 0:
                d_keys[:, :half] = d_key
                d_values[:, :half] = d_value
            else:
                d_keys[:, :half] += d_key[:, :half]
                d_values[:, :half] += d_value[:, :half]
                d_keys[:, half:] = d_key[:, half:]
                d_values[:, half:] = d_value[:, half:]
        for block, found in ((0, d_queries), (1, d_keys)):
            start = block * part + h * HEAD_DIM
            front, back = found[:width], found[width:]
            d_project[start : start + width] = (front * cosine[...] + back * sine[...]).astype(BF16)
            d_project[start + width : start + HEAD_DIM] = (back * cosine[...] - front * sine[...]).astype(BF16)
        d_project[2 * part + h * HEAD_DIM : 2 * part + (h + 1) * HEAD_DIM] = d_values[...].astype(BF16)


def input_gradient_kernel(
    width, at_ref, counts_ref, d_project, w_qkv, x_all, stats, d_middle, norms, gains,
    send, send_far, keep, keep_far, sums, total, gain_sums, bias_sums,
):
    at = at_ref[0]
    model, half = d_middle.shape
    tokens = x_all.shape[1]
    part = send.shape[0]
    total[...] = dot(w_qkv[...], d_project[...], 0, 0)
    mean, scale = stats[0:1], stats[1:2]
    zero = jnp.zeros((STEP, tokens), F32)
    own = pl.ds(pl.multiple_of((at % 2) * half, half), half)

    def body(i, acc):
        rows = rows_at(i)
        grad = total[rows, :]
        xhat = (x_all[rows, :].astype(F32) - mean) * scale
        both = grad * xhat
        gain_sums[rows, :] = fold_lanes(both)
        bias_sums[rows, :] = fold_lanes(grad)
        gain = norms[rows, 0:1]
        lifted = grad * gain
        total[rows, :] = lifted * scale
        total[rows, own] += 0.5 * d_middle[rows, :]
        return acc[0] + lifted, acc[1] + both * gain

    first, second = each_rows(model, body, (zero, zero))
    store_blocks(at, total, part, (1, 3, 0, 2), send, send_far, keep, keep_far)
    sums[...] = jnp.zeros_like(sums)
    sums[0:1] = as_row(gain_sums)
    sums[1:2] = as_row(bias_sums)
    sums[2:4] = 0.5 * gains[...]
    sums[4:5, :tokens] = column_sum(first) / model
    sums[5:6, :tokens] = column_sum(second) / model
    sums[7:8] = jnp.zeros((1, model), F32) + counts_ref[0].astype(F32) / width


def mixed_kernel(
    self_ref, counts_ref, own, near, far, running, cotangent, d_mix, sums, mixed, all_sums, table
):
    layers = d_mix.shape[0]
    part, tokens = own.shape
    live = live_row(counts_ref, tokens, 0)

    def body(i, acc):
        rows = rows_at(i)
        output = own[rows, :] + near[rows, :].astype(F32) + far[rows, :].astype(F32)
        mixed[rows, :] = (self_ref[0] * output + running[rows, :]).astype(BF16)
        return acc + fold_lanes(cotangent[rows, :].astype(F32) * live * output)

    found = each_rows(part, body, jnp.zeros((STEP, 128), F32))
    table[...] = jnp.zeros_like(table)
    table[:layers] = jnp.sum(d_mix[...], axis=1)
    table[layers : layers + 1] = column_sum(found)
    all_sums[...] = sums[...]
    all_sums[6:7, :128] = as_row(table)


def ends_kernel(all_tokens, layers, width, at_ref, sums, d_mix, d_self, *ends):
    part = ends[0].shape[1]
    scale = loss_scale(all_tokens, sums, sums.shape[1])
    d_mix[...] = sums[6:7, :layers] * scale[:, :layers]
    d_self[...] = sums[6:7, layers : layers + 1] * scale[:, :1]
    for i, end in enumerate(ends):
        scaled = sums[i : i + 1] * scale
        found = scaled[:, :part]
        for w in range(1, width):
            found = jnp.where(at_ref[0] == w, scaled[:, w * part : (w + 1) * part], found)
        end[...] = found


def d_input_kernel(own, near, far, x_in, stats, row_sums, found):
    part, tokens = own.shape
    mean, scale = stats[0:1], stats[1:2]
    first, second = row_sums[4:5, :tokens], row_sums[5:6, :tokens]

    def body(i, _):
        rows = rows_at(i)
        xhat = (x_in[rows, :].astype(F32) - mean) * scale
        total = own[rows, :] + near[rows, :].astype(F32) + far[rows, :].astype(F32)
        found[rows, :] = total - scale * (first + xhat * second)

    each_rows(part, body)


def scale_kernel(all_tokens, found, sums, d_input):
    factor = loss_scale(all_tokens, sums, found.shape[1])

    def body(i, _):
        d_input[rows_at(i), :] = found[rows_at(i), :] * factor

    each_rows(found.shape[0], body)


def local(
    width,
    row_devices,
    x_in,
    history,
    cotangent,
    counts,
    positions,
    mix_weights,
    self_weight,
    first_norm_gain,
    first_norm_bias,
    w_qkv,
    w_out,
    second_norm_gain,
    second_norm_bias,
    w_up,
    w_down,
):
    part, tokens = x_in.shape
    model = w_out.shape[1]
    hidden_units = w_up.shape[1]
    half = tokens // 2
    layers = mix_weights.shape[0]
    all_tokens = float(tokens * row_devices)
    at = lax.axis_index("width").astype(jnp.int32)[None]
    me = lax.axis_index("rows").astype(jnp.int32)[None]
    Order.last, Order.cost = None, 10**8
    to_width = lambda value, offset: xor_send(value, "width", width, offset)
    to_row = lambda value, offset: xor_send(value, "rows", row_devices, offset)
    w_qkv = w_qkv.reshape(3 * part, model)
    rates = 1.0 / 10000.0 ** (np.arange(HEAD_DIM // 2) * 2.0 / HEAD_DIM)
    x_in, cotangent, counts = after((x_in, cotangent, counts), at, me)

    x_far, x_near = to_width(x_in, 2), to_width(x_in, 1)
    norms, cosine, sine = prepare(
        [x_near],
        positions[None, :],
        jnp.asarray(rates[:, None], F32),
        *(v[None, :] for v in (first_norm_gain, first_norm_bias, second_norm_gain, second_norm_bias)),
    )
    strides = [1 << i for i in range(row_devices.bit_length() - 1)]
    norms_near = join([norms, to_width(norms, 1)])
    norms_far = to_width(norms_near, 2)
    norms = kernel(norms_kernel, shape(model, 8), [at], [norms_near, norms_far])
    x_both = to_width(after(x_far, norms), 1)
    cot_now = after(cotangent, norms_near)
    cot_far, cot_near = to_width(cot_now, 2), to_width(cot_now, 1)

    x_all, normed_one, stats_one, qkv = kernel(
        project_kernel,
        (
            shape(model, tokens, kind=BF16),
            shape(model, tokens, kind=BF16),
            shape(2, tokens),
            shape(3 * part, tokens, kind=BF16),
        ),
        [at],
        [x_near, x_far, x_both, norms, cosine, sine, w_qkv],
        [pltpu.VMEM((3 * part, tokens), F32), pltpu.VMEM((part, tokens), BF16), pltpu.SemaphoreType.DMA],
        streamed=[x_in],
    )
    Order.cost = 10**9
    send, keep, x_half, heads_out, probs = kernel(
        attention_kernel,
        (
            shape(model, half, kind=BF16),
            shape(model, half),
            shape(model, half, kind=BF16),
            shape(part, tokens, kind=BF16),
            shape(part // HEAD_DIM, tokens, tokens, kind=BF16),
        ),
        [at],
        [after(qkv, cot_far), x_all],
        [pltpu.VMEM((tokens, half), F32), pltpu.VMEM((part, model), BF16), pltpu.SemaphoreType.DMA],
        streamed=[w_out],
    )
    chip, send = add([keep, to_width(send, 1)], (0, model, F32), (0, model, BF16))
    received = to_width(send, 2)
    cot_both = to_width(after(cot_far, chip), 1)

    running, d_mix = history_call(
        functools.partial(history_kernel, 32),
        (shape(part, tokens), shape(layers, STEP // 2, 128)),
        (False, True),
        (False, False),
        [mix_weights, counts],
        [cotangent, pltpu.with_memory_space_constraint(history, pltpu.HBM)],
    )
    g_out, d_active, cot_half = kernel(
        output_gradient_kernel,
        (shape(model, tokens, kind=BF16), shape(hidden_units, tokens), shape(model, half, kind=BF16)),
        [at, self_weight, counts],
        [cotangent, cot_near, cot_far, cot_both, w_down],
        [pltpu.VMEM((model, tokens), BF16)],
    )

    middle, stats_two, normed_own = kernel(
        middle_kernel,
        (shape(model, half), shape(2, half), shape(model, half, kind=BF16)),
        [],
        [x_half, chip, received, norms],
    )
    normed_two, active, d_hidden, send, keep = kernel(
        feed_forward_kernel,
        (
            shape(model, tokens, kind=BF16),
            shape(hidden_units, tokens, kind=BF16),
            shape(hidden_units, tokens, kind=BF16),
            shape(model, half, kind=BF16),
            shape(model, half),
        ),
        [],
        [normed_own, to_width(normed_own, 1), w_up, d_active],
        [pltpu.VMEM((hidden_units, tokens), F32)],
    )

    down = Stream(row_devices, 0, hidden_units, "halving")
    up = Stream(row_devices, 0, model, "crossed")
    down_parts = weight_gradient(me, [down], active, g_out)[0]
    down_got = start_stage(down, down_parts, 0)
    chip, send = add([keep, to_width(send, 1)], (0, model, F32), (0, model, BF16))
    received = to_width(send, 2)
    up_parts = weight_gradient(me, [up], normed_two, d_hidden)[0]
    up_got = start_stage(up, up_parts, 0)
    blocks = (shape(part, tokens, kind=BF16),) * 2 + (shape(part, tokens),) * 2
    out_send, out_send_far, out_keep, out_keep_far = kernel(
        output_kernel, blocks, [at], [active, w_down, middle], [pltpu.VMEM((model, tokens), F32)]
    )
    out_got = to_width(out_send, 1), to_width(out_send_far, 1)

    d_middle, g_own, gains_two = kernel(
        middle_gradient_kernel,
        (shape(model, half), shape(model, half, kind=BF16), shape(2, model)),
        [at, self_weight, counts],
        [chip, received, middle, stats_two, cot_half, norms],
        [pltpu.VMEM((model, half), F32), pltpu.VMEM((model, 128), F32), pltpu.VMEM((model, 128), F32)],
    )
    g_other = to_width(g_own, 1)
    out_send = add([out_keep_far, out_got[1]], (0, part, BF16))[0]
    out_far = to_width(out_send, 2)
    down_parts = add_stage(down, down_parts, down_got, 0)
    down_got = start_stage(down, down_parts, 1)
    up_parts = add_stage(up, up_parts, up_got, 0)
    up_got = start_stage(up, up_parts, 1)
    d_project, g_mid = kernel(
        attention_gradient_kernel,
        (shape(3 * part, tokens, kind=BF16), shape(model, tokens, kind=BF16)),
        [at],
        [g_own, g_other, w_out, qkv, probs, cosine, sine],
        [
            pltpu.VMEM((part, tokens), BF16),
            pltpu.VMEM((tokens, half), BF16),
            pltpu.VMEM((tokens, half), F32),
            pltpu.VMEM((HEAD_DIM, tokens), F32),
            pltpu.VMEM((HEAD_DIM, tokens), F32),
            pltpu.VMEM((HEAD_DIM, tokens), F32),
        ],
    )
    tail_rows = 4 * part
    tail = [
        Stream(row_devices, 0, tail_rows // 2, "halving"),
        Stream(row_devices, tail_rows // 2, tail_rows // 2, "crossed"),
    ]
    first, second = tail
    first_parts, second_parts = weight_gradient(me, tail, d_project, normed_one, heads_out, g_mid)
    first_got = start_stage(first, first_parts, 0)
    second_got = start_stage(second, second_parts, 0)

    Order.cost = 10**8
    down_parts = add_stage(down, down_parts, down_got, 1)
    down_got = start_stage(down, down_parts, 2)
    up_parts = add_stage(up, up_parts, up_got, 1)
    up_got = start_stage(up, up_parts, 2)
    in_send, in_send_far, in_keep, in_keep_far, sums = kernel(
        functools.partial(input_gradient_kernel, width),
        blocks + (shape(8, model),),
        [at, counts],
        [d_project, w_qkv, x_all, stats_one, d_middle, norms, gains_two],
        [pltpu.VMEM((model, tokens), F32), pltpu.VMEM((model, 128), F32), pltpu.VMEM((model, 128), F32)],
    )
    in_got = to_width(in_send, 1), to_width(in_send_far, 1)
    last = len(down.digits) - 1
    mixed, sums = kernel(
        mixed_kernel,
        (shape(part, tokens, kind=BF16), shape(8, model)),
        [self_weight, counts],
        [out_keep, out_got[0], out_far, running, cotangent, d_mix, sums],
        [pltpu.VMEM((128, 128), F32)],
    )
    sums_got = to_width(sums, 1)
    first_parts = add_stage(first, first_parts, first_got, 0)
    first_got = start_stage(first, first_parts, 1)
    second_parts = add_stage(second, second_parts, second_got, 0)
    second_got = start_stage(second, second_parts, 1)
    down_value = sum_rest(down, add_stage(down, down_parts, down_got, 2)[0])
    down_pieces = gather_stage(down, down_value, last)
    up_value = sum_rest(up, add_stage(up, up_parts, up_got, 2)[0])
    up_pieces = gather_stage(up, up_value, last)
    first_parts = add_stage(first, first_parts, first_got, 1)
    first_got = start_stage(first, first_parts, 2)
    second_parts = add_stage(second, second_parts, second_got, 1)
    second_got = start_stage(second, second_parts, 2)
    sums = add([sums, sums_got], (0, 8, F32))[0]
    sums_got = to_width(sums, 2)
    row_sums = add([sums, sums_got], (0, 8, F32))[0]
    sums_got = to_row(row_sums, strides[0])
    down_pieces = gather_stage(down, join(down_pieces), last - 1)
    up_pieces = gather_stage(up, join(up_pieces), last - 1)
    in_send = add([in_keep_far, in_got[1]], (0, part, BF16))[0]
    in_far = to_width(in_send, 2)
    sums = row_sums
    for stride in strides[1:-1]:
        sums = add([sums, sums_got], (0, 8, F32))[0]
        sums_got = to_row(sums, stride)
    first_value = sum_rest(first, add_stage(first, first_parts, first_got, 2)[0])
    first_pieces = gather_stage(first, first_value, last)
    second_value = sum_rest(second, add_stage(second, second_parts, second_got, 2)[0])
    second_pieces = gather_stage(second, second_value, last)
    sums = add([sums, sums_got], (0, 8, F32))[0]
    sums_got = to_row(sums, strides[-1])
    in_total = kernel(d_input_kernel, shape(part, tokens), [], [in_keep, in_got[0], in_far, x_in, stats_one, row_sums])
    down_pieces = gather_stage(down, join(down_pieces), 0)
    up_pieces = gather_stage(up, join(up_pieces), 0)
    first_pieces = gather_stage(first, join(first_pieces), last - 1)
    second_pieces = gather_stage(second, join(second_pieces), last - 1)
    sums = add([sums, sums_got], (0, 8, F32))[0]
    d_input = kernel(
        functools.partial(scale_kernel, all_tokens), shape(part, tokens), [], [in_total, sums]
    )
    d_history = history_call(
        functools.partial(d_history_kernel, all_tokens, 32),
        (shape(*history.shape, kind=BF16),),
        (False, False),
        (True,),
        [mix_weights, counts],
        [cotangent, sums],
    )[0]
    d_mix, d_self, *ends = kernel(
        functools.partial(ends_kernel, all_tokens, layers, width),
        (shape(1, layers), shape(1, 1)) + (shape(1, part),) * 4,
        [at],
        [sums],
    )
    first_pieces = gather_stage(first, join(first_pieces), 0)
    Order.cost = 2 * 10**10
    second_pieces = gather_stage(second, join(second_pieces), 0)
    Order.cost = 10**8
    d_w_down = place(all_tokens, me, sums, [down], down_pieces, (hidden_units,))[0]
    d_w_up = place(all_tokens, me, sums, [up], up_pieces, (model,))[0]
    d_w_qkv, d_w_out = place(all_tokens, me, sums, tail, first_pieces + second_pieces, (3 * part, part))
    return (
        mixed,
        d_input,
        d_history,
        d_mix[0],
        d_self[0],
        ends[0][0],
        ends[1][0],
        d_w_qkv.reshape(3, part, model),
        d_w_out,
        ends[2][0],
        ends[3][0],
        d_w_up,
        d_w_down,
    )


def solution(mesh):
    return jax.shard_map(
        functools.partial(local, mesh.shape["width"], mesh.shape["rows"]),
        mesh=mesh,
        in_specs=(
            P("width", "rows"),
            P(None, "width", "rows"),
            P("width", "rows"),
            P("rows"),
            P("rows"),
            P(),
            P(),
            P("width"),
            P("width"),
            P(None, "width", None),
            P("width", None),
            P("width"),
            P("width"),
            P(None, "width"),
            P("width", None),
        ),
        out_specs=(
            P("width", "rows"),
            P("width", "rows"),
            P(None, "width", "rows"),
            P(),
            P(),
            P("width"),
            P("width"),
            P(None, "width", None),
            P("width", None),
            P("width"),
            P("width"),
            P(None, "width"),
            P("width", None),
        ),
        check_vma=False,
    )
```

```python
import functools

import jax
import jax.numpy as jnp
import numpy as np
from jax import lax
from jax.experimental import pallas as pl
from jax.experimental.pallas import tpu as pltpu
from jax.sharding import PartitionSpec as P

HEAD_DIM = 64
EPSILON = 1e-05
BF16 = jnp.bfloat16
F32 = jnp.float32
STEP = 16


SCHEDULE = (
    ("down", 10),
    ("chip", 8),
    ("up", 10),
    ("out", 100),
    ("middle", 10),
    ("out_sum", 10),
    ("down1", 10),
    ("up1", 100),
    ("attention", 8),
    ("tail", 4),
    ("down2", 100),
    ("up2", 0.3),
    ("input", 1),
    ("mix", 8),
    ("first1", 1),
    ("second1", 1),
    ("up3", 100),
    ("down3", 1),
    ("first2", 2),
    ("sums1", 4),
    ("sums2", 1),
    ("input_sum", 1),
    ("second2", 1),
    ("sums3", 1),
    ("up4", 2),
    ("sums4", 1),
    ("down4", 4),
    ("first3", 40),
    ("input_total", 1),
    ("second3", 2),
    ("down5", 1),
    ("first4", 200),
    ("up5", 0.3),
    ("second4", 16),
    ("sums5", 1),
    ("scale", 0.1),
    ("first5", 40),
    ("ends", 1),
    ("history", 1),
    ("place_down", 1),
    ("second5", 200),
    ("place_up", 4),
    ("place_tail", 1),
)

FRONT = (1, 1, 1, 1, 1, 1, 10, 10, 10, 10, 10)


def shape(*dims, kind=F32):
    return jax.ShapeDtypeStruct(dims, kind)


class Values:
    pass


class Order:
    last = None
    cost = 0
    front = ()

    @classmethod
    def estimate(cls):
        if cls.front:
            cls.cost, *cls.front = cls.front
        return pl.CostEstimate(flops=int(cls.cost * 10**8), bytes_accessed=1024, transcendentals=0)


def kernel(body, outs, scalars, arrays, scratch=(), limit=12, streamed=()):
    arrays = list(arrays)
    if Order.last is not None:
        arrays[0] = after(arrays[0], Order.last)
    spaces = [pltpu.VMEM] * len(arrays) + [pltpu.HBM] * len(streamed)
    arrays += [pltpu.with_memory_space_constraint(v, pltpu.HBM) for v in streamed]
    found = pl.pallas_call(
        body,
        out_shape=outs,
        in_specs=[pl.BlockSpec(memory_space=pltpu.SMEM)] * len(scalars)
        + [pl.BlockSpec(memory_space=space) for space in spaces],
        out_specs=jax.tree.map(lambda _: pl.BlockSpec(memory_space=pltpu.VMEM), outs),
        scratch_shapes=list(scratch),
        compiler_params=pltpu.CompilerParams(vmem_limit_bytes=limit * 1024 * 1024),
        cost_estimate=Order.estimate(),
    )(*scalars, *arrays)
    Order.last = jax.tree.leaves(found)[0]
    return found


def after(value, *others):
    return lax.optimization_barrier((value, others))[0]


def dot(left, right, left_dim, right_dim):
    return lax.dot_general(left, right, (((left_dim,), (right_dim,)), ((), ())), preferred_element_type=F32)


def rows_at(i):
    return pl.ds(pl.multiple_of(i * STEP, STEP), STEP)


def each_rows(count, body, start=None, first=0):
    return lax.fori_loop(first // STEP, count // STEP, body, start, unroll=4)


def column_sum(value):
    return jnp.sum(value, axis=0, keepdims=True)


def xor_send(value, axis, size, offset):
    return lax.ppermute(value, axis, [(i, i ^ offset) for i in range(size)])


def add_kernel(count, cuts, *refs):
    parts, outs = refs[:count], refs[count:]

    def one(rows):
        found = parts[0][rows, :].astype(F32)
        for part in parts[1:]:
            found = found + part[rows, :].astype(F32)
        return found

    for (first, last), out in zip(cuts, outs):
        if (last - first) % STEP:
            out[...] = one(slice(first, last)).astype(out.dtype)
        else:

            def body(i, _, first=first, out=out):
                out[rows_at(i), :] = one(pl.ds(pl.multiple_of(first + i * STEP, STEP), STEP)).astype(out.dtype)

            each_rows(last - first, body)


def add(parts, *cuts):
    columns = parts[0].shape[1]
    outs = tuple(shape(last - first, columns, kind=kind) for first, last, kind in cuts)
    return list(kernel(functools.partial(add_kernel, len(parts), [cut[:2] for cut in cuts]), outs, [], parts))


def sum_small(value, axis, size):
    stride = 1
    while stride < size:
        value = add([value, xor_send(value, axis, size, stride)], (0, value.shape[0], F32))[0]
        stride *= 2
    return value


def join_kernel(*refs):
    out, start = refs[-1], 0
    for piece in refs[:-1]:
        out[start : start + piece.shape[0]] = piece[...]
        start += piece.shape[0]


def join(pieces):
    rows = sum(piece.shape[0] for piece in pieces)
    return kernel(join_kernel, shape(rows, pieces[0].shape[1], kind=pieces[0].dtype), [], pieces)


def chunks_of(count, rows):
    count = min(count, 8)
    while rows % (16 * count):
        count //= 2
    return count


def digits_of(count, kind):
    if kind == "halving":
        strides = []
        stride = 1
        while stride < count:
            strides.append((stride, 2))
            stride *= 2
        return strides
    strides = digits_of(count, "halving")
    return [strides[1], strides[0]] + strides[2:]


def offsets_of(digits):
    found = [0]
    for stride, radix in digits:
        found = [low + e * stride for low in found for e in range(radix)]
    return found


class Stream:
    def __init__(self, row_devices, first, rows, kind):
        self.first, self.rows = first, rows
        self.count = chunks_of(row_devices, rows)
        self.row_devices = row_devices
        self.digits = digits_of(self.count, kind)
        self.chunk = rows // self.count

    def parts(self):
        stride, radix = self.digits[0]
        rest = offsets_of(self.digits[1:])
        return [[e * stride + low for low in rest] for e in range(radix)]

    def send(self, value, offset):
        return xor_send(value, "rows", self.row_devices, offset)


def weight_gradient_kernel(streams, pairs, me_ref, *refs):
    operands, outs, scratch = refs[: 2 * pairs], list(refs[2 * pairs : -1]), refs[-1]
    start = 0
    for i in range(pairs):
        left, right = operands[2 * i], operands[2 * i + 1]
        count = left.shape[0]
        scratch[start : start + count] = dot(left[...], right[...], 1, 1).astype(BF16)
        start += count
    for stream in streams:
        for offsets in stream.parts():
            out = outs.pop(0)
            for place, offset in enumerate(offsets):
                chunk = (me_ref[0] % stream.count) ^ offset
                at = pl.multiple_of(stream.first + chunk * stream.chunk, 16)
                out[place * stream.chunk : (place + 1) * stream.chunk] = scratch[pl.ds(at, stream.chunk), :]


def weight_gradient(me, streams, *operands):
    pairs = len(operands) // 2
    total = sum(operands[2 * i].shape[0] for i in range(pairs))
    columns = operands[1].shape[0]
    outs = tuple(
        shape(len(offsets) * stream.chunk, columns, kind=BF16) for stream in streams for offsets in stream.parts()
    )
    found = list(
        kernel(
            functools.partial(weight_gradient_kernel, streams, pairs),
            outs,
            [me],
            operands,
            [pltpu.VMEM((total, columns), BF16)],
        )
    )
    return [[found.pop(0) for _ in stream.parts()] for stream in streams]


def start_stage(stream, parts, stage):
    stride, radix = stream.digits[stage]
    return [stream.send(parts[e], e * stride) for e in range(1, radix)]


def add_stage(stream, parts, received, stage):
    rows = parts[0].shape[0]
    radix = 1 if stage + 1 == len(stream.digits) else stream.digits[stage + 1][1]
    size = rows // radix
    return add([parts[0]] + received, *((e * size, (e + 1) * size, BF16) for e in range(radix)))


def sum_rest(stream, value):
    stride = stream.count
    while stride < stream.row_devices:
        value = add([value, stream.send(value, stride)], (0, value.shape[0], BF16))[0]
        stride *= 2
    return value


def gather_stage(stream, value, stage):
    stride, radix = stream.digits[stage]
    return [value] + [stream.send(value, e * stride) for e in range(1, radix)]


def place_kernel(all_tokens, streams, bounds, me_ref, sums, *refs):
    outs, found, sems = refs[-len(bounds) - 2 : -2], refs[-2], refs[-1]
    pieces = list(refs[: -len(bounds) - 2])
    scale = loss_scale(all_tokens, sums, found.shape[1])
    copies, start = [], 0
    for stream in streams:
        for offsets in stream.parts():
            piece, size = pieces.pop(0), stream.chunk
            for place, offset in enumerate(offsets):
                row = stream.first + ((me_ref[0] % stream.count) ^ offset) * size
                here = slice(start, start + size)
                found[here] = piece[place * size : (place + 1) * size].astype(F32) * scale
                for (first, last), out in zip(bounds, outs):
                    at = pl.ds(pl.multiple_of(jnp.clip(row - first, 0, last - first - size), 16), size)
                    copy = pltpu.make_async_copy(found.at[here], out.at[at, :], sems.at[len(copies)])
                    inside = None if len(bounds) == 1 else (row >= first) & (row < last)
                    copies.append((copy, inside))
                    copy.start() if inside is None else pl.when(inside)(copy.start)
                start += size
    for copy, inside in copies:
        copy.wait() if inside is None else pl.when(inside)(copy.wait)


def place(all_tokens, me, sums, streams, pieces, sizes):
    columns = pieces[0].shape[1]
    bounds, start = [], 0
    for size in sizes:
        bounds.append((start, start + size))
        start += size
    count = len(sizes) * sum(stream.count for stream in streams)
    vmem, hbm = pl.BlockSpec(memory_space=pltpu.VMEM), pl.BlockSpec(memory_space=pltpu.HBM)
    found = pl.pallas_call(
        functools.partial(place_kernel, all_tokens, streams, bounds),
        out_shape=tuple(shape(size, columns) for size in sizes),
        in_specs=[pl.BlockSpec(memory_space=pltpu.SMEM)] + [vmem] * (1 + len(pieces)),
        out_specs=(hbm,) * len(sizes),
        scratch_shapes=[pltpu.VMEM((start, columns), F32), pltpu.SemaphoreType.DMA((count,))],
        compiler_params=pltpu.CompilerParams(vmem_limit_bytes=12 * 1024 * 1024),
        cost_estimate=Order.estimate(),
    )(me, after(sums, Order.last), *pieces)
    Order.last = found[0]
    return found


def live_row(counts_ref, width, first):
    place = lax.broadcasted_iota(jnp.int32, (1, width), 1) + first
    return jnp.where(place < counts_ref[0], 1.0, 0.0)


def loss_scale(all_tokens, sums, width):
    return jnp.full((1, width), all_tokens, F32) / jnp.broadcast_to(sums[7:8, 0:1], (1, width))


def history_kernel(block, mix_ref, counts_ref, cot_ref, history_ref, running_ref, d_mix_ref):
    layers, features, tokens = history_ref.shape
    live = live_row(counts_ref, tokens, 0)
    d_mix_ref[...] = jnp.zeros_like(d_mix_ref)

    def body(history_part):
        for i in range(block // STEP):
            rows = slice(i * STEP, (i + 1) * STEP)
            own = pl.ds(pl.multiple_of(pl.program_id(0) * block + i * STEP, STEP), STEP)
            grad = cot_ref[own].astype(F32) * live
            running = jnp.zeros_like(grad)
            for j in range(layers):
                layer = history_part[j, rows].astype(F32)
                running = running + mix_ref[j] * layer
                terms = grad * layer
                terms = terms[: STEP // 2] + terms[STEP // 2 :]
                d_mix_ref[j] += sum(terms[:, k : k + 128] for k in range(0, tokens, 128))
            running_ref[own] = running

    whole = pl.BlockSpec((layers, block, tokens), lambda i: (0, i, 0))
    pltpu.emit_pipeline(body, grid=(features // block,), in_specs=[whole])(history_ref)


def d_history_kernel(all_tokens, block, mix_ref, counts_ref, cot_ref, sums, d_history_ref):
    layers, features, tokens = d_history_ref.shape
    factor = live_row(counts_ref, tokens, 0) * loss_scale(all_tokens, sums, tokens)

    def body(part):
        for i in range(block // STEP):
            rows = slice(i * STEP, (i + 1) * STEP)
            own = pl.ds(pl.multiple_of(pl.program_id(0) * block + i * STEP, STEP), STEP)
            grad = cot_ref[own].astype(F32) * factor
            for j in range(layers):
                part[j, rows] = (mix_ref[j] * grad).astype(BF16)

    whole = pl.BlockSpec((layers, block, tokens), lambda i: (0, i, 0))
    pltpu.emit_pipeline(body, grid=(features // block,), out_specs=[whole])(d_history_ref)


def history_call(body, outs, in_hbm, out_hbm, scalars, arrays):
    vmem, hbm = pl.BlockSpec(memory_space=pltpu.VMEM), pl.BlockSpec(memory_space=pltpu.HBM)
    arrays = [after(arrays[0], Order.last), *arrays[1:]]
    found = pl.pallas_call(
        body,
        out_shape=outs,
        in_specs=[pl.BlockSpec(memory_space=pltpu.SMEM)] * len(scalars) + [hbm if h else vmem for h in in_hbm],
        out_specs=tuple(hbm if h else vmem for h in out_hbm),
        compiler_params=pltpu.CompilerParams(vmem_limit_bytes=12 * 1024 * 1024),
        cost_estimate=Order.estimate(),
    )(*scalars, *arrays)
    Order.last = found[0]
    return found


def spread_of(load, count, width, total=None):
    zero = jnp.zeros((STEP, width), F32)
    if total is None:
        total = each_rows(count, lambda i, acc: acc + load(i), zero)
    mean = column_sum(total) / count

    def squares(i, acc):
        centred = load(i) - mean
        return acc + centred * centred

    return mean, lax.rsqrt(column_sum(each_rows(count, squares, zero)) / count + EPSILON)


def prepare_kernel(held, *refs):
    refs = refs[held:]
    sources, x_in, (own, norms, cosine, sine), places, sem = refs[:6], refs[6], refs[7:11], refs[11:17], refs[17]
    copies = [pltpu.make_async_copy(*pair, sem.at[i]) for i, pair in enumerate(zip(sources, places))]
    whole = pltpu.make_async_copy(x_in, own, sem.at[6])
    for copy in [*copies, whole]:
        copy.start()
    norms[...] = jnp.zeros_like(norms)
    for copy in copies:
        copy.wait()
    positions, rates, *vectors = places
    for i, ref in enumerate(vectors):
        norms[i : i + 1, : ref.shape[1]] = ref[...]
    angles = positions[...].astype(F32) * rates[...]
    cosine[...] = jnp.cos(angles)
    sine[...] = jnp.sin(angles)
    whole.wait()


def prepare(held, x_in, *sources):
    tokens, part = sources[0].shape[1], sources[2].shape[1]
    rates = sources[1].shape[0]
    vmem = pl.BlockSpec(memory_space=pltpu.VMEM)
    found = pl.pallas_call(
        functools.partial(prepare_kernel, len(held)),
        out_shape=(
            shape(part, tokens, kind=BF16),
            shape(8, -(-part // 128) * 128),
            shape(rates, tokens),
            shape(rates, tokens),
        ),
        in_specs=[vmem] * len(held) + [pl.BlockSpec(memory_space=pltpu.HBM)] * (len(sources) + 1),
        out_specs=(vmem,) * 4,
        scratch_shapes=[pltpu.VMEM(v.shape, v.dtype) for v in sources] + [pltpu.SemaphoreType.DMA((len(sources) + 1,))],
        compiler_params=pltpu.CompilerParams(vmem_limit_bytes=4 * 1024 * 1024),
        cost_estimate=Order.estimate(),
    )(*held, *(pltpu.with_memory_space_constraint(v, pltpu.HBM) for v in (*sources, x_in)))
    Order.last = found[0]
    return found


def norms_kernel(at_ref, n01, n23, norms):
    part = norms.shape[0] // 4
    near, far = n01[...].T, n23[...].T
    for e, norm in enumerate((near, near, far, far)):
        rows = pl.ds(pl.multiple_of((at_ref[0] ^ e) * part, 64), part)
        norms[rows, :] = norm[:part, 8 * (e % 2) : 8 * (e % 2) + 8]


def project_kernel(
    at_ref, x0, x1, x2, x3, norms, cosine, sine, w_qkv, x_all, normed, stats, qkv, project
):
    at = at_ref[0]
    part, tokens = x0.shape
    model = w_qkv.shape[1]
    for e, piece in enumerate((x0, x1, x2, x3)):
        x_all[pl.ds(pl.multiple_of((at ^ e) * part, 64), part), :] = piece[...]
    mean, scale = spread_of(lambda i: x_all[rows_at(i), :].astype(F32), model, tokens)
    stats[0:1] = mean
    stats[1:2] = scale

    def normalise(i, _):
        rows = rows_at(i)
        xhat = (x_all[rows, :].astype(F32) - mean) * scale
        normed[rows, :] = (xhat * norms[rows, 0:1] + norms[rows, 1:2]).astype(BF16)

    each_rows(model, normalise)
    project[...] = dot(w_qkv[...], normed[...], 1, 0)
    width = HEAD_DIM // 2
    for block, factor in ((0, HEAD_DIM ** (-0.5)), (1, 1.0)):
        for start in range(block * part, (block + 1) * part, HEAD_DIM):
            front, back = project[start : start + width], project[start + width : start + HEAD_DIM]
            cos, sin = cosine[...] * factor, sine[...] * factor
            qkv[start : start + width] = (front * cos - back * sin).astype(BF16)
            qkv[start + width : start + HEAD_DIM] = (back * cos + front * sin).astype(BF16)
    qkv[2 * part :] = project[2 * part :].astype(BF16)


def attention_kernel(
    at_ref, qkv, x_all, heads_send, heads_own, x_half, heads_out, probs, scores
):
    at = at_ref[0]
    part, tokens = heads_out.shape
    half = tokens // 2
    for h in range(part // HEAD_DIM):
        head = slice(h * HEAD_DIM, (h + 1) * HEAD_DIM)
        for t in range(2):
            now = slice(t * half, (t + 1) * half)
            count = (t + 1) * half
            query = qkv[head, now]
            key = qkv[part + h * HEAD_DIM : part + (h + 1) * HEAD_DIM, :count]
            value = qkv[2 * part + h * HEAD_DIM : 2 * part + (h + 1) * HEAD_DIM, :count]
            scores[:count] = dot(key, query, 0, 0)

            def masked(i):
                behind = lax.broadcasted_iota(jnp.int32, (STEP, half), 0) + (i * STEP - t * half)
                ahead = lax.broadcasted_iota(jnp.int32, (STEP, half), 1)
                return jnp.where(behind <= ahead, scores[rows_at(i), :], -1e30)

            def raised(found, i, acc):
                found = jnp.exp(found - top)
                scores[rows_at(i), :] = found
                return acc + found

            def settle(i, _):
                rows = rows_at(i)
                probs[h, rows, now] = (scores[rows, :] * divisor).astype(BF16)

            top = each_rows(
                t * half, lambda i, acc: jnp.maximum(acc, scores[rows_at(i), :]), jnp.full((STEP, half), -1e30, F32)
            )
            top = each_rows(count, lambda i, acc: jnp.maximum(acc, masked(i)), top, first=t * half)
            top = jnp.max(top, axis=0, keepdims=True)
            total = each_rows(
                t * half, lambda i, acc: raised(scores[rows_at(i), :], i, acc), jnp.zeros((STEP, half), F32)
            )
            total = each_rows(count, lambda i, acc: raised(masked(i), i, acc), total, first=t * half)
            divisor = 1.0 / column_sum(total)
            each_rows(count, settle)
            heads_out[head, now] = dot(value, probs[h, :count, now], 1, 0).astype(BF16)
    own = pl.multiple_of((at % 2) * half, half)
    other = pl.multiple_of((1 - at % 2) * half, half)
    heads_send[...] = heads_out[:, pl.ds(other, half)]
    heads_own[...] = heads_out[:, pl.ds(own, half)]
    x_half[...] = x_all[:, pl.ds(own, half)]


def output_gradient_kernel(
    at_ref, self_ref, counts_ref, c0, c1, c2, c3, w_down, g_out, d_active, cot_all
):
    at = at_ref[0]
    part, tokens = c0.shape
    half = tokens // 2
    for e, piece in enumerate((c0, c1, c2, c3)):
        cot_all[pl.ds(pl.multiple_of((at ^ e) * part, 64), part), :] = piece[...]
    for place, side in enumerate((at % 2, 1 - at % 2)):
        now = pl.ds(pl.multiple_of(side * half, half), half)
        factor = live_row(counts_ref, half, side * half)

        def scale(i, _, now=now, factor=factor, place=place):
            rows = rows_at(i)
            grad = cot_all[rows, now].astype(F32) * factor
            g_out[rows, place * half : (place + 1) * half] = (self_ref[0] * grad).astype(BF16)

        each_rows(cot_all.shape[0], scale)
    d_active[...] = dot(w_down[...], g_out[...], 1, 0)


def rows_kernel(at_ref, *refs):
    out = refs[-1]
    for e, piece in enumerate(refs[:-1]):
        rows = piece.shape[0]
        out[pl.ds(pl.multiple_of((at_ref[0] ^ e) * rows, 64), rows), :] = piece[...]


def middle_kernel(at_ref, pair, pair_far, w_all, x_half, norms, middle, stats, normed, heads):
    model, half = x_half.shape
    part = pair.shape[0] // 2
    for e, piece in enumerate((pair[:part], pair[part:], pair_far[:part], pair_far[part:])):
        heads[pl.ds(pl.multiple_of((at_ref[0] ^ e) * part, 64), part), :] = piece
    middle[...] = dot(w_all[...], heads[...], 0, 0)

    def add(i, acc):
        rows = rows_at(i)
        found = x_half[rows, :].astype(F32) + middle[rows, :]
        middle[rows, :] = found
        return acc + found

    total = each_rows(model, add, jnp.zeros((STEP, half), F32))
    mean, scale = spread_of(lambda i: middle[rows_at(i), :], model, half, total)
    stats[0:1] = mean
    stats[1:2] = scale

    def normalise(i, _):
        rows = rows_at(i)
        xhat = (middle[rows, :] - mean) * scale
        normed[rows, :] = (xhat * norms[rows, 2:3] + norms[rows, 3:4]).astype(BF16)

    each_rows(model, normalise)


def feed_forward_kernel(own, other, w_up, d_active, normed, active, d_hidden, send, keep, hidden):
    half = own.shape[1]
    normed[:, :half] = own[...]
    normed[:, half:] = other[...]
    hidden[...] = dot(w_up[...], normed[...], 0, 0)

    def bend(i, _):
        rows = rows_at(i)
        u = hidden[rows, :]
        squared = u * u
        curve = jnp.tanh(0.7978845608028654 * u * (1.0 + 0.044715 * squared))
        lifted = 0.5 * (1.0 + curve)
        active[rows, :] = (u * lifted).astype(BF16)
        slope = lifted + u * (0.5 * (1.0 - curve * curve)) * (
            0.7978845608028654 + (3 * 0.044715 * 0.7978845608028654) * squared
        )
        d_hidden[rows, :] = (slope * d_active[rows, :]).astype(BF16)

    each_rows(hidden.shape[0], bend)
    send[...] = dot(w_up[...], d_hidden[:, half:], 1, 0).astype(BF16)
    keep[...] = dot(w_up[...], d_hidden[:, :half], 1, 0)


def store_blocks(at, total, part, near, *outs):
    for e, out in zip(near, outs):
        out[...] = total[pl.ds(pl.multiple_of((at ^ e) * part, 64), part), :].astype(out.dtype)


def output_kernel(at_ref, counts_ref, active, w_down, middle, cot_all, send, send_far, keep, keep_far, product, total):
    at = at_ref[0]
    model, half = middle.shape
    part = send.shape[0]
    own = pl.ds(pl.multiple_of((at % 2) * half, half), half)
    other = pl.ds(pl.multiple_of((1 - at % 2) * half, half), half)
    total[:, own] = dot(w_down[...], active[:, :half], 0, 0) + 0.5 * middle[...]
    total[:, other] = dot(w_down[...], active[:, half:], 0, 0)
    live = live_row(counts_ref, 2 * half, 0)

    def weigh(i, acc):
        rows = rows_at(i)
        return acc + fold_lanes(total[rows, :] * (cot_all[rows, :].astype(F32) * live))

    product[...] = each_rows(model, weigh, jnp.zeros((STEP, 128), F32))
    store_blocks(at, total, part, (1, 3, 0, 2), send, send_far, keep, keep_far)


def fold_lanes(value):
    return sum(value[:, k : k + 128] for k in range(0, value.shape[1], 128))


def as_row(columns):
    return column_sum(columns[...].T)


def middle_gradient_kernel(
    at_ref, self_ref, counts_ref, chip, received, middle, stats, cot_all, norms,
    d_middle, g_mid, gains, d_normed, gain_sums, bias_sums,
):
    model, half = chip.shape
    mean, scale = stats[0:1], stats[1:2]
    zero = jnp.zeros((STEP, half), F32)

    def sums(i, acc):
        rows = rows_at(i)
        grad = chip[rows, :] + received[rows, :].astype(F32)
        d_normed[rows, :] = grad
        xhat = (middle[rows, :] - mean) * scale
        both = grad * xhat
        gain_sums[rows, :] = fold_lanes(both)
        bias_sums[rows, :] = fold_lanes(grad)
        gain = norms[rows, 2:3]
        return acc[0] + grad * gain, acc[1] + both * gain

    first, second = (column_sum(v) / model for v in each_rows(model, sums, (zero, zero)))
    side = (at_ref[0] % 2) * half
    factor = self_ref[0] * live_row(counts_ref, half, side)
    own = pl.ds(pl.multiple_of(side, half), half)

    def finish(i, _):
        rows = rows_at(i)
        xhat = (middle[rows, :] - mean) * scale
        found = cot_all[rows, own].astype(F32) * factor + scale * (
            d_normed[rows, :] * norms[rows, 2:3] - first - xhat * second
        )
        d_middle[rows, :] = found
        g_mid[rows, :] = found.astype(BF16)

    each_rows(model, finish)
    gains[0:1] = as_row(gain_sums)
    gains[1:2] = as_row(bias_sums)


def attention_gradient_kernel(
    at_ref, own, other, w_out, qkv, probs, cosine, sine,
    d_project, g_mid, d_heads, d_scores, products, d_queries, d_keys, d_values,
):
    at = at_ref[0]
    half = own.shape[1]
    part = w_out.shape[0]
    g_mid[:, pl.ds(pl.multiple_of((at % 2) * half, half), half)] = own[...]
    g_mid[:, pl.ds(pl.multiple_of((1 - at % 2) * half, half), half)] = other[...]
    d_heads[...] = dot(w_out[...], g_mid[...], 1, 0).astype(BF16)
    width = HEAD_DIM // 2
    for h in range(part // HEAD_DIM):
        head = slice(h * HEAD_DIM, (h + 1) * HEAD_DIM)
        query = qkv[head]
        key = qkv[part + h * HEAD_DIM : part + (h + 1) * HEAD_DIM]
        value = qkv[2 * part + h * HEAD_DIM : 2 * part + (h + 1) * HEAD_DIM]
        for t in range(2):
            now = slice(t * half, (t + 1) * half)
            count = (t + 1) * half
            products[:count] = dot(value[:, :count], d_heads[head, now], 0, 0)

            def weigh(i, acc):
                rows = rows_at(i)
                return acc + products[rows, :] * probs[h, rows, now].astype(F32)

            inner = column_sum(each_rows(count, weigh, jnp.zeros((STEP, half), F32)))

            def settle(i, _):
                rows = rows_at(i)
                d_scores[rows, :] = (probs[h, rows, now].astype(F32) * (products[rows, :] - inner)).astype(BF16)

            each_rows(count, settle)
            d_queries[:, now] = dot(key[:, :count], d_scores[:count], 1, 0) * HEAD_DIM ** (-0.5)
            d_key = dot(query[:, now], d_scores[:count], 1, 1)
            d_value = dot(d_heads[head, now], probs[h, :count, now], 1, 1)
            if t == 0:
                d_keys[:, :half] = d_key
                d_values[:, :half] = d_value
            else:
                d_keys[:, :half] += d_key[:, :half]
                d_values[:, :half] += d_value[:, :half]
                d_keys[:, half:] = d_key[:, half:]
                d_values[:, half:] = d_value[:, half:]
        for block, found in ((0, d_queries), (1, d_keys)):
            start = block * part + h * HEAD_DIM
            front, back = found[:width], found[width:]
            d_project[start : start + width] = (front * cosine[...] + back * sine[...]).astype(BF16)
            d_project[start + width : start + HEAD_DIM] = (back * cosine[...] - front * sine[...]).astype(BF16)
        d_project[2 * part + h * HEAD_DIM : 2 * part + (h + 1) * HEAD_DIM] = d_values[...].astype(BF16)


def input_gradient_kernel(
    width, at_ref, counts_ref, d_project, w_qkv, x_all, stats, d_middle, norms, gains,
    send, send_far, keep, keep_far, sums, total, gain_sums, bias_sums,
):
    at = at_ref[0]
    model, half = d_middle.shape
    tokens = x_all.shape[1]
    part = send.shape[0]
    total[...] = dot(w_qkv[...], d_project[...], 0, 0)
    mean, scale = stats[0:1], stats[1:2]
    zero = jnp.zeros((STEP, tokens), F32)
    own = pl.ds(pl.multiple_of((at % 2) * half, half), half)

    def body(i, acc):
        rows = rows_at(i)
        grad = total[rows, :]
        xhat = (x_all[rows, :].astype(F32) - mean) * scale
        both = grad * xhat
        gain_sums[rows, :] = fold_lanes(both)
        bias_sums[rows, :] = fold_lanes(grad)
        gain = norms[rows, 0:1]
        lifted = grad * gain
        total[rows, :] = lifted * scale
        total[rows, own] += 0.5 * d_middle[rows, :]
        return acc[0] + lifted, acc[1] + both * gain

    first, second = each_rows(model, body, (zero, zero))
    store_blocks(at, total, part, (1, 3, 0, 2), send, send_far, keep, keep_far)
    sums[...] = jnp.zeros_like(sums)
    sums[0:1] = as_row(gain_sums)
    sums[1:2] = as_row(bias_sums)
    sums[2:4] = 0.5 * gains[...]
    sums[4:5, :tokens] = column_sum(first) / model
    sums[5:6, :tokens] = column_sum(second) / model
    sums[7:8] = jnp.zeros((1, model), F32) + counts_ref[0].astype(F32) / width


def mixed_kernel(self_ref, own, near, far, running, d_mix, product, sums, mixed, all_sums, table):
    layers = d_mix.shape[0]

    def body(i, _):
        rows = rows_at(i)
        output = own[rows, :] + near[rows, :].astype(F32) + far[rows, :].astype(F32)
        mixed[rows, :] = (self_ref[0] * output + running[rows, :]).astype(BF16)

    each_rows(own.shape[0], body)
    table[...] = jnp.zeros_like(table)
    table[:layers] = jnp.sum(d_mix[...], axis=1)
    table[layers : layers + 1] = column_sum(product[...])
    all_sums[...] = sums[...]
    all_sums[6:7, :128] = as_row(table)


def ends_kernel(all_tokens, layers, width, at_ref, sums, d_mix, d_self, *ends):
    part = ends[0].shape[1]
    scale = loss_scale(all_tokens, sums, sums.shape[1])
    d_mix[...] = sums[6:7, :layers] * scale[:, :layers]
    d_self[...] = sums[6:7, layers : layers + 1] * scale[:, :1]
    for i, end in enumerate(ends):
        scaled = sums[i : i + 1] * scale
        found = scaled[:, :part]
        for w in range(1, width):
            found = jnp.where(at_ref[0] == w, scaled[:, w * part : (w + 1) * part], found)
        end[...] = found


def d_input_kernel(own, near, far, x_in, stats, row_sums, found):
    part, tokens = own.shape
    mean, scale = stats[0:1], stats[1:2]
    first, second = row_sums[4:5, :tokens], row_sums[5:6, :tokens]

    def body(i, _):
        rows = rows_at(i)
        xhat = (x_in[rows, :].astype(F32) - mean) * scale
        total = own[rows, :] + near[rows, :].astype(F32) + far[rows, :].astype(F32)
        found[rows, :] = total - scale * (first + xhat * second)

    each_rows(part, body)


def scale_kernel(all_tokens, found, sums, d_input):
    factor = loss_scale(all_tokens, sums, found.shape[1])

    def body(i, _):
        d_input[rows_at(i), :] = found[rows_at(i), :] * factor

    each_rows(found.shape[0], body)


def local(
    width,
    row_devices,
    x_in,
    history,
    cotangent,
    counts,
    positions,
    mix_weights,
    self_weight,
    first_norm_gain,
    first_norm_bias,
    w_qkv,
    w_out,
    second_norm_gain,
    second_norm_bias,
    w_up,
    w_down,
):
    part, tokens = x_in.shape
    model = w_out.shape[1]
    hidden_units = w_up.shape[1]
    half = tokens // 2
    layers = mix_weights.shape[0]
    all_tokens = float(tokens * row_devices)
    at = lax.axis_index("width").astype(jnp.int32)[None]
    me = lax.axis_index("rows").astype(jnp.int32)[None]
    Order.last, Order.front = None, FRONT
    to_width = lambda value, offset: xor_send(value, "width", width, offset)
    to_row = lambda value, offset: xor_send(value, "rows", row_devices, offset)
    w_qkv = w_qkv.reshape(3 * part, model)
    rates = 1.0 / 10000.0 ** (np.arange(HEAD_DIM // 2) * 2.0 / HEAD_DIM)
    x_in, cotangent, counts = after((x_in, cotangent, counts), at, me)

    x_far, x_near = to_width(x_in, 2), to_width(x_in, 1)
    x_own, norms, cosine, sine = prepare(
        [x_near],
        x_in,
        positions[None, :],
        jnp.asarray(rates[:, None], F32),
        *(v[None, :] for v in (first_norm_gain, first_norm_bias, second_norm_gain, second_norm_bias)),
    )
    norms_near = join([norms, to_width(norms, 1)])
    norms_far = to_width(norms_near, 2)
    norms = kernel(norms_kernel, shape(model, 8), [at], [norms_near, norms_far])
    x_both = to_width(after(x_far, norms), 1)
    cot_now, w_now = after((cotangent, w_out), norms_near)
    cot_far, cot_near = to_width(cot_now, 2), to_width(cot_now, 1)
    w_far, w_near = to_width(w_now, 2), to_width(w_now, 1)

    x_all, normed_one, stats_one, qkv = kernel(
        project_kernel,
        (
            shape(model, tokens, kind=BF16),
            shape(model, tokens, kind=BF16),
            shape(2, tokens),
            shape(3 * part, tokens, kind=BF16),
        ),
        [at],
        [x_own, x_near, x_far, x_both, norms, cosine, sine, w_qkv],
        [pltpu.VMEM((3 * part, tokens), F32)],
    )
    heads_send, heads_own, x_half, heads_out, probs = kernel(
        attention_kernel,
        (
            shape(part, half, kind=BF16),
            shape(part, half, kind=BF16),
            shape(model, half, kind=BF16),
            shape(part, tokens, kind=BF16),
            shape(part // HEAD_DIM, tokens, tokens, kind=BF16),
        ),
        [at],
        [qkv, x_all],
        [pltpu.VMEM((tokens, half), F32)],
    )
    pair = join([after(heads_own, cot_far, w_far), to_width(heads_send, 1)])
    pair_far = to_width(pair, 2)
    cot_both = to_width(after(cot_far, pair), 1)
    w_both = to_width(after(w_far, pair), 1)

    running, d_mix = history_call(
        functools.partial(history_kernel, 32),
        (shape(part, tokens), shape(layers, STEP // 2, 128)),
        (False, True),
        (False, False),
        [mix_weights, counts],
        [cotangent, pltpu.with_memory_space_constraint(history, pltpu.HBM)],
    )
    g_out, d_active, cot_all = kernel(
        output_gradient_kernel,
        (shape(model, tokens, kind=BF16), shape(hidden_units, tokens), shape(model, tokens, kind=BF16)),
        [at, self_weight, counts],
        [cotangent, cot_near, cot_far, cot_both, w_down],
    )

    w_all = kernel(rows_kernel, shape(model, model, kind=BF16), [at], [w_out, w_near, w_far, w_both])
    middle, stats_two, normed_own = kernel(
        middle_kernel,
        (shape(model, half), shape(2, half), shape(model, half, kind=BF16)),
        [at],
        [pair, pair_far, w_all, x_half, norms],
        [pltpu.VMEM((model, half), BF16)],
    )
    normed_two, active, d_hidden, send, keep = kernel(
        feed_forward_kernel,
        (
            shape(model, tokens, kind=BF16),
            shape(hidden_units, tokens, kind=BF16),
            shape(hidden_units, tokens, kind=BF16),
            shape(model, half, kind=BF16),
            shape(model, half),
        ),
        [],
        [normed_own, to_width(normed_own, 1), w_up, d_active],
        [pltpu.VMEM((hidden_units, tokens), F32)],
    )

    v = Values()
    v.send, v.keep = send, keep
    down = Stream(row_devices, 0, hidden_units, "halving")
    up = Stream(row_devices, 0, model, "crossed")
    first = Stream(row_devices, 0, 2 * part, "halving")
    second = Stream(row_devices, 2 * part, 2 * part, "crossed")
    strides = [1 << i for i in range(row_devices.bit_length() - 1)]
    blocks = (shape(part, tokens, kind=BF16),) * 2 + (shape(part, tokens),) * 2
    last = len(down.digits) - 1

    def scatter(stream, stage):
        stream.held = add_stage(stream, stream.held, stream.got, stage)
        stream.got = start_stage(stream, stream.held, stage + 1)

    def turn(stream):
        value = sum_rest(stream, add_stage(stream, stream.held, stream.got, last)[0])
        stream.pieces = gather_stage(stream, value, last)

    def gather(stream, stage):
        stream.pieces = gather_stage(stream, join(stream.pieces), stage)

    def steps_of(stream):
        return (
            *(functools.partial(scatter, stream, stage) for stage in range(last)),
            functools.partial(turn, stream),
            *(functools.partial(gather, stream, stage) for stage in range(last - 1, -1, -1)),
        )

    def begin(streams, found):
        for stream, parts in zip(streams, found):
            stream.held, stream.got = parts, start_stage(stream, parts, 0)

    def down_product():
        begin([down], weight_gradient(me, [down], active, g_out))

    def up_product():
        begin([up], weight_gradient(me, [up], normed_two, d_hidden))

    def tail_product():
        found = weight_gradient(me, [first, second], v.d_project, normed_one, heads_out, v.g_mid)
        begin([first, second], found)

    def middle_sum():
        v.chip, sent = add([v.keep, to_width(v.send, 1)], (0, model, F32), (0, model, BF16))
        v.received = to_width(sent, 2)

    def output_product():
        near, far, v.out, v.out_far, v.product = kernel(
            output_kernel,
            blocks + (shape(STEP, 128),),
            [at, counts],
            [active, w_down, middle, cot_all],
            [pltpu.VMEM((model, tokens), F32)],
        )
        v.out_got = to_width(near, 1), to_width(far, 1)

    def output_sum():
        v.out_last = to_width(add([v.out_far, v.out_got[1]], (0, part, BF16))[0], 2)

    def middle_gradient():
        v.d_middle, v.g_own, v.gains = kernel(
            middle_gradient_kernel,
            (shape(model, half), shape(model, half, kind=BF16), shape(2, model)),
            [at, self_weight, counts],
            [v.chip, v.received, middle, stats_two, cot_all, norms],
            [pltpu.VMEM((model, half), F32), pltpu.VMEM((model, 128), F32), pltpu.VMEM((model, 128), F32)],
        )
        v.g_other = to_width(v.g_own, 1)

    def attention_gradient():
        v.d_project, v.g_mid = kernel(
            attention_gradient_kernel,
            (shape(3 * part, tokens, kind=BF16), shape(model, tokens, kind=BF16)),
            [at],
            [v.g_own, v.g_other, w_out, qkv, probs, cosine, sine],
            [
                pltpu.VMEM((part, tokens), BF16),
                pltpu.VMEM((tokens, half), BF16),
                pltpu.VMEM((tokens, half), F32),
                pltpu.VMEM((HEAD_DIM, tokens), F32),
                pltpu.VMEM((HEAD_DIM, tokens), F32),
                pltpu.VMEM((HEAD_DIM, tokens), F32),
            ],
        )

    def input_gradient():
        near, far, v.own_in, v.in_far, v.sums = kernel(
            functools.partial(input_gradient_kernel, width),
            blocks + (shape(8, model),),
            [at, counts],
            [v.d_project, w_qkv, x_all, stats_one, v.d_middle, norms, v.gains],
            [pltpu.VMEM((model, tokens), F32), pltpu.VMEM((model, 128), F32), pltpu.VMEM((model, 128), F32)],
        )
        v.in_got = to_width(near, 1), to_width(far, 1)

    def input_sum():
        v.in_last = to_width(add([v.in_far, v.in_got[1]], (0, part, BF16))[0], 2)

    def input_total():
        v.in_total = kernel(
            d_input_kernel,
            shape(part, tokens),
            [],
            [v.own_in, v.in_got[0], v.in_last, x_own, stats_one, v.row_sums],
        )

    def mix():
        v.mixed, v.sums = kernel(
            mixed_kernel,
            (shape(part, tokens, kind=BF16), shape(8, model)),
            [self_weight],
            [
                v.out,
                v.out_got[0],
                v.out_last,
                running,
                d_mix,
                v.product,
                v.sums,
            ],
            [pltpu.VMEM((128, 128), F32)],
        )
        v.sums_got = to_width(v.sums, 1)

    def sums_step(*sends):
        for send_on in sends:
            v.sums = add([v.sums, v.sums_got], (0, 8, F32))[0]
            v.sums_got = send_on(v.sums)

    def sums_1():
        sums_step(lambda value: to_width(value, 2))

    def sums_2():
        sums_step(row_send(strides[0]))
        v.row_sums = v.sums

    def sums_3():
        sums_step(row_send(strides[1]))

    def sums_4():
        sums_step(*(row_send(stride) for stride in strides[2:]))

    def last_sums():
        v.sums = add([v.sums, v.sums_got], (0, 8, F32))[0]

    def scale_input():
        v.d_input = kernel(
            functools.partial(scale_kernel, all_tokens), shape(part, tokens), [], [v.in_total, v.sums]
        )

    def history_gradient():
        v.d_history = history_call(
            functools.partial(d_history_kernel, all_tokens, 32),
            (shape(*history.shape, kind=BF16),),
            (False, False),
            (True,),
            [mix_weights, counts],
            [cotangent, v.sums],
        )[0]

    def ends():
        v.ends = kernel(
            functools.partial(ends_kernel, all_tokens, layers, width),
            (shape(1, layers), shape(1, 1)) + (shape(1, part),) * 4,
            [at],
            [v.sums],
        )

    def placed(streams, *sizes):
        pieces = [piece for stream in streams for piece in stream.pieces]
        return place(all_tokens, me, v.sums, streams, pieces, sizes)

    def place_down():
        v.d_w_down = placed([down], hidden_units)[0]

    def place_up():
        v.d_w_up = placed([up], model)[0]

    def place_tail():
        v.d_w_qkv, v.d_w_out = placed([first, second], 3 * part, part)

    row_send = lambda stride: lambda value: to_row(value, stride)
    down_1, down_2, down_3, down_4, down_5 = steps_of(down)
    up_1, up_2, up_3, up_4, up_5 = steps_of(up)
    first_1, first_2, first_3, first_4, first_5 = steps_of(first)
    second_1, second_2, second_3, second_4, second_5 = steps_of(second)
    schedule = (
        (down_product, 10),
        (middle_sum, 8),
        (up_product, 10),
        (output_product, 100),
        (middle_gradient, 10),
        (output_sum, 10),
        (down_1, 10),
        (up_1, 100),
        (attention_gradient, 8),
        (tail_product, 4),
        (down_2, 100),
        (up_2, 0.3),
        (input_gradient, 1),
        (mix, 8),
        (first_1, 1),
        (second_1, 1),
        (up_3, 100),
        (down_3, 1),
        (first_2, 2),
        (sums_1, 4),
        (sums_2, 1),
        (input_sum, 1),
        (second_2, 1),
        (sums_3, 1),
        (up_4, 2),
        (sums_4, 1),
        (down_4, 4),
        (first_3, 40),
        (input_total, 1),
        (second_3, 2),
        (down_5, 1),
        (first_4, 200),
        (up_5, 0.3),
        (second_4, 16),
        (last_sums, 1),
        (scale_input, 0.1),
        (first_5, 40),
        (ends, 1),
        (history_gradient, 1),
        (place_down, 1),
        (second_5, 200),
        (place_up, 4),
        (place_tail, 1),
    )
    for step, weight in schedule:
        Order.cost = weight
        step()
    d_mix, d_self, *vectors = v.ends
    return (
        v.mixed,
        v.d_input,
        v.d_history,
        d_mix[0],
        d_self[0],
        vectors[0][0],
        vectors[1][0],
        v.d_w_qkv.reshape(3, part, model),
        v.d_w_out,
        vectors[2][0],
        vectors[3][0],
        v.d_w_up,
        v.d_w_down,
    )


def solution(mesh):
    return jax.shard_map(
        functools.partial(local, mesh.shape["width"], mesh.shape["rows"]),
        mesh=mesh,
        in_specs=(
            P("width", "rows"),
            P(None, "width", "rows"),
            P("width", "rows"),
            P("rows"),
            P("rows"),
            P(),
            P(),
            P("width"),
            P("width"),
            P(None, "width", None),
            P("width", None),
            P("width"),
            P("width"),
            P(None, "width"),
            P("width", None),
        ),
        out_specs=(
            P("width", "rows"),
            P("width", "rows"),
            P(None, "width", "rows"),
            P(),
            P(),
            P("width"),
            P("width"),
            P(None, "width", None),
            P("width", None),
            P("width"),
            P("width"),
            P(None, "width"),
            P("width", None),
        ),
        check_vma=False,
    )
```

```python
import functools

import jax
import jax.numpy as jnp
import numpy as np
from jax import lax
from jax.experimental import pallas as pl
from jax.experimental.pallas import tpu as pltpu
from jax.sharding import PartitionSpec as P

HEAD_DIM = 64
EPSILON = 1e-05
BF16 = jnp.bfloat16
F32 = jnp.float32
STEP = 16


SCHEDULE = (
    ("down", 10),
    ("chip", 8),
    ("up", 10),
    ("out", 100),
    ("middle", 10),
    ("out_sum", 10),
    ("down1", 10),
    ("up1", 100),
    ("attention", 8),
    ("tail", 4),
    ("down2", 100),
    ("up2", 0.3),
    ("input", 1),
    ("mix", 8),
    ("first1", 1),
    ("second1", 1),
    ("up3", 100),
    ("down3", 1),
    ("first2", 2),
    ("sums1", 4),
    ("sums2", 1),
    ("input_sum", 1),
    ("second2", 1),
    ("sums3", 1),
    ("up4", 2),
    ("sums4", 1),
    ("down4", 4),
    ("first3", 40),
    ("input_total", 1),
    ("second3", 2),
    ("down5", 1),
    ("first4", 200),
    ("up5", 0.3),
    ("second4", 16),
    ("sums5", 1),
    ("scale", 0.1),
    ("first5", 40),
    ("ends", 1),
    ("history", 1),
    ("place_down", 1),
    ("second5", 200),
    ("place_up", 4),
    ("place_tail", 1),
)

FRONT = (1, 1, 1, 1, 1, 1, 10, 10, 10, 10)


def shape(*dims, kind=F32):
    return jax.ShapeDtypeStruct(dims, kind)


class Values:
    pass


class Order:
    last = None
    cost = 0
    front = ()

    @classmethod
    def estimate(cls):
        if cls.front:
            cls.cost, *cls.front = cls.front
        return pl.CostEstimate(flops=int(cls.cost * 10**8), bytes_accessed=1024, transcendentals=0)


def kernel(body, outs, scalars, arrays, scratch=(), limit=12, streamed=()):
    arrays = list(arrays)
    if Order.last is not None:
        arrays[0] = after(arrays[0], Order.last)
    spaces = [pltpu.VMEM] * len(arrays) + [pltpu.HBM] * len(streamed)
    arrays += [pltpu.with_memory_space_constraint(v, pltpu.HBM) for v in streamed]
    found = pl.pallas_call(
        body,
        out_shape=outs,
        in_specs=[pl.BlockSpec(memory_space=pltpu.SMEM)] * len(scalars)
        + [pl.BlockSpec(memory_space=space) for space in spaces],
        out_specs=jax.tree.map(lambda _: pl.BlockSpec(memory_space=pltpu.VMEM), outs),
        scratch_shapes=list(scratch),
        compiler_params=pltpu.CompilerParams(vmem_limit_bytes=limit * 1024 * 1024),
        cost_estimate=Order.estimate(),
    )(*scalars, *arrays)
    Order.last = jax.tree.leaves(found)[0]
    return found


def after(value, *others):
    return lax.optimization_barrier((value, others))[0]


def dot(left, right, left_dim, right_dim):
    return lax.dot_general(left, right, (((left_dim,), (right_dim,)), ((), ())), preferred_element_type=F32)


def rows_at(i):
    return pl.ds(pl.multiple_of(i * STEP, STEP), STEP)


def each_rows(count, body, start=None, first=0):
    return lax.fori_loop(first // STEP, count // STEP, body, start, unroll=4)


def column_sum(value):
    return jnp.sum(value, axis=0, keepdims=True)


def xor_send(value, axis, size, offset):
    return lax.ppermute(value, axis, [(i, i ^ offset) for i in range(size)])


def add_kernel(count, cuts, *refs):
    parts, outs = refs[:count], refs[count:]

    def one(rows):
        found = parts[0][rows, :].astype(F32)
        for part in parts[1:]:
            found = found + part[rows, :].astype(F32)
        return found

    for (first, last), out in zip(cuts, outs):
        if (last - first) % STEP:
            out[...] = one(slice(first, last)).astype(out.dtype)
        else:

            def body(i, _, first=first, out=out):
                out[rows_at(i), :] = one(pl.ds(pl.multiple_of(first + i * STEP, STEP), STEP)).astype(out.dtype)

            each_rows(last - first, body)


def add(parts, *cuts):
    columns = parts[0].shape[1]
    outs = tuple(shape(last - first, columns, kind=kind) for first, last, kind in cuts)
    return list(kernel(functools.partial(add_kernel, len(parts), [cut[:2] for cut in cuts]), outs, [], parts))


def sum_small(value, axis, size):
    stride = 1
    while stride < size:
        value = add([value, xor_send(value, axis, size, stride)], (0, value.shape[0], F32))[0]
        stride *= 2
    return value


def join_kernel(*refs):
    out, start = refs[-1], 0
    for piece in refs[:-1]:
        out[start : start + piece.shape[0]] = piece[...]
        start += piece.shape[0]


def join(pieces):
    rows = sum(piece.shape[0] for piece in pieces)
    return kernel(join_kernel, shape(rows, pieces[0].shape[1], kind=pieces[0].dtype), [], pieces)


def chunks_of(count, rows):
    count = min(count, 8)
    while rows % (16 * count):
        count //= 2
    return count


def digits_of(count, kind):
    if kind == "halving":
        strides = []
        stride = 1
        while stride < count:
            strides.append((stride, 2))
            stride *= 2
        return strides
    strides = digits_of(count, "halving")
    return [strides[1], strides[0]] + strides[2:]


def offsets_of(digits):
    found = [0]
    for stride, radix in digits:
        found = [low + e * stride for low in found for e in range(radix)]
    return found


class Stream:
    def __init__(self, row_devices, first, rows, kind):
        self.first, self.rows = first, rows
        self.count = chunks_of(row_devices, rows)
        self.row_devices = row_devices
        self.digits = digits_of(self.count, kind)
        self.chunk = rows // self.count

    def parts(self):
        stride, radix = self.digits[0]
        rest = offsets_of(self.digits[1:])
        return [[e * stride + low for low in rest] for e in range(radix)]

    def send(self, value, offset):
        return xor_send(value, "rows", self.row_devices, offset)


def weight_gradient_kernel(streams, pairs, me_ref, *refs):
    operands, outs, scratch = refs[: 2 * pairs], list(refs[2 * pairs : -1]), refs[-1]
    start = 0
    for i in range(pairs):
        left, right = operands[2 * i], operands[2 * i + 1]
        count = left.shape[0]
        scratch[start : start + count] = dot(left[...], right[...], 1, 1).astype(BF16)
        start += count
    for stream in streams:
        for offsets in stream.parts():
            out = outs.pop(0)
            for place, offset in enumerate(offsets):
                chunk = (me_ref[0] % stream.count) ^ offset
                at = pl.multiple_of(stream.first + chunk * stream.chunk, 16)
                out[place * stream.chunk : (place + 1) * stream.chunk] = scratch[pl.ds(at, stream.chunk), :]


def weight_gradient(me, streams, *operands):
    pairs = len(operands) // 2
    total = sum(operands[2 * i].shape[0] for i in range(pairs))
    columns = operands[1].shape[0]
    outs = tuple(
        shape(len(offsets) * stream.chunk, columns, kind=BF16) for stream in streams for offsets in stream.parts()
    )
    found = list(
        kernel(
            functools.partial(weight_gradient_kernel, streams, pairs),
            outs,
            [me],
            operands,
            [pltpu.VMEM((total, columns), BF16)],
        )
    )
    return [[found.pop(0) for _ in stream.parts()] for stream in streams]


def start_stage(stream, parts, stage):
    stride, radix = stream.digits[stage]
    return [stream.send(parts[e], e * stride) for e in range(1, radix)]


def add_stage(stream, parts, received, stage):
    rows = parts[0].shape[0]
    radix = 1 if stage + 1 == len(stream.digits) else stream.digits[stage + 1][1]
    size = rows // radix
    return add([parts[0]] + received, *((e * size, (e + 1) * size, BF16) for e in range(radix)))


def sum_rest(stream, value):
    stride = stream.count
    while stride < stream.row_devices:
        value = add([value, stream.send(value, stride)], (0, value.shape[0], BF16))[0]
        stride *= 2
    return value


def gather_stage(stream, value, stage):
    stride, radix = stream.digits[stage]
    return [value] + [stream.send(value, e * stride) for e in range(1, radix)]


def place_kernel(all_tokens, streams, bounds, me_ref, sums, *refs):
    outs, found, sems = refs[-len(bounds) - 2 : -2], refs[-2], refs[-1]
    pieces = list(refs[: -len(bounds) - 2])
    scale = loss_scale(all_tokens, sums, found.shape[1])
    copies, start = [], 0
    for stream in streams:
        for offsets in stream.parts():
            piece, size = pieces.pop(0), stream.chunk
            for place, offset in enumerate(offsets):
                row = stream.first + ((me_ref[0] % stream.count) ^ offset) * size
                here = slice(start, start + size)
                found[here] = piece[place * size : (place + 1) * size].astype(F32) * scale
                for (first, last), out in zip(bounds, outs):
                    at = pl.ds(pl.multiple_of(jnp.clip(row - first, 0, last - first - size), 16), size)
                    copy = pltpu.make_async_copy(found.at[here], out.at[at, :], sems.at[len(copies)])
                    inside = None if len(bounds) == 1 else (row >= first) & (row < last)
                    copies.append((copy, inside))
                    copy.start() if inside is None else pl.when(inside)(copy.start)
                start += size
    for copy, inside in copies:
        copy.wait() if inside is None else pl.when(inside)(copy.wait)


def place(all_tokens, me, sums, streams, pieces, sizes):
    columns = pieces[0].shape[1]
    bounds, start = [], 0
    for size in sizes:
        bounds.append((start, start + size))
        start += size
    count = len(sizes) * sum(stream.count for stream in streams)
    vmem, hbm = pl.BlockSpec(memory_space=pltpu.VMEM), pl.BlockSpec(memory_space=pltpu.HBM)
    found = pl.pallas_call(
        functools.partial(place_kernel, all_tokens, streams, bounds),
        out_shape=tuple(shape(size, columns) for size in sizes),
        in_specs=[pl.BlockSpec(memory_space=pltpu.SMEM)] + [vmem] * (1 + len(pieces)),
        out_specs=(hbm,) * len(sizes),
        scratch_shapes=[pltpu.VMEM((start, columns), F32), pltpu.SemaphoreType.DMA((count,))],
        compiler_params=pltpu.CompilerParams(vmem_limit_bytes=12 * 1024 * 1024),
        cost_estimate=Order.estimate(),
    )(me, after(sums, Order.last), *pieces)
    Order.last = found[0]
    return found


def live_row(counts_ref, width, first):
    place = lax.broadcasted_iota(jnp.int32, (1, width), 1) + first
    return jnp.where(place < counts_ref[0], 1.0, 0.0)


def loss_scale(all_tokens, sums, width):
    return jnp.full((1, width), all_tokens, F32) / jnp.broadcast_to(sums[7:8, 0:1], (1, width))


def history_kernel(block, mix_ref, counts_ref, cot_ref, history_ref, running_ref, d_mix_ref):
    layers, features, tokens = history_ref.shape
    live = live_row(counts_ref, tokens, 0)
    d_mix_ref[...] = jnp.zeros_like(d_mix_ref)

    def body(history_part):
        for i in range(block // STEP):
            rows = slice(i * STEP, (i + 1) * STEP)
            own = pl.ds(pl.multiple_of(pl.program_id(0) * block + i * STEP, STEP), STEP)
            grad = cot_ref[own].astype(F32) * live
            running = jnp.zeros_like(grad)
            for j in range(layers):
                layer = history_part[j, rows].astype(F32)
                running = running + mix_ref[j] * layer
                terms = grad * layer
                terms = terms[: STEP // 2] + terms[STEP // 2 :]
                d_mix_ref[j] += sum(terms[:, k : k + 128] for k in range(0, tokens, 128))
            running_ref[own] = running

    whole = pl.BlockSpec((layers, block, tokens), lambda i: (0, i, 0))
    pltpu.emit_pipeline(body, grid=(features // block,), in_specs=[whole])(history_ref)


def d_history_kernel(all_tokens, block, mix_ref, counts_ref, cot_ref, sums, d_history_ref):
    layers, features, tokens = d_history_ref.shape
    factor = live_row(counts_ref, tokens, 0) * loss_scale(all_tokens, sums, tokens)

    def body(part):
        for i in range(block // STEP):
            rows = slice(i * STEP, (i + 1) * STEP)
            own = pl.ds(pl.multiple_of(pl.program_id(0) * block + i * STEP, STEP), STEP)
            grad = cot_ref[own].astype(F32) * factor
            for j in range(layers):
                part[j, rows] = (mix_ref[j] * grad).astype(BF16)

    whole = pl.BlockSpec((layers, block, tokens), lambda i: (0, i, 0))
    pltpu.emit_pipeline(body, grid=(features // block,), out_specs=[whole])(d_history_ref)


def history_call(body, outs, in_hbm, out_hbm, scalars, arrays):
    vmem, hbm = pl.BlockSpec(memory_space=pltpu.VMEM), pl.BlockSpec(memory_space=pltpu.HBM)
    arrays = [after(arrays[0], Order.last), *arrays[1:]]
    found = pl.pallas_call(
        body,
        out_shape=outs,
        in_specs=[pl.BlockSpec(memory_space=pltpu.SMEM)] * len(scalars) + [hbm if h else vmem for h in in_hbm],
        out_specs=tuple(hbm if h else vmem for h in out_hbm),
        compiler_params=pltpu.CompilerParams(vmem_limit_bytes=12 * 1024 * 1024),
        cost_estimate=Order.estimate(),
    )(*scalars, *arrays)
    Order.last = found[0]
    return found


def spread_of(load, count, width, total=None):
    zero = jnp.zeros((STEP, width), F32)
    if total is None:
        total = each_rows(count, lambda i, acc: acc + load(i), zero)
    mean = column_sum(total) / count

    def squares(i, acc):
        centred = load(i) - mean
        return acc + centred * centred

    return mean, lax.rsqrt(column_sum(each_rows(count, squares, zero)) / count + EPSILON)


def prepare_kernel(held, *refs):
    refs = refs[held:]
    sources, x_in, (own, norms, cosine, sine), places, sem = refs[:6], refs[6], refs[7:11], refs[11:17], refs[17]
    copies = [pltpu.make_async_copy(*pair, sem.at[i]) for i, pair in enumerate(zip(sources, places))]
    whole = pltpu.make_async_copy(x_in, own, sem.at[6])
    for copy in [*copies, whole]:
        copy.start()
    norms[...] = jnp.zeros_like(norms)
    for copy in copies:
        copy.wait()
    positions, rates, *vectors = places
    for i, ref in enumerate(vectors):
        norms[i : i + 1, : ref.shape[1]] = ref[...]
    angles = positions[...].astype(F32) * rates[...]
    cosine[...] = jnp.cos(angles)
    sine[...] = jnp.sin(angles)
    whole.wait()


def prepare(held, x_in, *sources):
    tokens, part = sources[0].shape[1], sources[2].shape[1]
    rates = sources[1].shape[0]
    vmem = pl.BlockSpec(memory_space=pltpu.VMEM)
    found = pl.pallas_call(
        functools.partial(prepare_kernel, len(held)),
        out_shape=(
            shape(part, tokens, kind=BF16),
            shape(8, -(-part // 128) * 128),
            shape(rates, tokens),
            shape(rates, tokens),
        ),
        in_specs=[vmem] * len(held) + [pl.BlockSpec(memory_space=pltpu.HBM)] * (len(sources) + 1),
        out_specs=(vmem,) * 4,
        scratch_shapes=[pltpu.VMEM(v.shape, v.dtype) for v in sources] + [pltpu.SemaphoreType.DMA((len(sources) + 1,))],
        compiler_params=pltpu.CompilerParams(vmem_limit_bytes=4 * 1024 * 1024),
        cost_estimate=Order.estimate(),
    )(*held, *(pltpu.with_memory_space_constraint(v, pltpu.HBM) for v in (*sources, x_in)))
    Order.last = found[0]
    return found


def norms_kernel(at_ref, n01, n23, norms):
    part = norms.shape[0] // 4
    near, far = n01[...].T, n23[...].T
    for e, norm in enumerate((near, near, far, far)):
        rows = pl.ds(pl.multiple_of((at_ref[0] ^ e) * part, 64), part)
        norms[rows, :] = norm[:part, 8 * (e % 2) : 8 * (e % 2) + 8]


def project_kernel(
    at_ref, x0, x1, x2, x3, norms, cosine, sine, w_qkv, x_all, normed, stats, qkv, project
):
    at = at_ref[0]
    part, tokens = x0.shape
    model = w_qkv.shape[1]
    for e, piece in enumerate((x0, x1, x2, x3)):
        x_all[pl.ds(pl.multiple_of((at ^ e) * part, 64), part), :] = piece[...]
    mean, scale = spread_of(lambda i: x_all[rows_at(i), :].astype(F32), model, tokens)
    stats[0:1] = mean
    stats[1:2] = scale

    def normalise(i, _):
        rows = rows_at(i)
        xhat = (x_all[rows, :].astype(F32) - mean) * scale
        normed[rows, :] = (xhat * norms[rows, 0:1] + norms[rows, 1:2]).astype(BF16)

    each_rows(model, normalise)
    project[...] = dot(w_qkv[...], normed[...], 1, 0)
    width = HEAD_DIM // 2
    for block, factor in ((0, HEAD_DIM ** (-0.5)), (1, 1.0)):
        for start in range(block * part, (block + 1) * part, HEAD_DIM):
            front, back = project[start : start + width], project[start + width : start + HEAD_DIM]
            cos, sin = cosine[...] * factor, sine[...] * factor
            qkv[start : start + width] = (front * cos - back * sin).astype(BF16)
            qkv[start + width : start + HEAD_DIM] = (back * cos + front * sin).astype(BF16)
    qkv[2 * part :] = project[2 * part :].astype(BF16)


def attention_kernel(
    at_ref, qkv, x_all, heads_send, heads_own, x_half, heads_out, probs, scores
):
    at = at_ref[0]
    part, tokens = heads_out.shape
    half = tokens // 2
    for h in range(part // HEAD_DIM):
        head = slice(h * HEAD_DIM, (h + 1) * HEAD_DIM)
        for t in range(2):
            now = slice(t * half, (t + 1) * half)
            count = (t + 1) * half
            query = qkv[head, now]
            key = qkv[part + h * HEAD_DIM : part + (h + 1) * HEAD_DIM, :count]
            value = qkv[2 * part + h * HEAD_DIM : 2 * part + (h + 1) * HEAD_DIM, :count]
            scores[:count] = dot(key, query, 0, 0)

            def masked(i):
                behind = lax.broadcasted_iota(jnp.int32, (STEP, half), 0) + (i * STEP - t * half)
                ahead = lax.broadcasted_iota(jnp.int32, (STEP, half), 1)
                return jnp.where(behind <= ahead, scores[rows_at(i), :], -1e30)

            def raised(found, i, acc):
                found = jnp.exp(found - top)
                scores[rows_at(i), :] = found
                return acc + found

            def settle(i, _):
                rows = rows_at(i)
                probs[h, rows, now] = (scores[rows, :] * divisor).astype(BF16)

            top = each_rows(
                t * half, lambda i, acc: jnp.maximum(acc, scores[rows_at(i), :]), jnp.full((STEP, half), -1e30, F32)
            )
            top = each_rows(count, lambda i, acc: jnp.maximum(acc, masked(i)), top, first=t * half)
            top = jnp.max(top, axis=0, keepdims=True)
            total = each_rows(
                t * half, lambda i, acc: raised(scores[rows_at(i), :], i, acc), jnp.zeros((STEP, half), F32)
            )
            total = each_rows(count, lambda i, acc: raised(masked(i), i, acc), total, first=t * half)
            divisor = 1.0 / column_sum(total)
            each_rows(count, settle)
            heads_out[head, now] = dot(value, probs[h, :count, now], 1, 0).astype(BF16)
    own = pl.multiple_of((at % 2) * half, half)
    other = pl.multiple_of((1 - at % 2) * half, half)
    heads_send[...] = heads_out[:, pl.ds(other, half)]
    heads_own[...] = heads_out[:, pl.ds(own, half)]
    x_half[...] = x_all[:, pl.ds(own, half)]


def output_gradient_kernel(
    at_ref, self_ref, counts_ref, c0, c1, c2, c3, w_down, g_out, d_active, cot_all
):
    at = at_ref[0]
    part, tokens = c0.shape
    half = tokens // 2
    for e, piece in enumerate((c0, c1, c2, c3)):
        cot_all[pl.ds(pl.multiple_of((at ^ e) * part, 64), part), :] = piece[...]
    for place, side in enumerate((at % 2, 1 - at % 2)):
        now = pl.ds(pl.multiple_of(side * half, half), half)
        factor = live_row(counts_ref, half, side * half)

        def scale(i, _, now=now, factor=factor, place=place):
            rows = rows_at(i)
            grad = cot_all[rows, now].astype(F32) * factor
            g_out[rows, place * half : (place + 1) * half] = (self_ref[0] * grad).astype(BF16)

        each_rows(cot_all.shape[0], scale)
    d_active[...] = dot(w_down[...], g_out[...], 1, 0)


def rows_kernel(at_ref, *refs):
    out = refs[-1]
    for e, piece in enumerate(refs[:-1]):
        rows = piece.shape[0]
        out[pl.ds(pl.multiple_of((at_ref[0] ^ e) * rows, 64), rows), :] = piece[...]


def middle_kernel(at_ref, pair, pair_far, w_all, x_half, norms, middle, stats, normed, heads):
    model, half = x_half.shape
    part = pair.shape[0] // 2
    for e, piece in enumerate((pair[:part], pair[part:], pair_far[:part], pair_far[part:])):
        heads[pl.ds(pl.multiple_of((at_ref[0] ^ e) * part, 64), part), :] = piece
    middle[...] = dot(w_all[...], heads[...], 0, 0)

    def add(i, acc):
        rows = rows_at(i)
        found = x_half[rows, :].astype(F32) + middle[rows, :]
        middle[rows, :] = found
        return acc + found

    total = each_rows(model, add, jnp.zeros((STEP, half), F32))
    mean, scale = spread_of(lambda i: middle[rows_at(i), :], model, half, total)
    stats[0:1] = mean
    stats[1:2] = scale

    def normalise(i, _):
        rows = rows_at(i)
        xhat = (middle[rows, :] - mean) * scale
        normed[rows, :] = (xhat * norms[rows, 2:3] + norms[rows, 3:4]).astype(BF16)

    each_rows(model, normalise)


def feed_forward_kernel(own, other, w_up, d_active, normed, active, d_hidden, send, keep, hidden):
    half = own.shape[1]
    normed[:, :half] = own[...]
    normed[:, half:] = other[...]
    hidden[...] = dot(w_up[...], normed[...], 0, 0)

    def bend(i, _):
        rows = rows_at(i)
        u = hidden[rows, :]
        squared = u * u
        curve = jnp.tanh(0.7978845608028654 * u * (1.0 + 0.044715 * squared))
        lifted = 0.5 * (1.0 + curve)
        active[rows, :] = (u * lifted).astype(BF16)
        slope = lifted + u * (0.5 * (1.0 - curve * curve)) * (
            0.7978845608028654 + (3 * 0.044715 * 0.7978845608028654) * squared
        )
        d_hidden[rows, :] = (slope * d_active[rows, :]).astype(BF16)

    each_rows(hidden.shape[0], bend)
    send[...] = dot(w_up[...], d_hidden[:, half:], 1, 0).astype(BF16)
    keep[...] = dot(w_up[...], d_hidden[:, :half], 1, 0)


def store_blocks(at, total, part, near, *outs):
    for e, out in zip(near, outs):
        out[...] = total[pl.ds(pl.multiple_of((at ^ e) * part, 64), part), :].astype(out.dtype)


def output_kernel(at_ref, counts_ref, active, w_down, middle, cot_all, send, send_far, keep, keep_far, product, total):
    at = at_ref[0]
    model, half = middle.shape
    part = send.shape[0]
    own = pl.ds(pl.multiple_of((at % 2) * half, half), half)
    other = pl.ds(pl.multiple_of((1 - at % 2) * half, half), half)
    total[:, own] = dot(w_down[...], active[:, :half], 0, 0) + 0.5 * middle[...]
    total[:, other] = dot(w_down[...], active[:, half:], 0, 0)
    live = live_row(counts_ref, 2 * half, 0)

    def weigh(i, acc):
        rows = rows_at(i)
        return acc + fold_lanes(total[rows, :] * (cot_all[rows, :].astype(F32) * live))

    product[...] = each_rows(model, weigh, jnp.zeros((STEP, 128), F32))
    store_blocks(at, total, part, (1, 3, 0, 2), send, send_far, keep, keep_far)


def fold_lanes(value):
    return sum(value[:, k : k + 128] for k in range(0, value.shape[1], 128))


def as_row(columns):
    return column_sum(columns[...].T)


def middle_gradient_kernel(
    at_ref, self_ref, counts_ref, chip, received, middle, stats, cot_all, norms,
    d_middle, g_mid, gains, d_normed, gain_sums, bias_sums,
):
    model, half = chip.shape
    mean, scale = stats[0:1], stats[1:2]
    zero = jnp.zeros((STEP, half), F32)

    def sums(i, acc):
        rows = rows_at(i)
        grad = chip[rows, :] + received[rows, :].astype(F32)
        d_normed[rows, :] = grad
        xhat = (middle[rows, :] - mean) * scale
        both = grad * xhat
        gain_sums[rows, :] = fold_lanes(both)
        bias_sums[rows, :] = fold_lanes(grad)
        gain = norms[rows, 2:3]
        return acc[0] + grad * gain, acc[1] + both * gain

    first, second = (column_sum(v) / model for v in each_rows(model, sums, (zero, zero)))
    side = (at_ref[0] % 2) * half
    factor = self_ref[0] * live_row(counts_ref, half, side)
    own = pl.ds(pl.multiple_of(side, half), half)

    def finish(i, _):
        rows = rows_at(i)
        xhat = (middle[rows, :] - mean) * scale
        found = cot_all[rows, own].astype(F32) * factor + scale * (
            d_normed[rows, :] * norms[rows, 2:3] - first - xhat * second
        )
        d_middle[rows, :] = found
        g_mid[rows, :] = found.astype(BF16)

    each_rows(model, finish)
    gains[0:1] = as_row(gain_sums)
    gains[1:2] = as_row(bias_sums)


def attention_gradient_kernel(
    at_ref, own, other, w_out, qkv, probs, cosine, sine,
    d_project, g_mid, d_heads, d_scores, products, d_queries, d_keys, d_values,
):
    at = at_ref[0]
    half = own.shape[1]
    part = w_out.shape[0]
    g_mid[:, pl.ds(pl.multiple_of((at % 2) * half, half), half)] = own[...]
    g_mid[:, pl.ds(pl.multiple_of((1 - at % 2) * half, half), half)] = other[...]
    d_heads[...] = dot(w_out[...], g_mid[...], 1, 0).astype(BF16)
    width = HEAD_DIM // 2
    for h in range(part // HEAD_DIM):
        head = slice(h * HEAD_DIM, (h + 1) * HEAD_DIM)
        query = qkv[head]
        key = qkv[part + h * HEAD_DIM : part + (h + 1) * HEAD_DIM]
        value = qkv[2 * part + h * HEAD_DIM : 2 * part + (h + 1) * HEAD_DIM]
        for t in range(2):
            now = slice(t * half, (t + 1) * half)
            count = (t + 1) * half
            products[:count] = dot(value[:, :count], d_heads[head, now], 0, 0)

            def weigh(i, acc):
                rows = rows_at(i)
                return acc + products[rows, :] * probs[h, rows, now].astype(F32)

            inner = column_sum(each_rows(count, weigh, jnp.zeros((STEP, half), F32)))

            def settle(i, _):
                rows = rows_at(i)
                d_scores[rows, :] = (probs[h, rows, now].astype(F32) * (products[rows, :] - inner)).astype(BF16)

            each_rows(count, settle)
            d_queries[:, now] = dot(key[:, :count], d_scores[:count], 1, 0) * HEAD_DIM ** (-0.5)
            d_key = dot(query[:, now], d_scores[:count], 1, 1)
            d_value = dot(d_heads[head, now], probs[h, :count, now], 1, 1)
            if t == 0:
                d_keys[:, :half] = d_key
                d_values[:, :half] = d_value
            else:
                d_keys[:, :half] += d_key[:, :half]
                d_values[:, :half] += d_value[:, :half]
                d_keys[:, half:] = d_key[:, half:]
                d_values[:, half:] = d_value[:, half:]
        for block, found in ((0, d_queries), (1, d_keys)):
            start = block * part + h * HEAD_DIM
            front, back = found[:width], found[width:]
            d_project[start : start + width] = (front * cosine[...] + back * sine[...]).astype(BF16)
            d_project[start + width : start + HEAD_DIM] = (back * cosine[...] - front * sine[...]).astype(BF16)
        d_project[2 * part + h * HEAD_DIM : 2 * part + (h + 1) * HEAD_DIM] = d_values[...].astype(BF16)


def input_gradient_kernel(
    width, at_ref, counts_ref, d_project, w_qkv, x_all, stats, d_middle, norms, gains,
    send, send_far, keep, keep_far, sums, total, gain_sums, bias_sums,
):
    at = at_ref[0]
    model, half = d_middle.shape
    tokens = x_all.shape[1]
    part = send.shape[0]
    total[...] = dot(w_qkv[...], d_project[...], 0, 0)
    mean, scale = stats[0:1], stats[1:2]
    zero = jnp.zeros((STEP, tokens), F32)
    own = pl.ds(pl.multiple_of((at % 2) * half, half), half)

    def body(i, acc):
        rows = rows_at(i)
        grad = total[rows, :]
        xhat = (x_all[rows, :].astype(F32) - mean) * scale
        both = grad * xhat
        gain_sums[rows, :] = fold_lanes(both)
        bias_sums[rows, :] = fold_lanes(grad)
        gain = norms[rows, 0:1]
        lifted = grad * gain
        total[rows, :] = lifted * scale
        total[rows, own] += 0.5 * d_middle[rows, :]
        return acc[0] + lifted, acc[1] + both * gain

    first, second = each_rows(model, body, (zero, zero))
    store_blocks(at, total, part, (1, 3, 0, 2), send, send_far, keep, keep_far)
    sums[...] = jnp.zeros_like(sums)
    sums[0:1] = as_row(gain_sums)
    sums[1:2] = as_row(bias_sums)
    sums[2:4] = 0.5 * gains[...]
    sums[4:5, :tokens] = column_sum(first) / model
    sums[5:6, :tokens] = column_sum(second) / model
    sums[7:8] = jnp.zeros((1, model), F32) + counts_ref[0].astype(F32) / width


def mixed_kernel(self_ref, own, near, far, running, d_mix, product, sums, mixed, all_sums, table):
    layers = d_mix.shape[0]

    def body(i, _):
        rows = rows_at(i)
        output = own[rows, :] + near[rows, :].astype(F32) + far[rows, :].astype(F32)
        mixed[rows, :] = (self_ref[0] * output + running[rows, :]).astype(BF16)

    each_rows(own.shape[0], body)
    table[...] = jnp.zeros_like(table)
    table[:layers] = jnp.sum(d_mix[...], axis=1)
    table[layers : layers + 1] = column_sum(product[...])
    all_sums[...] = sums[...]
    all_sums[6:7, :128] = as_row(table)


def ends_kernel(all_tokens, layers, width, at_ref, sums, d_mix, d_self, *ends):
    part = ends[0].shape[1]
    scale = loss_scale(all_tokens, sums, sums.shape[1])
    d_mix[...] = sums[6:7, :layers] * scale[:, :layers]
    d_self[...] = sums[6:7, layers : layers + 1] * scale[:, :1]
    for i, end in enumerate(ends):
        scaled = sums[i : i + 1] * scale
        found = scaled[:, :part]
        for w in range(1, width):
            found = jnp.where(at_ref[0] == w, scaled[:, w * part : (w + 1) * part], found)
        end[...] = found


def d_input_kernel(own, near, far, x_in, stats, row_sums, found):
    part, tokens = own.shape
    mean, scale = stats[0:1], stats[1:2]
    first, second = row_sums[4:5, :tokens], row_sums[5:6, :tokens]

    def body(i, _):
        rows = rows_at(i)
        xhat = (x_in[rows, :].astype(F32) - mean) * scale
        total = own[rows, :] + near[rows, :].astype(F32) + far[rows, :].astype(F32)
        found[rows, :] = total - scale * (first + xhat * second)

    each_rows(part, body)


def scale_kernel(all_tokens, found, sums, d_input):
    factor = loss_scale(all_tokens, sums, found.shape[1])

    def body(i, _):
        d_input[rows_at(i), :] = found[rows_at(i), :] * factor

    each_rows(found.shape[0], body)


def local(
    width,
    row_devices,
    x_in,
    history,
    cotangent,
    counts,
    positions,
    mix_weights,
    self_weight,
    first_norm_gain,
    first_norm_bias,
    w_qkv,
    w_out,
    second_norm_gain,
    second_norm_bias,
    w_up,
    w_down,
):
    part, tokens = x_in.shape
    model = w_out.shape[1]
    hidden_units = w_up.shape[1]
    half = tokens // 2
    layers = mix_weights.shape[0]
    all_tokens = float(tokens * row_devices)
    at = lax.axis_index("width").astype(jnp.int32)[None]
    me = lax.axis_index("rows").astype(jnp.int32)[None]
    Order.last, Order.front = None, FRONT
    to_width = lambda value, offset: xor_send(value, "width", width, offset)
    to_row = lambda value, offset: xor_send(value, "rows", row_devices, offset)
    w_qkv = w_qkv.reshape(3 * part, model)
    rates = 1.0 / 10000.0 ** (np.arange(HEAD_DIM // 2) * 2.0 / HEAD_DIM)
    x_in, cotangent, counts = after((x_in, cotangent, counts), at, me)

    x_far, x_near = to_width(x_in, 2), to_width(x_in, 1)
    x_own, norms, cosine, sine = prepare(
        [x_near],
        x_in,
        positions[None, :],
        jnp.asarray(rates[:, None], F32),
        *(v[None, :] for v in (first_norm_gain, first_norm_bias, second_norm_gain, second_norm_bias)),
    )
    norms_near = join([norms, to_width(norms, 1)])
    norms_far = to_width(norms_near, 2)
    norms = kernel(norms_kernel, shape(model, 8), [at], [norms_near, norms_far])
    x_both = to_width(after(x_far, norms), 1)
    w_now = after(w_out, norms_near)
    w_far, w_near = to_width(w_now, 2), to_width(w_now, 1)

    x_all, normed_one, stats_one, qkv = kernel(
        project_kernel,
        (
            shape(model, tokens, kind=BF16),
            shape(model, tokens, kind=BF16),
            shape(2, tokens),
            shape(3 * part, tokens, kind=BF16),
        ),
        [at],
        [x_own, x_near, x_far, x_both, norms, cosine, sine, w_qkv],
        [pltpu.VMEM((3 * part, tokens), F32)],
    )
    heads_send, heads_own, x_half, heads_out, probs = kernel(
        attention_kernel,
        (
            shape(part, half, kind=BF16),
            shape(part, half, kind=BF16),
            shape(model, half, kind=BF16),
            shape(part, tokens, kind=BF16),
            shape(part // HEAD_DIM, tokens, tokens, kind=BF16),
        ),
        [at],
        [qkv, x_all],
        [pltpu.VMEM((tokens, half), F32)],
    )
    pair = join([after(heads_own, w_far), to_width(heads_send, 1)])
    pair_far = to_width(pair, 2)
    cot_now = after(cotangent, pair)
    cot_far, cot_near = to_width(cot_now, 2), to_width(cot_now, 1)
    w_both = to_width(after(w_far, pair), 1)

    w_all = kernel(rows_kernel, shape(model, model, kind=BF16), [at], [w_out, w_near, w_far, w_both])
    middle, stats_two, normed_own = kernel(
        middle_kernel,
        (shape(model, half), shape(2, half), shape(model, half, kind=BF16)),
        [at],
        [pair, pair_far, w_all, x_half, norms],
        [pltpu.VMEM((model, half), BF16)],
    )
    normed_near = to_width(normed_own, 1)
    cot_both = to_width(after(cot_far, middle), 1)
    g_out, d_active, cot_all = kernel(
        output_gradient_kernel,
        (shape(model, tokens, kind=BF16), shape(hidden_units, tokens), shape(model, tokens, kind=BF16)),
        [at, self_weight, counts],
        [cotangent, cot_near, cot_far, cot_both, w_down],
    )

    normed_two, active, d_hidden, send, keep = kernel(
        feed_forward_kernel,
        (
            shape(model, tokens, kind=BF16),
            shape(hidden_units, tokens, kind=BF16),
            shape(hidden_units, tokens, kind=BF16),
            shape(model, half, kind=BF16),
            shape(model, half),
        ),
        [],
        [normed_own, normed_near, w_up, d_active],
        [pltpu.VMEM((hidden_units, tokens), F32)],
    )

    v = Values()
    v.send, v.keep = send, keep
    down = Stream(row_devices, 0, hidden_units, "halving")
    up = Stream(row_devices, 0, model, "crossed")
    first = Stream(row_devices, 0, 2 * part, "halving")
    second = Stream(row_devices, 2 * part, 2 * part, "crossed")
    strides = [1 << i for i in range(row_devices.bit_length() - 1)]
    blocks = (shape(part, tokens, kind=BF16),) * 2 + (shape(part, tokens),) * 2
    last = len(down.digits) - 1

    def scatter(stream, stage):
        stream.held = add_stage(stream, stream.held, stream.got, stage)
        stream.got = start_stage(stream, stream.held, stage + 1)

    def turn(stream):
        value = sum_rest(stream, add_stage(stream, stream.held, stream.got, last)[0])
        stream.pieces = gather_stage(stream, value, last)

    def gather(stream, stage):
        stream.pieces = gather_stage(stream, join(stream.pieces), stage)

    def steps_of(stream):
        return (
            *(functools.partial(scatter, stream, stage) for stage in range(last)),
            functools.partial(turn, stream),
            *(functools.partial(gather, stream, stage) for stage in range(last - 1, -1, -1)),
        )

    def begin(streams, found):
        for stream, parts in zip(streams, found):
            stream.held, stream.got = parts, start_stage(stream, parts, 0)

    def down_product():
        begin([down], weight_gradient(me, [down], active, g_out))

    def up_product():
        begin([up], weight_gradient(me, [up], normed_two, d_hidden))

    def tail_product():
        found = weight_gradient(me, [first, second], v.d_project, normed_one, heads_out, v.g_mid)
        begin([first, second], found)

    def middle_sum():
        v.chip, sent = add([v.keep, to_width(v.send, 1)], (0, model, F32), (0, model, BF16))
        v.received = to_width(sent, 2)

    def output_product():
        near, far, v.out, v.out_far, v.product = kernel(
            output_kernel,
            blocks + (shape(STEP, 128),),
            [at, counts],
            [active, w_down, middle, cot_all],
            [pltpu.VMEM((model, tokens), F32)],
        )
        v.out_got = to_width(near, 1), to_width(far, 1)

    def history_sums():
        v.running, v.d_mix = history_call(
            functools.partial(history_kernel, 32),
            (shape(part, tokens), shape(layers, STEP // 2, 128)),
            (False, True),
            (False, False),
            [mix_weights, counts],
            [cotangent, pltpu.with_memory_space_constraint(history, pltpu.HBM)],
        )

    def output_sum():
        v.out_last = to_width(add([v.out_far, v.out_got[1]], (0, part, BF16))[0], 2)

    def middle_gradient():
        v.d_middle, v.g_own, v.gains = kernel(
            middle_gradient_kernel,
            (shape(model, half), shape(model, half, kind=BF16), shape(2, model)),
            [at, self_weight, counts],
            [v.chip, v.received, middle, stats_two, cot_all, norms],
            [pltpu.VMEM((model, half), F32), pltpu.VMEM((model, 128), F32), pltpu.VMEM((model, 128), F32)],
        )
        v.g_other = to_width(v.g_own, 1)

    def attention_gradient():
        v.d_project, v.g_mid = kernel(
            attention_gradient_kernel,
            (shape(3 * part, tokens, kind=BF16), shape(model, tokens, kind=BF16)),
            [at],
            [v.g_own, v.g_other, w_out, qkv, probs, cosine, sine],
            [
                pltpu.VMEM((part, tokens), BF16),
                pltpu.VMEM((tokens, half), BF16),
                pltpu.VMEM((tokens, half), F32),
                pltpu.VMEM((HEAD_DIM, tokens), F32),
                pltpu.VMEM((HEAD_DIM, tokens), F32),
                pltpu.VMEM((HEAD_DIM, tokens), F32),
            ],
        )

    def input_gradient():
        near, far, v.own_in, v.in_far, v.sums = kernel(
            functools.partial(input_gradient_kernel, width),
            blocks + (shape(8, model),),
            [at, counts],
            [v.d_project, w_qkv, x_all, stats_one, v.d_middle, norms, v.gains],
            [pltpu.VMEM((model, tokens), F32), pltpu.VMEM((model, 128), F32), pltpu.VMEM((model, 128), F32)],
        )
        v.in_got = to_width(near, 1), to_width(far, 1)

    def input_sum():
        v.in_last = to_width(add([v.in_far, v.in_got[1]], (0, part, BF16))[0], 2)

    def input_total():
        v.in_total = kernel(
            d_input_kernel,
            shape(part, tokens),
            [],
            [v.own_in, v.in_got[0], v.in_last, x_own, stats_one, v.row_sums],
        )

    def mix():
        v.mixed, v.sums = kernel(
            mixed_kernel,
            (shape(part, tokens, kind=BF16), shape(8, model)),
            [self_weight],
            [
                v.out,
                v.out_got[0],
                v.out_last,
                v.running,
                v.d_mix,
                v.product,
                v.sums,
            ],
            [pltpu.VMEM((128, 128), F32)],
        )
        v.sums_got = to_width(v.sums, 1)

    def sums_step(*sends):
        for send_on in sends:
            v.sums = add([v.sums, v.sums_got], (0, 8, F32))[0]
            v.sums_got = send_on(v.sums)

    def sums_1():
        sums_step(lambda value: to_width(value, 2))

    def sums_2():
        sums_step(row_send(strides[0]))
        v.row_sums = v.sums

    def sums_3():
        sums_step(row_send(strides[1]))

    def sums_4():
        sums_step(*(row_send(stride) for stride in strides[2:]))

    def last_sums():
        v.sums = add([v.sums, v.sums_got], (0, 8, F32))[0]

    def scale_input():
        v.d_input = kernel(
            functools.partial(scale_kernel, all_tokens), shape(part, tokens), [], [v.in_total, v.sums]
        )

    def history_gradient():
        v.d_history = history_call(
            functools.partial(d_history_kernel, all_tokens, 32),
            (shape(*history.shape, kind=BF16),),
            (False, False),
            (True,),
            [mix_weights, counts],
            [cotangent, v.sums],
        )[0]

    def ends():
        v.ends = kernel(
            functools.partial(ends_kernel, all_tokens, layers, width),
            (shape(1, layers), shape(1, 1)) + (shape(1, part),) * 4,
            [at],
            [v.sums],
        )

    def placed(streams, *sizes):
        pieces = [piece for stream in streams for piece in stream.pieces]
        return place(all_tokens, me, v.sums, streams, pieces, sizes)

    def place_down():
        v.d_w_down = placed([down], hidden_units)[0]

    def place_up():
        v.d_w_up = placed([up], model)[0]

    def place_tail():
        v.d_w_qkv, v.d_w_out = placed([first, second], 3 * part, part)

    row_send = lambda stride: lambda value: to_row(value, stride)
    down_1, down_2, down_3, down_4, down_5 = steps_of(down)
    up_1, up_2, up_3, up_4, up_5 = steps_of(up)
    first_1, first_2, first_3, first_4, first_5 = steps_of(first)
    second_1, second_2, second_3, second_4, second_5 = steps_of(second)
    schedule = (
        (down_product, 10),
        (middle_sum, 8),
        (up_product, 10),
        (output_product, 100),
        (history_sums, 10),
        (middle_gradient, 10),
        (output_sum, 10),
        (down_1, 10),
        (up_1, 100),
        (attention_gradient, 8),
        (tail_product, 4),
        (down_2, 100),
        (up_2, 0.3),
        (input_gradient, 1),
        (mix, 8),
        (first_1, 1),
        (second_1, 1),
        (up_3, 100),
        (down_3, 1),
        (first_2, 2),
        (sums_1, 4),
        (sums_2, 1),
        (input_sum, 1),
        (second_2, 1),
        (sums_3, 1),
        (up_4, 2),
        (sums_4, 1),
        (down_4, 4),
        (first_3, 40),
        (input_total, 1),
        (second_3, 2),
        (down_5, 1),
        (first_4, 200),
        (up_5, 0.3),
        (second_4, 16),
        (last_sums, 1),
        (scale_input, 0.1),
        (first_5, 40),
        (ends, 1),
        (history_gradient, 1),
        (place_down, 1),
        (second_5, 200),
        (place_up, 4),
        (place_tail, 1),
    )
    for step, weight in schedule:
        Order.cost = weight
        step()
    d_mix, d_self, *vectors = v.ends
    return (
        v.mixed,
        v.d_input,
        v.d_history,
        d_mix[0],
        d_self[0],
        vectors[0][0],
        vectors[1][0],
        v.d_w_qkv.reshape(3, part, model),
        v.d_w_out,
        vectors[2][0],
        vectors[3][0],
        v.d_w_up,
        v.d_w_down,
    )


def solution(mesh):
    return jax.shard_map(
        functools.partial(local, mesh.shape["width"], mesh.shape["rows"]),
        mesh=mesh,
        in_specs=(
            P("width", "rows"),
            P(None, "width", "rows"),
            P("width", "rows"),
            P("rows"),
            P("rows"),
            P(),
            P(),
            P("width"),
            P("width"),
            P(None, "width", None),
            P("width", None),
            P("width"),
            P("width"),
            P(None, "width"),
            P("width", None),
        ),
        out_specs=(
            P("width", "rows"),
            P("width", "rows"),
            P(None, "width", "rows"),
            P(),
            P(),
            P("width"),
            P("width"),
            P(None, "width", None),
            P("width", None),
            P("width"),
            P("width"),
            P(None, "width"),
            P("width", None),
        ),
        check_vma=False,
    )
```

```python
import functools

import jax
import jax.numpy as jnp
import numpy as np
from jax import lax
from jax.experimental import pallas as pl
from jax.experimental.pallas import tpu as pltpu
from jax.sharding import PartitionSpec as P

HEAD_DIM = 64
EPSILON = 1e-05
BF16 = jnp.bfloat16
F32 = jnp.float32
STEP = 16


SCHEDULE = (
    ("down", 10),
    ("chip", 8),
    ("up", 10),
    ("out", 100),
    ("middle", 10),
    ("out_sum", 10),
    ("down1", 10),
    ("up1", 100),
    ("attention", 8),
    ("tail", 4),
    ("down2", 100),
    ("up2", 0.3),
    ("input", 1),
    ("mix", 8),
    ("first1", 1),
    ("second1", 1),
    ("up3", 100),
    ("down3", 1),
    ("first2", 2),
    ("sums1", 4),
    ("sums2", 1),
    ("input_sum", 1),
    ("second2", 1),
    ("sums3", 1),
    ("up4", 2),
    ("sums4", 1),
    ("down4", 4),
    ("first3", 40),
    ("input_total", 1),
    ("second3", 2),
    ("down5", 1),
    ("first4", 200),
    ("up5", 0.3),
    ("second4", 16),
    ("sums5", 1),
    ("scale", 0.1),
    ("first5", 40),
    ("ends", 1),
    ("history", 1),
    ("place_down", 1),
    ("second5", 200),
    ("place_up", 4),
    ("place_tail", 1),
)

FRONT = (0.3, 0.1, 0.3, 4, 2, 4, 0.1, 0.3, 100, 10)


def shape(*dims, kind=F32):
    return jax.ShapeDtypeStruct(dims, kind)


class Values:
    pass


class Order:
    last = None
    cost = 0
    front = ()

    @classmethod
    def estimate(cls):
        if cls.front:
            cls.cost, *cls.front = cls.front
        return pl.CostEstimate(flops=int(cls.cost * 10**8), bytes_accessed=1024, transcendentals=0)


def kernel(body, outs, scalars, arrays, scratch=(), limit=12, streamed=()):
    arrays = list(arrays)
    if Order.last is not None:
        arrays[0] = after(arrays[0], Order.last)
    spaces = [pltpu.VMEM] * len(arrays) + [pltpu.HBM] * len(streamed)
    arrays += [pltpu.with_memory_space_constraint(v, pltpu.HBM) for v in streamed]
    found = pl.pallas_call(
        body,
        out_shape=outs,
        in_specs=[pl.BlockSpec(memory_space=pltpu.SMEM)] * len(scalars)
        + [pl.BlockSpec(memory_space=space) for space in spaces],
        out_specs=jax.tree.map(lambda _: pl.BlockSpec(memory_space=pltpu.VMEM), outs),
        scratch_shapes=list(scratch),
        compiler_params=pltpu.CompilerParams(vmem_limit_bytes=limit * 1024 * 1024),
        cost_estimate=Order.estimate(),
    )(*scalars, *arrays)
    Order.last = jax.tree.leaves(found)[0]
    return found


def after(value, *others):
    return lax.optimization_barrier((value, others))[0]


def dot(left, right, left_dim, right_dim):
    return lax.dot_general(left, right, (((left_dim,), (right_dim,)), ((), ())), preferred_element_type=F32)


def rows_at(i):
    return pl.ds(pl.multiple_of(i * STEP, STEP), STEP)


def each_rows(count, body, start=None, first=0):
    return lax.fori_loop(first // STEP, count // STEP, body, start, unroll=4)


def column_sum(value):
    return jnp.sum(value, axis=0, keepdims=True)


def xor_send(value, axis, size, offset):
    return lax.ppermute(value, axis, [(i, i ^ offset) for i in range(size)])


def add_kernel(count, cuts, *refs):
    parts, outs = refs[:count], refs[count:]

    def one(rows):
        found = parts[0][rows, :].astype(F32)
        for part in parts[1:]:
            found = found + part[rows, :].astype(F32)
        return found

    for (first, last), out in zip(cuts, outs):
        if (last - first) % STEP:
            out[...] = one(slice(first, last)).astype(out.dtype)
        else:

            def body(i, _, first=first, out=out):
                out[rows_at(i), :] = one(pl.ds(pl.multiple_of(first + i * STEP, STEP), STEP)).astype(out.dtype)

            each_rows(last - first, body)


def add(parts, *cuts):
    columns = parts[0].shape[1]
    outs = tuple(shape(last - first, columns, kind=kind) for first, last, kind in cuts)
    return list(kernel(functools.partial(add_kernel, len(parts), [cut[:2] for cut in cuts]), outs, [], parts))


def sum_small(value, axis, size):
    stride = 1
    while stride < size:
        value = add([value, xor_send(value, axis, size, stride)], (0, value.shape[0], F32))[0]
        stride *= 2
    return value


def join_kernel(*refs):
    out, start = refs[-1], 0
    for piece in refs[:-1]:
        out[start : start + piece.shape[0]] = piece[...]
        start += piece.shape[0]


def join(pieces):
    rows = sum(piece.shape[0] for piece in pieces)
    return kernel(join_kernel, shape(rows, pieces[0].shape[1], kind=pieces[0].dtype), [], pieces)


def chunks_of(count, rows):
    count = min(count, 8)
    while rows % (16 * count):
        count //= 2
    return count


def digits_of(count, kind):
    if kind == "halving":
        strides = []
        stride = 1
        while stride < count:
            strides.append((stride, 2))
            stride *= 2
        return strides
    strides = digits_of(count, "halving")
    return [strides[1], strides[0]] + strides[2:]


def offsets_of(digits):
    found = [0]
    for stride, radix in digits:
        found = [low + e * stride for low in found for e in range(radix)]
    return found


class Stream:
    def __init__(self, row_devices, first, rows, kind):
        self.first, self.rows = first, rows
        self.count = chunks_of(row_devices, rows)
        self.row_devices = row_devices
        self.digits = digits_of(self.count, kind)
        self.chunk = rows // self.count

    def parts(self):
        stride, radix = self.digits[0]
        rest = offsets_of(self.digits[1:])
        return [[e * stride + low for low in rest] for e in range(radix)]

    def send(self, value, offset):
        return xor_send(value, "rows", self.row_devices, offset)


def weight_gradient_kernel(streams, pairs, me_ref, *refs):
    operands, outs, scratch = refs[: 2 * pairs], list(refs[2 * pairs : -1]), refs[-1]
    start = 0
    for i in range(pairs):
        left, right = operands[2 * i], operands[2 * i + 1]
        count = left.shape[0]
        scratch[start : start + count] = dot(left[...], right[...], 1, 1).astype(BF16)
        start += count
    for stream in streams:
        for offsets in stream.parts():
            out = outs.pop(0)
            for place, offset in enumerate(offsets):
                chunk = (me_ref[0] % stream.count) ^ offset
                at = pl.multiple_of(stream.first + chunk * stream.chunk, 16)
                out[place * stream.chunk : (place + 1) * stream.chunk] = scratch[pl.ds(at, stream.chunk), :]


def weight_gradient(me, streams, *operands):
    pairs = len(operands) // 2
    total = sum(operands[2 * i].shape[0] for i in range(pairs))
    columns = operands[1].shape[0]
    outs = tuple(
        shape(len(offsets) * stream.chunk, columns, kind=BF16) for stream in streams for offsets in stream.parts()
    )
    found = list(
        kernel(
            functools.partial(weight_gradient_kernel, streams, pairs),
            outs,
            [me],
            operands,
            [pltpu.VMEM((total, columns), BF16)],
        )
    )
    return [[found.pop(0) for _ in stream.parts()] for stream in streams]


def start_stage(stream, parts, stage):
    stride, radix = stream.digits[stage]
    return [stream.send(parts[e], e * stride) for e in range(1, radix)]


def add_stage(stream, parts, received, stage):
    rows = parts[0].shape[0]
    radix = 1 if stage + 1 == len(stream.digits) else stream.digits[stage + 1][1]
    size = rows // radix
    return add([parts[0]] + received, *((e * size, (e + 1) * size, BF16) for e in range(radix)))


def sum_rest(stream, value):
    stride = stream.count
    while stride < stream.row_devices:
        value = add([value, stream.send(value, stride)], (0, value.shape[0], BF16))[0]
        stride *= 2
    return value


def gather_stage(stream, value, stage):
    stride, radix = stream.digits[stage]
    return [value] + [stream.send(value, e * stride) for e in range(1, radix)]


def place_kernel(all_tokens, streams, bounds, me_ref, sums, *refs):
    outs, found, sems = refs[-len(bounds) - 2 : -2], refs[-2], refs[-1]
    pieces = list(refs[: -len(bounds) - 2])
    scale = loss_scale(all_tokens, sums, found.shape[1])
    copies, start = [], 0
    for stream in streams:
        for offsets in stream.parts():
            piece, size = pieces.pop(0), stream.chunk
            for place, offset in enumerate(offsets):
                row = stream.first + ((me_ref[0] % stream.count) ^ offset) * size
                here = slice(start, start + size)
                found[here] = piece[place * size : (place + 1) * size].astype(F32) * scale
                for (first, last), out in zip(bounds, outs):
                    at = pl.ds(pl.multiple_of(jnp.clip(row - first, 0, last - first - size), 16), size)
                    copy = pltpu.make_async_copy(found.at[here], out.at[at, :], sems.at[len(copies)])
                    inside = None if len(bounds) == 1 else (row >= first) & (row < last)
                    copies.append((copy, inside))
                    copy.start() if inside is None else pl.when(inside)(copy.start)
                start += size
    for copy, inside in copies:
        copy.wait() if inside is None else pl.when(inside)(copy.wait)


def place(all_tokens, me, sums, streams, pieces, sizes):
    columns = pieces[0].shape[1]
    bounds, start = [], 0
    for size in sizes:
        bounds.append((start, start + size))
        start += size
    count = len(sizes) * sum(stream.count for stream in streams)
    vmem, hbm = pl.BlockSpec(memory_space=pltpu.VMEM), pl.BlockSpec(memory_space=pltpu.HBM)
    found = pl.pallas_call(
        functools.partial(place_kernel, all_tokens, streams, bounds),
        out_shape=tuple(shape(size, columns) for size in sizes),
        in_specs=[pl.BlockSpec(memory_space=pltpu.SMEM)] + [vmem] * (1 + len(pieces)),
        out_specs=(hbm,) * len(sizes),
        scratch_shapes=[pltpu.VMEM((start, columns), F32), pltpu.SemaphoreType.DMA((count,))],
        compiler_params=pltpu.CompilerParams(vmem_limit_bytes=12 * 1024 * 1024),
        cost_estimate=Order.estimate(),
    )(me, after(sums, Order.last), *pieces)
    Order.last = found[0]
    return found


def live_row(counts_ref, width, first):
    place = lax.broadcasted_iota(jnp.int32, (1, width), 1) + first
    return jnp.where(place < counts_ref[0], 1.0, 0.0)


def loss_scale(all_tokens, sums, width):
    return jnp.full((1, width), all_tokens, F32) / jnp.broadcast_to(sums[7:8, 0:1], (1, width))


def history_kernel(block, mix_ref, counts_ref, cot_ref, history_ref, running_ref, d_mix_ref):
    layers, features, tokens = history_ref.shape
    live = live_row(counts_ref, tokens, 0)
    d_mix_ref[...] = jnp.zeros_like(d_mix_ref)

    def body(history_part):
        for i in range(block // STEP):
            rows = slice(i * STEP, (i + 1) * STEP)
            own = pl.ds(pl.multiple_of(pl.program_id(0) * block + i * STEP, STEP), STEP)
            grad = cot_ref[own].astype(F32) * live
            running = jnp.zeros_like(grad)
            for j in range(layers):
                layer = history_part[j, rows].astype(F32)
                running = running + mix_ref[j] * layer
                terms = grad * layer
                terms = terms[: STEP // 2] + terms[STEP // 2 :]
                d_mix_ref[j] += sum(terms[:, k : k + 128] for k in range(0, tokens, 128))
            running_ref[own] = running

    whole = pl.BlockSpec((layers, block, tokens), lambda i: (0, i, 0))
    pltpu.emit_pipeline(body, grid=(features // block,), in_specs=[whole])(history_ref)


def d_history_kernel(all_tokens, block, mix_ref, counts_ref, cot_ref, sums, d_history_ref):
    layers, features, tokens = d_history_ref.shape
    factor = live_row(counts_ref, tokens, 0) * loss_scale(all_tokens, sums, tokens)

    def body(part):
        for i in range(block // STEP):
            rows = slice(i * STEP, (i + 1) * STEP)
            own = pl.ds(pl.multiple_of(pl.program_id(0) * block + i * STEP, STEP), STEP)
            grad = cot_ref[own].astype(F32) * factor
            for j in range(layers):
                part[j, rows] = (mix_ref[j] * grad).astype(BF16)

    whole = pl.BlockSpec((layers, block, tokens), lambda i: (0, i, 0))
    pltpu.emit_pipeline(body, grid=(features // block,), out_specs=[whole])(d_history_ref)


def history_call(body, outs, in_hbm, out_hbm, scalars, arrays):
    vmem, hbm = pl.BlockSpec(memory_space=pltpu.VMEM), pl.BlockSpec(memory_space=pltpu.HBM)
    arrays = [after(arrays[0], Order.last), *arrays[1:]]
    found = pl.pallas_call(
        body,
        out_shape=outs,
        in_specs=[pl.BlockSpec(memory_space=pltpu.SMEM)] * len(scalars) + [hbm if h else vmem for h in in_hbm],
        out_specs=tuple(hbm if h else vmem for h in out_hbm),
        compiler_params=pltpu.CompilerParams(vmem_limit_bytes=12 * 1024 * 1024),
        cost_estimate=Order.estimate(),
    )(*scalars, *arrays)
    Order.last = found[0]
    return found


def spread_of(load, count, width, total=None):
    zero = jnp.zeros((STEP, width), F32)
    if total is None:
        total = each_rows(count, lambda i, acc: acc + load(i), zero)
    mean = column_sum(total) / count

    def squares(i, acc):
        centred = load(i) - mean
        return acc + centred * centred

    return mean, lax.rsqrt(column_sum(each_rows(count, squares, zero)) / count + EPSILON)


def prepare_kernel(held, *refs):
    refs = refs[held:]
    sources, x_in, (own, norms, cosine, sine), places, sem = refs[:6], refs[6], refs[7:11], refs[11:17], refs[17]
    copies = [pltpu.make_async_copy(*pair, sem.at[i]) for i, pair in enumerate(zip(sources, places))]
    whole = pltpu.make_async_copy(x_in, own, sem.at[6])
    for copy in [*copies, whole]:
        copy.start()
    norms[...] = jnp.zeros_like(norms)
    for copy in copies:
        copy.wait()
    positions, rates, *vectors = places
    for i, ref in enumerate(vectors):
        norms[i : i + 1, : ref.shape[1]] = ref[...]
    angles = positions[...].astype(F32) * rates[...]
    cosine[...] = jnp.cos(angles)
    sine[...] = jnp.sin(angles)
    whole.wait()


def prepare(held, x_in, *sources):
    tokens, part = sources[0].shape[1], sources[2].shape[1]
    rates = sources[1].shape[0]
    vmem = pl.BlockSpec(memory_space=pltpu.VMEM)
    found = pl.pallas_call(
        functools.partial(prepare_kernel, len(held)),
        out_shape=(
            shape(part, tokens, kind=BF16),
            shape(8, -(-part // 128) * 128),
            shape(rates, tokens),
            shape(rates, tokens),
        ),
        in_specs=[vmem] * len(held) + [pl.BlockSpec(memory_space=pltpu.HBM)] * (len(sources) + 1),
        out_specs=(vmem,) * 4,
        scratch_shapes=[pltpu.VMEM(v.shape, v.dtype) for v in sources] + [pltpu.SemaphoreType.DMA((len(sources) + 1,))],
        compiler_params=pltpu.CompilerParams(vmem_limit_bytes=4 * 1024 * 1024),
        cost_estimate=Order.estimate(),
    )(*held, *(pltpu.with_memory_space_constraint(v, pltpu.HBM) for v in (*sources, x_in)))
    Order.last = found[0]
    return found


def norms_kernel(at_ref, n01, n23, norms):
    part = norms.shape[0] // 4
    near, far = n01[...].T, n23[...].T
    for e, norm in enumerate((near, near, far, far)):
        rows = pl.ds(pl.multiple_of((at_ref[0] ^ e) * part, 64), part)
        norms[rows, :] = norm[:part, 8 * (e % 2) : 8 * (e % 2) + 8]


def project_kernel(
    at_ref, x0, x1, x2, x3, norms, cosine, sine, w_qkv, x_all, normed, stats, qkv, project
):
    at = at_ref[0]
    part, tokens = x0.shape
    model = w_qkv.shape[1]
    for e, piece in enumerate((x0, x1, x2, x3)):
        x_all[pl.ds(pl.multiple_of((at ^ e) * part, 64), part), :] = piece[...]
    mean, scale = spread_of(lambda i: x_all[rows_at(i), :].astype(F32), model, tokens)
    stats[0:1] = mean
    stats[1:2] = scale

    def normalise(i, _):
        rows = rows_at(i)
        xhat = (x_all[rows, :].astype(F32) - mean) * scale
        normed[rows, :] = (xhat * norms[rows, 0:1] + norms[rows, 1:2]).astype(BF16)

    each_rows(model, normalise)
    project[...] = dot(w_qkv[...], normed[...], 1, 0)
    width = HEAD_DIM // 2
    for block, factor in ((0, HEAD_DIM ** (-0.5)), (1, 1.0)):
        for start in range(block * part, (block + 1) * part, HEAD_DIM):
            front, back = project[start : start + width], project[start + width : start + HEAD_DIM]
            cos, sin = cosine[...] * factor, sine[...] * factor
            qkv[start : start + width] = (front * cos - back * sin).astype(BF16)
            qkv[start + width : start + HEAD_DIM] = (back * cos + front * sin).astype(BF16)
    qkv[2 * part :] = project[2 * part :].astype(BF16)


def attention_kernel(
    at_ref, qkv, x_all, heads_send, heads_own, x_half, heads_out, probs, scores
):
    at = at_ref[0]
    part, tokens = heads_out.shape
    half = tokens // 2
    for h in range(part // HEAD_DIM):
        head = slice(h * HEAD_DIM, (h + 1) * HEAD_DIM)
        for t in range(2):
            now = slice(t * half, (t + 1) * half)
            count = (t + 1) * half
            query = qkv[head, now]
            key = qkv[part + h * HEAD_DIM : part + (h + 1) * HEAD_DIM, :count]
            value = qkv[2 * part + h * HEAD_DIM : 2 * part + (h + 1) * HEAD_DIM, :count]
            scores[:count] = dot(key, query, 0, 0)

            def masked(i):
                behind = lax.broadcasted_iota(jnp.int32, (STEP, half), 0) + (i * STEP - t * half)
                ahead = lax.broadcasted_iota(jnp.int32, (STEP, half), 1)
                return jnp.where(behind <= ahead, scores[rows_at(i), :], -1e30)

            def raised(found, i, acc):
                found = jnp.exp(found - top)
                scores[rows_at(i), :] = found
                return acc + found

            def settle(i, _):
                rows = rows_at(i)
                probs[h, rows, now] = (scores[rows, :] * divisor).astype(BF16)

            top = each_rows(
                t * half, lambda i, acc: jnp.maximum(acc, scores[rows_at(i), :]), jnp.full((STEP, half), -1e30, F32)
            )
            top = each_rows(count, lambda i, acc: jnp.maximum(acc, masked(i)), top, first=t * half)
            top = jnp.max(top, axis=0, keepdims=True)
            total = each_rows(
                t * half, lambda i, acc: raised(scores[rows_at(i), :], i, acc), jnp.zeros((STEP, half), F32)
            )
            total = each_rows(count, lambda i, acc: raised(masked(i), i, acc), total, first=t * half)
            divisor = 1.0 / column_sum(total)
            each_rows(count, settle)
            heads_out[head, now] = dot(value, probs[h, :count, now], 1, 0).astype(BF16)
    own = pl.multiple_of((at % 2) * half, half)
    other = pl.multiple_of((1 - at % 2) * half, half)
    heads_send[...] = heads_out[:, pl.ds(other, half)]
    heads_own[...] = heads_out[:, pl.ds(own, half)]
    x_half[...] = x_all[:, pl.ds(own, half)]


def output_gradient_kernel(
    at_ref, self_ref, counts_ref, c0, c1, c2, c3, w_down, g_out, d_active, cot_all
):
    at = at_ref[0]
    part, tokens = c0.shape
    half = tokens // 2
    for e, piece in enumerate((c0, c1, c2, c3)):
        cot_all[pl.ds(pl.multiple_of((at ^ e) * part, 64), part), :] = piece[...]
    for place, side in enumerate((at % 2, 1 - at % 2)):
        now = pl.ds(pl.multiple_of(side * half, half), half)
        factor = live_row(counts_ref, half, side * half)

        def scale(i, _, now=now, factor=factor, place=place):
            rows = rows_at(i)
            grad = cot_all[rows, now].astype(F32) * factor
            g_out[rows, place * half : (place + 1) * half] = (self_ref[0] * grad).astype(BF16)

        each_rows(cot_all.shape[0], scale)
    d_active[...] = dot(w_down[...], g_out[...], 1, 0)


def rows_kernel(at_ref, *refs):
    out = refs[-1]
    for e, piece in enumerate(refs[:-1]):
        rows = piece.shape[0]
        out[pl.ds(pl.multiple_of((at_ref[0] ^ e) * rows, 64), rows), :] = piece[...]


def middle_kernel(at_ref, pair, pair_far, w_all, x_half, norms, middle, stats, normed, heads):
    model, half = x_half.shape
    part = pair.shape[0] // 2
    for e, piece in enumerate((pair[:part], pair[part:], pair_far[:part], pair_far[part:])):
        heads[pl.ds(pl.multiple_of((at_ref[0] ^ e) * part, 64), part), :] = piece
    middle[...] = dot(w_all[...], heads[...], 0, 0)

    def add(i, acc):
        rows = rows_at(i)
        found = x_half[rows, :].astype(F32) + middle[rows, :]
        middle[rows, :] = found
        return acc + found

    total = each_rows(model, add, jnp.zeros((STEP, half), F32))
    mean, scale = spread_of(lambda i: middle[rows_at(i), :], model, half, total)
    stats[0:1] = mean
    stats[1:2] = scale

    def normalise(i, _):
        rows = rows_at(i)
        xhat = (middle[rows, :] - mean) * scale
        normed[rows, :] = (xhat * norms[rows, 2:3] + norms[rows, 3:4]).astype(BF16)

    each_rows(model, normalise)


def feed_forward_kernel(own, other, w_up, d_active, normed, active, d_hidden, send, keep, hidden):
    half = own.shape[1]
    normed[:, :half] = own[...]
    normed[:, half:] = other[...]
    hidden[...] = dot(w_up[...], normed[...], 0, 0)

    def bend(i, _):
        rows = rows_at(i)
        u = hidden[rows, :]
        squared = u * u
        curve = jnp.tanh(0.7978845608028654 * u * (1.0 + 0.044715 * squared))
        lifted = 0.5 * (1.0 + curve)
        active[rows, :] = (u * lifted).astype(BF16)
        slope = lifted + u * (0.5 * (1.0 - curve * curve)) * (
            0.7978845608028654 + (3 * 0.044715 * 0.7978845608028654) * squared
        )
        d_hidden[rows, :] = (slope * d_active[rows, :]).astype(BF16)

    each_rows(hidden.shape[0], bend)
    send[...] = dot(w_up[...], d_hidden[:, half:], 1, 0).astype(BF16)
    keep[...] = dot(w_up[...], d_hidden[:, :half], 1, 0)


def store_blocks(at, total, part, near, *outs):
    for e, out in zip(near, outs):
        out[...] = total[pl.ds(pl.multiple_of((at ^ e) * part, 64), part), :].astype(out.dtype)


def output_kernel(at_ref, counts_ref, active, w_down, middle, cot_all, send, send_far, keep, keep_far, product, total):
    at = at_ref[0]
    model, half = middle.shape
    part = send.shape[0]
    own = pl.ds(pl.multiple_of((at % 2) * half, half), half)
    other = pl.ds(pl.multiple_of((1 - at % 2) * half, half), half)
    total[:, own] = dot(w_down[...], active[:, :half], 0, 0) + 0.5 * middle[...]
    total[:, other] = dot(w_down[...], active[:, half:], 0, 0)
    live = live_row(counts_ref, 2 * half, 0)

    def weigh(i, acc):
        rows = rows_at(i)
        return acc + fold_lanes(total[rows, :] * (cot_all[rows, :].astype(F32) * live))

    product[...] = each_rows(model, weigh, jnp.zeros((STEP, 128), F32))
    store_blocks(at, total, part, (1, 3, 0, 2), send, send_far, keep, keep_far)


def fold_lanes(value):
    return sum(value[:, k : k + 128] for k in range(0, value.shape[1], 128))


def as_row(columns):
    return column_sum(columns[...].T)


def middle_gradient_kernel(
    at_ref, self_ref, counts_ref, chip, received, middle, stats, cot_all, norms,
    d_middle, g_mid, gains, d_normed, gain_sums, bias_sums,
):
    model, half = chip.shape
    mean, scale = stats[0:1], stats[1:2]
    zero = jnp.zeros((STEP, half), F32)

    def sums(i, acc):
        rows = rows_at(i)
        grad = chip[rows, :] + received[rows, :].astype(F32)
        d_normed[rows, :] = grad
        xhat = (middle[rows, :] - mean) * scale
        both = grad * xhat
        gain_sums[rows, :] = fold_lanes(both)
        bias_sums[rows, :] = fold_lanes(grad)
        gain = norms[rows, 2:3]
        return acc[0] + grad * gain, acc[1] + both * gain

    first, second = (column_sum(v) / model for v in each_rows(model, sums, (zero, zero)))
    side = (at_ref[0] % 2) * half
    factor = self_ref[0] * live_row(counts_ref, half, side)
    own = pl.ds(pl.multiple_of(side, half), half)

    def finish(i, _):
        rows = rows_at(i)
        xhat = (middle[rows, :] - mean) * scale
        found = cot_all[rows, own].astype(F32) * factor + scale * (
            d_normed[rows, :] * norms[rows, 2:3] - first - xhat * second
        )
        d_middle[rows, :] = found
        g_mid[rows, :] = found.astype(BF16)

    each_rows(model, finish)
    gains[0:1] = as_row(gain_sums)
    gains[1:2] = as_row(bias_sums)


def attention_gradient_kernel(
    at_ref, own, other, w_out, qkv, probs, cosine, sine,
    d_project, g_mid, d_heads, d_scores, products, d_queries, d_keys, d_values,
):
    at = at_ref[0]
    half = own.shape[1]
    part = w_out.shape[0]
    g_mid[:, pl.ds(pl.multiple_of((at % 2) * half, half), half)] = own[...]
    g_mid[:, pl.ds(pl.multiple_of((1 - at % 2) * half, half), half)] = other[...]
    d_heads[...] = dot(w_out[...], g_mid[...], 1, 0).astype(BF16)
    width = HEAD_DIM // 2
    for h in range(part // HEAD_DIM):
        head = slice(h * HEAD_DIM, (h + 1) * HEAD_DIM)
        query = qkv[head]
        key = qkv[part + h * HEAD_DIM : part + (h + 1) * HEAD_DIM]
        value = qkv[2 * part + h * HEAD_DIM : 2 * part + (h + 1) * HEAD_DIM]
        for t in range(2):
            now = slice(t * half, (t + 1) * half)
            count = (t + 1) * half
            products[:count] = dot(value[:, :count], d_heads[head, now], 0, 0)

            def weigh(i, acc):
                rows = rows_at(i)
                return acc + products[rows, :] * probs[h, rows, now].astype(F32)

            inner = column_sum(each_rows(count, weigh, jnp.zeros((STEP, half), F32)))

            def settle(i, _):
                rows = rows_at(i)
                d_scores[rows, :] = (probs[h, rows, now].astype(F32) * (products[rows, :] - inner)).astype(BF16)

            each_rows(count, settle)
            d_queries[:, now] = dot(key[:, :count], d_scores[:count], 1, 0) * HEAD_DIM ** (-0.5)
            d_key = dot(query[:, now], d_scores[:count], 1, 1)
            d_value = dot(d_heads[head, now], probs[h, :count, now], 1, 1)
            if t == 0:
                d_keys[:, :half] = d_key
                d_values[:, :half] = d_value
            else:
                d_keys[:, :half] += d_key[:, :half]
                d_values[:, :half] += d_value[:, :half]
                d_keys[:, half:] = d_key[:, half:]
                d_values[:, half:] = d_value[:, half:]
        for block, found in ((0, d_queries), (1, d_keys)):
            start = block * part + h * HEAD_DIM
            front, back = found[:width], found[width:]
            d_project[start : start + width] = (front * cosine[...] + back * sine[...]).astype(BF16)
            d_project[start + width : start + HEAD_DIM] = (back * cosine[...] - front * sine[...]).astype(BF16)
        d_project[2 * part + h * HEAD_DIM : 2 * part + (h + 1) * HEAD_DIM] = d_values[...].astype(BF16)


def input_gradient_kernel(
    width, at_ref, counts_ref, d_project, w_qkv, x_all, stats, d_middle, norms, gains,
    send, send_far, keep, keep_far, sums, total, gain_sums, bias_sums,
):
    at = at_ref[0]
    model, half = d_middle.shape
    tokens = x_all.shape[1]
    part = send.shape[0]
    total[...] = dot(w_qkv[...], d_project[...], 0, 0)
    mean, scale = stats[0:1], stats[1:2]
    zero = jnp.zeros((STEP, tokens), F32)
    own = pl.ds(pl.multiple_of((at % 2) * half, half), half)

    def body(i, acc):
        rows = rows_at(i)
        grad = total[rows, :]
        xhat = (x_all[rows, :].astype(F32) - mean) * scale
        both = grad * xhat
        gain_sums[rows, :] = fold_lanes(both)
        bias_sums[rows, :] = fold_lanes(grad)
        gain = norms[rows, 0:1]
        lifted = grad * gain
        total[rows, :] = lifted * scale
        total[rows, own] += 0.5 * d_middle[rows, :]
        return acc[0] + lifted, acc[1] + both * gain

    first, second = each_rows(model, body, (zero, zero))
    store_blocks(at, total, part, (1, 3, 0, 2), send, send_far, keep, keep_far)
    sums[...] = jnp.zeros_like(sums)
    sums[0:1] = as_row(gain_sums)
    sums[1:2] = as_row(bias_sums)
    sums[2:4] = 0.5 * gains[...]
    sums[4:5, :tokens] = column_sum(first) / model
    sums[5:6, :tokens] = column_sum(second) / model
    sums[7:8] = jnp.zeros((1, model), F32) + counts_ref[0].astype(F32) / width


def mixed_kernel(self_ref, own, near, far, running, d_mix, product, sums, mixed, all_sums, table):
    layers = d_mix.shape[0]

    def body(i, _):
        rows = rows_at(i)
        output = own[rows, :] + near[rows, :].astype(F32) + far[rows, :].astype(F32)
        mixed[rows, :] = (self_ref[0] * output + running[rows, :]).astype(BF16)

    each_rows(own.shape[0], body)
    table[...] = jnp.zeros_like(table)
    table[:layers] = jnp.sum(d_mix[...], axis=1)
    table[layers : layers + 1] = column_sum(product[...])
    all_sums[...] = sums[...]
    all_sums[6:7, :128] = as_row(table)


def ends_kernel(all_tokens, layers, width, at_ref, sums, d_mix, d_self, *ends):
    part = ends[0].shape[1]
    scale = loss_scale(all_tokens, sums, sums.shape[1])
    d_mix[...] = sums[6:7, :layers] * scale[:, :layers]
    d_self[...] = sums[6:7, layers : layers + 1] * scale[:, :1]
    for i, end in enumerate(ends):
        scaled = sums[i : i + 1] * scale
        found = scaled[:, :part]
        for w in range(1, width):
            found = jnp.where(at_ref[0] == w, scaled[:, w * part : (w + 1) * part], found)
        end[...] = found


def d_input_kernel(own, near, far, x_in, stats, row_sums, found):
    part, tokens = own.shape
    mean, scale = stats[0:1], stats[1:2]
    first, second = row_sums[4:5, :tokens], row_sums[5:6, :tokens]

    def body(i, _):
        rows = rows_at(i)
        xhat = (x_in[rows, :].astype(F32) - mean) * scale
        total = own[rows, :] + near[rows, :].astype(F32) + far[rows, :].astype(F32)
        found[rows, :] = total - scale * (first + xhat * second)

    each_rows(part, body)


def scale_kernel(all_tokens, found, sums, d_input):
    factor = loss_scale(all_tokens, sums, found.shape[1])

    def body(i, _):
        d_input[rows_at(i), :] = found[rows_at(i), :] * factor

    each_rows(found.shape[0], body)


def local(
    width,
    row_devices,
    x_in,
    history,
    cotangent,
    counts,
    positions,
    mix_weights,
    self_weight,
    first_norm_gain,
    first_norm_bias,
    w_qkv,
    w_out,
    second_norm_gain,
    second_norm_bias,
    w_up,
    w_down,
):
    part, tokens = x_in.shape
    model = w_out.shape[1]
    hidden_units = w_up.shape[1]
    half = tokens // 2
    layers = mix_weights.shape[0]
    all_tokens = float(tokens * row_devices)
    at = lax.axis_index("width").astype(jnp.int32)[None]
    me = lax.axis_index("rows").astype(jnp.int32)[None]
    Order.last, Order.front = None, FRONT
    to_width = lambda value, offset: xor_send(value, "width", width, offset)
    to_row = lambda value, offset: xor_send(value, "rows", row_devices, offset)
    w_qkv = w_qkv.reshape(3 * part, model)
    rates = 1.0 / 10000.0 ** (np.arange(HEAD_DIM // 2) * 2.0 / HEAD_DIM)
    x_in, cotangent, counts = after((x_in, cotangent, counts), at, me)

    x_far, x_near = to_width(x_in, 2), to_width(x_in, 1)
    x_own, norms, cosine, sine = prepare(
        [x_near],
        x_in,
        positions[None, :],
        jnp.asarray(rates[:, None], F32),
        *(v[None, :] for v in (first_norm_gain, first_norm_bias, second_norm_gain, second_norm_bias)),
    )
    norms_near = join([norms, to_width(norms, 1)])
    norms_far = to_width(norms_near, 2)
    norms = kernel(norms_kernel, shape(model, 8), [at], [norms_near, norms_far])
    x_both = to_width(after(x_far, norms), 1)
    w_now = after(w_out, norms_near)
    w_far, w_near = to_width(w_now, 2), to_width(w_now, 1)

    x_all, normed_one, stats_one, qkv = kernel(
        project_kernel,
        (
            shape(model, tokens, kind=BF16),
            shape(model, tokens, kind=BF16),
            shape(2, tokens),
            shape(3 * part, tokens, kind=BF16),
        ),
        [at],
        [x_own, x_near, x_far, x_both, norms, cosine, sine, w_qkv],
        [pltpu.VMEM((3 * part, tokens), F32)],
    )
    heads_send, heads_own, x_half, heads_out, probs = kernel(
        attention_kernel,
        (
            shape(part, half, kind=BF16),
            shape(part, half, kind=BF16),
            shape(model, half, kind=BF16),
            shape(part, tokens, kind=BF16),
            shape(part // HEAD_DIM, tokens, tokens, kind=BF16),
        ),
        [at],
        [qkv, x_all],
        [pltpu.VMEM((tokens, half), F32)],
    )
    pair = join([after(heads_own, w_far), to_width(heads_send, 1)])
    pair_far = to_width(pair, 2)
    cot_now = after(cotangent, pair)
    cot_far, cot_near = to_width(cot_now, 2), to_width(cot_now, 1)
    w_both = to_width(after(w_far, pair), 1)

    w_all = kernel(rows_kernel, shape(model, model, kind=BF16), [at], [w_out, w_near, w_far, w_both])
    middle, stats_two, normed_own = kernel(
        middle_kernel,
        (shape(model, half), shape(2, half), shape(model, half, kind=BF16)),
        [at],
        [pair, pair_far, w_all, x_half, norms],
        [pltpu.VMEM((model, half), BF16)],
    )
    normed_near = to_width(normed_own, 1)
    cot_both = to_width(after(cot_far, middle), 1)
    g_out, d_active, cot_all = kernel(
        output_gradient_kernel,
        (shape(model, tokens, kind=BF16), shape(hidden_units, tokens), shape(model, tokens, kind=BF16)),
        [at, self_weight, counts],
        [cotangent, cot_near, cot_far, cot_both, w_down],
    )

    normed_two, active, d_hidden, send, keep = kernel(
        feed_forward_kernel,
        (
            shape(model, tokens, kind=BF16),
            shape(hidden_units, tokens, kind=BF16),
            shape(hidden_units, tokens, kind=BF16),
            shape(model, half, kind=BF16),
            shape(model, half),
        ),
        [],
        [normed_own, normed_near, w_up, d_active],
        [pltpu.VMEM((hidden_units, tokens), F32)],
    )

    v = Values()
    v.send, v.keep = send, keep
    down = Stream(row_devices, 0, hidden_units, "halving")
    up = Stream(row_devices, 0, model, "crossed")
    first = Stream(row_devices, 0, 2 * part, "halving")
    second = Stream(row_devices, 2 * part, 2 * part, "crossed")
    strides = [1 << i for i in range(row_devices.bit_length() - 1)]
    blocks = (shape(part, tokens, kind=BF16),) * 2 + (shape(part, tokens),) * 2
    last = len(down.digits) - 1

    def scatter(stream, stage):
        stream.held = add_stage(stream, stream.held, stream.got, stage)
        stream.got = start_stage(stream, stream.held, stage + 1)

    def turn(stream):
        value = sum_rest(stream, add_stage(stream, stream.held, stream.got, last)[0])
        stream.pieces = gather_stage(stream, value, last)

    def gather(stream, stage):
        stream.pieces = gather_stage(stream, join(stream.pieces), stage)

    def steps_of(stream):
        return (
            *(functools.partial(scatter, stream, stage) for stage in range(last)),
            functools.partial(turn, stream),
            *(functools.partial(gather, stream, stage) for stage in range(last - 1, -1, -1)),
        )

    def begin(streams, found):
        for stream, parts in zip(streams, found):
            stream.held, stream.got = parts, start_stage(stream, parts, 0)

    def down_product():
        begin([down], weight_gradient(me, [down], active, g_out))

    def up_product():
        begin([up], weight_gradient(me, [up], normed_two, d_hidden))

    def tail_product():
        found = weight_gradient(me, [first, second], v.d_project, normed_one, heads_out, v.g_mid)
        begin([first, second], found)

    def middle_sum():
        v.chip, sent = add([v.keep, to_width(v.send, 1)], (0, model, F32), (0, model, BF16))
        v.received = to_width(sent, 2)

    def output_product():
        near, far, v.out, v.out_far, v.product = kernel(
            output_kernel,
            blocks + (shape(STEP, 128),),
            [at, counts],
            [active, w_down, middle, cot_all],
            [pltpu.VMEM((model, tokens), F32)],
        )
        v.out_got = to_width(near, 1), to_width(far, 1)

    def history_sums():
        v.running, v.d_mix = history_call(
            functools.partial(history_kernel, 32),
            (shape(part, tokens), shape(layers, STEP // 2, 128)),
            (False, True),
            (False, False),
            [mix_weights, counts],
            [cotangent, pltpu.with_memory_space_constraint(history, pltpu.HBM)],
        )

    def output_sum():
        v.out_last = to_width(add([v.out_far, v.out_got[1]], (0, part, BF16))[0], 2)

    def middle_gradient():
        v.d_middle, v.g_own, v.gains = kernel(
            middle_gradient_kernel,
            (shape(model, half), shape(model, half, kind=BF16), shape(2, model)),
            [at, self_weight, counts],
            [v.chip, v.received, middle, stats_two, cot_all, norms],
            [pltpu.VMEM((model, half), F32), pltpu.VMEM((model, 128), F32), pltpu.VMEM((model, 128), F32)],
        )
        v.g_other = to_width(v.g_own, 1)

    def attention_gradient():
        v.d_project, v.g_mid = kernel(
            attention_gradient_kernel,
            (shape(3 * part, tokens, kind=BF16), shape(model, tokens, kind=BF16)),
            [at],
            [v.g_own, v.g_other, w_out, qkv, probs, cosine, sine],
            [
                pltpu.VMEM((part, tokens), BF16),
                pltpu.VMEM((tokens, half), BF16),
                pltpu.VMEM((tokens, half), F32),
                pltpu.VMEM((HEAD_DIM, tokens), F32),
                pltpu.VMEM((HEAD_DIM, tokens), F32),
                pltpu.VMEM((HEAD_DIM, tokens), F32),
            ],
        )

    def input_gradient():
        near, far, v.own_in, v.in_far, v.sums = kernel(
            functools.partial(input_gradient_kernel, width),
            blocks + (shape(8, model),),
            [at, counts],
            [v.d_project, w_qkv, x_all, stats_one, v.d_middle, norms, v.gains],
            [pltpu.VMEM((model, tokens), F32), pltpu.VMEM((model, 128), F32), pltpu.VMEM((model, 128), F32)],
        )
        v.in_got = to_width(near, 1), to_width(far, 1)

    def input_sum():
        v.in_last = to_width(add([v.in_far, v.in_got[1]], (0, part, BF16))[0], 2)

    def input_total():
        v.in_total = kernel(
            d_input_kernel,
            shape(part, tokens),
            [],
            [v.own_in, v.in_got[0], v.in_last, x_own, stats_one, v.row_sums],
        )

    def mix():
        v.mixed, v.sums = kernel(
            mixed_kernel,
            (shape(part, tokens, kind=BF16), shape(8, model)),
            [self_weight],
            [
                v.out,
                v.out_got[0],
                v.out_last,
                v.running,
                v.d_mix,
                v.product,
                v.sums,
            ],
            [pltpu.VMEM((128, 128), F32)],
        )
        v.sums_got = to_width(v.sums, 1)

    def sums_step(*sends):
        for send_on in sends:
            v.sums = add([v.sums, v.sums_got], (0, 8, F32))[0]
            v.sums_got = send_on(v.sums)

    def sums_1():
        sums_step(lambda value: to_width(value, 2))

    def sums_2():
        sums_step(row_send(strides[0]))
        v.row_sums = v.sums

    def sums_3():
        sums_step(row_send(strides[1]))

    def sums_4():
        sums_step(*(row_send(stride) for stride in strides[2:]))

    def last_sums():
        v.sums = add([v.sums, v.sums_got], (0, 8, F32))[0]

    def scale_input():
        v.d_input = kernel(
            functools.partial(scale_kernel, all_tokens), shape(part, tokens), [], [v.in_total, v.sums]
        )

    def history_gradient():
        v.d_history = history_call(
            functools.partial(d_history_kernel, all_tokens, 32),
            (shape(*history.shape, kind=BF16),),
            (False, False),
            (True,),
            [mix_weights, counts],
            [cotangent, v.sums],
        )[0]

    def ends():
        v.ends = kernel(
            functools.partial(ends_kernel, all_tokens, layers, width),
            (shape(1, layers), shape(1, 1)) + (shape(1, part),) * 4,
            [at],
            [v.sums],
        )

    def placed(streams, *sizes):
        pieces = [piece for stream in streams for piece in stream.pieces]
        return place(all_tokens, me, v.sums, streams, pieces, sizes)

    def place_down():
        v.d_w_down = placed([down], hidden_units)[0]

    def place_up():
        v.d_w_up = placed([up], model)[0]

    def place_tail():
        v.d_w_qkv, v.d_w_out = placed([first, second], 3 * part, part)

    row_send = lambda stride: lambda value: to_row(value, stride)
    down_1, down_2, down_3, down_4, down_5 = steps_of(down)
    up_1, up_2, up_3, up_4, up_5 = steps_of(up)
    first_1, first_2, first_3, first_4, first_5 = steps_of(first)
    second_1, second_2, second_3, second_4, second_5 = steps_of(second)
    schedule = (
        (down_product, 2),
        (middle_sum, 200),
        (up_product, 10),
        (history_sums, 10),
        (output_product, 0.3),
        (middle_gradient, 8),
        (output_sum, 1),
        (down_1, 10),
        (up_1, 200),
        (attention_gradient, 200),
        (tail_product, 4),
        (down_2, 4),
        (up_2, 0.1),
        (input_gradient, 1),
        (mix, 4),
        (first_1, 1),
        (second_1, 1),
        (up_3, 100),
        (down_3, 0.1),
        (second_2, 1),
        (first_2, 0.1),
        (sums_1, 1),
        (sums_2, 1),
        (input_sum, 1),
        (sums_3, 1),
        (up_4, 0.1),
        (down_4, 200),
        (up_5, 1),
        (sums_4, 1),
        (first_3, 1),
        (second_3, 2),
        (down_5, 200),
        (input_total, 1),
        (first_4, 1),
        (second_4, 40),
        (last_sums, 0.1),
        (scale_input, 0.1),
        (first_5, 8),
        (ends, 0.3),
        (second_5, 0.3),
        (place_up, 40),
        (place_down, 2),
        (history_gradient, 4),
        (place_tail, 0.1),
    )
    for step, weight in schedule:
        Order.cost = weight
        step()
    d_mix, d_self, *vectors = v.ends
    return (
        v.mixed,
        v.d_input,
        v.d_history,
        d_mix[0],
        d_self[0],
        vectors[0][0],
        vectors[1][0],
        v.d_w_qkv.reshape(3, part, model),
        v.d_w_out,
        vectors[2][0],
        vectors[3][0],
        v.d_w_up,
        v.d_w_down,
    )


def solution(mesh):
    return jax.shard_map(
        functools.partial(local, mesh.shape["width"], mesh.shape["rows"]),
        mesh=mesh,
        in_specs=(
            P("width", "rows"),
            P(None, "width", "rows"),
            P("width", "rows"),
            P("rows"),
            P("rows"),
            P(),
            P(),
            P("width"),
            P("width"),
            P(None, "width", None),
            P("width", None),
            P("width"),
            P("width"),
            P(None, "width"),
            P("width", None),
        ),
        out_specs=(
            P("width", "rows"),
            P("width", "rows"),
            P(None, "width", "rows"),
            P(),
            P(),
            P("width"),
            P("width"),
            P(None, "width", None),
            P("width", None),
            P("width"),
            P("width"),
            P(None, "width"),
            P("width", None),
        ),
        check_vma=False,
    )
```

```python
import functools

import jax
import jax.numpy as jnp
import numpy as np
from jax import lax
from jax.experimental import pallas as pl
from jax.experimental.pallas import tpu as pltpu
from jax.sharding import PartitionSpec as P

HEAD_DIM = 64
EPSILON = 1e-05
BF16 = jnp.bfloat16
F32 = jnp.float32
STEP = 16


SCHEDULE = (
    ("down", 10),
    ("chip", 8),
    ("up", 10),
    ("out", 100),
    ("middle", 10),
    ("out_sum", 10),
    ("down1", 10),
    ("up1", 100),
    ("attention", 8),
    ("tail", 4),
    ("down2", 100),
    ("up2", 0.3),
    ("input", 1),
    ("mix", 8),
    ("first1", 1),
    ("second1", 1),
    ("up3", 100),
    ("down3", 1),
    ("first2", 2),
    ("sums1", 4),
    ("sums2", 1),
    ("input_sum", 1),
    ("second2", 1),
    ("sums3", 1),
    ("up4", 2),
    ("sums4", 1),
    ("down4", 4),
    ("first3", 40),
    ("input_total", 1),
    ("second3", 2),
    ("down5", 1),
    ("first4", 200),
    ("up5", 0.3),
    ("second4", 16),
    ("sums5", 1),
    ("scale", 0.1),
    ("first5", 40),
    ("ends", 1),
    ("history", 1),
    ("place_down", 1),
    ("second5", 200),
    ("place_up", 4),
    ("place_tail", 1),
)

FRONT = (1, 1, 1, 1, 1, 1, 10, 10, 10, 10)


def shape(*dims, kind=F32):
    return jax.ShapeDtypeStruct(dims, kind)


class Values:
    pass


class Order:
    last = None
    cost = 0
    front = ()

    @classmethod
    def estimate(cls):
        if cls.front:
            cls.cost, *cls.front = cls.front
        return pl.CostEstimate(flops=int(cls.cost * 10**8), bytes_accessed=1024, transcendentals=0)


def kernel(body, outs, scalars, arrays, scratch=(), limit=12, streamed=()):
    arrays = list(arrays)
    if Order.last is not None:
        arrays[0] = after(arrays[0], Order.last)
    spaces = [pltpu.VMEM] * len(arrays) + [pltpu.HBM] * len(streamed)
    arrays += [pltpu.with_memory_space_constraint(v, pltpu.HBM) for v in streamed]
    found = pl.pallas_call(
        body,
        out_shape=outs,
        in_specs=[pl.BlockSpec(memory_space=pltpu.SMEM)] * len(scalars)
        + [pl.BlockSpec(memory_space=space) for space in spaces],
        out_specs=jax.tree.map(lambda _: pl.BlockSpec(memory_space=pltpu.VMEM), outs),
        scratch_shapes=list(scratch),
        compiler_params=pltpu.CompilerParams(vmem_limit_bytes=limit * 1024 * 1024),
        cost_estimate=Order.estimate(),
    )(*scalars, *arrays)
    Order.last = jax.tree.leaves(found)[0]
    return found


def after(value, *others):
    return lax.optimization_barrier((value, others))[0]


def dot(left, right, left_dim, right_dim):
    return lax.dot_general(left, right, (((left_dim,), (right_dim,)), ((), ())), preferred_element_type=F32)


def rows_at(i):
    return pl.ds(pl.multiple_of(i * STEP, STEP), STEP)


def each_rows(count, body, start=None, first=0):
    return lax.fori_loop(first // STEP, count // STEP, body, start, unroll=8)


def column_sum(value):
    return jnp.sum(value, axis=0, keepdims=True)


def xor_send(value, axis, size, offset):
    return lax.ppermute(value, axis, [(i, i ^ offset) for i in range(size)])


def add_kernel(count, cuts, *refs):
    parts, outs = refs[:count], refs[count:]

    def one(rows):
        found = parts[0][rows, :].astype(F32)
        for part in parts[1:]:
            found = found + part[rows, :].astype(F32)
        return found

    for (first, last), out in zip(cuts, outs):
        if (last - first) % STEP:
            out[...] = one(slice(first, last)).astype(out.dtype)
        else:

            def body(i, _, first=first, out=out):
                out[rows_at(i), :] = one(pl.ds(pl.multiple_of(first + i * STEP, STEP), STEP)).astype(out.dtype)

            each_rows(last - first, body)


def add(parts, *cuts):
    columns = parts[0].shape[1]
    outs = tuple(shape(last - first, columns, kind=kind) for first, last, kind in cuts)
    return list(kernel(functools.partial(add_kernel, len(parts), [cut[:2] for cut in cuts]), outs, [], parts))


def sum_small(value, axis, size):
    stride = 1
    while stride < size:
        value = add([value, xor_send(value, axis, size, stride)], (0, value.shape[0], F32))[0]
        stride *= 2
    return value


def join_kernel(*refs):
    out, start = refs[-1], 0
    for piece in refs[:-1]:
        out[start : start + piece.shape[0]] = piece[...]
        start += piece.shape[0]


def join(pieces):
    rows = sum(piece.shape[0] for piece in pieces)
    return kernel(join_kernel, shape(rows, pieces[0].shape[1], kind=pieces[0].dtype), [], pieces)


def chunks_of(count, rows):
    count = min(count, 8)
    while rows % (16 * count):
        count //= 2
    return count


def digits_of(count, kind):
    if kind == "halving":
        strides = []
        stride = 1
        while stride < count:
            strides.append((stride, 2))
            stride *= 2
        return strides
    strides = digits_of(count, "halving")
    return [strides[1], strides[0]] + strides[2:]


def offsets_of(digits):
    found = [0]
    for stride, radix in digits:
        found = [low + e * stride for low in found for e in range(radix)]
    return found


class Stream:
    def __init__(self, row_devices, first, rows, kind):
        self.first, self.rows = first, rows
        self.count = chunks_of(row_devices, rows)
        self.row_devices = row_devices
        self.digits = digits_of(self.count, kind)
        self.chunk = rows // self.count

    def parts(self):
        stride, radix = self.digits[0]
        rest = offsets_of(self.digits[1:])
        return [[e * stride + low for low in rest] for e in range(radix)]

    def send(self, value, offset):
        return xor_send(value, "rows", self.row_devices, offset)


def weight_gradient_kernel(streams, pairs, me_ref, *refs):
    operands, outs, scratch = refs[: 2 * pairs], list(refs[2 * pairs : -1]), refs[-1]
    start = 0
    for i in range(pairs):
        left, right = operands[2 * i], operands[2 * i + 1]
        count = left.shape[0]
        scratch[start : start + count] = dot(left[...], right[...], 1, 1).astype(BF16)
        start += count
    for stream in streams:
        for offsets in stream.parts():
            out = outs.pop(0)
            for place, offset in enumerate(offsets):
                chunk = (me_ref[0] % stream.count) ^ offset
                at = pl.multiple_of(stream.first + chunk * stream.chunk, 16)
                out[place * stream.chunk : (place + 1) * stream.chunk] = scratch[pl.ds(at, stream.chunk), :]


def weight_gradient(me, streams, *operands):
    pairs = len(operands) // 2
    total = sum(operands[2 * i].shape[0] for i in range(pairs))
    columns = operands[1].shape[0]
    outs = tuple(
        shape(len(offsets) * stream.chunk, columns, kind=BF16) for stream in streams for offsets in stream.parts()
    )
    found = list(
        kernel(
            functools.partial(weight_gradient_kernel, streams, pairs),
            outs,
            [me],
            operands,
            [pltpu.VMEM((total, columns), BF16)],
        )
    )
    return [[found.pop(0) for _ in stream.parts()] for stream in streams]


def start_stage(stream, parts, stage):
    stride, radix = stream.digits[stage]
    return [stream.send(parts[e], e * stride) for e in range(1, radix)]


def add_stage(stream, parts, received, stage):
    rows = parts[0].shape[0]
    radix = 1 if stage + 1 == len(stream.digits) else stream.digits[stage + 1][1]
    size = rows // radix
    return add([parts[0]] + received, *((e * size, (e + 1) * size, BF16) for e in range(radix)))


def sum_rest(stream, value):
    stride = stream.count
    while stride < stream.row_devices:
        value = add([value, stream.send(value, stride)], (0, value.shape[0], BF16))[0]
        stride *= 2
    return value


def gather_stage(stream, value, stage):
    stride, radix = stream.digits[stage]
    return [value] + [stream.send(value, e * stride) for e in range(1, radix)]


def place_kernel(all_tokens, streams, bounds, me_ref, sums, *refs):
    outs, found, sems = refs[-len(bounds) - 2 : -2], refs[-2], refs[-1]
    pieces = list(refs[: -len(bounds) - 2])
    scale = loss_scale(all_tokens, sums, found.shape[1])
    copies, start = [], 0
    for stream in streams:
        for offsets in stream.parts():
            piece, size = pieces.pop(0), stream.chunk
            for place, offset in enumerate(offsets):
                row = stream.first + ((me_ref[0] % stream.count) ^ offset) * size
                here = slice(start, start + size)
                found[here] = piece[place * size : (place + 1) * size].astype(F32) * scale
                for (first, last), out in zip(bounds, outs):
                    at = pl.ds(pl.multiple_of(jnp.clip(row - first, 0, last - first - size), 16), size)
                    copy = pltpu.make_async_copy(found.at[here], out.at[at, :], sems.at[len(copies)])
                    inside = None if len(bounds) == 1 else (row >= first) & (row < last)
                    copies.append((copy, inside))
                    copy.start() if inside is None else pl.when(inside)(copy.start)
                start += size
    for copy, inside in copies:
        copy.wait() if inside is None else pl.when(inside)(copy.wait)


def place(all_tokens, me, sums, streams, pieces, sizes):
    columns = pieces[0].shape[1]
    bounds, start = [], 0
    for size in sizes:
        bounds.append((start, start + size))
        start += size
    count = len(sizes) * sum(stream.count for stream in streams)
    vmem, hbm = pl.BlockSpec(memory_space=pltpu.VMEM), pl.BlockSpec(memory_space=pltpu.HBM)
    found = pl.pallas_call(
        functools.partial(place_kernel, all_tokens, streams, bounds),
        out_shape=tuple(shape(size, columns) for size in sizes),
        in_specs=[pl.BlockSpec(memory_space=pltpu.SMEM)] + [vmem] * (1 + len(pieces)),
        out_specs=(hbm,) * len(sizes),
        scratch_shapes=[pltpu.VMEM((start, columns), F32), pltpu.SemaphoreType.DMA((count,))],
        compiler_params=pltpu.CompilerParams(vmem_limit_bytes=12 * 1024 * 1024),
        cost_estimate=Order.estimate(),
    )(me, after(sums, Order.last), *pieces)
    Order.last = found[0]
    return found


def live_row(counts_ref, width, first):
    place = lax.broadcasted_iota(jnp.int32, (1, width), 1) + first
    return jnp.where(place < counts_ref[0], 1.0, 0.0)


def loss_scale(all_tokens, sums, width):
    return jnp.full((1, width), all_tokens, F32) / jnp.broadcast_to(sums[7:8, 0:1], (1, width))


def history_kernel(block, mix_ref, counts_ref, cot_ref, history_ref, running_ref, d_mix_ref):
    layers, features, tokens = history_ref.shape
    live = live_row(counts_ref, tokens, 0)
    d_mix_ref[...] = jnp.zeros_like(d_mix_ref)

    def body(history_part):
        for i in range(block // STEP):
            rows = slice(i * STEP, (i + 1) * STEP)
            own = pl.ds(pl.multiple_of(pl.program_id(0) * block + i * STEP, STEP), STEP)
            grad = cot_ref[own].astype(F32) * live
            running = jnp.zeros_like(grad)
            for j in range(layers):
                layer = history_part[j, rows].astype(F32)
                running = running + mix_ref[j] * layer
                terms = grad * layer
                terms = terms[: STEP // 2] + terms[STEP // 2 :]
                d_mix_ref[j] += sum(terms[:, k : k + 128] for k in range(0, tokens, 128))
            running_ref[own] = running

    whole = pl.BlockSpec((layers, block, tokens), lambda i: (0, i, 0))
    pltpu.emit_pipeline(body, grid=(features // block,), in_specs=[whole])(history_ref)


def d_history_kernel(all_tokens, block, mix_ref, counts_ref, cot_ref, sums, d_history_ref):
    layers, features, tokens = d_history_ref.shape
    factor = live_row(counts_ref, tokens, 0) * loss_scale(all_tokens, sums, tokens)

    def body(part):
        for i in range(block // STEP):
            rows = slice(i * STEP, (i + 1) * STEP)
            own = pl.ds(pl.multiple_of(pl.program_id(0) * block + i * STEP, STEP), STEP)
            grad = cot_ref[own].astype(F32) * factor
            for j in range(layers):
                part[j, rows] = (mix_ref[j] * grad).astype(BF16)

    whole = pl.BlockSpec((layers, block, tokens), lambda i: (0, i, 0))
    pltpu.emit_pipeline(body, grid=(features // block,), out_specs=[whole])(d_history_ref)


def history_call(body, outs, in_hbm, out_hbm, scalars, arrays):
    vmem, hbm = pl.BlockSpec(memory_space=pltpu.VMEM), pl.BlockSpec(memory_space=pltpu.HBM)
    arrays = [after(arrays[0], Order.last), *arrays[1:]]
    found = pl.pallas_call(
        body,
        out_shape=outs,
        in_specs=[pl.BlockSpec(memory_space=pltpu.SMEM)] * len(scalars) + [hbm if h else vmem for h in in_hbm],
        out_specs=tuple(hbm if h else vmem for h in out_hbm),
        compiler_params=pltpu.CompilerParams(vmem_limit_bytes=12 * 1024 * 1024),
        cost_estimate=Order.estimate(),
    )(*scalars, *arrays)
    Order.last = found[0]
    return found


def spread_of(load, count, width, total=None):
    zero = jnp.zeros((STEP, width), F32)
    if total is None:
        total = each_rows(count, lambda i, acc: acc + load(i), zero)
    mean = column_sum(total) / count

    def squares(i, acc):
        centred = load(i) - mean
        return acc + centred * centred

    return mean, lax.rsqrt(column_sum(each_rows(count, squares, zero)) / count + EPSILON)


def prepare_kernel(held, *refs):
    refs = refs[held:]
    sources, x_in, (own, norms, cosine, sine), places, sem = refs[:6], refs[6], refs[7:11], refs[11:17], refs[17]
    copies = [pltpu.make_async_copy(*pair, sem.at[i]) for i, pair in enumerate(zip(sources, places))]
    whole = pltpu.make_async_copy(x_in, own, sem.at[6])
    for copy in [*copies, whole]:
        copy.start()
    norms[...] = jnp.zeros_like(norms)
    for copy in copies:
        copy.wait()
    positions, rates, *vectors = places
    for i, ref in enumerate(vectors):
        norms[i : i + 1, : ref.shape[1]] = ref[...]
    angles = positions[...].astype(F32) * rates[...]
    cosine[...] = jnp.cos(angles)
    sine[...] = jnp.sin(angles)
    whole.wait()


def prepare(held, x_in, *sources):
    tokens, part = sources[0].shape[1], sources[2].shape[1]
    rates = sources[1].shape[0]
    vmem = pl.BlockSpec(memory_space=pltpu.VMEM)
    found = pl.pallas_call(
        functools.partial(prepare_kernel, len(held)),
        out_shape=(
            shape(part, tokens, kind=BF16),
            shape(8, -(-part // 128) * 128),
            shape(rates, tokens),
            shape(rates, tokens),
        ),
        in_specs=[vmem] * len(held) + [pl.BlockSpec(memory_space=pltpu.HBM)] * (len(sources) + 1),
        out_specs=(vmem,) * 4,
        scratch_shapes=[pltpu.VMEM(v.shape, v.dtype) for v in sources] + [pltpu.SemaphoreType.DMA((len(sources) + 1,))],
        compiler_params=pltpu.CompilerParams(vmem_limit_bytes=4 * 1024 * 1024),
        cost_estimate=Order.estimate(),
    )(*held, *(pltpu.with_memory_space_constraint(v, pltpu.HBM) for v in (*sources, x_in)))
    Order.last = found[0]
    return found


def norms_kernel(at_ref, n01, n23, norms):
    part = norms.shape[0] // 4
    near, far = n01[...].T, n23[...].T
    for e, norm in enumerate((near, near, far, far)):
        rows = pl.ds(pl.multiple_of((at_ref[0] ^ e) * part, 64), part)
        norms[rows, :] = norm[:part, 8 * (e % 2) : 8 * (e % 2) + 8]


def project_kernel(
    at_ref, x0, x1, x2, x3, norms, cosine, sine, w_qkv, x_all, normed, stats, qkv, project
):
    at = at_ref[0]
    part, tokens = x0.shape
    model = w_qkv.shape[1]
    for e, piece in enumerate((x0, x1, x2, x3)):
        x_all[pl.ds(pl.multiple_of((at ^ e) * part, 64), part), :] = piece[...]
    mean, scale = spread_of(lambda i: x_all[rows_at(i), :].astype(F32), model, tokens)
    stats[0:1] = mean
    stats[1:2] = scale

    def normalise(i, _):
        rows = rows_at(i)
        xhat = (x_all[rows, :].astype(F32) - mean) * scale
        normed[rows, :] = (xhat * norms[rows, 0:1] + norms[rows, 1:2]).astype(BF16)

    each_rows(model, normalise)
    project[...] = dot(w_qkv[...], normed[...], 1, 0)
    width = HEAD_DIM // 2
    for block, factor in ((0, HEAD_DIM ** (-0.5)), (1, 1.0)):
        for start in range(block * part, (block + 1) * part, HEAD_DIM):
            front, back = project[start : start + width], project[start + width : start + HEAD_DIM]
            cos, sin = cosine[...] * factor, sine[...] * factor
            qkv[start : start + width] = (front * cos - back * sin).astype(BF16)
            qkv[start + width : start + HEAD_DIM] = (back * cos + front * sin).astype(BF16)
    qkv[2 * part :] = project[2 * part :].astype(BF16)


def attention_kernel(
    at_ref, qkv, x_all, heads_send, heads_own, x_half, heads_out, probs, scores
):
    at = at_ref[0]
    part, tokens = heads_out.shape
    half = tokens // 2
    for h in range(part // HEAD_DIM):
        head = slice(h * HEAD_DIM, (h + 1) * HEAD_DIM)
        for t in range(2):
            now = slice(t * half, (t + 1) * half)
            count = (t + 1) * half
            query = qkv[head, now]
            key = qkv[part + h * HEAD_DIM : part + (h + 1) * HEAD_DIM, :count]
            value = qkv[2 * part + h * HEAD_DIM : 2 * part + (h + 1) * HEAD_DIM, :count]
            scores[:count] = dot(key, query, 0, 0)

            def masked(i):
                behind = lax.broadcasted_iota(jnp.int32, (STEP, half), 0) + (i * STEP - t * half)
                ahead = lax.broadcasted_iota(jnp.int32, (STEP, half), 1)
                return jnp.where(behind <= ahead, scores[rows_at(i), :], -1e30)

            def raised(found, i, acc):
                found = jnp.exp(found - top)
                scores[rows_at(i), :] = found
                return acc + found

            def settle(i, _):
                rows = rows_at(i)
                probs[h, rows, now] = (scores[rows, :] * divisor).astype(BF16)

            top = each_rows(
                t * half, lambda i, acc: jnp.maximum(acc, scores[rows_at(i), :]), jnp.full((STEP, half), -1e30, F32)
            )
            top = each_rows(count, lambda i, acc: jnp.maximum(acc, masked(i)), top, first=t * half)
            top = jnp.max(top, axis=0, keepdims=True)
            total = each_rows(
                t * half, lambda i, acc: raised(scores[rows_at(i), :], i, acc), jnp.zeros((STEP, half), F32)
            )
            total = each_rows(count, lambda i, acc: raised(masked(i), i, acc), total, first=t * half)
            divisor = 1.0 / column_sum(total)
            each_rows(count, settle)
            heads_out[head, now] = dot(value, probs[h, :count, now], 1, 0).astype(BF16)
    own = pl.multiple_of((at % 2) * half, half)
    other = pl.multiple_of((1 - at % 2) * half, half)
    heads_send[...] = heads_out[:, pl.ds(other, half)]
    heads_own[...] = heads_out[:, pl.ds(own, half)]
    x_half[...] = x_all[:, pl.ds(own, half)]


def output_gradient_kernel(
    at_ref, self_ref, counts_ref, c0, c1, c2, c3, w_down, g_out, d_active, cot_all
):
    at = at_ref[0]
    part, tokens = c0.shape
    half = tokens // 2
    for e, piece in enumerate((c0, c1, c2, c3)):
        cot_all[pl.ds(pl.multiple_of((at ^ e) * part, 64), part), :] = piece[...]
    for place, side in enumerate((at % 2, 1 - at % 2)):
        now = pl.ds(pl.multiple_of(side * half, half), half)
        factor = live_row(counts_ref, half, side * half)

        def scale(i, _, now=now, factor=factor, place=place):
            rows = rows_at(i)
            grad = cot_all[rows, now].astype(F32) * factor
            g_out[rows, place * half : (place + 1) * half] = (self_ref[0] * grad).astype(BF16)

        each_rows(cot_all.shape[0], scale)
    d_active[...] = dot(w_down[...], g_out[...], 1, 0)


def rows_kernel(at_ref, *refs):
    out = refs[-1]
    for e, piece in enumerate(refs[:-1]):
        rows = piece.shape[0]
        out[pl.ds(pl.multiple_of((at_ref[0] ^ e) * rows, 64), rows), :] = piece[...]


def middle_kernel(at_ref, pair, pair_far, w_all, x_half, norms, middle, stats, normed, heads):
    model, half = x_half.shape
    part = pair.shape[0] // 2
    for e, piece in enumerate((pair[:part], pair[part:], pair_far[:part], pair_far[part:])):
        heads[pl.ds(pl.multiple_of((at_ref[0] ^ e) * part, 64), part), :] = piece
    middle[...] = dot(w_all[...], heads[...], 0, 0)

    def add(i, acc):
        rows = rows_at(i)
        found = x_half[rows, :].astype(F32) + middle[rows, :]
        middle[rows, :] = found
        return acc + found

    total = each_rows(model, add, jnp.zeros((STEP, half), F32))
    mean, scale = spread_of(lambda i: middle[rows_at(i), :], model, half, total)
    stats[0:1] = mean
    stats[1:2] = scale

    def normalise(i, _):
        rows = rows_at(i)
        xhat = (middle[rows, :] - mean) * scale
        normed[rows, :] = (xhat * norms[rows, 2:3] + norms[rows, 3:4]).astype(BF16)

    each_rows(model, normalise)


def feed_forward_kernel(own, other, w_up, d_active, normed, active, d_hidden, send, keep, hidden):
    half = own.shape[1]
    normed[:, :half] = own[...]
    normed[:, half:] = other[...]
    hidden[...] = dot(w_up[...], normed[...], 0, 0)

    def bend(i, _):
        rows = rows_at(i)
        u = hidden[rows, :]
        squared = u * u
        curve = jnp.tanh(0.7978845608028654 * u * (1.0 + 0.044715 * squared))
        lifted = 0.5 * (1.0 + curve)
        active[rows, :] = (u * lifted).astype(BF16)
        slope = lifted + u * (0.5 * (1.0 - curve * curve)) * (
            0.7978845608028654 + (3 * 0.044715 * 0.7978845608028654) * squared
        )
        d_hidden[rows, :] = (slope * d_active[rows, :]).astype(BF16)

    each_rows(hidden.shape[0], bend)
    send[...] = dot(w_up[...], d_hidden[:, half:], 1, 0).astype(BF16)
    keep[...] = dot(w_up[...], d_hidden[:, :half], 1, 0)


def store_blocks(at, total, part, near, *outs):
    for e, out in zip(near, outs):
        out[...] = total[pl.ds(pl.multiple_of((at ^ e) * part, 64), part), :].astype(out.dtype)


def output_kernel(at_ref, counts_ref, active, w_down, middle, cot_all, send, send_far, keep, keep_far, product, total):
    at = at_ref[0]
    model, half = middle.shape
    part = send.shape[0]
    own = pl.ds(pl.multiple_of((at % 2) * half, half), half)
    other = pl.ds(pl.multiple_of((1 - at % 2) * half, half), half)
    total[:, own] = dot(w_down[...], active[:, :half], 0, 0) + 0.5 * middle[...]
    total[:, other] = dot(w_down[...], active[:, half:], 0, 0)
    live = live_row(counts_ref, 2 * half, 0)

    def weigh(i, acc):
        rows = rows_at(i)
        return acc + fold_lanes(total[rows, :] * (cot_all[rows, :].astype(F32) * live))

    product[...] = each_rows(model, weigh, jnp.zeros((STEP, 128), F32))
    store_blocks(at, total, part, (1, 3, 0, 2), send, send_far, keep, keep_far)


def fold_lanes(value):
    return sum(value[:, k : k + 128] for k in range(0, value.shape[1], 128))


def as_row(columns):
    return column_sum(columns[...].T)


def middle_gradient_kernel(
    at_ref, self_ref, counts_ref, chip, received, middle, stats, cot_all, norms,
    d_middle, g_mid, gains, d_normed, gain_sums, bias_sums,
):
    model, half = chip.shape
    mean, scale = stats[0:1], stats[1:2]
    zero = jnp.zeros((STEP, half), F32)

    def sums(i, acc):
        rows = rows_at(i)
        grad = chip[rows, :] + received[rows, :].astype(F32)
        d_normed[rows, :] = grad
        xhat = (middle[rows, :] - mean) * scale
        both = grad * xhat
        gain_sums[rows, :] = fold_lanes(both)
        bias_sums[rows, :] = fold_lanes(grad)
        gain = norms[rows, 2:3]
        return acc[0] + grad * gain, acc[1] + both * gain

    first, second = (column_sum(v) / model for v in each_rows(model, sums, (zero, zero)))
    side = (at_ref[0] % 2) * half
    factor = self_ref[0] * live_row(counts_ref, half, side)
    own = pl.ds(pl.multiple_of(side, half), half)

    def finish(i, _):
        rows = rows_at(i)
        xhat = (middle[rows, :] - mean) * scale
        found = cot_all[rows, own].astype(F32) * factor + scale * (
            d_normed[rows, :] * norms[rows, 2:3] - first - xhat * second
        )
        d_middle[rows, :] = found
        g_mid[rows, :] = found.astype(BF16)

    each_rows(model, finish)
    gains[0:1] = as_row(gain_sums)
    gains[1:2] = as_row(bias_sums)


def attention_gradient_kernel(
    at_ref, own, other, w_out, qkv, probs, cosine, sine,
    d_project, g_mid, d_heads, d_scores, products, d_queries, d_keys, d_values,
):
    at = at_ref[0]
    half = own.shape[1]
    part = w_out.shape[0]
    g_mid[:, pl.ds(pl.multiple_of((at % 2) * half, half), half)] = own[...]
    g_mid[:, pl.ds(pl.multiple_of((1 - at % 2) * half, half), half)] = other[...]
    d_heads[...] = dot(w_out[...], g_mid[...], 1, 0).astype(BF16)
    width = HEAD_DIM // 2
    for h in range(part // HEAD_DIM):
        head = slice(h * HEAD_DIM, (h + 1) * HEAD_DIM)
        query = qkv[head]
        key = qkv[part + h * HEAD_DIM : part + (h + 1) * HEAD_DIM]
        value = qkv[2 * part + h * HEAD_DIM : 2 * part + (h + 1) * HEAD_DIM]
        for t in range(2):
            now = slice(t * half, (t + 1) * half)
            count = (t + 1) * half
            products[:count] = dot(value[:, :count], d_heads[head, now], 0, 0)

            def weigh(i, acc):
                rows = rows_at(i)
                return acc + products[rows, :] * probs[h, rows, now].astype(F32)

            inner = column_sum(each_rows(count, weigh, jnp.zeros((STEP, half), F32)))

            def settle(i, _):
                rows = rows_at(i)
                d_scores[rows, :] = (probs[h, rows, now].astype(F32) * (products[rows, :] - inner)).astype(BF16)

            each_rows(count, settle)
            d_queries[:, now] = dot(key[:, :count], d_scores[:count], 1, 0) * HEAD_DIM ** (-0.5)
            d_key = dot(query[:, now], d_scores[:count], 1, 1)
            d_value = dot(d_heads[head, now], probs[h, :count, now], 1, 1)
            if t == 0:
                d_keys[:, :half] = d_key
                d_values[:, :half] = d_value
            else:
                d_keys[:, :half] += d_key[:, :half]
                d_values[:, :half] += d_value[:, :half]
                d_keys[:, half:] = d_key[:, half:]
                d_values[:, half:] = d_value[:, half:]
        for block, found in ((0, d_queries), (1, d_keys)):
            start = block * part + h * HEAD_DIM
            front, back = found[:width], found[width:]
            d_project[start : start + width] = (front * cosine[...] + back * sine[...]).astype(BF16)
            d_project[start + width : start + HEAD_DIM] = (back * cosine[...] - front * sine[...]).astype(BF16)
        d_project[2 * part + h * HEAD_DIM : 2 * part + (h + 1) * HEAD_DIM] = d_values[...].astype(BF16)


def input_gradient_kernel(
    width, at_ref, counts_ref, d_project, w_qkv, x_all, stats, d_middle, norms, gains,
    send, send_far, keep, keep_far, sums, total, gain_sums, bias_sums,
):
    at = at_ref[0]
    model, half = d_middle.shape
    tokens = x_all.shape[1]
    part = send.shape[0]
    total[...] = dot(w_qkv[...], d_project[...], 0, 0)
    mean, scale = stats[0:1], stats[1:2]
    zero = jnp.zeros((STEP, tokens), F32)
    own = pl.ds(pl.multiple_of((at % 2) * half, half), half)

    def body(i, acc):
        rows = rows_at(i)
        grad = total[rows, :]
        xhat = (x_all[rows, :].astype(F32) - mean) * scale
        both = grad * xhat
        gain_sums[rows, :] = fold_lanes(both)
        bias_sums[rows, :] = fold_lanes(grad)
        gain = norms[rows, 0:1]
        lifted = grad * gain
        total[rows, :] = lifted * scale
        total[rows, own] += 0.5 * d_middle[rows, :]
        return acc[0] + lifted, acc[1] + both * gain

    first, second = each_rows(model, body, (zero, zero))
    store_blocks(at, total, part, (1, 3, 0, 2), send, send_far, keep, keep_far)
    sums[...] = jnp.zeros_like(sums)
    sums[0:1] = as_row(gain_sums)
    sums[1:2] = as_row(bias_sums)
    sums[2:4] = 0.5 * gains[...]
    sums[4:5, :tokens] = column_sum(first) / model
    sums[5:6, :tokens] = column_sum(second) / model
    sums[7:8] = jnp.zeros((1, model), F32) + counts_ref[0].astype(F32) / width


def mixed_kernel(self_ref, own, near, far, running, d_mix, product, sums, mixed, all_sums, table):
    layers = d_mix.shape[0]

    def body(i, _):
        rows = rows_at(i)
        output = own[rows, :] + near[rows, :].astype(F32) + far[rows, :].astype(F32)
        mixed[rows, :] = (self_ref[0] * output + running[rows, :]).astype(BF16)

    each_rows(own.shape[0], body)
    table[...] = jnp.zeros_like(table)
    table[:layers] = jnp.sum(d_mix[...], axis=1)
    table[layers : layers + 1] = column_sum(product[...])
    all_sums[...] = sums[...]
    all_sums[6:7, :128] = as_row(table)


def ends_kernel(all_tokens, layers, width, at_ref, sums, d_mix, d_self, *ends):
    part = ends[0].shape[1]
    scale = loss_scale(all_tokens, sums, sums.shape[1])
    d_mix[...] = sums[6:7, :layers] * scale[:, :layers]
    d_self[...] = sums[6:7, layers : layers + 1] * scale[:, :1]
    for i, end in enumerate(ends):
        scaled = sums[i : i + 1] * scale
        found = scaled[:, :part]
        for w in range(1, width):
            found = jnp.where(at_ref[0] == w, scaled[:, w * part : (w + 1) * part], found)
        end[...] = found


def d_input_kernel(own, near, far, x_in, stats, row_sums, found):
    part, tokens = own.shape
    mean, scale = stats[0:1], stats[1:2]
    first, second = row_sums[4:5, :tokens], row_sums[5:6, :tokens]

    def body(i, _):
        rows = rows_at(i)
        xhat = (x_in[rows, :].astype(F32) - mean) * scale
        total = own[rows, :] + near[rows, :].astype(F32) + far[rows, :].astype(F32)
        found[rows, :] = total - scale * (first + xhat * second)

    each_rows(part, body)


def scale_kernel(all_tokens, found, sums, d_input):
    factor = loss_scale(all_tokens, sums, found.shape[1])

    def body(i, _):
        d_input[rows_at(i), :] = found[rows_at(i), :] * factor

    each_rows(found.shape[0], body)


def local(
    width,
    row_devices,
    x_in,
    history,
    cotangent,
    counts,
    positions,
    mix_weights,
    self_weight,
    first_norm_gain,
    first_norm_bias,
    w_qkv,
    w_out,
    second_norm_gain,
    second_norm_bias,
    w_up,
    w_down,
):
    part, tokens = x_in.shape
    model = w_out.shape[1]
    hidden_units = w_up.shape[1]
    half = tokens // 2
    layers = mix_weights.shape[0]
    all_tokens = float(tokens * row_devices)
    at = lax.axis_index("width").astype(jnp.int32)[None]
    me = lax.axis_index("rows").astype(jnp.int32)[None]
    Order.last, Order.front = None, FRONT
    to_width = lambda value, offset: xor_send(value, "width", width, offset)
    to_row = lambda value, offset: xor_send(value, "rows", row_devices, offset)
    w_qkv = w_qkv.reshape(3 * part, model)
    rates = 1.0 / 10000.0 ** (np.arange(HEAD_DIM // 2) * 2.0 / HEAD_DIM)
    x_in, cotangent, counts = after((x_in, cotangent, counts), at, me)

    x_far, x_near = to_width(x_in, 2), to_width(x_in, 1)
    x_own, norms, cosine, sine = prepare(
        [x_near],
        x_in,
        positions[None, :],
        jnp.asarray(rates[:, None], F32),
        *(v[None, :] for v in (first_norm_gain, first_norm_bias, second_norm_gain, second_norm_bias)),
    )
    norms_near = join([norms, to_width(norms, 1)])
    norms_far = to_width(norms_near, 2)
    norms = kernel(norms_kernel, shape(model, 8), [at], [norms_near, norms_far])
    x_both = to_width(after(x_far, norms), 1)
    w_now = after(w_out, norms_near)
    w_far, w_near = to_width(w_now, 2), to_width(w_now, 1)

    x_all, normed_one, stats_one, qkv = kernel(
        project_kernel,
        (
            shape(model, tokens, kind=BF16),
            shape(model, tokens, kind=BF16),
            shape(2, tokens),
            shape(3 * part, tokens, kind=BF16),
        ),
        [at],
        [x_own, x_near, x_far, x_both, norms, cosine, sine, w_qkv],
        [pltpu.VMEM((3 * part, tokens), F32)],
    )
    heads_send, heads_own, x_half, heads_out, probs = kernel(
        attention_kernel,
        (
            shape(part, half, kind=BF16),
            shape(part, half, kind=BF16),
            shape(model, half, kind=BF16),
            shape(part, tokens, kind=BF16),
            shape(part // HEAD_DIM, tokens, tokens, kind=BF16),
        ),
        [at],
        [qkv, x_all],
        [pltpu.VMEM((tokens, half), F32)],
    )
    pair = join([after(heads_own, w_far), to_width(heads_send, 1)])
    pair_far = to_width(pair, 2)
    cot_now = after(cotangent, pair)
    cot_far, cot_near = to_width(cot_now, 2), to_width(cot_now, 1)
    w_both = to_width(after(w_far, pair), 1)

    w_all = kernel(rows_kernel, shape(model, model, kind=BF16), [at], [w_out, w_near, w_far, w_both])
    middle, stats_two, normed_own = kernel(
        middle_kernel,
        (shape(model, half), shape(2, half), shape(model, half, kind=BF16)),
        [at],
        [pair, pair_far, w_all, x_half, norms],
        [pltpu.VMEM((model, half), BF16)],
    )
    normed_near = to_width(normed_own, 1)
    cot_both = to_width(after(cot_far, middle), 1)
    g_out, d_active, cot_all = kernel(
        output_gradient_kernel,
        (shape(model, tokens, kind=BF16), shape(hidden_units, tokens), shape(model, tokens, kind=BF16)),
        [at, self_weight, counts],
        [cotangent, cot_near, cot_far, cot_both, w_down],
    )

    normed_two, active, d_hidden, send, keep = kernel(
        feed_forward_kernel,
        (
            shape(model, tokens, kind=BF16),
            shape(hidden_units, tokens, kind=BF16),
            shape(hidden_units, tokens, kind=BF16),
            shape(model, half, kind=BF16),
            shape(model, half),
        ),
        [],
        [normed_own, normed_near, w_up, d_active],
        [pltpu.VMEM((hidden_units, tokens), F32)],
    )

    v = Values()
    v.send, v.keep = send, keep
    down = Stream(row_devices, 0, hidden_units, "halving")
    up = Stream(row_devices, 0, model, "crossed")
    first = Stream(row_devices, 0, 2 * part, "halving")
    second = Stream(row_devices, 2 * part, 2 * part, "crossed")
    strides = [1 << i for i in range(row_devices.bit_length() - 1)]
    blocks = (shape(part, tokens, kind=BF16),) * 2 + (shape(part, tokens),) * 2
    last = len(down.digits) - 1

    def scatter(stream, stage):
        stream.held = add_stage(stream, stream.held, stream.got, stage)
        stream.got = start_stage(stream, stream.held, stage + 1)

    def turn(stream):
        value = sum_rest(stream, add_stage(stream, stream.held, stream.got, last)[0])
        stream.pieces = gather_stage(stream, value, last)

    def gather(stream, stage):
        stream.pieces = gather_stage(stream, join(stream.pieces), stage)

    def steps_of(stream):
        return (
            *(functools.partial(scatter, stream, stage) for stage in range(last)),
            functools.partial(turn, stream),
            *(functools.partial(gather, stream, stage) for stage in range(last - 1, -1, -1)),
        )

    def begin(streams, found):
        for stream, parts in zip(streams, found):
            stream.held, stream.got = parts, start_stage(stream, parts, 0)

    def down_product():
        begin([down], weight_gradient(me, [down], active, g_out))

    def up_product():
        begin([up], weight_gradient(me, [up], normed_two, d_hidden))

    def tail_product():
        found = weight_gradient(me, [first, second], v.d_project, normed_one, heads_out, v.g_mid)
        begin([first, second], found)

    def middle_sum():
        v.chip, sent = add([v.keep, to_width(v.send, 1)], (0, model, F32), (0, model, BF16))
        v.received = to_width(sent, 2)

    def output_product():
        near, far, v.out, v.out_far, v.product = kernel(
            output_kernel,
            blocks + (shape(STEP, 128),),
            [at, counts],
            [active, w_down, middle, cot_all],
            [pltpu.VMEM((model, tokens), F32)],
        )
        v.out_got = to_width(near, 1), to_width(far, 1)

    def history_sums():
        v.running, v.d_mix = history_call(
            functools.partial(history_kernel, 32),
            (shape(part, tokens), shape(layers, STEP // 2, 128)),
            (False, True),
            (False, False),
            [mix_weights, counts],
            [cotangent, pltpu.with_memory_space_constraint(history, pltpu.HBM)],
        )

    def output_sum():
        v.out_last = to_width(add([v.out_far, v.out_got[1]], (0, part, BF16))[0], 2)

    def middle_gradient():
        v.d_middle, v.g_own, v.gains = kernel(
            middle_gradient_kernel,
            (shape(model, half), shape(model, half, kind=BF16), shape(2, model)),
            [at, self_weight, counts],
            [v.chip, v.received, middle, stats_two, cot_all, norms],
            [pltpu.VMEM((model, half), F32), pltpu.VMEM((model, 128), F32), pltpu.VMEM((model, 128), F32)],
        )
        v.g_other = to_width(v.g_own, 1)

    def attention_gradient():
        v.d_project, v.g_mid = kernel(
            attention_gradient_kernel,
            (shape(3 * part, tokens, kind=BF16), shape(model, tokens, kind=BF16)),
            [at],
            [v.g_own, v.g_other, w_out, qkv, probs, cosine, sine],
            [
                pltpu.VMEM((part, tokens), BF16),
                pltpu.VMEM((tokens, half), BF16),
                pltpu.VMEM((tokens, half), F32),
                pltpu.VMEM((HEAD_DIM, tokens), F32),
                pltpu.VMEM((HEAD_DIM, tokens), F32),
                pltpu.VMEM((HEAD_DIM, tokens), F32),
            ],
        )

    def input_gradient():
        near, far, v.own_in, v.in_far, v.sums = kernel(
            functools.partial(input_gradient_kernel, width),
            blocks + (shape(8, model),),
            [at, counts],
            [v.d_project, w_qkv, x_all, stats_one, v.d_middle, norms, v.gains],
            [pltpu.VMEM((model, tokens), F32), pltpu.VMEM((model, 128), F32), pltpu.VMEM((model, 128), F32)],
        )
        v.in_got = to_width(near, 1), to_width(far, 1)

    def input_sum():
        v.in_last = to_width(add([v.in_far, v.in_got[1]], (0, part, BF16))[0], 2)

    def input_total():
        v.in_total = kernel(
            d_input_kernel,
            shape(part, tokens),
            [],
            [v.own_in, v.in_got[0], v.in_last, x_own, stats_one, v.row_sums],
        )

    def mix():
        v.mixed, v.sums = kernel(
            mixed_kernel,
            (shape(part, tokens, kind=BF16), shape(8, model)),
            [self_weight],
            [
                v.out,
                v.out_got[0],
                v.out_last,
                v.running,
                v.d_mix,
                v.product,
                v.sums,
            ],
            [pltpu.VMEM((128, 128), F32)],
        )
        v.sums_got = to_width(v.sums, 1)

    def sums_step(*sends):
        for send_on in sends:
            v.sums = add([v.sums, v.sums_got], (0, 8, F32))[0]
            v.sums_got = send_on(v.sums)

    def sums_1():
        sums_step(lambda value: to_width(value, 2))

    def sums_2():
        sums_step(row_send(strides[0]))
        v.row_sums = v.sums

    def sums_3():
        sums_step(row_send(strides[1]))

    def sums_4():
        sums_step(*(row_send(stride) for stride in strides[2:]))

    def last_sums():
        v.sums = add([v.sums, v.sums_got], (0, 8, F32))[0]

    def scale_input():
        v.d_input = kernel(
            functools.partial(scale_kernel, all_tokens), shape(part, tokens), [], [v.in_total, v.sums]
        )

    def history_gradient():
        v.d_history = history_call(
            functools.partial(d_history_kernel, all_tokens, 32),
            (shape(*history.shape, kind=BF16),),
            (False, False),
            (True,),
            [mix_weights, counts],
            [cotangent, v.sums],
        )[0]

    def ends():
        v.ends = kernel(
            functools.partial(ends_kernel, all_tokens, layers, width),
            (shape(1, layers), shape(1, 1)) + (shape(1, part),) * 4,
            [at],
            [v.sums],
        )

    def placed(streams, *sizes):
        pieces = [piece for stream in streams for piece in stream.pieces]
        return place(all_tokens, me, v.sums, streams, pieces, sizes)

    def place_down():
        v.d_w_down = placed([down], hidden_units)[0]

    def place_up():
        v.d_w_up = placed([up], model)[0]

    def place_tail():
        v.d_w_qkv, v.d_w_out = placed([first, second], 3 * part, part)

    row_send = lambda stride: lambda value: to_row(value, stride)
    down_1, down_2, down_3, down_4, down_5 = steps_of(down)
    up_1, up_2, up_3, up_4, up_5 = steps_of(up)
    first_1, first_2, first_3, first_4, first_5 = steps_of(first)
    second_1, second_2, second_3, second_4, second_5 = steps_of(second)
    schedule = (
        (down_product, 10),
        (middle_sum, 8),
        (up_product, 10),
        (output_product, 100),
        (history_sums, 10),
        (middle_gradient, 10),
        (output_sum, 10),
        (down_1, 10),
        (up_1, 100),
        (attention_gradient, 10),
        (tail_product, 4),
        (down_2, 100),
        (up_2, 0.3),
        (up_3, 100),
        (input_gradient, 1),
        (mix, 8),
        (first_1, 1),
        (second_1, 1),
        (down_3, 1),
        (first_2, 2),
        (sums_1, 4),
        (sums_2, 1),
        (input_sum, 1),
        (sums_3, 1),
        (second_2, 1),
        (up_4, 2),
        (sums_4, 1),
        (down_4, 4),
        (first_3, 40),
        (second_3, 2),
        (input_total, 1),
        (down_5, 1),
        (first_4, 200),
        (second_4, 16),
        (last_sums, 1),
        (up_5, 0.3),
        (first_5, 40),
        (second_5, 200),
        (ends, 200),
        (history_gradient, 1),
        (scale_input, 0.1),
        (place_down, 1),
        (place_up, 4),
        (place_tail, 1),
    )
    for step, weight in schedule:
        Order.cost = weight
        step()
    d_mix, d_self, *vectors = v.ends
    return (
        v.mixed,
        v.d_input,
        v.d_history,
        d_mix[0],
        d_self[0],
        vectors[0][0],
        vectors[1][0],
        v.d_w_qkv.reshape(3, part, model),
        v.d_w_out,
        vectors[2][0],
        vectors[3][0],
        v.d_w_up,
        v.d_w_down,
    )


def solution(mesh):
    return jax.shard_map(
        functools.partial(local, mesh.shape["width"], mesh.shape["rows"]),
        mesh=mesh,
        in_specs=(
            P("width", "rows"),
            P(None, "width", "rows"),
            P("width", "rows"),
            P("rows"),
            P("rows"),
            P(),
            P(),
            P("width"),
            P("width"),
            P(None, "width", None),
            P("width", None),
            P("width"),
            P("width"),
            P(None, "width"),
            P("width", None),
        ),
        out_specs=(
            P("width", "rows"),
            P("width", "rows"),
            P(None, "width", "rows"),
            P(),
            P(),
            P("width"),
            P("width"),
            P(None, "width", None),
            P("width", None),
            P("width"),
            P("width"),
            P(None, "width"),
            P("width", None),
        ),
        check_vma=False,
    )
```
